32 devices in a mesh: pages: 8 (over z, y), heads: 4 (over x, core).
Axes of the slice: x: 2, y: 2, z: 4, core: 2. Of those that a mesh axis runs over, the one named last changes fastest.
Arguments:
- tokens: bfloat16 [32, 561, 768], P(('pages', 'heads')), may hold values from -6 to 6
- w_qkv: bfloat16 [768, 3, 768], P(None, None, 'heads'), may hold values from -0.21875 to 0.21875
- qv_bias: float32 [2, 768], P(None, 'heads'), may hold values from -0.625 to 0.625
- w_out: bfloat16 [768, 768], P('heads'), may hold values from -2 to 2
- out_bias: float32 [768], replicated, may hold values from -1.75 to 1.75
- norm1_gain: float32 [768], replicated, may hold values from 0.5 to 1.5
- norm1_shift: float32 [768], replicated, may hold values from -1.75 to 1.75
- w_up: bfloat16 [768, 3072], P(None, 'heads'), may hold values from -0.21875 to 0.21875
- up_bias: bfloat16 [3072], P('heads'), may hold values from -1.75 to 1.75
- w_down: bfloat16 [3072, 768], P('heads'), may hold values from -0.109375 to 0.109375
- down_bias: float32 [768], replicated, may hold values from -1.75 to 1.75
- norm2_gain: float32 [768], replicated, may hold values from 0.5 to 1.5
- norm2_shift: float32 [768], replicated, may hold values from -1.75 to 1.75
- pos_table: float32 [12, 32], P('heads'), may hold values from -3 to 3
- box_table: float32 [2, 12, 64], P(None, 'heads'), may hold values from -3 to 3
- receipt_lengths: int32 [32, 8], P('pages'), may hold values from 1 to 128, 512 in all within a row
- page_boxes: int32 [32, 2, 561], P('pages'), may hold values from 0 to 1000
- out_cotangent: bfloat16 [32, 561, 768], P(('pages', 'heads')), may hold values from -6 to 6
Outputs:
- layer_out: bfloat16 [32, 561, 768], P(('pages', 'heads'))
- grad_tokens: bfloat16 [32, 561, 768], P(('pages', 'heads'))
- grad_w_qkv: float32 [768, 3, 768], P('pages', None, 'heads')
- grad_qv_bias: float32 [2, 768], P(None, 'heads')
- grad_w_out: float32 [768, 768], P('heads', 'pages')
- grad_out_bias: float32 [768], replicated
- grad_norm1_gain: float32 [768], replicated
- grad_norm1_shift: float32 [768], replicated
- grad_w_up: float32 [768, 3072], P('pages', 'heads')
- grad_up_bias: float32 [3072], P('heads')
- grad_w_down: float32 [3072, 768], P('heads', 'pages')
- grad_down_bias: float32 [768], replicated
- grad_norm2_gain: float32 [768], replicated
- grad_norm2_shift: float32 [768], replicated
- grad_pos_table: float32 [12, 32], P('heads')
- grad_box_table: float32 [2, 12, 64], P(None, 'heads')
The draws below stay inside these ranges and needn't reach their ends.
Inputs may be any that keep to these rules, and one draw needn't show every extreme that they name: `receipt_lengths`: each page's 8 receipt lengths sum to 512.
All inputs are finite; a program needn't handle non-finite values.
Results may differ from the reference program's by a relative error of at most 0.02.
Values may be sent and summed in bfloat16 or wider, within the bound.
No kernel may reach another device: no remote copies, remote signals or barrier semaphores. Data moves between devices by JAX's collectives and lax.ppermute only.
A program may use at most 256 MiB of HBM per device.

```python
import math
import jax
import jax.numpy as jnp
import numpy as np
from jax import lax

D = 768
HEADS = 12
HEAD_DIM = 64
FF = 3072
TEXT = 512
NB1 = 32
MD1 = 128
NB2 = 64
MD2 = 256
RECEIPTS = 8
MOST = 128
LEN = 561
PAGES = 32


def set_ends(entries, own_key, least, high):
    longest = entries.shape.index(max(entries.shape))
    spots = []
    for shift in (0, 1):
        where = [jax.random.randint(jax.random.fold_in(own_key, axis), (), 0, length) for axis, length in enumerate(entries.shape)]
        where[longest] = (where[longest] + shift) % entries.shape[longest]
        spots.append(tuple(where))
    return entries.at[spots[0]].set(least).at[spots[1]].set(high)


def level_of(rng, shape, shards, least, top_value):
    gain, own = 1.0, jax.random.fold_in(rng, 6)
    for dim, shards_of in shards:
        heights = jnp.exp(jax.random.uniform(jax.random.fold_in(own, dim), (shards_of,), jnp.float32, least / len(shards), top_value / len(shards)))
        gain = gain * jnp.repeat(heights, shape[dim] // shards_of).reshape([-1 if axis == dim else 1 for axis in range(len(shape))])
    return gain


def split_up(number_of, total, most, slope):
    portions = [(1 << 20) // math.isqrt(grade ** slope) + 1 for grade in range(2, number_of + 1)]
    spare, given = total - most - (number_of - 1), [1] * (number_of - 1)
    while spare > 0:
        candidates = [i for i in range(number_of - 1) if given[i] < most]
        mass, budget = sum([portions[i] for i in candidates]), spare
        for i in candidates:
            extra = min(most - given[i], max(1, budget * portions[i] // mass), spare)
            given[i] = given[i] + extra
            spare = spare - extra
    return np.array([most] + given)


def ragged(own_key, amount, total, reach, slope):
    if amount == 2:
        one = jax.random.randint(own_key, (), max(1, total - reach), min(reach, total - 1) + 1)
        return jnp.stack([one, total - one])
    tallies = jnp.asarray(split_up(amount, total, reach, slope), jnp.int32)
    twos = (amount - 1) // 2
    donor, sink = tallies[1:1 + 2 * twos:2], tallies[2:2 + 2 * twos:2]
    slack = jnp.minimum(donor - 1, reach - sink)
    moved = jax.random.randint(jax.random.fold_in(own_key, 1), (twos,), 0, 1 << 20) % (slack + 1)
    tallies = tallies.at[1:1 + 2 * twos:2].set(donor - moved).at[2:2 + 2 * twos:2].set(sink + moved)
    return tallies[jax.random.permutation(jax.random.fold_in(own_key, 2), amount)]


def noise(rng, extent, width, most, pieces=(), held_as=jnp.bfloat16):
    values = width * jax.random.normal(rng, extent, jnp.float32)
    if pieces:
        values = values * level_of(rng, extent, pieces, -0.22, 0.18)
    return jnp.clip(values, -most, most).astype(held_as)


def setup_inputs(seed: int = 0) -> dict:
    streams_of = jax.random.split(jax.random.key(seed), 19)
    return {
        "tokens": noise(streams_of[0], (PAGES, LEN, D), 1.0, 6.0, ((0, 32),)),
        "w_qkv": noise(streams_of[1], (D, 3, D), D ** -0.5, 0.21875, ((2, 4),)),
        "qv_bias": noise(streams_of[2], (2, D), 0.1, 0.625, ((1, 4),), jnp.float32),
        "w_out": noise(streams_of[3], (D, D), (max(D // 96, 1)) ** -0.5, 2.0, ((0, 4),)),
        "out_bias": noise(streams_of[4], (D,), 0.3, 1.75, (), jnp.float32),
        "norm1_gain": jnp.clip(1.0 + 0.1 * jax.random.normal(streams_of[5], (D,), jnp.float32), 0.5, 1.5),
        "norm1_shift": noise(streams_of[6], (D,), 0.3, 1.75, (), jnp.float32),
        "w_up": noise(streams_of[7], (D, FF), D ** -0.5, 0.21875, ((1, 4),)),
        "up_bias": noise(streams_of[8], (FF,), 0.3, 1.75, ((0, 4),)),
        "w_down": noise(streams_of[9], (FF, D), FF ** -0.5, 0.109375, ((0, 4),)),
        "down_bias": noise(streams_of[10], (D,), 0.3, 1.75, (), jnp.float32),
        "norm2_gain": jnp.clip(1.0 + 0.1 * jax.random.normal(streams_of[11], (D,), jnp.float32), 0.5, 1.5),
        "norm2_shift": noise(streams_of[12], (D,), 0.3, 1.75, (), jnp.float32),
        "pos_table": noise(streams_of[13], (HEADS, NB1), 0.5, 3.0, ((0, 4),), jnp.float32),
        "box_table": noise(streams_of[14], (2, HEADS, NB2), 0.5, 3.0, ((1, 4),), jnp.float32),
        "receipt_lengths": jax.vmap(lambda own: ragged(own, RECEIPTS, TEXT, MOST, 1))(jax.random.split(streams_of[15], PAGES)).reshape((PAGES, RECEIPTS)).astype(jnp.int32),
        "page_boxes": set_ends(jax.random.randint(streams_of[16], (PAGES, 2, LEN), 0, 1001), jax.random.fold_in(streams_of[16], 1), 0, 1000).astype(jnp.int32),
        "out_cotangent": noise(streams_of[17], (PAGES, LEN, D), 1.0, 6.0, ((0, 32),)),
    }


@jax.custom_vjp
def low(v):
    return lax.optimization_barrier(v.astype(jnp.bfloat16)).astype(jnp.float32)

@jax.custom_vjp
def low_back(v):
    return v

def low_keep(v):
    return (low(v), None)

def low_pass(kept, grad):
    return (grad,)

def back_keep(v):
    return (v, None)

def back_low(kept, grad):
    return (low(grad),)
low.defvjp(low_keep, low_pass)
low_back.defvjp(back_keep, back_low)
EPSILON = 1e-05
MASKED_SCORE = -1e+30
PRECISE = lax.Precision.HIGHEST

def thresholds(buckets, max_reach):
    half_range = buckets // 2
    exact_range = half_range // 2
    levels = half_range - exact_range
    return np.array([math.ceil(exact_range * (max_reach / exact_range) ** (step_index / levels) - 1e-09) for step_index in range(1, levels)], dtype=np.int32)

def bucketed(offsets, buckets, max_reach):
    half_range = buckets // 2
    exact_range = half_range // 2
    distance = jnp.abs(offsets)
    bounds = jnp.asarray(thresholds(buckets, max_reach), dtype=jnp.int32)
    passed = lax.optimization_barrier(jnp.sum((distance[..., None] >= bounds).astype(jnp.int32), axis=-1, dtype=jnp.int32))
    inside = jnp.where(distance < exact_range, distance, exact_range + passed).astype(jnp.int32)
    return jnp.where(offsets > 0, half_range, 0).astype(jnp.int32) + inside

def page_masks(lengths, page_boxes):
    receipt_ends = jnp.cumsum(lengths.astype(jnp.int32), dtype=jnp.int32)
    positions = jnp.arange(LEN, dtype=jnp.int32)
    segment = lax.optimization_barrier(jnp.sum((positions[:, None] >= receipt_ends[None, :]).astype(jnp.int32), axis=1, dtype=jnp.int32))
    visual = positions >= TEXT
    allowed = (segment[:, None] == segment[None, :]) | visual[:, None] | visual[None, :]
    pos_ids = bucketed(positions[None, :] - positions[:, None], NB1, MD1)
    x_ids = bucketed(page_boxes[0][None, :] - page_boxes[0][:, None], NB2, MD2)
    y_ids = bucketed(page_boxes[1][None, :] - page_boxes[1][:, None], NB2, MD2)
    return (allowed, pos_ids, x_ids, y_ids)

def lookup(pos_table, box_table, pos_ids, x_ids, y_ids):
    return jnp.take(pos_table, pos_ids, axis=1) + jnp.take(box_table[0], x_ids, axis=1) + jnp.take(box_table[1], y_ids, axis=1)

def layer_norm(values, gain_vec, shift_vec):
    centered = values - lax.optimization_barrier(jnp.mean(values, axis=-1, keepdims=True))
    inv_std = lax.rsqrt(lax.optimization_barrier(jnp.mean(centered * centered, axis=-1, keepdims=True)) + EPSILON)
    return centered * inv_std * gain_vec + shift_vec

def layer_page(tokens, params, lengths, page_boxes):
    w_qkv, qv_bias, w_out, out_bias, norm1_gain, norm1_shift, w_up, up_bias, w_down, down_bias, norm2_gain, norm2_shift, pos_table, box_table = params
    allowed, pos_ids, x_ids, y_ids = page_masks(lengths, page_boxes)
    mixed_proj = jnp.dot(tokens, w_qkv.reshape(D, 3 * D), precision=PRECISE).reshape(LEN, 3, HEADS, HEAD_DIM)
    queries = low(low_back(mixed_proj[:, 0] + qv_bias[0].reshape(HEADS, HEAD_DIM)))
    keys_low = low(low_back(mixed_proj[:, 1]))
    values = low(low_back(mixed_proj[:, 2] + qv_bias[1].reshape(HEADS, HEAD_DIM)))
    raw_scores = low_back(jnp.einsum('qhd,khd->hqk', queries, keys_low, precision=PRECISE) * (1.0 / math.sqrt(HEAD_DIM)))
    scores = jnp.where(allowed[None], raw_scores + lookup(pos_table, box_table, pos_ids, x_ids, y_ids), MASKED_SCORE)
    row_max = lax.optimization_barrier(jnp.max(scores, axis=-1, keepdims=True))
    exponent = jnp.exp(scores - row_max)
    attn_weights = low(exponent / lax.optimization_barrier(jnp.sum(exponent, axis=-1, keepdims=True)))
    attended = low(low_back(jnp.einsum('hqk,khd->qhd', attn_weights, values, precision=PRECISE).reshape(LEN, D)))
    projected = low_back(jnp.dot(attended, w_out, precision=PRECISE))
    first_out = layer_norm(projected + out_bias + tokens, norm1_gain, norm1_shift)
    first_low = low(first_out)
    up_proj = low_back(jnp.dot(first_low, w_up, precision=PRECISE) + up_bias)
    hidden = low(jax.nn.gelu(up_proj, approximate=False))
    ffn_out = low_back(jnp.dot(hidden, w_down, precision=PRECISE))
    return layer_norm(ffn_out + down_bias + first_out, norm2_gain, norm2_shift)

def forward(tokens_f32, params, receipt_lengths, page_boxes):

    def one_page(page_items):
        return layer_page(page_items[0], params, page_items[1], page_items[2])
    return lax.map(jax.checkpoint(one_page), (tokens_f32, receipt_lengths, page_boxes))

def reference(tokens, w_qkv, qv_bias, w_out, out_bias, norm1_gain, norm1_shift, w_up, up_bias, w_down, down_bias, norm2_gain, norm2_shift, pos_table, box_table, receipt_lengths, page_boxes, out_cotangent):
    params = tuple((weight.astype(jnp.float32) for weight in (w_qkv, qv_bias, w_out, out_bias, norm1_gain, norm1_shift, w_up, up_bias, w_down, down_bias, norm2_gain, norm2_shift, pos_table, box_table)))
    tokens_f32 = tokens.astype(jnp.float32)

    def whole_layer(inputs, weights):
        return forward(inputs, weights, receipt_lengths, page_boxes)
    result, backward_pull = jax.vjp(whole_layer, tokens_f32, params)
    grad_inputs, weight_grads = backward_pull(out_cotangent.astype(jnp.float32))
    return (result.astype(jnp.bfloat16), grad_inputs.astype(jnp.bfloat16), weight_grads[0], weight_grads[1], weight_grads[2], weight_grads[3], weight_grads[4], weight_grads[5], weight_grads[6], weight_grads[7], weight_grads[8], weight_grads[9], weight_grads[10], weight_grads[11], weight_grads[12], weight_grads[13])
```

```python
import math

import jax
import jax.numpy as jnp
from jax import lax
from jax.experimental import pallas as pl
from jax.experimental.pallas import tpu as pltpu
from jax.sharding import PartitionSpec as P

f32 = jnp.float32
bf16 = jnp.bfloat16
i32 = jnp.int32
EPSILON = 1e-05
MASKED_SCORE = -1e30
HEAD_DIM=64; TEXT=512; NB1=32; MD1=128; NB2=64; MD2=256
ROWS=576
QROWS=640
LANES=128
VIS=ROWS-TEXT
BLOCKS=((0,256),(0,384),(128,384),(256,256),(0,576))
OFFS=[]; _t=0
for _i,(_s,_n) in enumerate(BLOCKS):
    OFFS.append(_t); _t+=_n+(VIS if _i<4 else 0)
TOTAL=_t

def thresholds(buckets, max_reach):
    half_range = buckets // 2
    exact_range = half_range // 2
    levels = half_range - exact_range
    return [math.ceil(exact_range * (max_reach / exact_range) ** (k / levels) - 1e-09) for k in range(1, levels)]

def bucket_of(diff, buckets, reach):
    n=jnp.abs(diff)
    out=jnp.minimum(n,buckets//4)+jnp.where(diff>0,buckets//2,0)
    for t in thresholds(buckets,reach):
        out=out+jnp.where(n>=t,1,0)
    return out

def windows():
    for i,(s,n) in enumerate(BLOCKS):
        yield i,s,n,OFFS[i]
        if i<4: yield i,TEXT,VIS,OFFS[i]+n

def ids_kernel(kcol_ref, qrow_ref, out_ref, *, rows_valid):
    for blk,s,n,o in windows():
        for c in range(0,n,64):
            seg=kcol_ref[s+c:s+c+64,0:1]; kx=kcol_ref[s+c:s+c+64,1:2]; ky=kcol_ref[s+c:s+c+64,2:3]
            ql=slice(blk*LANES,(blk+1)*LANES)
            qseg=qrow_ref[0:1,ql]; qx=qrow_ref[1:2,ql]; qy=qrow_ref[2:3,ql]
            kpos=lax.broadcasted_iota(i32,(64,LANES),0)+(s+c)
            qpos=lax.broadcasted_iota(i32,(64,LANES),1)+blk*LANES
            xid=bucket_of(jnp.broadcast_to(kx,(64,LANES))-qx,NB2,MD2)
            yid=bucket_of(jnp.broadcast_to(ky,(64,LANES))-qy,NB2,MD2)
            pid=bucket_of(kpos-qpos,NB1,MD1)
            ok=(jnp.broadcast_to(seg,(64,LANES))==qseg)|(kpos>=TEXT)|(qpos>=TEXT)
            ok=ok&(kpos<rows_valid)
            pid=jnp.where(ok,pid,NB1)
            out_ref[0,o+c:o+c+64,:]=xid
            out_ref[1,o+c:o+c+64,:]=yid+NB2
            out_ref[2,o+c:o+c+64,:]=pid

def make_ids(kcol,qrow,rows_valid):
    return pl.pallas_call(lambda a,b,c: ids_kernel(a,b,c,rows_valid=rows_valid),
        out_shape=jax.ShapeDtypeStruct((3,TOTAL,LANES),i32), name="ids",
        compiler_params=pltpu.CompilerParams(vmem_limit_bytes=32<<20))(kcol,qrow)

def nt(a,b): return lax.dot_general(a,b,(((1,),(1,)),((),())),preferred_element_type=f32)
def nn(a,b): return lax.dot_general(a,b,(((1,),(0,)),((),())),preferred_element_type=f32)
def take(tab,idx): return jnp.take_along_axis(jnp.broadcast_to(tab,idx.shape),idx,axis=1,mode="promise_in_bounds")

def head_cols(h):
    j,l=divmod(h,3)
    return [j*576+p*192+l*64 for p in range(3)]

def fwd_kernel(mixed_ref, ids_ref, tab_ref, out_ref, p_ref, q_s, k_s, vt_s, s_s, o_s, *, heads):
    for h in range(heads):
        cq,ck,cv=head_cols(h)
        q_s[h,0:ROWS,:]=mixed_ref[:,cq:cq+64]
        q_s[h,ROWS:QROWS,:]=jnp.zeros((QROWS-ROWS,64),bf16)
        k_s[h]=mixed_ref[:,ck:ck+64]
        vt_s[h]=mixed_ref[:,cv:cv+64].astype(f32).T.astype(bf16)
    def head(h,_):
        txy=tab_ref[pl.ds(2*h,1),:]; tp=tab_ref[pl.ds(2*h+1,1),:]
        for blk in range(5):
            q=q_s[h,blk*LANES:(blk+1)*LANES,:]
            parts=[(s,n,o) for b,s,n,o in windows() if b==blk]
            m=jnp.full((1,LANES),-3e38,f32)
            for s,n,o in parts:
                sc=nt(k_s[h,s:s+n,:],q)
                for c in range(0,n,64):
                    r=slice(o+c,o+c+64)
                    v=sc[c:c+64]+(take(tp,ids_ref[2,r,:])+(take(txy,ids_ref[0,r,:])+take(txy,ids_ref[1,r,:])))
                    s_s[o-OFFS[blk]+c:o-OFFS[blk]+c+64,:]=v
                    m=jnp.maximum(m,jnp.max(v,axis=0,keepdims=True))
            l=jnp.zeros((1,LANES),f32)
            tot=sum(n for _,n,_ in parts)
            for c in range(0,tot,64):
                e=jnp.exp(s_s[c:c+64,:]-m)
                s_s[c:c+64,:]=e
                l=l+jnp.sum(e,axis=0,keepdims=True)
            inv=1.0/l
            for c in range(0,tot,64):
                p_ref[h,OFFS[blk]+c:OFFS[blk]+c+64,:]=(s_s[c:c+64,:]*inv).astype(bf16)
            ot=jnp.zeros((64,LANES),f32)
            for s,n,o in parts:
                ot=ot+nn(vt_s[h,:,s:s+n],p_ref[h,o:o+n,:])
            o_s[h,blk*LANES:(blk+1)*LANES,:]=ot.T
        return 0
    lax.fori_loop(0,heads,head,0)
    for h in range(heads):
        out_ref[:,h*64:h*64+64]=o_s[h,0:ROWS,:].astype(bf16)

def attn_fwd(mixed,ids,tab,heads=12):
    return pl.pallas_call(lambda *a: fwd_kernel(*a,heads=heads),
        out_shape=(jax.ShapeDtypeStruct((ROWS,heads*64),bf16),jax.ShapeDtypeStruct((heads,TOTAL,LANES),bf16)),
        scratch_shapes=[pltpu.VMEM((heads,QROWS,64),bf16),pltpu.VMEM((heads,ROWS,64),bf16),pltpu.VMEM((heads,64,ROWS),bf16),
            pltpu.VMEM((ROWS,LANES),f32),pltpu.VMEM((heads,QROWS,64),f32)], name="attn_fwd",
        compiler_params=pltpu.CompilerParams(vmem_limit_bytes=56<<20))(mixed,ids,tab)

STEP=16
def bwd_kernel(mixed_ref, do_ref, p_ref, ids_ref, out_ref, hist_ref, q_s, k_s, kt_s, v_s, do_s, dq_s, dk_s, dv_s, ds_s, *, heads):
    for h in range(heads):
        cq,ck,cv=head_cols(h)
        q_s[h,0:ROWS,:]=mixed_ref[:,cq:cq+64]
        q_s[h,ROWS:QROWS,:]=jnp.zeros((QROWS-ROWS,64),bf16)
        do_s[h,0:ROWS,:]=do_ref[:,h*64:h*64+64]
        do_s[h,ROWS:QROWS,:]=jnp.zeros((QROWS-ROWS,64),bf16)
        kk=mixed_ref[:,ck:ck+64]
        k_s[h]=kk
        kt_s[h]=kk.astype(f32).T.astype(bf16)
        v_s[h]=mixed_ref[:,cv:cv+64]
    for h in range(heads,16):
        ds_s[pl.ds(h,TOTAL,stride=16),:]=jnp.zeros((TOTAL,LANES),f32)
    def head(h,_):
        for blk in range(5):
            q=q_s[h,blk*LANES:(blk+1)*LANES,:]; do=do_s[h,blk*LANES:(blk+1)*LANES,:]
            parts=[(s,n,o) for b,s,n,o in windows() if b==blk]
            dps=[nt(v_s[h,s:s+n,:],do) for s,n,o in parts]
            D=jnp.zeros((1,LANES),f32)
            for (s,n,o),dp in zip(parts,dps):
                for c in range(0,n,64):
                    D=D+jnp.sum(p_ref[h,o+c:o+c+64,:].astype(f32)*dp[c:c+64],axis=0,keepdims=True)
            dqt=jnp.zeros((64,LANES),f32)
            for (s,n,o),dp in zip(parts,dps):
                dsb=[]
                for c in range(0,n,64):
                    ds=p_ref[h,o+c:o+c+64,:].astype(f32)*(dp[c:c+64]-D)
                    ds_s[pl.ds((o+c)*16+h,64,stride=16),:]=ds
                    dsb.append(ds.astype(bf16))
                dsb=jnp.concatenate(dsb,0)
                dqt=dqt+nn(kt_s[h,:,s:s+n],dsb)
                dv=nn(p_ref[h,o:o+n,:],do); dk=nn(dsb,q)
                if blk==0:
                    dv_s[h,s:s+n,:]=dv; dk_s[h,s:s+n,:]=dk
                elif blk==1 and s==0:
                    dv_s[h,0:256,:]+=dv[0:256]; dk_s[h,0:256,:]+=dk[0:256]
                    dv_s[h,256:384,:]=dv[256:]; dk_s[h,256:384,:]=dk[256:]
                elif blk==2 and s==128:
                    dv_s[h,128:384,:]+=dv[0:256]; dk_s[h,128:384,:]+=dk[0:256]
                    dv_s[h,384:512,:]=dv[256:]; dk_s[h,384:512,:]=dk[256:]
                else:
                    dv_s[h,s:s+n,:]+=dv; dk_s[h,s:s+n,:]+=dk
            dq_s[h,blk*LANES:(blk+1)*LANES,:]=dqt.T*0.125
        return 0
    lax.fori_loop(0,heads,head,0)
    for h in range(heads):
        cq,ck,cv=head_cols(h)
        out_ref[:,cq:cq+64]=dq_s[h,0:ROWS,:].astype(bf16)
        out_ref[:,ck:ck+64]=dk_s[h].astype(bf16)
        out_ref[:,cv:cv+64]=dv_s[h].astype(bf16)
    io=lax.broadcasted_iota(i32,(64,LANES),0)
    io2=io+64
    def rows(r,acc):
        lhs=[];rhs=[]
        for u in range(STEP):
            k=r*STEP+u
            x=ids_ref[0,pl.ds(k,1),:]; y=ids_ref[1,pl.ds(k,1),:]; p=ids_ref[2,pl.ds(k,1),:]
            rhs.append(jnp.concatenate([jnp.where(io==x,1.,0.),jnp.where(io2==y,1.,0.),jnp.where(io[:32]==p,1.,0.)],0).astype(bf16))
            lhs.append(ds_s[pl.ds(pl.multiple_of(k*16,16),16),:].astype(bf16))
        return acc+nt(jnp.concatenate(lhs,1),jnp.concatenate(rhs,1))
    hist_ref[...]=lax.fori_loop(0,TOTAL//STEP,rows,jnp.zeros((16,160),f32))

def attn_bwd(mixed,d_att,p,ids,heads=12):
    return pl.pallas_call(lambda *a: bwd_kernel(*a,heads=heads),
        out_shape=(jax.ShapeDtypeStruct((ROWS,heads*192),bf16),jax.ShapeDtypeStruct((16,160),f32)),
        scratch_shapes=[pltpu.VMEM((heads,QROWS,64),bf16),pltpu.VMEM((heads,ROWS,64),bf16),pltpu.VMEM((heads,64,ROWS),bf16),
            pltpu.VMEM((heads,ROWS,64),bf16),pltpu.VMEM((heads,QROWS,64),bf16),
            pltpu.VMEM((heads,QROWS,64),f32),pltpu.VMEM((heads,ROWS,64),f32),pltpu.VMEM((heads,ROWS,64),f32),
            pltpu.VMEM((TOTAL*16,LANES),f32)], name="attn_bwd",
        compiler_params=pltpu.CompilerParams(vmem_limit_bytes=60<<20))(mixed,d_att,p,ids)


def core_swap(v):
    return lax.ppermute(v, "heads", [(i, i ^ 1) for i in range(4)])


def x_swap(v):
    return lax.ppermute(v, "heads", [(i, i ^ 2) for i in range(4)])


def collect(shard):
    pair = jnp.concatenate((shard, x_swap(shard)), axis=0)
    return jnp.concatenate((pair, core_swap(pair)), axis=0)


def reduce_pages(part):
    pages = lax.axis_size("pages")
    me = lax.axis_index("pages")
    rows, cols = part.shape
    cur = part.reshape(pages, rows // pages, cols)
    bit = 1
    while bit < pages:
        view = cur.reshape(-1, 2, rows // pages, cols)
        mine = (me // bit) % 2
        keep = lax.dynamic_index_in_dim(view, mine, axis=1, keepdims=False)
        send = lax.dynamic_index_in_dim(view, 1 - mine, axis=1, keepdims=False)
        got = lax.ppermute(send, "pages", [(i, i ^ bit) for i in range(pages)])
        cur = keep.astype(f32) + got.astype(f32)
        bit *= 2
        if bit < pages:
            cur = cur.astype(bf16)
    return cur.reshape(rows // pages, cols)


def tn(a, b):
    return lax.dot_general(a, b, (((0,), (0,)), ((), ())), preferred_element_type=f32)


def reduce_heads(rows_mat, col_mat):
    width = col_mat.shape[1] // 4
    send = tn(rows_mat, col_mat[:, 2 * width :]).astype(bf16)
    got = core_swap(send)
    far = (tn(rows_mat, col_mat[:, width : 2 * width]) + got[:, width:].astype(f32)).astype(bf16)
    got_far = x_swap(far)
    own = tn(rows_mat, col_mat[:, :width]) + got[:, :width].astype(f32) + got_far.astype(f32)
    return own.astype(bf16)


def norm_parts(values):
    centered = values - jnp.mean(values, axis=-1, keepdims=True)
    inv_std = lax.rsqrt(jnp.mean(centered * centered, axis=-1, keepdims=True) + EPSILON)
    return centered * inv_std, inv_std


def norm_back(unit, inv_std, gain, dy):
    e = dy * gain
    dv = inv_std * (
        e - jnp.mean(e, axis=-1, keepdims=True) - unit * jnp.mean(e * unit, axis=-1, keepdims=True)
    )
    return dv, jnp.sum(dy * unit, axis=0), jnp.sum(dy, axis=0)


def on_device(
    tokens,
    w_qkv,
    qv_bias,
    w_out,
    out_bias,
    norm1_gain,
    norm1_shift,
    w_up,
    up_bias,
    w_down,
    down_bias,
    norm2_gain,
    norm2_shift,
    pos_table,
    box_table,
    receipt_lengths,
    page_boxes,
    out_cotangent,
):
    seq_len = tokens.shape[1]
    width = tokens.shape[2]
    heads_here = pos_table.shape[0]
    inner = heads_here * HEAD_DIM
    heads_all = 4 * heads_here
    units = w_up.shape[1]
    spare = ROWS - seq_len
    own_page = lax.axis_index("heads")

    wt_qkv = collect(w_qkv.reshape(width, 3 * inner).T)
    table_row = jnp.zeros((heads_here, 2, LANES), f32)
    table_row = table_row.at[:, 0, :NB2].set(box_table[0]).at[:, 0, NB2:].set(box_table[1])
    table_row = table_row.at[:, 1, :NB1].set(pos_table).at[:, 1, NB1].set(MASKED_SCORE)
    small = jnp.concatenate(
        (table_row.reshape(-1), qv_bias.reshape(-1), up_bias.astype(f32))
    )
    small = collect(small.reshape(1, -1))
    n_tab = heads_here * 2 * LANES
    tables = small[:, :n_tab].reshape(heads_all * 2, LANES)
    qv_all = small[:, n_tab : n_tab + 2 * inner].reshape(4, 2, inner)
    up_bias_all = small[:, n_tab + 2 * inner :].reshape(4 * units)
    wt_out = collect(w_out)
    wt_up = collect(w_up.T)
    wt_down = collect(w_down)

    lengths = lax.dynamic_index_in_dim(receipt_lengths, own_page, 0, keepdims=False)
    boxes = lax.dynamic_index_in_dim(page_boxes, own_page, 0, keepdims=False)
    ends = jnp.cumsum(lengths, dtype=i32)
    segment = jnp.sum((jnp.arange(QROWS, dtype=i32)[None, :] >= ends[:, None]).astype(i32), axis=0)
    q_row = jnp.concatenate((segment[None], jnp.pad(boxes, ((0, 0), (0, QROWS - seq_len)))), axis=0)
    k_col = jnp.pad(q_row[:, :ROWS].T, ((0, 0), (0, LANES - 3)))
    q_row = jnp.pad(q_row, ((0, 5), (0, 0)))
    ids = make_ids(k_col, q_row, seq_len)

    tok = jnp.pad(tokens.reshape(seq_len, width), ((0, spare), (0, 0)))
    ct = jnp.pad(out_cotangent.reshape(seq_len, width), ((0, spare), (0, 0))).astype(f32)
    tok32 = tok.astype(f32)

    bias_row = jnp.concatenate(
        (qv_all[:, 0:1], jnp.zeros((4, 1, inner), f32), qv_all[:, 1:2]), axis=1
    ).reshape(1, -1)
    scale_row = jnp.concatenate(
        (jnp.full((4, 1, inner), 0.125, f32), jnp.ones((4, 2, inner), f32)), axis=1
    ).reshape(1, -1)
    mixed = ((nt(tok, wt_qkv) + bias_row) * scale_row).astype(bf16)
    attended, probs = attn_fwd(mixed, ids, tables, heads_all)
    first_in = nn(attended, wt_out) + out_bias + tok32
    unit1, inv1 = norm_parts(first_in)
    first_out = unit1 * norm1_gain + norm1_shift
    first_low = first_out.astype(bf16)
    up = nt(first_low, wt_up) + up_bias_all
    cdf = 0.5 * (1.0 + lax.erf(up * math.sqrt(0.5)))
    hidden = (up * cdf).astype(bf16)
    slope = (cdf + up * jnp.exp(-0.5 * up * up) * (1.0 / math.sqrt(2.0 * math.pi))).astype(bf16)
    second_in = nn(hidden, wt_down) + down_bias + first_out
    unit2, inv2 = norm_parts(second_in)
    layer_out = (unit2 * norm2_gain + norm2_shift).astype(bf16)

    d_second, g_gain2, g_shift2 = norm_back(unit2, inv2, norm2_gain, ct)
    g_down_bias = jnp.sum(d_second, axis=0)
    d_ffn = d_second.astype(bf16)
    r_down = reduce_heads(d_ffn, hidden)
    d_up = (nt(d_ffn, wt_down) * slope.astype(f32)).astype(bf16)
    r_up = reduce_heads(first_low, d_up)
    g_up_bias = jnp.sum(d_up.astype(f32), axis=0)
    d_mid = nn(d_up, wt_up)
    d_first, g_gain1, g_shift1 = norm_back(unit1, inv1, norm1_gain, d_second + d_mid)
    g_out_bias = jnp.sum(d_first, axis=0)
    d_proj = d_first.astype(bf16)
    r_out = reduce_heads(d_proj, attended)
    d_attended = nt(d_proj, wt_out).astype(bf16)
    d_mixed, hist = attn_bwd(mixed, d_attended, probs, ids, heads_all)
    r_qkv = reduce_heads(tok, d_mixed)
    grad_tokens = (nn(d_mixed, wt_qkv) + d_first)[:seq_len].astype(bf16)

    g_w_down = reduce_pages(r_down).T
    g_w_up = reduce_pages(r_up)
    g_w_out = reduce_pages(r_out).T
    g_w_qkv = reduce_pages(r_qkv).reshape(-1, 3, inner)

    mixed_sums = jnp.sum(d_mixed.astype(f32), axis=0).reshape(4, 3, inner)
    split = jnp.concatenate(
        (
            mixed_sums[:, 0],
            mixed_sums[:, 2],
            hist[:heads_all].reshape(4, heads_here * 160),
            g_up_bias.reshape(4, units),
        ),
        axis=1,
    )
    split = split[:2] + core_swap(split[2:])
    split = split[0] + x_swap(split[1])
    split = lax.psum(split, "pages")
    g_qv_bias = split[: 2 * inner].reshape(2, inner)
    tab = split[2 * inner : 2 * inner + heads_here * 160].reshape(heads_here, 160)
    g_up_bias = split[2 * inner + heads_here * 160 :]
    g_box = jnp.stack((tab[:, :NB2], tab[:, NB2 : 2 * NB2]))
    g_pos = tab[:, 2 * NB2 :]
    shared = lax.psum(
        jnp.stack((g_out_bias, g_gain1, g_shift1, g_down_bias, g_gain2, g_shift2)),
        ("pages", "heads"),
    )
    return (
        layer_out[:seq_len].reshape(tokens.shape),
        grad_tokens.reshape(tokens.shape),
        g_w_qkv,
        g_qv_bias,
        g_w_out,
        shared[0],
        shared[1],
        shared[2],
        g_w_up,
        g_up_bias,
        g_w_down,
        shared[3],
        shared[4],
        shared[5],
        g_pos,
        g_box,
    )


def solution(mesh):
    placed = (
        P(("pages", "heads"), None, None),
        P(None, None, "heads"),
        P(None, "heads"),
        P("heads", None),
        P(),
        P(),
        P(),
        P(None, "heads"),
        P("heads"),
        P("heads", None),
        P(),
        P(),
        P(),
        P("heads", None),
        P(None, "heads", None),
        P("pages", None),
        P("pages", None, None),
        P(("pages", "heads"), None, None),
    )
    return jax.shard_map(
        on_device,
        mesh=mesh,
        in_specs=placed,
        out_specs=(
            P(("pages", "heads"), None, None),
            P(("pages", "heads"), None, None),
            P("pages", None, "heads"),
            P(None, "heads"),
            P("heads", "pages"),
            P(),
            P(),
            P(),
            P("pages", "heads"),
            P("heads"),
            P("heads", "pages"),
            P(),
            P(),
            P(),
            P("heads", None),
            P(None, "heads", None),
        ),
        check_vma=False,
    )
```

```python
import functools
import math

import jax
import jax.numpy as jnp
from jax import lax
from jax.experimental import pallas as pl
from jax.experimental.pallas import tpu as pltpu
from jax.sharding import PartitionSpec as P

f32 = jnp.float32
bf16 = jnp.bfloat16
i32 = jnp.int32
EPSILON = 1e-05
MASKED_SCORE = -1e30


HEAD_DIM = 64
TEXT = 512
NB1 = 32
MD1 = 128
NB2 = 64
MD2 = 256
ROWS = 576
VIS = ROWS - TEXT
QROWS = 640
LANES = 128
CHUNK = 64
UNIT = 2048.0
BLOCKS = ((0, 256), (0, 384), (128, 384), (256, 256))
OFFS = (0, 320, 768, 1216)
SPAN = 1536
TOTAL = SPAN + ROWS
SMALL = 24


def thresholds(buckets, max_reach):
    half_range = buckets // 2
    exact_range = half_range // 2
    levels = half_range - exact_range
    return [
        math.ceil(exact_range * (max_reach / exact_range) ** (k / levels) - 1e-09)
        for k in range(1, levels)
    ]


def bucket_of(diff, buckets, reach):
    n = jnp.abs(diff)
    out = jnp.minimum(n, buckets // 4) + jnp.where(diff > 0, buckets // 2, 0)
    for t in thresholds(buckets, reach):
        out = out + jnp.where(n >= t, 1, 0)
    return out


def parts_of(blk):
    s, n = BLOCKS[blk]
    return ((s, n, OFFS[blk]), (TEXT, VIS, OFFS[blk] + n))


def nt(a, b):
    return lax.dot_general(a, b, (((1,), (1,)), ((), ())), preferred_element_type=f32)


def nn(a, b):
    return lax.dot_general(a, b, (((1,), (0,)), ((), ())), preferred_element_type=f32)


def take(tab, idx):
    return jnp.take_along_axis(
        jnp.broadcast_to(tab, idx.shape), idx, axis=1, mode="promise_in_bounds"
    )


def ids_kernel(place_ref, len_ref, box_ref, ids_ref, mask_ref, c_s, r_s, *, valid):
    page = place_ref[0]
    row = lax.broadcasted_iota(i32, (8, ROWS), 1)
    segment = jnp.zeros((8, ROWS), i32)
    end = 0
    for i in range(len_ref.shape[1]):
        end = end + len_ref[page, i]
        segment = segment + jnp.where(row >= end, 1, 0)
    c_s[...] = jnp.zeros_like(c_s)
    c_s[0:8, :] = segment.astype(f32)
    c_s[8:10, 0:valid] = box_ref[page].astype(f32)
    r_s[...] = c_s[...].T.astype(i32)

    def query(lo, hi):
        return tuple(c_s[i : i + 1, lo:hi].astype(i32) for i in (0, 8, 9))

    def tile(row, out, q_first, q):
        qseg, qx, qy = q
        seg, kx, ky = (
            jnp.broadcast_to(r_s[row : row + CHUNK, i : i + 1], (CHUNK, LANES)) for i in (0, 8, 9)
        )
        k_pos = lax.broadcasted_iota(i32, (CHUNK, LANES), 0) + row
        lane = lax.broadcasted_iota(i32, (CHUNK, LANES), 1)
        if q_first == TEXT:
            q_pos, high = TEXT + (lane & (VIS - 1)), jnp.where(lane >= VIS, NB2, 0)
        else:
            q_pos, high = q_first + lane, 0
        x_id = bucket_of(kx - qx, NB2, MD2)
        y_id = bucket_of(ky - qy, NB2, MD2)
        p_id = bucket_of(k_pos - q_pos, NB1, MD1)
        ok = ((seg == qseg) | (k_pos >= TEXT) | (q_pos >= TEXT)) & (k_pos < valid)
        here = slice(out, out + CHUNK)
        ids_ref[0, here, :] = x_id + high
        ids_ref[1, here, :] = y_id + (high if q_first == TEXT else NB2)
        ids_ref[2, here, :] = p_id + high
        mask_ref[here, :] = jnp.where(ok, 0.0, MASKED_SCORE)

    for blk in range(4):
        q = query(blk * LANES, (blk + 1) * LANES)
        for s, n, o in parts_of(blk):
            for c in range(0, n, CHUNK):
                tile(s + c, o + c, blk * LANES, q)
    q = tuple(jnp.concatenate((v, v), axis=1) for v in query(TEXT, ROWS))
    for c in range(0, ROWS, CHUNK):
        tile(c, SPAN + c, TEXT, q)


def make_ids(place, lengths, boxes):
    return pl.pallas_call(
        functools.partial(ids_kernel, valid=boxes.shape[2]),
        in_specs=[
            pl.BlockSpec(memory_space=pltpu.SMEM),
            pl.BlockSpec(memory_space=pltpu.SMEM),
            pl.BlockSpec(memory_space=pltpu.VMEM),
        ],
        out_shape=(
            jax.ShapeDtypeStruct((3, TOTAL, LANES), i32),
            jax.ShapeDtypeStruct((TOTAL, LANES), f32),
        ),
        scratch_shapes=[pltpu.VMEM((LANES, ROWS), f32), pltpu.VMEM((ROWS, LANES), i32)],
        name="ids",
        cost_estimate=pl.CostEstimate(flops=0, bytes_accessed=1 << 20, transcendentals=0),
        compiler_params=pltpu.CompilerParams(vmem_limit_bytes=24 << 20),
    )(place, lengths, boxes)


def place(dst_ref, pair, side, cols):
    at = slice(side * 64, side * 64 + 64)
    for blk in range(4):
        first = blk * 256 + side * LANES
        dst_ref[pair, first : first + LANES, at] = cols[blk * LANES : (blk + 1) * LANES]
    first = 1024 + side * VIS
    dst_ref[pair, first : first + VIS, at] = cols[TEXT:]


def load_rows(refs, odd, dst):
    if len(refs) == 1:
        dst[0 : refs[0].shape[0], :] = refs[0][...]
    else:
        half = refs[0].shape[0]
        for first in range(2):

            @pl.when(odd == first)
            def _(first=first):
                dst[first * half : (first + 1) * half, :] = refs[0][...]
                dst[(1 - first) * half : (2 - first) * half, :] = refs[1][...]


def pad_rows(v):
    return jnp.concatenate((v, jnp.zeros((ROWS - v.shape[0], v.shape[1]), v.dtype)), 0)


def fold(both):
    n = both.shape[1] // 2
    t = both.T
    lane = lax.broadcasted_iota(i32, (n, LANES), 1)
    return jnp.where(lane < 64, t[:n], t[n:])


def fwd_kernel(place_ref, tok_ref, *refs, pieces, pairs):
    n = 2 * pieces
    weights = (refs[:pieces], refs[pieces:n])
    small, (ids_ref, mask_ref) = refs[n : n + 2], refs[n + 2 : n + 4]
    out_ref, out0_ref, out1_ref, q_s, k_s, v_s, p_ref, pv_ref, vt_s, s_s, w_s, i_s, f_s, o_s = refs[n + 4 :]
    inner = pairs * HEAD_DIM
    tok = pad_rows(tok_ref[...])
    q_s[...] = jnp.zeros_like(q_s)
    for g in range(2):
        load_rows(weights[g], place_ref[1], w_s)
        for part in range(3):
            mixed = nt(tok, w_s[part * inner : (part + 1) * inner, :])
            for local in range(pairs):
                pair, side = divmod(g * pairs + local, 2)
                at = slice(side * 64, side * 64 + 64)
                cols = mixed[:, local * 64 : local * 64 + 64]
                if part == 0:
                    cols = cols + small[g][2 * pairs + local : 2 * pairs + local + 1, :64]
                    place(q_s, pair, side, (cols * (UNIT / 8)).astype(bf16))
                elif part == 1:
                    k_s[pair, :, at] = cols.astype(bf16)
                else:
                    cols = cols + small[g][3 * pairs + local : 3 * pairs + local + 1, :64]
                    v_s[pair, :, at] = cols.astype(bf16)
                    vt_s[pair, at, :] = cols.T.astype(bf16)
    for pair in range(pairs):
        (ga, la), (gb, lb) = divmod(2 * pair, pairs), divmod(2 * pair + 1, pairs)
        for row, first in ((0, 0), (1, pairs)):
            a = small[ga][first + la : first + la + 1, :] * UNIT
            b = small[gb][first + lb : first + lb + 1, :] * UNIT
            i_s[pair, row : row + 1, :] = (
                jnp.round(a).astype(i32) * 65536 + jnp.round(b).astype(i32)
            )
            f_s[pair, 2 * row : 2 * row + 1, :] = jnp.concatenate((a[:, :64], b[:, :64]), 1)
            f_s[pair, 2 * row + 1 : 2 * row + 2, :] = jnp.concatenate((a[:, 64:], b[:, 64:]), 1)

    def softmax(total, wide, p_at):
        m = jnp.full((8, wide), -3e38, f32)
        for c in range(0, total, 8):
            m = jnp.maximum(m, s_s[c : c + 8, :wide])
        m = jnp.max(m, axis=0, keepdims=True)
        l = jnp.zeros((8, wide), f32)
        for c in range(0, total, 8):
            e = jnp.exp2((s_s[c : c + 8, :wide] - m) * (math.log2(math.e) / UNIT))
            s_s[c : c + 8, :wide] = e
            l = l + e
        inv = 1.0 / jnp.sum(l, axis=0, keepdims=True)
        for c in range(0, total, 16):
            p_at(c, (s_s[c : c + 16, :wide] * inv).astype(bf16))

    def one_pair(pair, _):
        t_xy, t_p = (i_s[pair, i : i + 1, :] for i in range(2))
        v_x, v_y, v_p = (f_s[pair, i : i + 1, :] for i in range(3))
        for blk in range(4):
            q = q_s[pair, blk * 256 : (blk + 1) * 256, :]
            first = OFFS[blk]
            for s, n, o in parts_of(blk):
                sc = nt(k_s[pair, s : s + n, :], q)
                for c in range(0, n, 16):
                    r = slice(o + c, o + c + 16)
                    b = take(t_xy, ids_ref[0, r, :]) + take(t_xy, ids_ref[1, r, :]) + take(t_p, ids_ref[2, r, :])
                    low = (b << 16) >> 16
                    high = (b - low) >> 16
                    add = mask_ref[r, :]
                    to = slice(o - first + c, o - first + c + 16)
                    s_s[to, :LANES] = sc[c : c + 16, :LANES] + (high.astype(f32) + add)
                    s_s[to, LANES:] = sc[c : c + 16, LANES:] + (low.astype(f32) + add)

            def put(c, v, first=first):
                p_ref[pair, first + c : first + c + 16, :] = v

            softmax(BLOCKS[blk][1] + VIS, 256, put)
            ot = sum(
                nn(vt_s[pair, :, s : s + n], p_ref[pair, o : o + n, :]) for s, n, o in parts_of(blk)
            )
            o_s[pair, blk * LANES : (blk + 1) * LANES, :] = fold(ot).astype(bf16)
        q = q_s[pair, 1024:1152, :]
        sc = nt(k_s[pair], q)
        for c in range(0, ROWS, 16):
            r = slice(SPAN + c, SPAN + c + 16)
            b = take(v_x, ids_ref[0, r, :]) + take(v_y, ids_ref[1, r, :]) + take(v_p, ids_ref[2, r, :])
            s_s[c : c + 16, :LANES] = sc[c : c + 16] + (b + mask_ref[r, :])

        def put_v(c, v):
            pv_ref[pair, c : c + 16, :] = v

        softmax(ROWS, LANES, put_v)
        o_s[pair, TEXT:ROWS, :] = fold(nn(vt_s[pair], pv_ref[pair])).astype(bf16)
        return 0

    lax.fori_loop(0, pairs, one_pair, 0)
    rows = out_ref.shape[0]
    for pair in range(pairs):
        out_ref[:, pair * LANES : (pair + 1) * LANES] = o_s[pair, 0:rows, :]
    for h in range(2 * pairs):
        g, local = divmod(h, pairs)
        here = o_s[h // 2, 0:rows, (h % 2) * 64 : (h % 2) * 64 + 64]
        (out0_ref, out1_ref)[g][:, local * 64 : local * 64 + 64] = here


def attn_fwd(place, tok, weights, small, ids, mask, pairs):
    pieces, rows = len(weights[0]), tok.shape[0]
    vmem = pl.BlockSpec(memory_space=pltpu.VMEM)
    return pl.pallas_call(
        functools.partial(fwd_kernel, pieces=pieces, pairs=pairs),
        in_specs=[pl.BlockSpec(memory_space=pltpu.SMEM)] + [vmem] * (5 + 2 * pieces),
        out_shape=(
            jax.ShapeDtypeStruct((rows, pairs * LANES), bf16),
            jax.ShapeDtypeStruct((rows, pairs * 64), bf16),
            jax.ShapeDtypeStruct((rows, pairs * 64), bf16),
            jax.ShapeDtypeStruct((pairs, 1152, LANES), bf16),
            jax.ShapeDtypeStruct((pairs, ROWS, LANES), bf16),
            jax.ShapeDtypeStruct((pairs, ROWS, LANES), bf16),
            jax.ShapeDtypeStruct((pairs, SPAN, 256), bf16),
            jax.ShapeDtypeStruct((pairs, ROWS, LANES), bf16),
        ),
        scratch_shapes=[
            pltpu.VMEM((pairs, LANES, ROWS), bf16),
            pltpu.VMEM((ROWS, 256), f32),
            pltpu.VMEM((4 * pairs * HEAD_DIM, tok.shape[1]), bf16),
            pltpu.VMEM((pairs, 8, LANES), i32),
            pltpu.VMEM((pairs, 8, LANES), f32),
            pltpu.VMEM((pairs, ROWS, LANES), bf16),
        ],
        name="attn_fwd",
        cost_estimate=pl.CostEstimate(flops=0, bytes_accessed=1 << 20, transcendentals=0),
        compiler_params=pltpu.CompilerParams(vmem_limit_bytes=40 << 20),
    )(place, tok, *weights[0], *weights[1], *small, ids, mask)


def bwd_kernel(q_s, k_ref, v_s, do_ref, p_ref, pv_ref, out0_ref, out1_ref, ds_ref, dsv_ref, do_s, kt_s, dq_s, dk_s, dv_s, *, pairs):
    rows = out0_ref.shape[0]
    do_s[...] = jnp.zeros_like(do_s)
    for h in range(2 * pairs):
        pair, side = divmod(h, 2)
        place(do_s, pair, side, pad_rows(do_ref[:, h * 64 : h * 64 + 64]))
    for pair in range(pairs):
        kt_s[pair] = k_ref[pair].astype(f32).T.astype(bf16)

    def grad_scores(dps, ps, put):
        d = jnp.zeros((8, dps[0].shape[1]), f32)
        for dp, p in zip(dps, ps):
            for c in range(0, dp.shape[0], 16):
                t = p(c).astype(f32) * dp[c : c + 16]
                d = d + (t[:8] + t[8:])
        d = jnp.sum(d, axis=0, keepdims=True)
        for i, (dp, p) in enumerate(zip(dps, ps)):
            for c in range(0, dp.shape[0], 16):
                put(i, c, (p(c).astype(f32) * (dp[c : c + 16] - d)).astype(bf16))

    def one_pair(pair, _):
        dv_s[...] = jnp.zeros_like(dv_s)
        dk_s[...] = jnp.zeros_like(dk_s)
        for blk in range(4):
            q = q_s[pair, blk * 256 : (blk + 1) * 256, :]
            do = do_s[pair, blk * 256 : (blk + 1) * 256, :]
            parts = parts_of(blk)

            def put(i, c, v, parts=parts):
                ds_ref[pair, parts[i][2] + c : parts[i][2] + c + 16, :] = v

            grad_scores(
                [nt(v_s[pair, s : s + n, :], do) for s, n, o in parts],
                [lambda c, o=o: p_ref[pair, o + c : o + c + 16, :] for s, n, o in parts],
                put,
            )
            dq = 0.0
            for s, n, o in parts:
                ds = ds_ref[pair, o : o + n, :]
                dq = dq + nn(kt_s[pair, :, s : s + n], ds)
                dv_s[s : s + n, :] += nn(p_ref[pair, o : o + n, :], do)
                dk_s[s : s + n, :] += nn(ds, q)
            dq_s[pair, 0, blk * LANES : (blk + 1) * LANES, :] = (fold(dq) * 0.125).astype(bf16)
        q = q_s[pair, 1024:1152, :]
        do = do_s[pair, 1024:1152, :]

        def put_v(i, c, v):
            dsv_ref[pair, c : c + 16, :] = v

        grad_scores([nt(v_s[pair], do)], [lambda c: pv_ref[pair, c : c + 16, :]], put_v)
        ds = dsv_ref[pair]
        dq_s[pair, 0, TEXT:ROWS, :] = (fold(nn(kt_s[pair], ds)) * 0.125).astype(bf16)
        dq_s[pair, 1] = ((dk_s[...] + nn(ds, q)) * (1.0 / UNIT)).astype(bf16)
        dq_s[pair, 2] = (dv_s[...] + nn(pv_ref[pair], do)).astype(bf16)
        return 0

    lax.fori_loop(0, pairs, one_pair, 0)
    for h in range(2 * pairs):
        pair, side = divmod(h, 2)
        g, local = divmod(h, pairs)
        for part in range(3):
            col = part * pairs * HEAD_DIM + local * HEAD_DIM
            here = dq_s[pair, part, 0:rows, side * 64 : side * 64 + 64]
            (out0_ref, out1_ref)[g][:, col : col + 64] = here


def attn_bwd(rows, q, k, v, d_att, p, pv):
    pairs = p.shape[0]
    out = jax.ShapeDtypeStruct((rows, 3 * pairs * HEAD_DIM), bf16)
    return pl.pallas_call(
        functools.partial(bwd_kernel, pairs=pairs),
        out_shape=(
            out,
            out,
            jax.ShapeDtypeStruct(p.shape, bf16),
            jax.ShapeDtypeStruct(pv.shape, bf16),
        ),
        scratch_shapes=[
            pltpu.VMEM((pairs, 1152, LANES), bf16),
            pltpu.VMEM((pairs, LANES, ROWS), bf16),
            pltpu.VMEM((pairs, 3, ROWS, LANES), bf16),
            pltpu.VMEM((ROWS, LANES), f32),
            pltpu.VMEM((ROWS, LANES), f32),
        ],
        name="attn_bwd",
        cost_estimate=pl.CostEstimate(flops=0, bytes_accessed=1 << 20, transcendentals=0),
        compiler_params=pltpu.CompilerParams(vmem_limit_bytes=40 << 20),
    )(q, k, v, d_att, p, pv)


HSTEP = 64
HBLOCK = 192


def hist_kernel(acc_ref, ids_ref, *refs, sets, pairs, visual):
    ds_refs, hist_ref, l_s = refs[:sets], refs[-2], refs[-1]
    io = lax.broadcasted_iota(i32, (NB2, LANES), 0)
    heads = 2 * sets * pairs

    @pl.when(pl.program_id(0) == 0)
    def _():
        hist_ref[...] = acc_ref[...]

    for h in range(heads, 16):
        l_s[pl.ds(h, HSTEP, stride=16), :] = jnp.zeros((HSTEP, LANES), f32)

    def step(r, acc):
        first = pl.multiple_of(r * HSTEP, HSTEP)
        lane = lax.broadcasted_iota(i32, (HSTEP, LANES), 1)
        for pair in range(sets * pairs):
            ref = ds_refs[pair // pairs]
            for side in range(2):
                if visual:
                    v = ref[pair % pairs, pl.ds(first, HSTEP), :].astype(f32)
                    v = jnp.where((lane >= VIS) == bool(side), v, 0.0)
                else:
                    at = slice(side * LANES, (side + 1) * LANES)
                    v = ref[pair % pairs, pl.ds(first, HSTEP), at].astype(f32)
                l_s[pl.ds(2 * pair + side, HSTEP, stride=16), :] = v
        lhs, rhs = [], []
        for u in range(HSTEP):
            x, y, p = (ids_ref[i, pl.ds(first + u, 1), :] for i in range(3))
            if visual:
                x, y, p = (v & (NB2 - 1) for v in (x, y, p))
            else:
                y = y - NB2
            hot = [jnp.where(io == x, 1.0, 0.0), jnp.where(io == y, 1.0, 0.0)]
            hot.append(jnp.where(io[:NB1] == p, 1.0, 0.0))
            rhs.append(jnp.concatenate(hot, 0).astype(bf16))
            lhs.append(l_s[u * 16 : u * 16 + 16, :].astype(bf16))
        return acc + nt(jnp.concatenate(lhs, 1), jnp.concatenate(rhs, 1))

    hist_ref[...] = lax.fori_loop(0, HBLOCK // HSTEP, step, hist_ref[...])


def add_hist(acc, ids, ds, first_row, rows, visual):
    first = first_row // HBLOCK
    first_id = first + (SPAN // HBLOCK if visual else 0)
    specs = [
        pl.BlockSpec((16, 160), lambda i: (0, 0)),
        pl.BlockSpec((3, HBLOCK, LANES), lambda i: (0, first_id + i, 0)),
    ]
    for t in ds:
        specs.append(pl.BlockSpec((t.shape[0], HBLOCK, t.shape[2]), lambda i: (0, first + i, 0)))
    return pl.pallas_call(
        functools.partial(hist_kernel, sets=len(ds), pairs=ds[0].shape[0], visual=visual),
        grid=(rows // HBLOCK,),
        in_specs=specs,
        out_specs=pl.BlockSpec((16, 160), lambda i: (0, 0)),
        out_shape=jax.ShapeDtypeStruct((16, 160), f32),
        scratch_shapes=[pltpu.VMEM((HSTEP * 16, LANES), f32)],
        name="hist",
        cost_estimate=pl.CostEstimate(flops=0, bytes_accessed=1 << 20, transcendentals=0),
        compiler_params=pltpu.CompilerParams(vmem_limit_bytes=24 << 20),
    )(acc, ids, *ds)


def call(kernel, name, args, outs, scratch=(), smem=0):
    vmem = pl.BlockSpec(memory_space=pltpu.VMEM)
    return pl.pallas_call(
        kernel,
        in_specs=[pl.BlockSpec(memory_space=pltpu.SMEM)] * smem + [vmem] * (len(args) - smem),
        out_shape=[jax.ShapeDtypeStruct(shape, dtype) for shape, dtype in outs],
        scratch_shapes=[pltpu.VMEM(shape, dtype) for shape, dtype in scratch],
        name=name,
        cost_estimate=pl.CostEstimate(flops=0, bytes_accessed=1 << 20, transcendentals=0),
        compiler_params=pltpu.CompilerParams(vmem_limit_bytes=32 << 20),
    )(*args)


def small_kernel(box_ref, pos_ref, qv_ref, up_ref, out_ref):
    heads = pos_ref.shape[0]
    out_ref[...] = jnp.zeros_like(out_ref)
    for h in range(heads):
        out_ref[h : h + 1, :NB2] = box_ref[0, h : h + 1, :]
        out_ref[h : h + 1, NB2:] = box_ref[1, h : h + 1, :]
        out_ref[heads + h : heads + h + 1, :NB1] = pos_ref[h : h + 1, :]
        for i in range(2):
            row = (2 + i) * heads + h
            out_ref[row : row + 1, :64] = qv_ref[i : i + 1, h * 64 : h * 64 + 64]
    for i in range(up_ref.shape[1] // LANES):
        row = 4 * heads + i
        out_ref[row : row + 1, :] = up_ref[:, i * LANES : (i + 1) * LANES].astype(f32)


def small_rows(box, pos, qv, up):
    args = (box, pos, qv, up.reshape(1, -1))
    return call(small_kernel, "small", args, [((SMALL, LANES), f32)])[0]


def tn(a, b):
    return lax.dot_general(a, b, (((0,), (0,)), ((), ())), preferred_element_type=f32)


def parity_split(cur_ref, keep_ref, send_ref, first, chunk, bit):
    for mine in range(2):

        @pl.when(bit == mine)
        def _(mine=mine):
            for i in range(cur_ref.shape[0] // chunk // 2):
                to = slice(first + i * chunk, first + (i + 1) * chunk)
                at = (2 * i + mine) * chunk
                keep_ref[to, :] = cur_ref[at : at + chunk, :]
                at = (2 * i + 1 - mine) * chunk
                send_ref[to, :] = cur_ref[at : at + chunk, :]


def products_kernel(place_ref, *refs, lefts, plan, chunk):
    left, refs = refs[:lefts], list(refs[lefts:])
    rights = [[refs.pop(0) for _ in terms] for terms, _, _ in plan]
    gots = [[refs.pop(0) for _ in range(n)] for _, n, _ in plan]
    cur_s = refs.pop()
    split = 0
    for (terms, _, halve), right, got in zip(plan, rights, gots):
        out = cur_s if halve else refs.pop(0)
        col = 0
        for i, r in zip(terms, right):
            at = slice(col, col + r.shape[1])
            total = tn(left[i][...], r[...])
            for g in got:
                total = total + g[:, at].astype(f32)
            out[:, at] = total.astype(bf16)
            col += r.shape[1]
        if halve:
            if split == 0:
                keep, send = refs.pop(0), refs.pop(0)
            parity_split(cur_s, keep, send, split, chunk, place_ref[1])
            split += cur_s.shape[0] // 2


def plain_split(place, cur, bit, chunk):
    view = cur.reshape(-1, 2, chunk, cur.shape[1])
    pick = lambda i: lax.dynamic_index_in_dim(view, i, axis=1, keepdims=False)
    mine = place[1 + bit]
    return tuple(pick(i).reshape(-1, cur.shape[1]) for i in (mine, 1 - mine))


def products(place, lefts, specs, chunk):
    width = lefts[0].shape[1]
    if chunk % 16 and any(halve for _, _, halve in specs):
        whole = products(place, lefts, [(t, g, False) for t, g, _ in specs], chunk)
        parts = [plain_split(place, cur, 0, chunk) for cur in whole]
        return [jnp.concatenate(side, axis=0) for side in zip(*parts)]
    plan = [([i for i, _ in terms], len(gots), halve) for terms, gots, halve in specs]
    args = [place, *lefts]
    args += [r for terms, _, _ in specs for _, r in terms]
    args += [g for _, gots, _ in specs for g in gots]
    cols = sum(r.shape[1] for _, r in specs[0][0])
    outs = [((width, cols), bf16) for _, _, halve in specs if not halve]
    halved = sum(halve for _, _, halve in specs)
    if halved:
        outs += [((halved * width // 2, cols), bf16)] * 2
    kernel = functools.partial(products_kernel, lefts=len(lefts), plan=plan, chunk=chunk)
    return call(kernel, "products", args, outs, [((width, cols), bf16)], smem=1)


def add_split_kernel(place_ref, keep_ref, got_ref, out_ref, send_ref, cur_s, *, bit, chunk):
    total = keep_ref[...].astype(f32) + got_ref[...].astype(f32)
    cur_s[...] = total.astype(bf16)
    parity_split(cur_s, out_ref, send_ref, 0, chunk, place_ref[1 + bit])


def add_split(place, keep, got, bit, chunk):
    rows, cols = keep.shape
    if chunk % 16:
        total = keep.astype(f32) + got.astype(f32)
        return plain_split(place, total.astype(bf16), bit, chunk)
    half = ((rows // 2, cols), bf16)
    kernel = functools.partial(add_split_kernel, bit=bit, chunk=chunk)
    return call(kernel, "add_split", (place, keep, got), [half, half], [((rows, cols), bf16)], smem=1)


def tokens_kernel(place_ref, d0, d1, d2, d3, w0, w1, w2a, w2b, w3a, w3b, first_ref, out_ref, sum_ref, w_s):
    total = first_ref[...]
    sum_ref[...] = jnp.zeros_like(sum_ref)
    cols = d0.shape[1]
    for i, (d, ws) in enumerate(((d0, (w0,)), (d1, (w1,)), (d2, (w2a, w2b)), (d3, (w3a, w3b)))):
        load_rows(ws, place_ref[1], w_s)
        total = total + nn(d[...], w_s[0:cols, :])
        sum_ref[i : i + 1, :] = jnp.sum(d[...].astype(f32), axis=0, keepdims=True)
    out_ref[...] = total.astype(bf16)


def tokens_grad(place, dmixed, weights, d_first):
    rows, width = d_first.shape
    cols = dmixed[0].shape[1]
    args = (place, *dmixed, *weights, d_first)
    outs = [((rows, width), bf16), ((8, cols), f32)]
    return call(tokens_kernel, "tokens_grad", args, outs, [((width, width), bf16)], smem=1)


SHARED = 40
EACH = 16


def pack_kernel(hist_ref, mix_ref, u0, u1, u2, u3, v0, v1, v2, v3, v4, v5, keep_ref, send_ref, *, heads):
    keep_ref[...] = jnp.zeros_like(keep_ref)
    send_ref[...] = jnp.zeros_like(send_ref)
    for g, up in enumerate((u0, u1, u2, u3)):
        ref, first = (keep_ref, send_ref)[g // 2], (g % 2) * EACH
        for h in range(heads):
            for i, part in ((0, 0), (1, 2)):
                col = (part * heads + h) * HEAD_DIM
                ref[first + h : first + h + 1, i * 64 : i * 64 + 64] = mix_ref[g : g + 1, col : col + 64]
            row = hist_ref[g * heads + h : g * heads + h + 1, :]
            ref[first + heads + h : first + heads + h + 1, :] = row[:, :LANES]
            ref[first + 2 * heads + h : first + 2 * heads + h + 1, :NB1] = row[:, LANES:]
        for i in range(6):
            at = slice(first + 3 * heads + i, first + 3 * heads + i + 1)
            ref[at, :] = up[:, i * LANES : (i + 1) * LANES]
    for j, v in enumerate((v0, v1, v2, v3, v4, v5)):
        for i in range(6):
            at = slice(2 * EACH + 6 * j + i, 2 * EACH + 6 * j + i + 1)
            row = v[:, i * LANES : (i + 1) * LANES]
            keep_ref[at, :] = row
            send_ref[at, :] = row


def pack_sums(hist, mixed_sums, ups, shared):
    args = (hist, mixed_sums, *(v.reshape(1, -1) for v in ups), *(v.reshape(1, -1) for v in shared))
    outs = [((2 * EACH + SHARED, LANES), f32)] * 2
    heads = mixed_sums.shape[1] // (3 * HEAD_DIM)
    return call(functools.partial(pack_kernel, heads=heads), "pack_sums", args, outs)


def core_swap(v):
    return lax.ppermute(v, "heads", [(i, i ^ 1) for i in range(4)])


def x_swap(v):
    return lax.ppermute(v, "heads", [(i, i ^ 2) for i in range(4)])


def page_swap(v, bit):
    return lax.ppermute(v, "pages", [(i, i ^ bit) for i in range(lax.axis_size("pages"))])


def after(value, *others):
    return lax.optimization_barrier((value, *others))[0]


def half_rows(shard):
    half = shard.shape[0] // 2
    odd = lax.axis_index("pages") % 2
    return lax.dynamic_slice_in_dim(shard, odd * half, half, 0)


def join_rows(mine, theirs):
    odd = lax.axis_index("pages") % 2
    return jnp.where(
        odd == 0, jnp.concatenate((mine, theirs), 0), jnp.concatenate((theirs, mine), 0)
    )


def finish(place, keep, got, bit, chunk):
    last = lax.axis_size("pages").bit_length() - 1
    while bit + 1 < last:
        bit += 1
        keep, send = add_split(place, keep, got, bit, chunk)
        got = page_swap(send, 1 << bit)
    return keep.astype(f32) + got.astype(f32)


def add_all(v, bits):
    for bit in bits:
        v = v + page_swap(v, bit)
    return v


def unit_norm(values):
    centered = values - jnp.mean(values, axis=-1, keepdims=True)
    inv_std = lax.rsqrt(jnp.mean(centered * centered, axis=-1, keepdims=True) + EPSILON)
    return centered * inv_std, inv_std


def norm_grad(unit, inv_std, e):
    return inv_std * (
        e - jnp.mean(e, axis=-1, keepdims=True) - unit * jnp.mean(e * unit, axis=-1, keepdims=True)
    )


def on_device(
    tokens,
    w_qkv,
    qv_bias,
    w_out,
    out_bias,
    norm1_gain,
    norm1_shift,
    w_up,
    up_bias,
    w_down,
    down_bias,
    norm2_gain,
    norm2_shift,
    pos_table,
    box_table,
    receipt_lengths,
    page_boxes,
    out_cotangent,
):
    seq_len = tokens.shape[1]
    width = tokens.shape[2]
    heads_here = pos_table.shape[0]
    inner = heads_here * HEAD_DIM
    units = w_up.shape[1]
    own_page = lax.axis_index("heads")
    page_bits = [1 << b for b in range(lax.axis_size("pages").bit_length() - 1)]
    chunk = width // lax.axis_size("pages")
    me = lax.axis_index("pages")
    place = jnp.stack([own_page] + [(me >> b) & 1 for b in range(len(page_bits))]).astype(i32)
    tok = tokens.reshape(seq_len, width)

    own_qkv = w_qkv.reshape(width, 3 * inner).T
    c_qkv, c_out = core_swap(own_qkv), core_swap(w_out)
    half_a = half_rows(jnp.concatenate((own_qkv, w_out), axis=0))
    half_b, half_c = half_rows(w_up), half_rows(w_down)
    small = small_rows(box_table, pos_table, qv_bias, up_bias)
    c_small, x_small = core_swap(small), x_swap(small)
    mine_a = x_swap(half_a)
    mine_b = x_swap(half_b)
    mine_c = x_swap(half_c)
    ids, mask = make_ids(place, receipt_lengths, page_boxes)

    near_w = ((own_qkv,), (after(c_qkv, mine_a, half_b, half_c),))
    near_att, own_att, c_att, *near = attn_fwd(
        place, tok, near_w, (small, c_small), ids, mask, heads_here
    )
    theirs_a = page_swap(mine_a, 1)
    xc_mine_a, xc_theirs_a = core_swap(mine_a), core_swap(after(theirs_a, near_att))
    x_small, mine_b = lax.optimization_barrier((x_small, mine_b, near_att))[:2]
    xc_small = core_swap(x_small)
    theirs_b = page_swap(mine_b, 1)
    far_w = ((mine_a, theirs_a), (after(xc_mine_a, mine_b), xc_theirs_a))
    far_att, x_att, xc_att, *far = attn_fwd(
        place, tok, far_w, (x_small, xc_small), ids, mask, heads_here
    )
    mine_c = after(mine_c, far_att)
    theirs_c = page_swap(mine_c, 1)
    c_up, c_down = core_swap(w_up), core_swap(w_down)
    c_up, c_down, mine_a, theirs_a, xc_mine_a, xc_theirs_a, mine_b, theirs_b = (
        lax.optimization_barrier(
            (c_up, c_down, mine_a, theirs_a, xc_mine_a, xc_theirs_a, mine_b, theirs_b, far_att)
        )[:-1]
    )
    odd = me % 2
    pick = lambda m, t: jnp.where(odd == 1, m, t)[-inner:]
    out_all = jnp.concatenate(
        (w_out, c_out, pick(mine_a, theirs_a), pick(xc_mine_a, xc_theirs_a)), axis=0
    )
    near_out, far_out = out_all[: 2 * inner], out_all[2 * inner :]
    x_up = join_rows(mine_b, theirs_b)
    xc_up = core_swap(x_up)
    first_in = nn(near_att, near_out) + nn(far_att, far_out) + out_bias + tok.astype(f32)
    unit1, inv1 = unit_norm(first_in)
    first_out = unit1 * norm1_gain + norm1_shift
    first_low = first_out.astype(bf16)

    def units_of(weights, little):
        up = nn(first_low, weights) + little[4 * heads_here :].reshape(-1)[:units]
        cdf = 0.5 * (1.0 + lax.erf(up * math.sqrt(0.5)))
        slope = cdf + up * jnp.exp(-0.5 * up * up) * (1.0 / math.sqrt(2.0 * math.pi))
        return (up * cdf).astype(bf16), slope.astype(bf16)

    littles = (small, c_small, x_small, xc_small)
    ups = (w_up, c_up, x_up, xc_up)
    hiddens, slopes = zip(*(units_of(w, t) for w, t in zip(ups, littles)))
    x_down = join_rows(after(mine_c, first_low), theirs_c)
    downs = (w_down, c_down, x_down, core_swap(x_down))
    second_in = sum(nn(h, w) for h, w in zip(hiddens, downs)) + down_bias + first_out
    unit2, inv2 = unit_norm(second_in)
    layer_out = (unit2 * norm2_gain + norm2_shift).astype(bf16)

    def norm_back(unit, inv_std, gain, dy):
        return norm_grad(unit, inv_std, dy * gain), jnp.sum(dy * unit, axis=0), jnp.sum(dy, axis=0)

    ct = out_cotangent.reshape(seq_len, width).astype(f32)
    d_second, g_gain2, g_shift2 = norm_back(unit2, inv2, norm2_gain, ct)
    g_down_bias = jnp.sum(d_second, axis=0)
    d_ffn = d_second.astype(bf16)

    to_x, to_c = products(
        place, [d_ffn], [([(0, hiddens[3])], [], False), ([(0, hiddens[1])], [], False)], chunk
    )
    got_xc, got_c = core_swap(to_x), core_swap(to_c)
    d_ups = [(nt(d_ffn, w) * s.astype(f32)).astype(bf16) for w, s in zip(downs, slopes)]
    far_gd, own_gd = products(
        place,
        [after(d_ffn, *d_ups)],
        [([(0, hiddens[2])], [got_xc], False), ([(0, hiddens[0])], [got_c], False)],
        chunk,
    )
    got_xd = x_swap(far_gd)

    to_x, to_c = products(
        place,
        [after(first_low, far_gd)],
        [([(0, d_ups[3])], [], False), ([(0, d_ups[1])], [], False)],
        chunk,
    )
    got_xc, got_c = core_swap(to_x), core_swap(to_c)
    d_mid = sum(nt(d, w) for d, w in zip([after(d_ups[0], to_x), *d_ups[1:]], ups))
    keep_u, send_u = products(
        place,
        [after(first_low, d_mid)],
        [([(0, d_ups[0])], [got_c], True), ([(0, d_ups[2])], [got_xc], True)],
        chunk,
    )
    got_yu = page_swap(send_u, 1)
    d_first, g_gain1, g_shift1 = norm_back(unit1, inv1, norm1_gain, after(d_second, send_u) + d_mid)
    g_out_bias = jnp.sum(d_first, axis=0)
    d_proj = d_first.astype(bf16)
    far_datt = nt(d_proj, far_out).astype(bf16)
    near_datt = nt(d_proj, near_out).astype(bf16)
    x_dmixed, xc_dmixed, far_ds, far_dsv = attn_bwd(seq_len, *far[:3], far_datt, *far[3:])

    lefts = [tok, d_proj]
    (to_x,) = products(place, lefts, [([(0, xc_dmixed), (1, xc_att)], [], False)], chunk)
    got_xc = core_swap(to_x)
    keep_d, send_d = add_split(place, own_gd, after(got_xd, to_x), 0, chunk)
    got_yd = page_swap(send_d, 1)
    (far_gq,) = products(
        place, [after(tok, send_d), d_proj], [([(0, x_dmixed), (1, x_att)], [got_xc], False)], chunk
    )
    got_xq = x_swap(far_gq)
    own_dmixed, c_dmixed, near_ds, near_dsv = attn_bwd(
        seq_len, *near[:3], after(near_datt, far_gq), *near[3:]
    )
    (to_c,) = products(place, lefts, [([(0, c_dmixed), (1, c_att)], [], False)], chunk)
    got_cq = core_swap(to_c)
    dmixed = (own_dmixed, c_dmixed, x_dmixed, xc_dmixed)

    half = width // 2
    keep_d, send_d = add_split(place, keep_d, after(got_yd, to_c), 1, chunk)
    got_zd = page_swap(send_d, 2)
    acc = jnp.zeros((16, 160), f32)
    acc = add_hist(after(acc, send_d), ids, (near_ds, far_ds), 0, SPAN // 2, False)
    got_yu = after(got_yu, acc)
    far_gu = (keep_u[half:].astype(f32) + got_yu[half:].astype(f32)).astype(bf16)
    own_gu = (keep_u[:half].astype(f32) + got_yu[:half].astype(f32)).astype(bf16)
    got_xu = x_swap(far_gu)
    keep_d, send_d = add_split(place, keep_d, after(got_zd, acc), 2, chunk)
    got_zd = page_swap(send_d, 4)
    acc = add_hist(
        after(acc, far_gu, send_d), ids, (near_ds, far_ds), SPAN // 2, SPAN // 2, False
    )
    keep_q, send_q = products(
        place,
        [after(tok, acc), d_proj],
        [([(0, own_dmixed), (1, own_att)], [got_cq, got_xq], True)],
        chunk,
    )
    got_yq = page_swap(send_q, 1)
    acc = add_hist(after(acc, send_q, got_zd), ids, (near_dsv, far_dsv), 0, ROWS, True)
    weights = (own_qkv, c_qkv, mine_a, theirs_a, xc_mine_a, xc_theirs_a)
    grad_tokens, mixed_sums = tokens_grad(
        place, dmixed, (after(own_qkv, acc), *weights[1:]), d_first
    )
    g_up_bias = [jnp.sum(d.astype(f32), axis=0) for d in d_ups]
    shared = (g_out_bias, g_gain1, g_shift1, g_down_bias, g_gain2, g_shift2)
    keep, send = pack_sums(acc, mixed_sums, g_up_bias, shared)
    got = x_swap(send)
    keep_u, send_u = add_split(place, own_gu, after(got_xu, send), 1, chunk)
    got_zu = page_swap(send_u, 2)
    sums = keep + after(got, send_u)
    sums = jnp.concatenate((sums[:EACH], sums[2 * EACH :])) + core_swap(sums[EACH:])
    got = page_swap(sums, 1)
    keep_q, send_q = add_split(place, keep_q, after(got_yq, sums), 1, chunk)
    got_zq = page_swap(send_q, 2)
    sums = sums + after(got, send_q)
    got = page_swap(sums, 2)
    keep_u, send_u = add_split(place, keep_u, after(got_zu, sums), 2, chunk)
    got_zu = page_swap(send_u, 4)
    sums = sums + after(got, send_u)
    got = page_swap(sums, 4)
    keep_q, send_q = add_split(place, keep_q, after(got_zq, sums), 2, chunk)
    got_zq = page_swap(send_q, 4)
    sums = add_all(sums + got, page_bits[3:])
    g_w_down = finish(place, keep_d, got_zd, 2, chunk).T
    g_w_up = finish(place, keep_u, got_zu, 2, chunk)
    qo = finish(place, keep_q, got_zq, 2, chunk)
    g_w_qkv = qo[:, : 3 * inner].reshape(-1, 3, inner)
    g_w_out = qo[:, 3 * inner :].T

    both = sums[:heads_here].reshape(heads_here, 2, HEAD_DIM)
    g_qv_bias = both.transpose(1, 0, 2).reshape(2, inner)
    g_box = sums[heads_here : 2 * heads_here].reshape(heads_here, 2, NB2).transpose(1, 0, 2)
    g_pos = sums[2 * heads_here : 3 * heads_here, :NB1]
    g_up_bias = sums[3 * heads_here : 3 * heads_here + 6].reshape(units)
    shared = sums[EACH : EACH + 36].reshape(6, width)
    return (
        layer_out.reshape(tokens.shape),
        grad_tokens.reshape(tokens.shape),
        g_w_qkv,
        g_qv_bias,
        g_w_out,
        shared[0],
        shared[1],
        shared[2],
        g_w_up,
        g_up_bias,
        g_w_down,
        shared[3],
        shared[4],
        shared[5],
        g_pos,
        g_box,
    )


def solution(mesh):
    placed = (
        P(("pages", "heads"), None, None),
        P(None, None, "heads"),
        P(None, "heads"),
        P("heads", None),
        P(),
        P(),
        P(),
        P(None, "heads"),
        P("heads"),
        P("heads", None),
        P(),
        P(),
        P(),
        P("heads", None),
        P(None, "heads", None),
        P("pages", None),
        P("pages", None, None),
        P(("pages", "heads"), None, None),
    )
    return jax.shard_map(
        on_device,
        mesh=mesh,
        in_specs=placed,
        out_specs=(
            P(("pages", "heads"), None, None),
            P(("pages", "heads"), None, None),
            P("pages", None, "heads"),
            P(None, "heads"),
            P("heads", "pages"),
            P(),
            P(),
            P(),
            P("pages", "heads"),
            P("heads"),
            P("heads", "pages"),
            P(),
            P(),
            P(),
            P("heads", None),
            P(None, "heads", None),
        ),
        check_vma=False,
    )
```

```python
import functools
import math

import jax
import jax.numpy as jnp
from jax import lax
from jax.experimental import pallas as pl
from jax.experimental.pallas import tpu as pltpu
from jax.sharding import PartitionSpec as P

f32 = jnp.float32
bf16 = jnp.bfloat16
i32 = jnp.int32
EPSILON = 1e-05
MASKED_SCORE = -1e30


HEAD_DIM = 64
TEXT = 512
NB1 = 32
MD1 = 128
NB2 = 64
MD2 = 256
ROWS = 576
VIS = ROWS - TEXT
QROWS = 640
LANES = 128
CHUNK = 64
UNIT = 2048.0
BLOCKS = ((0, 256), (0, 384), (128, 384), (256, 256))
OFFS = (0, 320, 768, 1216)
SPAN = 1536
TOTAL = SPAN + ROWS
SMALL = 24


def thresholds(buckets, max_reach):
    half_range = buckets // 2
    exact_range = half_range // 2
    levels = half_range - exact_range
    return [
        math.ceil(exact_range * (max_reach / exact_range) ** (k / levels) - 1e-09)
        for k in range(1, levels)
    ]


def bucket_of(diff, buckets, reach):
    n = jnp.abs(diff)
    out = jnp.minimum(n, buckets // 4) + jnp.where(diff > 0, buckets // 2, 0)
    for t in thresholds(buckets, reach):
        out = out + jnp.where(n >= t, 1, 0)
    return out


def parts_of(blk):
    s, n = BLOCKS[blk]
    return ((s, n, OFFS[blk]), (TEXT, VIS, OFFS[blk] + n))


def nt(a, b):
    return lax.dot_general(a, b, (((1,), (1,)), ((), ())), preferred_element_type=f32)


def nn(a, b):
    return lax.dot_general(a, b, (((1,), (0,)), ((), ())), preferred_element_type=f32)


def unpack(ids):
    return ids & 255, (ids >> 8) & 255, ids >> 16


def take(tab, idx):
    return jnp.take_along_axis(
        jnp.broadcast_to(tab, idx.shape), idx, axis=1, mode="promise_in_bounds"
    )


def ids_kernel(place_ref, len_ref, box_ref, ids_ref, c_s, r_s, *, valid):
    page = place_ref[0]
    row = lax.broadcasted_iota(i32, (8, ROWS), 1)
    segment = jnp.zeros((8, ROWS), i32)
    end = 0
    for i in range(len_ref.shape[1]):
        end = end + len_ref[page, i]
        segment = segment + jnp.where(row >= end, 1, 0)
    c_s[...] = jnp.zeros_like(c_s)
    c_s[0:8, :] = segment.astype(f32)
    c_s[8:10, 0:valid] = box_ref[page].astype(f32)
    r_s[...] = c_s[...].T.astype(i32)

    def query(lo, hi):
        return tuple(c_s[i : i + 1, lo:hi].astype(i32) for i in (0, 8, 9))

    def tiles(row, out, rows, q_first, q):
        qseg, qx, qy = (jnp.broadcast_to(v, (CHUNK, LANES)) for v in q)
        lane = lax.broadcasted_iota(i32, (CHUNK, LANES), 1)
        if q_first == TEXT:
            q_pos, high = TEXT + (lane & (VIS - 1)), jnp.where(lane >= VIS, NB2, 0)
        else:
            q_pos, high = q_first + lane, 0

        def tile(c, _):
            at = pl.ds(pl.multiple_of(row + c * CHUNK, CHUNK), CHUNK)
            here = pl.ds(pl.multiple_of(out + c * CHUNK, CHUNK), CHUNK)
            seg, kx, ky = (jnp.broadcast_to(r_s[at, i : i + 1], (CHUNK, LANES)) for i in (0, 8, 9))
            k_pos = lax.broadcasted_iota(i32, (CHUNK, LANES), 0) + (row + c * CHUNK)
            x_id = bucket_of(kx - qx, NB2, MD2)
            y_id = bucket_of(ky - qy, NB2, MD2)
            p_id = bucket_of(k_pos - q_pos, NB1, MD1)
            ok = ((seg == qseg) | (k_pos >= TEXT) | (q_pos >= TEXT)) & (k_pos < valid)
            p_id = jnp.where(ok, p_id, NB1)
            y_id = y_id + (high if q_first == TEXT else NB2)
            ids_ref[here, :] = (x_id + high) + y_id * 256 + (p_id + high) * 65536
            return 0

        lax.fori_loop(0, rows // CHUNK, tile, 0)

    for blk in range(4):
        q = query(blk * LANES, (blk + 1) * LANES)
        for s, n, o in parts_of(blk):
            tiles(s, o, n, blk * LANES, q)
    q = tuple(jnp.concatenate((v, v), axis=1) for v in query(TEXT, ROWS))
    tiles(0, SPAN, ROWS, TEXT, q)


def make_ids(place, lengths, boxes):
    return pl.pallas_call(
        functools.partial(ids_kernel, valid=boxes.shape[2]),
        in_specs=[
            pl.BlockSpec(memory_space=pltpu.SMEM),
            pl.BlockSpec(memory_space=pltpu.SMEM),
            pl.BlockSpec(memory_space=pltpu.VMEM),
        ],
        out_shape=jax.ShapeDtypeStruct((TOTAL, LANES), i32),
        scratch_shapes=[pltpu.VMEM((LANES, ROWS), f32), pltpu.VMEM((ROWS, LANES), i32)],
        name="ids",
        cost_estimate=pl.CostEstimate(flops=0, bytes_accessed=0, transcendentals=0),
        compiler_params=pltpu.CompilerParams(vmem_limit_bytes=12 << 20),
    )(place, lengths, boxes)


def place(dst_ref, pair, side, cols):
    at = slice(side * 64, side * 64 + 64)
    for blk in range(4):
        first = blk * 256 + side * LANES
        dst_ref[pair, first : first + LANES, at] = cols[blk * LANES : (blk + 1) * LANES]
    first = 1024 + side * VIS
    dst_ref[pair, first : first + VIS, at] = cols[TEXT:]


def row_copies(refs, odd, dst, sems):
    if len(refs) == 1:
        rows = refs[0].shape[0]
        return [pltpu.make_async_copy(refs[0], dst.at[0:rows, :], sems.at[0])]
    half = dst.shape[0] // 2
    firsts = (odd * half, (1 - odd) * half)
    return [
        pltpu.make_async_copy(
            ref.at[0:half, :], dst.at[pl.ds(pl.multiple_of(first, half), half), :], sems.at[i]
        )
        for i, (ref, first) in enumerate(zip(refs, firsts))
    ]


def load_rows(refs, odd, dst):
    if len(refs) == 1:
        dst[0 : refs[0].shape[0], :] = refs[0][...]
    else:
        half = dst.shape[0] // 2
        for first in range(2):

            @pl.when(odd == first)
            def _(first=first):
                dst[first * half : (first + 1) * half, :] = refs[0][0:half, :]
                dst[(1 - first) * half : (2 - first) * half, :] = refs[1][0:half, :]


def pad_rows(v):
    return jnp.concatenate((v, jnp.zeros((ROWS - v.shape[0], v.shape[1]), v.dtype)), 0)


def fold(both):
    n = both.shape[1] // 2
    t = both.T
    lane = lax.broadcasted_iota(i32, (n, LANES), 1)
    return jnp.where(lane < 64, t[:n], t[n:])


def fwd_kernel(place_ref, tok_ref, *refs, pieces, pairs):
    n = 2 * pieces
    weights = (refs[:pieces], refs[pieces:n])
    small, ids_ref = refs[n : n + 2], refs[n + 2]
    out_ref, out0_ref, out1_ref, bias_ref, *kept = refs[n + 3 : n + 12]
    q_s, k_s, v_s, p_ref, pv_ref, vt_s, s_s, w_s, i_s, f_s, o_s, l_s, sems, load_sems = refs[n + 12 :]
    first = small[0].shape[0] - 16

    def copy(i, pair=None):
        src, dst = (q_s, k_s, v_s, p_ref, pv_ref)[i], kept[i]
        if pair is None:
            return pltpu.make_async_copy(src, dst, sems.at[i, 0])
        return pltpu.make_async_copy(src.at[pair], dst.at[pair], sems.at[i, pair])

    loads = [
        row_copies(weights[g], place_ref[1], w_s.at[g], load_sems.at[g]) for g in range(2)
    ]
    for c in loads[0] + loads[1]:
        c.start()
    units = 4 * pairs // 6
    bias_ref[...] = jnp.zeros_like(bias_ref)
    for g in range(2):
        bias_ref[g : g + 1, :] = small[g][first + units : first + units + 1, :].astype(f32)
    inner = pairs * HEAD_DIM
    for g in range(2):
        for i in range(4 * pairs):
            at = slice(i % 6 * LANES, (i % 6 + 1) * LANES)
            row = first + i // 6
            high, rest = (small[g][r : r + 1, at].astype(f32) for r in (row, row + 8))
            l_s[g, i : i + 1, :] = high + rest
    small = [l_s.at[g] for g in range(2)]
    tok = pad_rows(tok_ref[...])
    q_s[...] = jnp.zeros_like(q_s)
    for g in range(2):
        for c in loads[g]:
            c.wait()
        for part in range(3):
            mixed = nt(tok, w_s[g, part * inner : (part + 1) * inner, :])
            for local in range(pairs):
                pair, side = divmod(g * pairs + local, 2)
                at = slice(side * 64, side * 64 + 64)
                cols = mixed[:, local * 64 : local * 64 + 64]
                if part == 0:
                    cols = cols + small[g][2 * pairs + local : 2 * pairs + local + 1, :64]
                    place(q_s, pair, side, (cols * (UNIT / 8)).astype(bf16))
                elif part == 1:
                    k_s[pair, :, at] = cols.astype(bf16)
                else:
                    cols = cols + small[g][3 * pairs + local : 3 * pairs + local + 1, :64]
                    v_s[pair, :, at] = cols.astype(bf16)
                    vt_s[pair, at, :] = cols.T.astype(bf16)
    for i in range(3):
        copy(i).start()
    for pair in range(pairs):
        (ga, la), (gb, lb) = divmod(2 * pair, pairs), divmod(2 * pair + 1, pairs)
        for row, first in ((0, 0), (1, pairs)):
            a = small[ga][first + la : first + la + 1, :] * UNIT
            b = small[gb][first + lb : first + lb + 1, :] * UNIT
            i_s[pair, row : row + 1, :] = (
                jnp.round(a).astype(i32) * 65536 + jnp.round(b).astype(i32)
            )
            f_s[pair, 2 * row : 2 * row + 1, :] = jnp.concatenate((a[:, :64], b[:, :64]), 1)
            f_s[pair, 2 * row + 1 : 2 * row + 2, :] = jnp.concatenate((a[:, 64:], b[:, 64:]), 1)

    def softmax(total, wide, p_at):
        m = jnp.full((8, wide), -3e38, f32)
        for c in range(0, total, 8):
            m = jnp.maximum(m, s_s[c : c + 8, :wide])
        m = jnp.max(m, axis=0, keepdims=True)
        l = jnp.zeros((8, wide), f32)
        for c in range(0, total, 8):
            e = jnp.exp2((s_s[c : c + 8, :wide] - m) * (math.log2(math.e) / UNIT))
            s_s[c : c + 8, :wide] = e
            l = l + e
        inv = 1.0 / jnp.sum(l, axis=0, keepdims=True)
        for c in range(0, total, 16):
            p_at(c, (s_s[c : c + 16, :wide] * inv).astype(bf16))

    def one_pair(pair, _):
        t_xy, t_p = (i_s[pair, i : i + 1, :] for i in range(2))
        v_x, v_y, v_p = (f_s[pair, i : i + 1, :] for i in range(3))
        for blk in range(4):
            q = q_s[pair, blk * 256 : (blk + 1) * 256, :]
            first = OFFS[blk]
            for s, n, o in parts_of(blk):
                sc = nt(k_s[pair, s : s + n, :], q)
                for c in range(0, n, 16):
                    r = slice(o + c, o + c + 16)
                    x, y, p = unpack(ids_ref[r, :])
                    b = take(t_xy, x) + take(t_xy, y) + take(t_p, p)
                    low = (b << 16) >> 16
                    high = (b - low) >> 16
                    add = jnp.where(p == NB1, MASKED_SCORE, 0.0)
                    to = slice(o - first + c, o - first + c + 16)
                    s_s[to, :LANES] = sc[c : c + 16, :LANES] + (high.astype(f32) + add)
                    s_s[to, LANES:] = sc[c : c + 16, LANES:] + (low.astype(f32) + add)

            def put(c, v, first=first):
                p_ref[pair, first + c : first + c + 16, :] = v

            softmax(BLOCKS[blk][1] + VIS, 256, put)
            ot = sum(
                nn(vt_s[pair, :, s : s + n], p_ref[pair, o : o + n, :]) for s, n, o in parts_of(blk)
            )
            o_s[pair, blk * LANES : (blk + 1) * LANES, :] = fold(ot).astype(bf16)
        q = q_s[pair, 1024:1152, :]
        sc = nt(k_s[pair], q)
        for c in range(0, ROWS, 16):
            r = slice(SPAN + c, SPAN + c + 16)
            x, y, p = unpack(ids_ref[r, :])
            b = take(v_x, x) + take(v_y, y) + take(v_p, p)
            add = jnp.where((p & (NB2 - 1)) == NB1, MASKED_SCORE, 0.0)
            s_s[c : c + 16, :LANES] = sc[c : c + 16] + (b + add)

        def put_v(c, v):
            pv_ref[pair, c : c + 16, :] = v

        softmax(ROWS, LANES, put_v)
        o_s[pair, TEXT:ROWS, :] = fold(nn(vt_s[pair], pv_ref[pair])).astype(bf16)
        copy(3, pair).start()
        copy(4, pair).start()
        return 0

    lax.fori_loop(0, pairs, one_pair, 0)
    rows = out_ref.shape[0]
    for pair in range(pairs):
        out_ref[:, pair * LANES : (pair + 1) * LANES] = o_s[pair, 0:rows, :]
    for h in range(2 * pairs):
        g, local = divmod(h, pairs)
        here = o_s[h // 2, 0:rows, (h % 2) * 64 : (h % 2) * 64 + 64]
        (out0_ref, out1_ref)[g][:, local * 64 : local * 64 + 64] = here
    for i in range(3):
        copy(i).wait()
    for pair in range(pairs):
        copy(3, pair).wait()
        copy(4, pair).wait()


def attn_fwd(place, tok, weights, small, ids, pairs):
    pieces, rows = len(weights[0]), tok.shape[0]
    kept = [(pairs, 1152, LANES)] + [(pairs, ROWS, LANES)] * 2
    kept += [(pairs, SPAN, 256), (pairs, ROWS, LANES)]
    vmem = pl.BlockSpec(memory_space=pltpu.VMEM)
    return pl.pallas_call(
        functools.partial(fwd_kernel, pieces=pieces, pairs=pairs),
        in_specs=[pl.BlockSpec(memory_space=pltpu.SMEM), vmem]
        + [pl.BlockSpec(memory_space=pltpu.HBM)] * (2 * pieces)
        + [vmem] * 3,
        out_shape=[
            jax.ShapeDtypeStruct((rows, pairs * LANES), bf16),
            jax.ShapeDtypeStruct((rows, pairs * 64), bf16),
            jax.ShapeDtypeStruct((rows, pairs * 64), bf16),
            jax.ShapeDtypeStruct((8, tok.shape[1]), f32),
        ]
        + [jax.ShapeDtypeStruct(shape, bf16) for shape in kept],
        out_specs=[vmem] * 4 + [pl.BlockSpec(memory_space=pltpu.HBM)] * 5,
        scratch_shapes=[pltpu.VMEM(shape, bf16) for shape in kept]
        + [
            pltpu.VMEM((pairs, LANES, ROWS), bf16),
            pltpu.VMEM((ROWS, 256), f32),
            pltpu.VMEM((2, 4 * pairs * HEAD_DIM, tok.shape[1]), bf16),
            pltpu.VMEM((pairs, 8, LANES), i32),
            pltpu.VMEM((pairs, 8, LANES), f32),
            pltpu.VMEM((pairs, ROWS, LANES), bf16),
            pltpu.VMEM((2, SMALL, LANES), f32),
            pltpu.SemaphoreType.DMA((5, pairs)),
            pltpu.SemaphoreType.DMA((2, 2)),
        ],
        name="attn_fwd",
        cost_estimate=pl.CostEstimate(flops=0, bytes_accessed=0, transcendentals=0),
        compiler_params=pltpu.CompilerParams(vmem_limit_bytes=22 << 20),
    )(place, tok, *weights[0], *weights[1], *small, ids)


def bwd_kernel(q_s, k_ref, v_s, do_ref, p_ref, pv_ref, out0_ref, out1_ref, sum_ref, ds_out, dsv_out, ds_ref, dsv_ref, do_s, kt_s, dq_s, dk_s, dv_s, sems, *, pairs):
    def copies(pair):
        return [
            pltpu.make_async_copy(src.at[pair], dst.at[pair], sems.at[i, pair])
            for i, (src, dst) in enumerate(((ds_ref, ds_out), (dsv_ref, dsv_out)))
        ]

    rows = out0_ref.shape[0]
    sum_ref[...] = jnp.zeros_like(sum_ref)
    do_s[...] = jnp.zeros_like(do_s)
    for h in range(2 * pairs):
        pair, side = divmod(h, 2)
        place(do_s, pair, side, pad_rows(do_ref[:, h * 64 : h * 64 + 64]))
    for pair in range(pairs):
        kt_s[pair] = k_ref[pair].astype(f32).T.astype(bf16)

    def grad_scores(dps, ps, put):
        d = jnp.zeros((8, dps[0].shape[1]), f32)
        for dp, p in zip(dps, ps):
            for c in range(0, dp.shape[0], 16):
                t = p(c).astype(f32) * dp[c : c + 16]
                d = d + (t[:8] + t[8:])
        d = jnp.sum(d, axis=0, keepdims=True)
        for i, (dp, p) in enumerate(zip(dps, ps)):
            for c in range(0, dp.shape[0], 16):
                put(i, c, (p(c).astype(f32) * (dp[c : c + 16] - d)).astype(bf16))

    def one_pair(pair, _):
        dv_s[...] = jnp.zeros_like(dv_s)
        dk_s[...] = jnp.zeros_like(dk_s)
        for blk in range(4):
            q = q_s[pair, blk * 256 : (blk + 1) * 256, :]
            do = do_s[pair, blk * 256 : (blk + 1) * 256, :]
            parts = parts_of(blk)

            def put(i, c, v, parts=parts):
                ds_ref[pair, parts[i][2] + c : parts[i][2] + c + 16, :] = v

            grad_scores(
                [nt(v_s[pair, s : s + n, :], do) for s, n, o in parts],
                [lambda c, o=o: p_ref[pair, o + c : o + c + 16, :] for s, n, o in parts],
                put,
            )
            dq = 0.0
            for s, n, o in parts:
                ds = ds_ref[pair, o : o + n, :]
                dq = dq + nn(kt_s[pair, :, s : s + n], ds)
                dv_s[s : s + n, :] += nn(p_ref[pair, o : o + n, :], do)
                dk_s[s : s + n, :] += nn(ds, q)
            dq_s[pair, 0, blk * LANES : (blk + 1) * LANES, :] = (fold(dq) * 0.125).astype(bf16)
        q = q_s[pair, 1024:1152, :]
        do = do_s[pair, 1024:1152, :]

        def put_v(i, c, v):
            dsv_ref[pair, c : c + 16, :] = v

        grad_scores([nt(v_s[pair], do)], [lambda c: pv_ref[pair, c : c + 16, :]], put_v)
        ds = dsv_ref[pair]
        dq_s[pair, 0, TEXT:ROWS, :] = (fold(nn(kt_s[pair], ds)) * 0.125).astype(bf16)
        dq_s[pair, 1] = ((dk_s[...] + nn(ds, q)) * (1.0 / UNIT)).astype(bf16)
        dq_s[pair, 2] = (dv_s[...] + nn(pv_ref[pair], do)).astype(bf16)
        for copy in copies(pair):
            copy.start()
        return 0

    lax.fori_loop(0, pairs, one_pair, 0)
    for h in range(2 * pairs):
        pair, side = divmod(h, 2)
        g, local = divmod(h, pairs)
        for part in range(3):
            col = part * pairs * HEAD_DIM + local * HEAD_DIM
            here = dq_s[pair, part, 0:rows, side * 64 : side * 64 + 64]
            (out0_ref, out1_ref)[g][:, col : col + 64] = here
            if part != 1:
                total = jnp.sum(here.astype(f32), axis=0, keepdims=True)
                sum_ref[g : g + 1, col : col + 64] = total
    for pair in range(pairs):
        for copy in copies(pair):
            copy.wait()


def attn_bwd(rows, q, k, v, d_att, p, pv):
    pairs = p.shape[0]
    out = jax.ShapeDtypeStruct((rows, 3 * pairs * HEAD_DIM), bf16)
    return pl.pallas_call(
        functools.partial(bwd_kernel, pairs=pairs),
        out_shape=(
            out,
            out,
            jax.ShapeDtypeStruct((8, out.shape[1]), f32),
            jax.ShapeDtypeStruct(p.shape, bf16),
            jax.ShapeDtypeStruct(pv.shape, bf16),
        ),
        out_specs=[pl.BlockSpec(memory_space=pltpu.VMEM)] * 3
        + [pl.BlockSpec(memory_space=pltpu.HBM)] * 2,
        scratch_shapes=[
            pltpu.VMEM(p.shape, bf16),
            pltpu.VMEM(pv.shape, bf16),
            pltpu.VMEM((pairs, 1152, LANES), bf16),
            pltpu.VMEM((pairs, LANES, ROWS), bf16),
            pltpu.VMEM((pairs, 3, ROWS, LANES), bf16),
            pltpu.VMEM((ROWS, LANES), f32),
            pltpu.VMEM((ROWS, LANES), f32),
            pltpu.SemaphoreType.DMA((2, pairs)),
        ],
        name="attn_bwd",
        cost_estimate=pl.CostEstimate(flops=0, bytes_accessed=0, transcendentals=0),
        compiler_params=pltpu.CompilerParams(vmem_limit_bytes=22 << 20),
    )(q, k, v, d_att, p, pv)


HSTEP = 64
HBLOCK = 192


def hist_kernel(acc_ref, ids_ref, *refs, sets, pairs, visual):
    ds_refs, hist_ref, l_s = refs[:sets], refs[-2], refs[-1]
    io = lax.broadcasted_iota(i32, (NB2, LANES), 0)
    heads = 2 * sets * pairs

    @pl.when(pl.program_id(0) == 0)
    def _():
        hist_ref[...] = acc_ref[...]

    for h in range(heads, 16):
        l_s[pl.ds(h, HSTEP, stride=16), :] = jnp.zeros((HSTEP, LANES), f32)

    def step(r, acc):
        first = pl.multiple_of(r * HSTEP, HSTEP)
        lane = lax.broadcasted_iota(i32, (HSTEP, LANES), 1)
        for pair in range(sets * pairs):
            ref = ds_refs[pair // pairs]
            for side in range(2):
                if visual:
                    v = ref[pair % pairs, pl.ds(first, HSTEP), :].astype(f32)
                    v = jnp.where((lane >= VIS) == bool(side), v, 0.0)
                else:
                    at = slice(side * LANES, (side + 1) * LANES)
                    v = ref[pair % pairs, pl.ds(first, HSTEP), at].astype(f32)
                l_s[pl.ds(2 * pair + side, HSTEP, stride=16), :] = v
        lhs, rhs = [], []
        for u in range(HSTEP):
            x, y, p = unpack(ids_ref[pl.ds(first + u, 1), :])
            if visual:
                x, y, p = (v & (NB2 - 1) for v in (x, y, p))
            else:
                y = y - NB2
            hot = [jnp.where(io == x, 1.0, 0.0), jnp.where(io == y, 1.0, 0.0)]
            hot.append(jnp.where(io[:NB1] == p, 1.0, 0.0))
            rhs.append(jnp.concatenate(hot, 0).astype(bf16))
            lhs.append(l_s[u * 16 : u * 16 + 16, :].astype(bf16))
        return acc + nt(jnp.concatenate(lhs, 1), jnp.concatenate(rhs, 1))

    hist_ref[...] = lax.fori_loop(0, HBLOCK // HSTEP, step, hist_ref[...])


def add_hist(acc, ids, ds, first_row, rows, visual):
    first = first_row // HBLOCK
    first_id = first + (SPAN // HBLOCK if visual else 0)
    specs = [
        pl.BlockSpec((16, 160), lambda i: (0, 0)),
        pl.BlockSpec((HBLOCK, LANES), lambda i: (first_id + i, 0)),
    ]
    for t in ds:
        specs.append(pl.BlockSpec((t.shape[0], HBLOCK, t.shape[2]), lambda i: (0, first + i, 0)))
    return pl.pallas_call(
        functools.partial(hist_kernel, sets=len(ds), pairs=ds[0].shape[0], visual=visual),
        grid=(rows // HBLOCK,),
        in_specs=specs,
        out_specs=pl.BlockSpec((16, 160), lambda i: (0, 0)),
        out_shape=jax.ShapeDtypeStruct((16, 160), f32),
        scratch_shapes=[pltpu.VMEM((HSTEP * 16, LANES), f32)],
        name="hist",
        cost_estimate=pl.CostEstimate(flops=0, bytes_accessed=0, transcendentals=0),
        compiler_params=pltpu.CompilerParams(vmem_limit_bytes=12 << 20),
    )(acc, ids, *ds)


def call(kernel, name, args, outs, scratch=(), smem=0):
    vmem = pl.BlockSpec(memory_space=pltpu.VMEM)
    return pl.pallas_call(
        kernel,
        in_specs=[pl.BlockSpec(memory_space=pltpu.SMEM)] * smem + [vmem] * (len(args) - smem),
        out_shape=[jax.ShapeDtypeStruct(shape, dtype) for shape, dtype in outs],
        scratch_shapes=[pltpu.VMEM(shape, dtype) for shape, dtype in scratch],
        name=name,
        cost_estimate=pl.CostEstimate(flops=0, bytes_accessed=0, transcendentals=0),
        compiler_params=pltpu.CompilerParams(vmem_limit_bytes=20 << 20),
    )(*args)


def start_kernel(place_ref, qkv_ref, wo_ref, up_ref, down_ref, box_ref, pos_ref, qv_ref, ub_ref, a_ref, bc_ref, small_ref, s_s, o_s, sems):
    half = bc_ref.shape[0] // 2
    inner = wo_ref.shape[0]
    odd = place_ref[1]

    def copy(src, dst, i):
        return pltpu.make_async_copy(src, dst, sems.at[i])

    tail = qkv_ref.shape[0] - half
    firsts = [copy(qkv_ref.at[0:half, :], a_ref.at[0:half, :], 0)]
    seconds = [
        copy(qkv_ref.at[half:, :], a_ref.at[0:tail, :], 0),
        copy(wo_ref, a_ref.at[tail:half, :], 1),
    ]

    @pl.when(odd == 0)
    def _():
        for c in firsts:
            c.start()

    @pl.when(odd == 1)
    def _():
        for c in seconds:
            c.start()

    at = pl.ds(pl.multiple_of(odd * half, half), half)
    others = [
        copy(up_ref.at[at, :], bc_ref.at[0:half, :], 2),
        copy(down_ref.at[at, :], bc_ref.at[half:, :], 3),
    ]
    for c in others:
        c.start()
    heads = pos_ref.shape[0]
    s_s[...] = jnp.zeros_like(s_s)
    for h in range(heads):
        s_s[h : h + 1, :NB2] = box_ref[0, h : h + 1, :]
        s_s[h : h + 1, NB2:] = box_ref[1, h : h + 1, :]
        s_s[heads + h : heads + h + 1, :NB1] = pos_ref[h : h + 1, :]
        for i in range(2):
            row = (2 + i) * heads + h
            s_s[row : row + 1, :64] = qv_ref[i : i + 1, h * 64 : h * 64 + 64]
    for i in range(ub_ref.shape[1] // LANES):
        row = 4 * heads + i
        s_s[row : row + 1, :] = ub_ref[:, i * LANES : (i + 1) * LANES].astype(f32)
    o_s[...] = jnp.zeros_like(o_s)
    for i in range(SMALL):
        at = slice(i % 6 * LANES, (i % 6 + 1) * LANES)
        value = s_s[i : i + 1, :]
        high = value.astype(bf16).astype(f32)
        o_s[i // 6 : i // 6 + 1, at] = high
        o_s[8 + i // 6 : 9 + i // 6, at] = value - high
    small_ref[...] = o_s[...].astype(bf16)
    last = copy(small_ref, a_ref.at[half : half + 16, :], 4)
    last.start()

    @pl.when(odd == 0)
    def _():
        for c in firsts:
            c.wait()

    @pl.when(odd == 1)
    def _():
        for c in seconds:
            c.wait()

    for c in others + [last]:
        c.wait()


def start_parts(place, qkv, w_out, w_up, w_down, box, pos, qv, up):
    width = qkv.shape[1]
    vmem, hbm = (pl.BlockSpec(memory_space=m) for m in (pltpu.VMEM, pltpu.HBM))
    shapes = [(width // 2 + 16, width), (width, width), (16, width)]
    return pl.pallas_call(
        start_kernel,
        in_specs=[pl.BlockSpec(memory_space=pltpu.SMEM)] + [hbm] * 4 + [vmem] * 4,
        out_specs=[hbm] * 2 + [vmem],
        out_shape=[jax.ShapeDtypeStruct(shape, bf16) for shape in shapes],
        scratch_shapes=[
            pltpu.VMEM((SMALL, LANES), f32),
            pltpu.VMEM((16, width), f32),
            pltpu.SemaphoreType.DMA((5,)),
        ],
        name="start_parts",
        cost_estimate=pl.CostEstimate(flops=0, bytes_accessed=0, transcendentals=0),
        compiler_params=pltpu.CompilerParams(vmem_limit_bytes=12 << 20),
    )(place, qkv, w_out, w_up, w_down, box, pos, qv, up.reshape(1, -1))


def join_kernel(place_ref, *refs, number):
    sems = refs[-1]
    copies = []
    for i in range(number):
        copies += row_copies(refs[2 * i : 2 * i + 2], place_ref[1], refs[2 * number + i], sems.at[i])
    for c in copies:
        c.start()
    for c in copies:
        c.wait()


def join_rows(place, *pairs):
    hbm = pl.BlockSpec(memory_space=pltpu.HBM)
    outs = [jax.ShapeDtypeStruct((2 * b.shape[0], b.shape[1]), bf16) for _, b in pairs]
    return pl.pallas_call(
        functools.partial(join_kernel, number=len(pairs)),
        in_specs=[pl.BlockSpec(memory_space=pltpu.SMEM)] + [hbm] * (2 * len(pairs)),
        out_specs=[pl.BlockSpec(memory_space=pltpu.VMEM)] * len(pairs),
        out_shape=outs,
        scratch_shapes=[pltpu.SemaphoreType.DMA((len(pairs), 2))],
        name="join_rows",
        cost_estimate=pl.CostEstimate(flops=0, bytes_accessed=0, transcendentals=0),
        compiler_params=pltpu.CompilerParams(vmem_limit_bytes=8 << 20),
    )(place, *(v for pair in pairs for v in pair))


def tn(a, b):
    return lax.dot_general(a, b, (((0,), (0,)), ((), ())), preferred_element_type=f32)


def parity_split(cur_ref, keep_ref, send_ref, first, chunk, bit):
    for mine in range(2):

        @pl.when(bit == mine)
        def _(mine=mine):
            for i in range(cur_ref.shape[0] // chunk // 2):
                to = slice(first + i * chunk, first + (i + 1) * chunk)
                at = (2 * i + mine) * chunk
                keep_ref[to, :] = cur_ref[at : at + chunk, :]
                at = (2 * i + 1 - mine) * chunk
                send_ref[to, :] = cur_ref[at : at + chunk, :]


def products_kernel(place_ref, *refs, lefts, plan, chunk):
    left, refs = refs[:lefts], list(refs[lefts:])
    rights = [[refs.pop(0) for _ in terms] for terms, _, _ in plan]
    gots = [[[refs.pop(0) for _ in range(n)] for n in counts] for _, counts, _ in plan]
    cur_s = refs.pop()
    split = 0
    for (terms, _, mode), right, got in zip(plan, rights, gots):
        outs = [cur_s] if mode == "halve" else [refs.pop(0) for _ in range(mode)]
        col = 0
        for i, r in zip(terms, right):
            at = slice(col, col + r.shape[1])
            total = tn(left[i][...], r[...])
            for pieces in got:
                wide = [g[:, at].astype(f32) for g in pieces]
                total = total + (wide[0] if len(wide) == 1 else jnp.concatenate(wide, 0))
            rows = total.shape[0] // len(outs)
            for k, out in enumerate(outs):
                out[:, at] = total[k * rows : (k + 1) * rows].astype(bf16)
            col += r.shape[1]
        if mode == "halve":
            if split == 0:
                keep, send = refs.pop(0), refs.pop(0)
            parity_split(cur_s, keep, send, split, chunk, place_ref[1])
            split += cur_s.shape[0] // 2


def plain_split(place, cur, bit, chunk):
    view = cur.reshape(-1, 2, chunk, cur.shape[1])
    pick = lambda i: lax.dynamic_index_in_dim(view, i, axis=1, keepdims=False)
    mine = place[1 + bit]
    return tuple(pick(i).reshape(-1, cur.shape[1]) for i in (mine, 1 - mine))


def products(place, lefts, specs, chunk):
    width = lefts[0].shape[1]
    halved = sum(mode == "halve" for _, _, mode in specs)
    if chunk % 16 and halved:
        whole = products(place, lefts, [(t, g, 1) for t, g, _ in specs], chunk)
        parts = [plain_split(place, cur, 0, chunk) for cur in whole]
        return [jnp.concatenate(side, axis=0) for side in zip(*parts)]
    plan = [([i for i, _ in terms], [len(p) for p in gots], mode) for terms, gots, mode in specs]
    args = [place, *lefts]
    args += [r for terms, _, _ in specs for _, r in terms]
    args += [g for _, gots, _ in specs for pieces in gots for g in pieces]
    cols = sum(r.shape[1] for _, r in specs[0][0])
    outs = []
    for _, _, mode in specs:
        if mode != "halve":
            outs += [((width // mode, cols), bf16)] * mode
    if halved:
        outs += [((halved * width // 2, cols), bf16)] * 2
    kernel = functools.partial(products_kernel, lefts=len(lefts), plan=plan, chunk=chunk)
    return call(kernel, "products", args, outs, [((width, cols), bf16)], smem=1)


def add_split_kernel(place_ref, *refs, number, bit, chunk):
    keep_ref, send_ref, cur_s = refs[2 * number :]
    first = 0
    for a, b in zip(refs[:number], refs[number : 2 * number]):
        rows = a.shape[0]
        cur_s[first : first + rows] = (a[...].astype(f32) + b[...].astype(f32)).astype(bf16)
        first += rows
    parity_split(cur_s, keep_ref, send_ref, 0, chunk, place_ref[1 + bit])


def add_split(place, keeps, gots, bit, chunk):
    rows, cols = sum(v.shape[0] for v in keeps), keeps[0].shape[1]
    if chunk % 16:
        parts = [(a.astype(f32) + b.astype(f32)).astype(bf16) for a, b in zip(keeps, gots)]
        return plain_split(place, jnp.concatenate(parts, axis=0), bit, chunk)
    half = ((rows // 2, cols), bf16)
    kernel = functools.partial(add_split_kernel, number=len(keeps), bit=bit, chunk=chunk)
    args = (place, *keeps, *gots)
    return call(kernel, "add_split", args, [half, half], [((rows, cols), bf16)], smem=1)


def tokens_kernel(place_ref, d0, d1, d2, d3, w0, w1, w2a, w2b, w3a, w3b, first_ref, out_ref, w_s):
    total = first_ref[...]
    cols = d0.shape[1]
    for i, (d, ws) in enumerate(((d0, (w0,)), (d1, (w1,)), (d2, (w2a, w2b)), (d3, (w3a, w3b)))):
        load_rows(ws, place_ref[1], w_s)
        total = total + nn(d[...], w_s[0:cols, :])
    out_ref[...] = total.astype(bf16)


def tokens_grad(place, dmixed, weights, d_first):
    rows, width = d_first.shape
    args = (place, *dmixed, *weights, d_first)
    outs = [((rows, width), bf16)]
    return call(tokens_kernel, "tokens_grad", args, outs, [((width, width), bf16)], smem=1)[0]


SHARED = 40
EACH = 16


def pack_kernel(hist_ref, near_ref, far_ref, u0, u1, u2, u3, v0, v1, v2, v3, v4, v5, keep_ref, send_ref, *, heads):
    keep_ref[...] = jnp.zeros_like(keep_ref)
    send_ref[...] = jnp.zeros_like(send_ref)
    for g, up in enumerate((u0, u1, u2, u3)):
        ref, first = (keep_ref, send_ref)[g // 2], (g % 2) * EACH
        for h in range(heads):
            for i, part in ((0, 0), (1, 2)):
                col = (part * heads + h) * HEAD_DIM
                row = (near_ref, far_ref)[g // 2][g % 2 : g % 2 + 1, col : col + 64]
                ref[first + h : first + h + 1, i * 64 : i * 64 + 64] = row
            row = hist_ref[g * heads + h : g * heads + h + 1, :]
            ref[first + heads + h : first + heads + h + 1, :] = row[:, :LANES]
            ref[first + 2 * heads + h : first + 2 * heads + h + 1, :NB1] = row[:, LANES:]
        for i in range(6):
            at = slice(first + 3 * heads + i, first + 3 * heads + i + 1)
            ref[at, :] = up[:, i * LANES : (i + 1) * LANES]
    for j, v in enumerate((v0, v1, v2, v3, v4, v5)):
        for i in range(6):
            at = slice(2 * EACH + 6 * j + i, 2 * EACH + 6 * j + i + 1)
            row = v[:, i * LANES : (i + 1) * LANES]
            keep_ref[at, :] = row
            send_ref[at, :] = row


def pack_sums(hist, near, far, ups, shared):
    args = (hist, near, far, *(v.reshape(1, -1) for v in ups), *(v.reshape(1, -1) for v in shared))
    outs = [((2 * EACH + SHARED, LANES), f32)] * 2
    heads = near.shape[1] // (3 * HEAD_DIM)
    return call(functools.partial(pack_kernel, heads=heads), "pack_sums", args, outs)


def core_swap(v):
    return lax.ppermute(v, "heads", [(i, i ^ 1) for i in range(4)])


def x_swap(v):
    return lax.ppermute(v, "heads", [(i, i ^ 2) for i in range(4)])


def page_swap(v, bit):
    return lax.ppermute(v, "pages", [(i, i ^ bit) for i in range(lax.axis_size("pages"))])


def after(value, *others):
    return lax.optimization_barrier((value, *others))[0]


def finish(place, keep, got, bit, chunk):
    last = lax.axis_size("pages").bit_length() - 1
    while bit + 1 < last:
        bit += 1
        keep, send = add_split(place, [keep], [got], bit, chunk)
        got = page_swap(send, 1 << bit)
    return keep.astype(f32) + got.astype(f32)


def add_all(v, bits):
    for bit in bits:
        v = v + page_swap(v, bit)
    return v


def unit_norm(values):
    centered = values - jnp.mean(values, axis=-1, keepdims=True)
    inv_std = lax.rsqrt(jnp.mean(centered * centered, axis=-1, keepdims=True) + EPSILON)
    return centered * inv_std, inv_std


def norm_grad(unit, inv_std, e):
    return inv_std * (
        e - jnp.mean(e, axis=-1, keepdims=True) - unit * jnp.mean(e * unit, axis=-1, keepdims=True)
    )


def on_device(
    tokens,
    w_qkv,
    qv_bias,
    w_out,
    out_bias,
    norm1_gain,
    norm1_shift,
    w_up,
    up_bias,
    w_down,
    down_bias,
    norm2_gain,
    norm2_shift,
    pos_table,
    box_table,
    receipt_lengths,
    page_boxes,
    out_cotangent,
):
    seq_len = tokens.shape[1]
    width = tokens.shape[2]
    heads_here = pos_table.shape[0]
    inner = heads_here * HEAD_DIM
    units = w_up.shape[1]
    own_page = lax.axis_index("heads")
    page_bits = [1 << b for b in range(lax.axis_size("pages").bit_length() - 1)]
    chunk = width // lax.axis_size("pages")
    me = lax.axis_index("pages")
    place = jnp.stack([own_page] + [(me >> b) & 1 for b in range(len(page_bits))]).astype(i32)
    tok = tokens.reshape(seq_len, width)

    own_qkv = w_qkv.reshape(width, 3 * inner).T
    c_qkv, c_out = core_swap(own_qkv), core_swap(w_out)
    half_a, half_bc, small = start_parts(
        place, own_qkv, w_out, w_up, w_down, box_table, pos_table, qv_bias, up_bias
    )
    c_small = core_swap(small)
    mine_a = x_swap(half_a)
    mine_bc = x_swap(half_bc)
    ids = make_ids(place, receipt_lengths, page_boxes)
    mine_a = after(mine_a, ids)

    near_w = ((own_qkv,), (after(c_qkv, mine_a),))
    near_att, own_att, c_att, near_bias, *near = attn_fwd(
        place, tok, near_w, (small, c_small), ids, heads_here
    )
    half = width // 2
    theirs_a = page_swap(mine_a, 1)
    xc_mine_a, xc_theirs_a = core_swap(mine_a), core_swap(after(theirs_a, near_att))
    mine_bc, xc_theirs_a = lax.optimization_barrier((mine_bc, xc_theirs_a))
    mine_b, mine_c = mine_bc[:half], mine_bc[half:]
    theirs_b, theirs_c = page_swap(mine_b, 1), page_swap(mine_c, 1)
    far_w = ((mine_a, theirs_a), (after(xc_mine_a, mine_b, mine_c), xc_theirs_a))
    far_att, x_att, xc_att, far_bias, *far = attn_fwd(
        place, tok, far_w, (mine_a, xc_mine_a), ids, heads_here
    )
    c_up, c_down = core_swap(after(w_up, far_att)), core_swap(after(w_down, far_att))
    theirs_b, mine_b, mine_c, c_out, mine_a, theirs_a, xc_mine_a, xc_theirs_a = (
        lax.optimization_barrier(
            (theirs_b, mine_b, mine_c, c_out, mine_a, theirs_a, xc_mine_a, xc_theirs_a, far_att)
        )[:-1]
    )
    odd = me % 2
    pick = lambda m, t: jnp.where(odd == 1, m, t)[half - inner : half]
    out_all = jnp.concatenate(
        (w_out, c_out, pick(mine_a, theirs_a), pick(xc_mine_a, xc_theirs_a)), axis=0
    )
    near_out, far_out = out_all[: 2 * inner], out_all[2 * inner :]
    xc_mine_b, xc_theirs_b = core_swap(mine_b), core_swap(theirs_b)
    xc_mine_c = core_swap(mine_c)
    first_in = nn(near_att, near_out) + nn(far_att, far_out) + out_bias + tok.astype(f32)
    unit1, inv1 = unit_norm(first_in)
    first_out = unit1 * norm1_gain + norm1_shift
    first_low = first_out.astype(bf16)

    def units_of(weights, little):
        up = nn(first_low, weights) + little
        cdf = 0.5 * (1.0 + lax.erf(up * math.sqrt(0.5)))
        slope = cdf + up * jnp.exp(-0.5 * up * up) * (1.0 / math.sqrt(2.0 * math.pi))
        return (up * cdf).astype(bf16), slope.astype(bf16)

    littles = (near_bias[0], near_bias[1], far_bias[0], far_bias[1])
    near_units = [units_of(w, t) for w, t in zip((w_up, c_up), littles)]
    xc_theirs_b = after(xc_theirs_b, near_units[0][0], near_units[1][0])
    x_up, xc_up = join_rows(place, (mine_b, theirs_b), (xc_mine_b, xc_theirs_b))
    ups = (w_up, c_up, x_up, xc_up)
    far_units = [units_of(w, t) for w, t in zip((x_up, xc_up), littles[2:])]
    hiddens, slopes = zip(*near_units, *far_units)
    xc_theirs_c = core_swap(after(theirs_c, x_up))
    x_down, xc_down = join_rows(
        place, (mine_c, theirs_c), (xc_mine_c, after(xc_theirs_c, *hiddens))
    )
    downs = (w_down, c_down, x_down, xc_down)
    second_in = sum(nn(h, w) for h, w in zip(hiddens, downs)) + down_bias + first_out
    unit2, inv2 = unit_norm(second_in)
    layer_out = (unit2 * norm2_gain + norm2_shift).astype(bf16)

    def norm_back(unit, inv_std, gain, dy):
        return norm_grad(unit, inv_std, dy * gain), jnp.sum(dy * unit, axis=0), jnp.sum(dy, axis=0)

    ct = out_cotangent.reshape(seq_len, width).astype(f32)
    d_second, g_gain2, g_shift2 = norm_back(unit2, inv2, norm2_gain, ct)
    g_down_bias = jnp.sum(d_second, axis=0)
    d_ffn = d_second.astype(bf16)

    def core_swaps(pieces):
        return [core_swap(v) for v in pieces]

    to_c = products(
        place, [d_ffn], [([(0, hiddens[3])], [], 2), ([(0, hiddens[1])], [], 2)], chunk
    )
    got_xc, got_c = core_swaps(to_c[:2]), core_swaps(to_c[2:])
    d_ups = [(nt(d_ffn, w) * s.astype(f32)).astype(bf16) for w, s in zip(downs, slopes)]
    far_gd, own_gd = products(
        place,
        [after(d_ffn, *d_ups)],
        [([(0, hiddens[2])], [got_xc], 1), ([(0, hiddens[0])], [got_c], 1)],
        chunk,
    )
    got_xd = x_swap(far_gd)

    to_c = products(
        place,
        [after(first_low, far_gd)],
        [([(0, d_ups[3])], [], 2), ([(0, d_ups[1])], [], 2)],
        chunk,
    )
    got_xc, got_c = core_swaps(to_c[:2]), core_swaps(to_c[2:])
    d_mid = sum(nt(d, w) for d, w in zip([after(d_ups[0], *to_c), *d_ups[1:]], ups))
    keep_u, send_u = products(
        place,
        [after(first_low, d_mid)],
        [([(0, d_ups[0])], [got_c], "halve"), ([(0, d_ups[2])], [got_xc], "halve")],
        chunk,
    )
    got_yu = page_swap(send_u, 1)
    d_first, g_gain1, g_shift1 = norm_back(unit1, inv1, norm1_gain, after(d_second, send_u) + d_mid)
    g_out_bias = jnp.sum(d_first, axis=0)
    d_proj = d_first.astype(bf16)
    far_datt = nt(d_proj, far_out).astype(bf16)
    x_dmixed, xc_dmixed, far_sums, far_ds, far_dsv = attn_bwd(seq_len, *far[:3], far_datt, *far[3:])

    lefts = [tok, d_proj]
    to_c = products(place, lefts, [([(0, xc_dmixed), (1, xc_att)], [], 2)], chunk)
    got_xc = core_swaps(to_c)
    near_datt = nt(after(d_proj, *to_c), near_out).astype(bf16)
    (far_gq,) = products(
        place, [after(tok, near_datt), d_proj], [([(0, x_dmixed), (1, x_att)], [got_xc], 1)], chunk
    )
    got_xq = x_swap(far_gq)
    own_dmixed, c_dmixed, near_sums, near_ds, near_dsv = attn_bwd(
        seq_len, *near[:3], after(near_datt, far_gq), *near[3:]
    )
    dmixed = (own_dmixed, c_dmixed, x_dmixed, xc_dmixed)

    got_xd, got_yu = lax.optimization_barrier((got_xd, got_yu, near_sums))[:2]
    keep_d, send_d = add_split(place, [own_gd], [got_xd], 0, chunk)
    got_yd = page_swap(send_d, 1)
    far_gu = (keep_u[half:].astype(f32) + got_yu[half:].astype(f32)).astype(bf16)
    own_gu = (keep_u[:half].astype(f32) + got_yu[:half].astype(f32)).astype(bf16)
    got_xu = x_swap(far_gu)
    to_c = products(
        place,
        [after(tok, far_gu, send_d), d_proj],
        [([(0, c_dmixed), (1, c_att)], [], 2)],
        chunk,
    )
    got_cq = core_swaps(to_c)
    text, near_far = (near_ds, far_ds), (near_dsv, far_dsv)
    acc = after(jnp.zeros((16, 160), f32), *to_c)
    acc = add_hist(acc, ids, text, 0, SPAN // 2, False)
    keep_q, send_q = products(
        place,
        [after(tok, acc), d_proj],
        [([(0, own_dmixed), (1, own_att)], [got_cq, [got_xq]], "halve")],
        chunk,
    )
    got_yq = page_swap(send_q, 1)
    keep_d, send_d = add_split(place, [keep_d], [after(got_yd, send_q)], 1, chunk)
    got_zd = page_swap(send_d, 2)
    acc = add_hist(after(acc, send_q, send_d), ids, text, SPAN // 2, SPAN // 2, False)
    keep_u, send_u = add_split(place, [own_gu], [after(got_xu, acc)], 1, chunk)
    got_zu = page_swap(send_u, 2)
    keep_q, send_q = add_split(place, [keep_q], [after(got_yq, send_u)], 1, chunk)
    got_zq = page_swap(send_q, 2)
    keep_d, send_d = add_split(place, [keep_d], [after(got_zd, send_q)], 2, chunk)
    got_zd = page_swap(send_d, 4)
    acc = add_hist(after(acc, send_d), ids, near_far, 0, ROWS, True)
    g_up_bias = [jnp.sum(d.astype(f32), axis=0) for d in d_ups]
    shared = (g_out_bias, g_gain1, g_shift1, g_down_bias, g_gain2, g_shift2)
    keep, send = pack_sums(acc, near_sums, far_sums, g_up_bias, shared)
    got = x_swap(send)
    keep_q, send_q = add_split(place, [keep_q], [after(got_zq, send)], 2, chunk)
    got_zq = page_swap(send_q, 4)
    keep_u, send_u = add_split(place, [keep_u], [after(got_zu, send_q)], 2, chunk)
    got_zu = page_swap(send_u, 4)
    weights = (own_qkv, c_qkv, mine_a, theirs_a, xc_mine_a, xc_theirs_a)
    grad_tokens = tokens_grad(
        place, dmixed, (after(own_qkv, send_u), *weights[1:]), d_first
    )
    sums = keep + after(got, send_u)
    sums = jnp.concatenate((sums[:EACH], sums[2 * EACH :])) + core_swap(sums[EACH:])
    sums = sums + page_swap(sums, 1)
    sums = sums + page_swap(sums, 2)
    got = page_swap(sums, 4)
    sums = add_all(sums + got, page_bits[3:])
    g_w_down = finish(place, keep_d, got_zd, 2, chunk).T
    g_w_up = finish(place, keep_u, got_zu, 2, chunk)
    qo = finish(place, keep_q, got_zq, 2, chunk)
    g_w_qkv = qo[:, : 3 * inner].reshape(-1, 3, inner)
    g_w_out = qo[:, 3 * inner :].T

    both = sums[:heads_here].reshape(heads_here, 2, HEAD_DIM)
    g_qv_bias = both.transpose(1, 0, 2).reshape(2, inner)
    g_box = sums[heads_here : 2 * heads_here].reshape(heads_here, 2, NB2).transpose(1, 0, 2)
    g_pos = sums[2 * heads_here : 3 * heads_here, :NB1]
    g_up_bias = sums[3 * heads_here : 3 * heads_here + 6].reshape(units)
    shared = sums[EACH : EACH + 36].reshape(6, width)
    return (
        layer_out.reshape(tokens.shape),
        grad_tokens.reshape(tokens.shape),
        g_w_qkv,
        g_qv_bias,
        g_w_out,
        shared[0],
        shared[1],
        shared[2],
        g_w_up,
        g_up_bias,
        g_w_down,
        shared[3],
        shared[4],
        shared[5],
        g_pos,
        g_box,
    )


def solution(mesh):
    placed = (
        P(("pages", "heads"), None, None),
        P(None, None, "heads"),
        P(None, "heads"),
        P("heads", None),
        P(),
        P(),
        P(),
        P(None, "heads"),
        P("heads"),
        P("heads", None),
        P(),
        P(),
        P(),
        P("heads", None),
        P(None, "heads", None),
        P("pages", None),
        P("pages", None, None),
        P(("pages", "heads"), None, None),
    )
    return jax.shard_map(
        on_device,
        mesh=mesh,
        in_specs=placed,
        out_specs=(
            P(("pages", "heads"), None, None),
            P(("pages", "heads"), None, None),
            P("pages", None, "heads"),
            P(None, "heads"),
            P("heads", "pages"),
            P(),
            P(),
            P(),
            P("pages", "heads"),
            P("heads"),
            P("heads", "pages"),
            P(),
            P(),
            P(),
            P("heads", None),
            P(None, "heads", None),
        ),
        check_vma=False,
    )
```

```python
import functools
import math

import jax
import jax.numpy as jnp
from jax import lax
from jax.experimental import pallas as pl
from jax.experimental.pallas import tpu as pltpu
from jax.sharding import PartitionSpec as P

f32 = jnp.float32
bf16 = jnp.bfloat16
i32 = jnp.int32
EPSILON = 1e-05
MASKED_SCORE = -1e30


HEAD_DIM = 64
TEXT = 512
NB1 = 32
MD1 = 128
NB2 = 64
MD2 = 256
ROWS = 576
VIS = ROWS - TEXT
QROWS = 640
LANES = 128
CHUNK = 64
UNIT = 2048.0
BLOCKS = ((0, 256), (0, 384), (128, 384), (256, 256))
OFFS = (0, 320, 768, 1216)
SPAN = 1536
TOTAL = SPAN + ROWS
Q_AT = SPAN
KV_AT = Q_AT + ROWS
PV_AT = KV_AT + ROWS
KEPT = PV_AT + ROWS // 2
SMALL = 24


def thresholds(buckets, max_reach):
    half_range = buckets // 2
    exact_range = half_range // 2
    levels = half_range - exact_range
    return [
        math.ceil(exact_range * (max_reach / exact_range) ** (k / levels) - 1e-09)
        for k in range(1, levels)
    ]


def bucket_of(diff, buckets, reach):
    n = jnp.abs(diff)
    out = jnp.minimum(n, buckets // 4) + jnp.where(diff > 0, buckets // 2, 0)
    for t in thresholds(buckets, reach):
        out = out + jnp.where(n >= t, 1, 0)
    return out


def parts_of(blk):
    s, n = BLOCKS[blk]
    return ((s, n, OFFS[blk]), (TEXT, VIS, OFFS[blk] + n))


def nt(a, b):
    return lax.dot_general(a, b, (((1,), (1,)), ((), ())), preferred_element_type=f32)


def nn(a, b):
    return lax.dot_general(a, b, (((1,), (0,)), ((), ())), preferred_element_type=f32)


def unpack(ids):
    return ids & 255, (ids >> 8) & 255, ids >> 16


def take(tab, idx):
    return jnp.take_along_axis(
        jnp.broadcast_to(tab, idx.shape), idx, axis=1, mode="promise_in_bounds"
    )


def ids_kernel(place_ref, len_ref, box_ref, ids_ref, some_ref, c_s, r_s, *, valid):
    page = place_ref[0]
    row = lax.broadcasted_iota(i32, (8, ROWS), 1)
    segment = jnp.zeros((8, ROWS), i32)
    end = 0
    for i in range(len_ref.shape[1]):
        end = end + len_ref[page, i]
        segment = segment + jnp.where(row >= end, 1, 0)
    c_s[...] = jnp.zeros_like(c_s)
    c_s[0:8, :] = segment.astype(f32)
    c_s[8:10, 0:valid] = box_ref[page].astype(f32)
    r_s[...] = c_s[...].T.astype(i32)

    def query(lo, hi):
        return tuple(c_s[i : i + 1, lo:hi].astype(i32) for i in (0, 8, 9))

    def tiles(row, out, rows, q_first, q):
        qseg, qx, qy = (jnp.broadcast_to(v, (CHUNK, LANES)) for v in q)
        lane = lax.broadcasted_iota(i32, (CHUNK, LANES), 1)
        if q_first == TEXT:
            q_pos, high = TEXT + (lane & (VIS - 1)), jnp.where(lane >= VIS, NB2, 0)
        else:
            q_pos, high = q_first + lane, 0

        def tile(c, _):
            at = pl.ds(pl.multiple_of(row + c * CHUNK, CHUNK), CHUNK)
            here = pl.ds(pl.multiple_of(out + c * CHUNK, CHUNK), CHUNK)
            seg, kx, ky = (jnp.broadcast_to(r_s[at, i : i + 1], (CHUNK, LANES)) for i in (0, 8, 9))
            k_pos = lax.broadcasted_iota(i32, (CHUNK, LANES), 0) + (row + c * CHUNK)
            x_id = bucket_of(kx - qx, NB2, MD2)
            y_id = bucket_of(ky - qy, NB2, MD2)
            p_id = bucket_of(k_pos - q_pos, NB1, MD1)
            ok = ((seg == qseg) | (k_pos >= TEXT) | (q_pos >= TEXT)) & (k_pos < valid)
            p_id = jnp.where(ok, p_id, NB1)
            y_id = y_id + (high if q_first == TEXT else NB2)
            ids_ref[here, :] = (x_id + high) + y_id * 256 + (p_id + high) * 65536
            some_ref[out // CHUNK + c] = jnp.max(jnp.where(ok, 1, 0))
            return 0

        lax.fori_loop(0, rows // CHUNK, tile, 0)

    for blk in range(4):
        q = query(blk * LANES, (blk + 1) * LANES)
        for s, n, o in parts_of(blk):
            tiles(s, o, n, blk * LANES, q)
    q = tuple(jnp.concatenate((v, v), axis=1) for v in query(TEXT, ROWS))
    tiles(0, SPAN, ROWS, TEXT, q)


def make_ids(place, lengths, boxes):
    return pl.pallas_call(
        functools.partial(ids_kernel, valid=boxes.shape[2]),
        in_specs=[
            pl.BlockSpec(memory_space=pltpu.SMEM),
            pl.BlockSpec(memory_space=pltpu.SMEM),
            pl.BlockSpec(memory_space=pltpu.VMEM),
        ],
        out_specs=[
            pl.BlockSpec(memory_space=pltpu.VMEM),
            pl.BlockSpec(memory_space=pltpu.SMEM),
        ],
        out_shape=[
            jax.ShapeDtypeStruct((TOTAL, LANES), i32),
            jax.ShapeDtypeStruct((TOTAL // CHUNK,), i32),
        ],
        scratch_shapes=[pltpu.VMEM((LANES, ROWS), f32), pltpu.VMEM((ROWS, LANES), i32)],
        name="ids",
        cost_estimate=pl.CostEstimate(flops=0, bytes_accessed=0, transcendentals=0),
        compiler_params=pltpu.CompilerParams(vmem_limit_bytes=12 << 20),
    )(place, lengths, boxes)


def place(dst_ref, pair, first, side, cols):
    at = slice(side * 192, side * 192 + 64)
    dst_ref[pair, first : first + ROWS, at] = cols


def stacked(both):
    return jnp.concatenate((both[:, :LANES], both[:, LANES:]), 0)


def block(ref, pair, first, blk):
    rows = LANES if blk < 4 else VIS
    return stacked(ref[pair, first + blk * LANES : first + blk * LANES + rows, :])


def load_rows(refs, odd, dst):
    if len(refs) == 1:
        dst[0 : refs[0].shape[0], :] = refs[0][...]
    else:
        half = dst.shape[0] // 2
        for first in range(2):

            @pl.when(odd == first)
            def _(first=first):
                dst[first * half : (first + 1) * half, :] = refs[0][0:half, :]
                dst[(1 - first) * half : (2 - first) * half, :] = refs[1][0:half, :]


def pad_rows(v):
    return jnp.concatenate((v, jnp.zeros((ROWS - v.shape[0], v.shape[1]), v.dtype)), 0)


def fold(both):
    n = both.shape[1] // 2
    t = both.T
    lane = lax.broadcasted_iota(i32, (n, LANES), 1)
    return jnp.where(lane < 64, t[:n], t[n:])


def fwd_kernel(place_ref, tok_ref, *refs, pieces, pairs):
    n = 2 * pieces
    weights = (refs[:pieces], refs[pieces:n])
    small, ids_ref = refs[n : n + 2], refs[n + 2]
    wo_refs, refs = (refs[n + 3 : n + 5], refs[n + 5 :]) if pieces == 1 else (None, refs[n + 3 :])
    out_ref, bias_ref, wo_ref, kept_ref = refs[:4]
    w_s = refs[4] if pieces > 1 else None
    vt_s, s_s, i_s, f_s, o_s, l_s = refs[-6:]
    first = small[0].shape[0] - 16
    inner = pairs * HEAD_DIM
    units = 4 * pairs // 6
    bias_ref[...] = jnp.zeros_like(bias_ref)
    for g in range(2):
        bias_ref[g : g + 1, :] = small[g][first + units : first + units + 1, :].astype(f32)
        for i in range(4 * pairs):
            at = slice(i % 6 * LANES, (i % 6 + 1) * LANES)
            row = first + i // 6
            high, rest = (small[g][r : r + 1, at].astype(f32) for r in (row, row + 8))
            l_s[g, i : i + 1, :] = high + rest
    small = [l_s.at[g] for g in range(2)]
    tok = pad_rows(tok_ref[...])
    for pair in range(pairs):
        kept_ref[pair, Q_AT:KV_AT, :] = jnp.zeros((ROWS, 256), bf16)
    for g in range(2):
        if pieces > 1:
            load_rows(weights[g], place_ref[1], w_s.at[g])
            w_ref = w_s.at[g]
            wo_ref[g * inner : (g + 1) * inner, :] = w_ref[3 * inner :, :]
        else:
            w_ref = weights[g][0]
            wo_ref[g * inner : (g + 1) * inner, :] = wo_refs[g][...]
        for part in range(3):
            mixed = nt(tok, w_ref[part * inner : (part + 1) * inner, :])
            for local in range(pairs):
                pair, side = divmod(g * pairs + local, 2)
                at = slice(side * 64, side * 64 + 64)
                cols = mixed[:, local * 64 : local * 64 + 64]
                if part == 0:
                    cols = cols + small[g][2 * pairs + local : 2 * pairs + local + 1, :64]
                    place(kept_ref, pair, Q_AT, side, (cols * (UNIT / 8)).astype(bf16))
                elif part == 1:
                    kept_ref[pair, KV_AT:PV_AT, at] = cols.astype(bf16)
                else:
                    cols = cols + small[g][3 * pairs + local : 3 * pairs + local + 1, :64]
                    low = slice(LANES + side * 64, LANES + side * 64 + 64)
                    kept_ref[pair, KV_AT:PV_AT, low] = cols.astype(bf16)
                    vt_s[pair, at, :] = cols.T.astype(bf16)
    for pair in range(pairs):
        (ga, la), (gb, lb) = divmod(2 * pair, pairs), divmod(2 * pair + 1, pairs)
        for row, start in ((0, 0), (1, pairs)):
            a = small[ga][start + la : start + la + 1, :] * UNIT
            b = small[gb][start + lb : start + lb + 1, :] * UNIT
            i_s[pair, row : row + 1, :] = (
                jnp.round(a).astype(i32) * 65536 + jnp.round(b).astype(i32)
            )
            f_s[pair, 2 * row : 2 * row + 1, :] = jnp.concatenate((a[:, :64], b[:, :64]), 1)
            f_s[pair, 2 * row + 1 : 2 * row + 2, :] = jnp.concatenate((a[:, 64:], b[:, 64:]), 1)

    def softmax(total, wide, p_at):
        m = jnp.full((8, wide), -3e38, f32)
        for c in range(0, total, 8):
            m = jnp.maximum(m, s_s[c : c + 8, :wide])
        m = jnp.max(m, axis=0, keepdims=True)
        l = jnp.zeros((8, wide), f32)
        for c in range(0, total, 8):
            e = jnp.exp2((s_s[c : c + 8, :wide] - m) * (math.log2(math.e) / UNIT))
            s_s[c : c + 8, :wide] = e
            l = l + e
        inv = 1.0 / jnp.sum(l, axis=0, keepdims=True)
        for c in range(0, total, 16):
            p_at(c, (s_s[c : c + 16, :wide] * inv).astype(bf16))

    def one_pair(pair, _):
        t_xy, t_p = (i_s[pair, i : i + 1, :] for i in range(2))
        v_x, v_y, v_p = (f_s[pair, i : i + 1, :] for i in range(3))
        for blk in range(4):
            q = block(kept_ref, pair, Q_AT, blk)
            first = OFFS[blk]
            for s, n, o in parts_of(blk):
                sc = nt(kept_ref[pair, KV_AT + s : KV_AT + s + n, :LANES], q)
                for c in range(0, n, 16):
                    r = slice(o + c, o + c + 16)
                    x, y, p = unpack(ids_ref[r, :])
                    b = take(t_xy, x) + take(t_xy, y) + take(t_p, p)
                    low = (b << 16) >> 16
                    high = (b - low) >> 16
                    add = jnp.where(p == NB1, MASKED_SCORE, 0.0)
                    to = slice(o - first + c, o - first + c + 16)
                    s_s[to, :LANES] = sc[c : c + 16, :LANES] + (high.astype(f32) + add)
                    s_s[to, LANES:] = sc[c : c + 16, LANES:] + (low.astype(f32) + add)

            def put(c, v, first=first):
                kept_ref[pair, first + c : first + c + 16, :] = v

            softmax(BLOCKS[blk][1] + VIS, 256, put)
            ot = sum(
                nn(vt_s[pair, :, s : s + n], kept_ref[pair, o : o + n, :]) for s, n, o in parts_of(blk)
            )
            o_s[pair, blk * LANES : (blk + 1) * LANES, :] = fold(ot).astype(bf16)
        q = block(kept_ref, pair, Q_AT, 4)
        sc = nt(kept_ref[pair, KV_AT:PV_AT, :LANES], q)
        for c in range(0, ROWS, 16):
            r = slice(SPAN + c, SPAN + c + 16)
            x, y, p = unpack(ids_ref[r, :])
            b = take(v_x, x) + take(v_y, y) + take(v_p, p)
            add = jnp.where((p & (NB2 - 1)) == NB1, MASKED_SCORE, 0.0)
            s_s[c : c + 16, :LANES] = sc[c : c + 16] + (b + add)

        def put_v(c, v):
            side, row = divmod(c, ROWS // 2)
            at = slice(side * LANES, (side + 1) * LANES)
            kept_ref[pair, PV_AT + row : PV_AT + row + 16, at] = v

        softmax(ROWS, LANES, put_v)
        o_s[pair, TEXT:ROWS, :] = fold(nn(vt_s[pair], stacked(kept_ref[pair, PV_AT:KEPT, :]))).astype(bf16)
        return 0

    lax.fori_loop(0, pairs, one_pair, 0)
    rows = out_ref.shape[0]
    for pair in range(pairs):
        out_ref[:, pair * LANES : (pair + 1) * LANES] = o_s[pair, 0:rows, :]


def attn_fwd(place, tok, weights, small, ids, pairs, w_out=()):
    pieces, (rows, width) = len(weights[0]), tok.shape
    vmem = pl.BlockSpec(memory_space=pltpu.VMEM)
    outs = [((rows, pairs * LANES), bf16), ((8, width), f32), ((pairs * LANES, width), bf16)]
    outs += [((pairs, KEPT, 256), bf16)]
    if pieces > 1:
        outs += [((2, 4 * pairs * HEAD_DIM, width), bf16)]
    args = (place, tok, *weights[0], *weights[1], *small, ids, *w_out)
    return pl.pallas_call(
        functools.partial(fwd_kernel, pieces=pieces, pairs=pairs),
        in_specs=[pl.BlockSpec(memory_space=pltpu.SMEM)] + [vmem] * (len(args) - 1),
        out_specs=[vmem] * len(outs),
        out_shape=[jax.ShapeDtypeStruct(shape, dtype) for shape, dtype in outs],
        scratch_shapes=[
            pltpu.VMEM((pairs, LANES, ROWS), bf16),
            pltpu.VMEM((ROWS, 256), f32),
            pltpu.VMEM((pairs, 8, LANES), i32),
            pltpu.VMEM((pairs, 8, LANES), f32),
            pltpu.VMEM((pairs, ROWS, LANES), bf16),
            pltpu.VMEM((2, SMALL, LANES), f32),
        ],
        name="attn_fwd",
        cost_estimate=pl.CostEstimate(flops=0, bytes_accessed=0, transcendentals=0),
        compiler_params=pltpu.CompilerParams(vmem_limit_bytes=22 << 20),
    )(*args)


def bwd_kernel(kept_ref, do_ref, out0_ref, out1_ref, sum_ref, ds_ref, dsv_ref, do_s, kt_s, dq_s, dk_s, dv_s, *, pairs):
    rows = out0_ref.shape[0]
    sum_ref[...] = jnp.zeros_like(sum_ref)
    do_s[...] = jnp.zeros_like(do_s)
    for h in range(2 * pairs):
        pair, side = divmod(h, 2)
        place(do_s, pair, 0, side, pad_rows(do_ref[:, h * 64 : h * 64 + 64]))
    for pair in range(pairs):
        kt_s[pair] = kept_ref[pair, KV_AT:PV_AT, :LANES].astype(f32).T.astype(bf16)

    def grad_scores(dps, ps, put):
        d = jnp.zeros((8, dps[0].shape[1]), f32)
        for dp, p in zip(dps, ps):
            for c in range(0, dp.shape[0], 16):
                t = p(c).astype(f32) * dp[c : c + 16]
                d = d + (t[:8] + t[8:])
        d = jnp.sum(d, axis=0, keepdims=True)
        for i, (dp, p) in enumerate(zip(dps, ps)):
            for c in range(0, dp.shape[0], 16):
                put(i, c, (p(c).astype(f32) * (dp[c : c + 16] - d)).astype(bf16))

    def one_pair(pair, _):
        dv_s[...] = jnp.zeros_like(dv_s)
        dk_s[...] = jnp.zeros_like(dk_s)
        for blk in range(4):
            q = block(kept_ref, pair, Q_AT, blk)
            do = block(do_s, pair, 0, blk)
            parts = parts_of(blk)

            def put(i, c, v, parts=parts):
                ds_ref[pair, parts[i][2] + c : parts[i][2] + c + 16, :] = v

            grad_scores(
                [nt(kept_ref[pair, KV_AT + s : KV_AT + s + n, LANES:], do) for s, n, o in parts],
                [lambda c, o=o: kept_ref[pair, o + c : o + c + 16, :] for s, n, o in parts],
                put,
            )
            dq = 0.0
            for s, n, o in parts:
                ds = ds_ref[pair, o : o + n, :]
                dq = dq + nn(kt_s[pair, :, s : s + n], ds)
                dv_s[s : s + n, :] += nn(kept_ref[pair, o : o + n, :], do)
                dk_s[s : s + n, :] += nn(ds, q)
            dq_s[pair, 0, blk * LANES : (blk + 1) * LANES, :] = (fold(dq) * 0.125).astype(bf16)
        q = block(kept_ref, pair, Q_AT, 4)
        do = block(do_s, pair, 0, 4)
        pv = stacked(kept_ref[pair, PV_AT:KEPT, :])

        def put_v(i, c, v):
            dsv_ref[pair, c : c + 16, :] = v

        grad_scores([nt(kept_ref[pair, KV_AT:PV_AT, LANES:], do)], [lambda c: pv[c : c + 16]], put_v)
        ds = dsv_ref[pair]
        dq_s[pair, 0, TEXT:ROWS, :] = (fold(nn(kt_s[pair], ds)) * 0.125).astype(bf16)
        dq_s[pair, 1] = ((dk_s[...] + nn(ds, q)) * (1.0 / UNIT)).astype(bf16)
        dq_s[pair, 2] = (dv_s[...] + nn(pv, do)).astype(bf16)
        return 0

    lax.fori_loop(0, pairs, one_pair, 0)
    for h in range(2 * pairs):
        pair, side = divmod(h, 2)
        g, local = divmod(h, pairs)
        for part in range(3):
            col = part * pairs * HEAD_DIM + local * HEAD_DIM
            here = dq_s[pair, part, 0:rows, side * 64 : side * 64 + 64]
            (out0_ref, out1_ref)[g][:, col : col + 64] = here
            if part != 1:
                total = jnp.sum(here.astype(f32), axis=0, keepdims=True)
                sum_ref[g : g + 1, col : col + 64] = total


def attn_bwd(rows, kept, d_att):
    pairs = kept.shape[0]
    cols = 3 * pairs * HEAD_DIM
    vmem = pl.BlockSpec(memory_space=pltpu.VMEM)
    outs = [((rows, cols), bf16)] * 2 + [((8, cols), f32)]
    outs += [((pairs, SPAN, 256), bf16), ((pairs, ROWS, LANES), bf16)]
    return pl.pallas_call(
        functools.partial(bwd_kernel, pairs=pairs),
        in_specs=[vmem] * 2,
        out_specs=[vmem] * 5,
        out_shape=[jax.ShapeDtypeStruct(shape, dtype) for shape, dtype in outs],
        scratch_shapes=[
            pltpu.VMEM((pairs, ROWS, 256), bf16),
            pltpu.VMEM((pairs, LANES, ROWS), bf16),
            pltpu.VMEM((pairs, 3, ROWS, LANES), bf16),
            pltpu.VMEM((ROWS, LANES), f32),
            pltpu.VMEM((ROWS, LANES), f32),
        ],
        name="attn_bwd",
        cost_estimate=pl.CostEstimate(flops=0, bytes_accessed=0, transcendentals=0),
        compiler_params=pltpu.CompilerParams(vmem_limit_bytes=22 << 20),
    )(kept, d_att)


HSTEP = 64
HBLOCK = 192


def hist_kernel(some_ref, acc_ref, ids_ref, *refs, sets, pairs, visual, first_id):
    ds_refs, hist_ref, l_s = refs[:sets], refs[-2], refs[-1]
    io = lax.broadcasted_iota(i32, (NB2, LANES), 0)
    heads = 2 * sets * pairs

    @pl.when(pl.program_id(0) == 0)
    def _():
        hist_ref[...] = acc_ref[...]

    for h in range(heads, 16):
        l_s[pl.ds(h, HSTEP, stride=16), :] = jnp.zeros((HSTEP, LANES), f32)

    def step(r):
        first = pl.multiple_of(r * HSTEP, HSTEP)
        lane = lax.broadcasted_iota(i32, (HSTEP, LANES), 1)
        for pair in range(sets * pairs):
            ref = ds_refs[pair // pairs]
            for side in range(2):
                if visual:
                    v = ref[pair % pairs, pl.ds(first, HSTEP), :].astype(f32)
                    v = jnp.where((lane >= VIS) == bool(side), v, 0.0)
                else:
                    at = slice(side * LANES, (side + 1) * LANES)
                    v = ref[pair % pairs, pl.ds(first, HSTEP), at].astype(f32)
                l_s[pl.ds(2 * pair + side, HSTEP, stride=16), :] = v
        lhs, rhs = [], []
        for u in range(HSTEP):
            x, y, p = unpack(ids_ref[pl.ds(first + u, 1), :])
            if visual:
                x, y, p = (v & (NB2 - 1) for v in (x, y, p))
            else:
                y = y - NB2
            hot = [jnp.where(io == x, 1.0, 0.0), jnp.where(io == y, 1.0, 0.0)]
            hot.append(jnp.where(io[:NB1] == p, 1.0, 0.0))
            rhs.append(jnp.concatenate(hot, 0).astype(bf16))
            lhs.append(l_s[u * 16 : u * 16 + 16, :].astype(bf16))
        hist_ref[...] += nt(jnp.concatenate(lhs, 1), jnp.concatenate(rhs, 1))

    steps = HBLOCK // HSTEP

    @pl.loop(0, steps)
    def _(r):
        @pl.when(some_ref[(first_id + pl.program_id(0)) * steps + r] > 0)
        def _():
            step(r)


def add_hist(acc, ids, some, ds, first_row, rows, visual):
    first = first_row // HBLOCK
    first_id = first + (SPAN // HBLOCK if visual else 0)
    specs = [
        pl.BlockSpec(memory_space=pltpu.SMEM),
        pl.BlockSpec((16, 160), lambda i: (0, 0)),
        pl.BlockSpec((HBLOCK, LANES), lambda i: (first_id + i, 0)),
    ]
    for t in ds:
        specs.append(pl.BlockSpec((t.shape[0], HBLOCK, t.shape[2]), lambda i: (0, first + i, 0)))
    return pl.pallas_call(
        functools.partial(hist_kernel, sets=len(ds), pairs=ds[0].shape[0], visual=visual, first_id=first_id),
        grid=(rows // HBLOCK,),
        in_specs=specs,
        out_specs=pl.BlockSpec((16, 160), lambda i: (0, 0)),
        out_shape=jax.ShapeDtypeStruct((16, 160), f32),
        scratch_shapes=[pltpu.VMEM((HSTEP * 16, LANES), f32)],
        name="hist",
        cost_estimate=pl.CostEstimate(flops=0, bytes_accessed=0, transcendentals=0),
        compiler_params=pltpu.CompilerParams(vmem_limit_bytes=12 << 20),
    )(some, acc, ids, *ds)


def call(kernel, name, args, outs, scratch=(), smem=0):
    vmem = pl.BlockSpec(memory_space=pltpu.VMEM)
    return pl.pallas_call(
        kernel,
        in_specs=[pl.BlockSpec(memory_space=pltpu.SMEM)] * smem + [vmem] * (len(args) - smem),
        out_shape=[jax.ShapeDtypeStruct(shape, dtype) for shape, dtype in outs],
        scratch_shapes=[pltpu.VMEM(shape, dtype) for shape, dtype in scratch],
        name=name,
        cost_estimate=pl.CostEstimate(flops=0, bytes_accessed=0, transcendentals=0),
        compiler_params=pltpu.CompilerParams(vmem_limit_bytes=20 << 20),
    )(*args)


def start_kernel(place_ref, qkv_ref, wo_ref, up_ref, down_ref, box_ref, pos_ref, qv_ref, ub_ref, a_ref, b_ref, c_ref, small_ref, s_s, o_s, sems):
    half = b_ref.shape[0]
    inner = wo_ref.shape[0]
    odd = place_ref[1]

    def copy(src, dst, i):
        return pltpu.make_async_copy(src, dst, sems.at[i])

    tail = qkv_ref.shape[0] - half
    firsts = [copy(qkv_ref.at[0:half, :], a_ref.at[0:half, :], 0)]
    seconds = [
        copy(qkv_ref.at[half:, :], a_ref.at[0:tail, :], 0),
        copy(wo_ref, a_ref.at[tail:half, :], 1),
    ]

    @pl.when(odd == 0)
    def _():
        for c in firsts:
            c.start()

    @pl.when(odd == 1)
    def _():
        for c in seconds:
            c.start()

    at = pl.ds(pl.multiple_of(odd * half, half), half)
    others = [copy(up_ref.at[at, :], b_ref, 2), copy(down_ref.at[at, :], c_ref, 3)]
    for c in others:
        c.start()
    heads = pos_ref.shape[0]
    s_s[...] = jnp.zeros_like(s_s)
    for h in range(heads):
        s_s[h : h + 1, :NB2] = box_ref[h, 0:1, :]
        s_s[h : h + 1, NB2:] = box_ref[h, 1:2, :]
        s_s[heads + h : heads + h + 1, :NB1] = pos_ref[h : h + 1, :]
        for i in range(2):
            row = (2 + i) * heads + h
            s_s[row : row + 1, :64] = qv_ref[i : i + 1, h * 64 : h * 64 + 64]
    for i in range(ub_ref.shape[1] // LANES):
        row = 4 * heads + i
        s_s[row : row + 1, :] = ub_ref[:, i * LANES : (i + 1) * LANES].astype(f32)
    o_s[...] = jnp.zeros_like(o_s)
    for i in range(SMALL):
        at = slice(i % 6 * LANES, (i % 6 + 1) * LANES)
        value = s_s[i : i + 1, :]
        high = value.astype(bf16).astype(f32)
        o_s[i // 6 : i // 6 + 1, at] = high
        o_s[8 + i // 6 : 9 + i // 6, at] = value - high
    small_ref[...] = o_s[...].astype(bf16)
    last = copy(small_ref, a_ref.at[half : half + 16, :], 4)
    last.start()

    @pl.when(odd == 0)
    def _():
        for c in firsts:
            c.wait()

    @pl.when(odd == 1)
    def _():
        for c in seconds:
            c.wait()

    for c in others + [last]:
        c.wait()


def start_parts(place, qkv, w_out, w_up, w_down, box, pos, qv, up):
    width = qkv.shape[1]
    vmem, hbm = (pl.BlockSpec(memory_space=m) for m in (pltpu.VMEM, pltpu.HBM))
    shapes = [(width // 2 + 16, width)] + [(width // 2, width)] * 2 + [(16, width)]
    return pl.pallas_call(
        start_kernel,
        in_specs=[pl.BlockSpec(memory_space=pltpu.SMEM)] + [hbm] * 4 + [vmem] * 4,
        out_specs=[vmem] * 4,
        out_shape=[jax.ShapeDtypeStruct(shape, bf16) for shape in shapes],
        scratch_shapes=[
            pltpu.VMEM((SMALL, LANES), f32),
            pltpu.VMEM((16, width), f32),
            pltpu.SemaphoreType.DMA((5,)),
        ],
        name="start_parts",
        cost_estimate=pl.CostEstimate(flops=0, bytes_accessed=0, transcendentals=0),
        compiler_params=pltpu.CompilerParams(vmem_limit_bytes=58 << 20),
    )(place, qkv, w_out, w_up, w_down, box.transpose(1, 0, 2), pos, qv, up.reshape(1, -1))


def join_kernel(place_ref, mine_ref, theirs_ref, *refs):
    outs, sems = refs[:-1], refs[-1]
    half = mine_ref.shape[0] // len(outs)
    odd = place_ref[1]
    copies = []
    for i, out in enumerate(outs):
        for j, (ref, first) in enumerate(((mine_ref, odd * half), (theirs_ref, (1 - odd) * half))):
            to = out.at[pl.ds(pl.multiple_of(first, half), half), :]
            at = slice(i * half, (i + 1) * half)
            copies.append(pltpu.make_async_copy(ref.at[at, :], to, sems.at[i, j]))
    for c in copies:
        c.start()
    for c in copies:
        c.wait()


def join_rows(place, mine, theirs, number):
    rows, cols = mine.shape
    vmem = pl.BlockSpec(memory_space=pltpu.VMEM)
    return pl.pallas_call(
        join_kernel,
        in_specs=[pl.BlockSpec(memory_space=pltpu.SMEM), vmem, vmem],
        out_specs=[vmem] * number,
        out_shape=[jax.ShapeDtypeStruct((2 * rows // number, cols), bf16)] * number,
        scratch_shapes=[pltpu.SemaphoreType.DMA((number, 2))],
        name="join_rows",
        cost_estimate=pl.CostEstimate(flops=0, bytes_accessed=0, transcendentals=0),
        compiler_params=pltpu.CompilerParams(vmem_limit_bytes=8 << 20),
    )(place, mine, theirs)


def tn(a, b):
    return lax.dot_general(a, b, (((0,), (0,)), ((), ())), preferred_element_type=f32)


def parity_split(cur_ref, keep_ref, send_ref, first, chunk, bit):
    for mine in range(2):

        @pl.when(bit == mine)
        def _(mine=mine):
            for i in range(cur_ref.shape[0] // chunk // 2):
                to = slice(first + i * chunk, first + (i + 1) * chunk)
                at = (2 * i + mine) * chunk
                keep_ref[to, :] = cur_ref[at : at + chunk, :]
                at = (2 * i + 1 - mine) * chunk
                send_ref[to, :] = cur_ref[at : at + chunk, :]


def products_kernel(place_ref, *refs, lefts, plan, chunk):
    left, refs = refs[:lefts], list(refs[lefts:])
    rights = [[refs.pop(0) for _ in terms] for terms, _, _ in plan]
    gots = [[[refs.pop(0) for _ in range(n)] for n in counts] for _, counts, _ in plan]
    cur_s = refs.pop()
    split = 0
    for (terms, _, mode), right, got in zip(plan, rights, gots):
        outs = [cur_s] if mode == "halve" else [refs.pop(0) for _ in range(mode)]
        col = 0
        for (i, lanes), r in zip(terms, right):
            lanes = lanes or (0, r.shape[1])
            at = slice(col, col + lanes[1] - lanes[0])
            total = tn(left[i][...], r[:, lanes[0] : lanes[1]])
            for pieces in got:
                wide = [g[:, at].astype(f32) for g in pieces]
                total = total + (wide[0] if len(wide) == 1 else jnp.concatenate(wide, 0))
            rows = total.shape[0] // len(outs)
            for k, out in enumerate(outs):
                out[:, at] = total[k * rows : (k + 1) * rows].astype(bf16)
            col += lanes[1] - lanes[0]
        if mode == "halve":
            if split == 0:
                keep, send = refs.pop(0), refs.pop(0)
            parity_split(cur_s, keep, send, split, chunk, place_ref[1])
            split += cur_s.shape[0] // 2


def plain_split(place, cur, bit, chunk):
    view = cur.reshape(-1, 2, chunk, cur.shape[1])
    pick = lambda i: lax.dynamic_index_in_dim(view, i, axis=1, keepdims=False)
    mine = place[1 + bit]
    return tuple(pick(i).reshape(-1, cur.shape[1]) for i in (mine, 1 - mine))


def products(place, lefts, specs, chunk):
    width = lefts[0].shape[1]
    halved = sum(mode == "halve" for _, _, mode in specs)
    if chunk % 16 and halved:
        whole = products(place, lefts, [(t, g, 1) for t, g, _ in specs], chunk)
        parts = [plain_split(place, cur, 0, chunk) for cur in whole]
        return [jnp.concatenate(side, axis=0) for side in zip(*parts)]
    plan = [
        ([(t[0], t[2] if len(t) > 2 else None) for t in terms], [len(p) for p in gots], mode)
        for terms, gots, mode in specs
    ]
    args = [place, *lefts]
    args += [t[1] for terms, _, _ in specs for t in terms]
    args += [g for _, gots, _ in specs for pieces in gots for g in pieces]
    cols = sum(t[2][1] - t[2][0] if len(t) > 2 else t[1].shape[1] for t in specs[0][0])
    outs = []
    for _, _, mode in specs:
        if mode != "halve":
            outs += [((width // mode, cols), bf16)] * mode
    if halved:
        outs += [((halved * width // 2, cols), bf16)] * 2
    kernel = functools.partial(products_kernel, lefts=len(lefts), plan=plan, chunk=chunk)
    return call(kernel, "products", args, outs, [((width, cols), bf16)], smem=1)


def add_split_kernel(place_ref, *refs, number, bit, chunk):
    keep_ref, send_ref, cur_s = refs[2 * number :]
    first = 0
    for a, b in zip(refs[:number], refs[number : 2 * number]):
        rows = a.shape[0]
        cur_s[first : first + rows] = (a[...].astype(f32) + b[...].astype(f32)).astype(bf16)
        first += rows
    parity_split(cur_s, keep_ref, send_ref, 0, chunk, place_ref[1 + bit])


def add_split(place, keeps, gots, bit, chunk):
    rows, cols = sum(v.shape[0] for v in keeps), keeps[0].shape[1]
    if chunk % 16:
        parts = [(a.astype(f32) + b.astype(f32)).astype(bf16) for a, b in zip(keeps, gots)]
        return plain_split(place, jnp.concatenate(parts, axis=0), bit, chunk)
    half = ((rows // 2, cols), bf16)
    kernel = functools.partial(add_split_kernel, number=len(keeps), bit=bit, chunk=chunk)
    args = (place, *keeps, *gots)
    return call(kernel, "add_split", args, [half, half], [((rows, cols), bf16)], smem=1)


def tokens_kernel(d0, d1, d2, d3, w0, w1, w_ref, first_ref, out_ref):
    cols = d0.shape[1]
    total = first_ref[...] + nn(d0[...], w0[...]) + nn(d1[...], w1[...])
    total = total + nn(d2[...], w_ref[0, 0:cols, :]) + nn(d3[...], w_ref[1, 0:cols, :])
    out_ref[...] = total.astype(bf16)


def tokens_grad(dmixed, weights, d_first):
    args = (*dmixed, *weights, d_first)
    return call(tokens_kernel, "tokens_grad", args, [(d_first.shape, bf16)])[0]


SHARED = 40
EACH = 16


def pack_kernel(hist_ref, near_ref, far_ref, u0, u1, u2, u3, v0, v1, v2, v3, v4, v5, keep_ref, send_ref, *, heads):
    keep_ref[...] = jnp.zeros_like(keep_ref)
    send_ref[...] = jnp.zeros_like(send_ref)
    for g, up in enumerate((u0, u1, u2, u3)):
        ref, first = (keep_ref, send_ref)[g // 2], (g % 2) * EACH
        for h in range(heads):
            for i, part in ((0, 0), (1, 2)):
                col = (part * heads + h) * HEAD_DIM
                row = (near_ref, far_ref)[g // 2][g % 2 : g % 2 + 1, col : col + 64]
                ref[first + h : first + h + 1, i * 64 : i * 64 + 64] = row
            row = hist_ref[g * heads + h : g * heads + h + 1, :]
            ref[first + heads + h : first + heads + h + 1, :] = row[:, :LANES]
            ref[first + 2 * heads + h : first + 2 * heads + h + 1, :NB1] = row[:, LANES:]
        for i in range(6):
            at = slice(first + 3 * heads + i, first + 3 * heads + i + 1)
            ref[at, :] = up[:, i * LANES : (i + 1) * LANES]
    for j, v in enumerate((v0, v1, v2, v3, v4, v5)):
        for i in range(6):
            at = slice(2 * EACH + 6 * j + i, 2 * EACH + 6 * j + i + 1)
            row = v[:, i * LANES : (i + 1) * LANES]
            keep_ref[at, :] = row
            send_ref[at, :] = row


def pack_sums(hist, near, far, ups, shared):
    args = (hist, near, far, *(v.reshape(1, -1) for v in ups), *(v.reshape(1, -1) for v in shared))
    outs = [((2 * EACH + SHARED, LANES), f32)] * 2
    heads = near.shape[1] // (3 * HEAD_DIM)
    return call(functools.partial(pack_kernel, heads=heads), "pack_sums", args, outs)


def core_swap(v):
    return lax.ppermute(v, "heads", [(i, i ^ 1) for i in range(4)])


def x_swap(v):
    return lax.ppermute(v, "heads", [(i, i ^ 2) for i in range(4)])


def page_swap(v, bit):
    return lax.ppermute(v, "pages", [(i, i ^ bit) for i in range(lax.axis_size("pages"))])


def after(value, *others):
    return lax.optimization_barrier((value, *others))[0]


def finish(place, keep, got, bit, chunk):
    last = lax.axis_size("pages").bit_length() - 1
    while bit + 1 < last:
        bit += 1
        keep, send = add_split(place, [keep], [got], bit, chunk)
        got = page_swap(send, 1 << bit)
    return keep.astype(f32) + got.astype(f32)


def add_all(v, bits):
    for bit in bits:
        v = v + page_swap(v, bit)
    return v


def unit_norm(values):
    centered = values - jnp.mean(values, axis=-1, keepdims=True)
    inv_std = lax.rsqrt(jnp.mean(centered * centered, axis=-1, keepdims=True) + EPSILON)
    return centered * inv_std, inv_std


def norm_grad(unit, inv_std, e):
    return inv_std * (
        e - jnp.mean(e, axis=-1, keepdims=True) - unit * jnp.mean(e * unit, axis=-1, keepdims=True)
    )


def on_device(
    tokens,
    w_qkv,
    qv_bias,
    w_out,
    out_bias,
    norm1_gain,
    norm1_shift,
    w_up,
    up_bias,
    w_down,
    down_bias,
    norm2_gain,
    norm2_shift,
    pos_table,
    box_table,
    receipt_lengths,
    page_boxes,
    out_cotangent,
):
    seq_len = tokens.shape[1]
    width = tokens.shape[2]
    heads_here = pos_table.shape[0]
    inner = heads_here * HEAD_DIM
    units = w_up.shape[1]
    own_page = lax.axis_index("heads")
    page_bits = [1 << b for b in range(lax.axis_size("pages").bit_length() - 1)]
    chunk = width // lax.axis_size("pages")
    me = lax.axis_index("pages")
    place = jnp.stack([own_page] + [(me >> b) & 1 for b in range(len(page_bits))]).astype(i32)
    tok = tokens.reshape(seq_len, width)

    own_qkv = w_qkv.reshape(width, 3 * inner).T
    c_qkv, c_out = core_swap(own_qkv), core_swap(w_out)
    half_a, half_b, half_c, small = start_parts(
        place, own_qkv, w_out, w_up, w_down, box_table, pos_table, qv_bias, up_bias
    )
    c_small = core_swap(small)
    mine_a = x_swap(half_a)
    mine_b = x_swap(half_b)
    mine_c = x_swap(half_c)
    ids, some = make_ids(place, receipt_lengths, page_boxes)
    mine_a = after(mine_a, ids)

    c_up, c_down = core_swap(w_up), core_swap(w_down)
    near_w = ((own_qkv,), (after(c_qkv, mine_a, c_up, c_down),))
    near_att, near_bias, near_out, near_kept = attn_fwd(
        place, tok, near_w, (small, c_small), ids, heads_here, (w_out, c_out)
    )
    half = width // 2
    theirs_a = page_swap(mine_a, 1)
    xc_mine_a, xc_theirs_a = core_swap(mine_a), core_swap(after(theirs_a, near_att))
    theirs_b = page_swap(after(mine_b, near_att), 1)
    xc_mine_b = core_swap(after(mine_b, near_att))
    far_w = ((mine_a, theirs_a), (after(xc_mine_a, xc_mine_b), xc_theirs_a))
    far_att, far_bias, far_out, far_kept, far_w = attn_fwd(
        place, tok, far_w, (mine_a, xc_mine_a), ids, heads_here
    )
    far_proj = nn(far_att, far_out)
    mine_b, mine_c, theirs_b = lax.optimization_barrier((mine_b, mine_c, theirs_b, far_proj))[:3]
    theirs_c = page_swap(mine_c, 1)
    xc_mine_c = core_swap(mine_c)
    xc_theirs_b = core_swap(theirs_b)
    first_in = nn(near_att, near_out) + far_proj + out_bias + tok.astype(f32)
    unit1, inv1 = unit_norm(first_in)
    first_out = unit1 * norm1_gain + norm1_shift
    first_low = first_out.astype(bf16)

    def units_of(weights, little):
        up = nn(first_low, weights) + little
        cdf = 0.5 * (1.0 + lax.erf(up * math.sqrt(0.5)))
        slope = cdf + up * jnp.exp(-0.5 * up * up) * (1.0 / math.sqrt(2.0 * math.pi))
        return (up * cdf).astype(bf16), slope.astype(bf16)

    littles = (near_bias[0], near_bias[1], far_bias[0], far_bias[1])
    own_units = units_of(w_up, littles[0])
    theirs_b = after(theirs_b, own_units[0])
    (x_up,) = join_rows(place, mine_b, theirs_b, 1)
    c_units = units_of(after(c_up, theirs_b), littles[1])
    (xc_up,) = join_rows(place, xc_mine_b, after(xc_theirs_b, x_up), 1)
    x_units = units_of(x_up, littles[2])
    theirs_c = after(theirs_c, x_units[0])
    xc_theirs_c = core_swap(theirs_c)
    far_units = [x_units, units_of(after(xc_up, theirs_c), littles[3])]
    (x_down,) = join_rows(place, mine_c, theirs_c, 1)
    (xc_down,) = join_rows(place, xc_mine_c, after(xc_theirs_c, x_down), 1)
    ups, downs = (w_up, c_up, x_up, xc_up), (w_down, c_down, x_down, xc_down)
    hiddens, slopes = zip(own_units, c_units, *far_units)
    second_in = sum(nn(h, w) for h, w in zip(hiddens, downs)) + down_bias + first_out
    unit2, inv2 = unit_norm(second_in)
    layer_out = (unit2 * norm2_gain + norm2_shift).astype(bf16)

    def norm_back(unit, inv_std, gain, dy):
        return norm_grad(unit, inv_std, dy * gain), jnp.sum(dy * unit, axis=0), jnp.sum(dy, axis=0)

    ct = out_cotangent.reshape(seq_len, width).astype(f32)
    d_second, g_gain2, g_shift2 = norm_back(unit2, inv2, norm2_gain, ct)
    g_down_bias = jnp.sum(d_second, axis=0)
    d_ffn = d_second.astype(bf16)

    def core_swaps(pieces):
        return [core_swap(v) for v in pieces]

    to_c = products(
        place, [d_ffn], [([(0, hiddens[3])], [], 2), ([(0, hiddens[1])], [], 2)], chunk
    )
    got_xc, got_c = core_swaps(to_c[:2]), core_swaps(to_c[2:])
    d_ups = [(nt(d_ffn, w) * s.astype(f32)).astype(bf16) for w, s in zip(downs, slopes)]
    far_gd, own_gd = products(
        place,
        [after(d_ffn, *d_ups)],
        [([(0, hiddens[2])], [got_xc], 1), ([(0, hiddens[0])], [got_c], 1)],
        chunk,
    )
    got_xd = x_swap(far_gd)

    to_c = products(
        place,
        [after(first_low, far_gd)],
        [([(0, d_ups[3])], [], 2), ([(0, d_ups[1])], [], 2)],
        chunk,
    )
    got_xc, got_c = core_swaps(to_c[:2]), core_swaps(to_c[2:])
    d_mid = sum(nt(d, w) for d, w in zip([after(d_ups[0], *to_c), *d_ups[1:]], ups))
    keep_u, send_u = products(
        place,
        [after(first_low, d_mid)],
        [([(0, d_ups[0])], [got_c], "halve"), ([(0, d_ups[2])], [got_xc], "halve")],
        chunk,
    )
    got_yu = page_swap(send_u, 1)
    d_first, g_gain1, g_shift1 = norm_back(unit1, inv1, norm1_gain, after(d_second, send_u) + d_mid)
    g_out_bias = jnp.sum(d_first, axis=0)
    d_proj = d_first.astype(bf16)
    far_datt = nt(d_proj, far_out).astype(bf16)
    x_dmixed, xc_dmixed, far_sums, far_ds, far_dsv = attn_bwd(seq_len, far_kept, far_datt)

    lefts = [tok, d_proj]
    low, high = (0, inner), (inner, 2 * inner)
    to_c = products(place, lefts, [([(0, xc_dmixed), (1, far_att, high)], [], 2)], chunk)
    got_xc = core_swaps(to_c)
    near_datt = nt(after(d_proj, *to_c), near_out).astype(bf16)
    (far_gq,) = products(
        place, [after(tok, near_datt), d_proj], [([(0, x_dmixed), (1, far_att, low)], [got_xc], 1)], chunk
    )
    got_xq = x_swap(far_gq)
    own_dmixed, c_dmixed, near_sums, near_ds, near_dsv = attn_bwd(
        seq_len, near_kept, after(near_datt, far_gq)
    )
    dmixed = (own_dmixed, c_dmixed, x_dmixed, xc_dmixed)

    got_xd, got_yu = lax.optimization_barrier((got_xd, got_yu, near_sums))[:2]
    keep_d, send_d = add_split(place, [own_gd], [got_xd], 0, chunk)
    got_yd = page_swap(send_d, 1)
    keep_u, send_u = add_split(place, [keep_u], [got_yu], 1, chunk)
    got_zu = page_swap(send_u, 2)
    to_c = products(
        place,
        [after(tok, send_u, send_d), d_proj],
        [([(0, c_dmixed), (1, near_att, high)], [], 2)],
        chunk,
    )
    got_cq = core_swaps(to_c)
    text, near_far = (near_ds, far_ds), (near_dsv, far_dsv)
    acc = after(jnp.zeros((16, 160), f32), *to_c)
    acc = add_hist(acc, ids, some, text, 0, SPAN // 2, False)
    keep_q, send_q = products(
        place,
        [after(tok, acc), d_proj],
        [([(0, own_dmixed), (1, near_att, low)], [got_cq, [got_xq]], "halve")],
        chunk,
    )
    got_yq = page_swap(send_q, 1)
    keep_u, send_u = add_split(place, [keep_u], [after(got_zu, send_q)], 2, chunk)
    got_zu = page_swap(send_u, 4)
    keep_d, send_d = add_split(place, [keep_d], [after(got_yd, send_u)], 1, chunk)
    got_zd = page_swap(send_d, 2)
    acc = add_hist(after(acc, send_q, send_d), ids, some, text, SPAN // 2, SPAN // 2, False)
    keep_q, send_q = add_split(place, [keep_q], [after(got_yq, acc)], 1, chunk)
    got_zq = page_swap(send_q, 2)
    keep_d, send_d = add_split(place, [keep_d], [after(got_zd, send_q)], 2, chunk)
    got_zd = page_swap(send_d, 4)
    acc = add_hist(after(acc, send_d), ids, some, near_far, 0, ROWS, True)
    g_up_bias = [jnp.sum(d.astype(f32), axis=0) for d in d_ups]
    shared = (g_out_bias, g_gain1, g_shift1, g_down_bias, g_gain2, g_shift2)
    keep, send = pack_sums(acc, near_sums, far_sums, g_up_bias, shared)
    got = x_swap(send)
    keep_q, send_q = add_split(place, [keep_q], [after(got_zq, send)], 2, chunk)
    got_zq = page_swap(send_q, 4)
    got_zu, got_zd = lax.optimization_barrier((got_zu, got_zd, send_q))[:2]
    both_u = finish(place, keep_u, got_zu, 2, chunk)
    got_xu = x_swap(both_u[chunk:].astype(bf16))
    grad_tokens = tokens_grad(dmixed, (own_qkv, c_qkv, after(far_w, send_q)), d_first)
    sums = keep + after(got, grad_tokens)
    sums = jnp.concatenate((sums[:EACH], sums[2 * EACH :])) + core_swap(sums[EACH:])
    sums = sums + page_swap(sums, 1)
    got, got_zq = lax.optimization_barrier((page_swap(sums, 2), got_zq))
    sums = sums + got
    got = page_swap(sums, 4)
    sums = add_all(sums + got, page_bits[3:])
    g_w_down = finish(place, keep_d, got_zd, 2, chunk).T
    qo = finish(place, keep_q, got_zq, 2, chunk)
    g_w_up = both_u[:chunk] + got_xu.astype(f32)
    g_w_qkv = qo[:, : 3 * inner].reshape(-1, 3, inner)
    g_w_out = qo[:, 3 * inner :].T

    both = sums[:heads_here].reshape(heads_here, 2, HEAD_DIM)
    g_qv_bias = both.transpose(1, 0, 2).reshape(2, inner)
    g_box = sums[heads_here : 2 * heads_here].reshape(heads_here, 2, NB2).transpose(1, 0, 2)
    g_pos = sums[2 * heads_here : 3 * heads_here, :NB1]
    g_up_bias = sums[3 * heads_here : 3 * heads_here + 6].reshape(units)
    shared = sums[EACH : EACH + 36].reshape(6, width)
    return (
        layer_out.reshape(tokens.shape),
        grad_tokens.reshape(tokens.shape),
        g_w_qkv,
        g_qv_bias,
        g_w_out,
        shared[0],
        shared[1],
        shared[2],
        g_w_up,
        g_up_bias,
        g_w_down,
        shared[3],
        shared[4],
        shared[5],
        g_pos,
        g_box,
    )


def solution(mesh):
    placed = (
        P(("pages", "heads"), None, None),
        P(None, None, "heads"),
        P(None, "heads"),
        P("heads", None),
        P(),
        P(),
        P(),
        P(None, "heads"),
        P("heads"),
        P("heads", None),
        P(),
        P(),
        P(),
        P("heads", None),
        P(None, "heads", None),
        P("pages", None),
        P("pages", None, None),
        P(("pages", "heads"), None, None),
    )
    return jax.shard_map(
        on_device,
        mesh=mesh,
        in_specs=placed,
        out_specs=(
            P(("pages", "heads"), None, None),
            P(("pages", "heads"), None, None),
            P("pages", None, "heads"),
            P(None, "heads"),
            P("heads", "pages"),
            P(),
            P(),
            P(),
            P("pages", "heads"),
            P("heads"),
            P("heads", "pages"),
            P(),
            P(),
            P(),
            P("heads", None),
            P(None, "heads", None),
        ),
        check_vma=False,
    )
```

```python
import functools
import math

import jax
import jax.numpy as jnp
from jax import lax
from jax.experimental import pallas as pl
from jax.experimental.pallas import tpu as pltpu
from jax.sharding import PartitionSpec as P

f32 = jnp.float32
bf16 = jnp.bfloat16
i32 = jnp.int32
EPSILON = 1e-05
MASKED_SCORE = -1e30


HEAD_DIM = 64
TEXT = 512
NB1 = 32
MD1 = 128
NB2 = 64
MD2 = 256
ROWS = 576
VIS = ROWS - TEXT
QROWS = 640
LANES = 128
CHUNK = 64
UNIT = 2048.0
BLOCKS = ((0, 256), (0, 384), (128, 384), (256, 256))
OFFS = (0, 320, 768, 1216)
SPAN = 1536
Q_AT = SPAN
KV_AT = Q_AT + ROWS
PV_AT = KV_AT + ROWS
KEPT = PV_AT + ROWS // 2
SMALL = 24


def thresholds(buckets, max_reach):
    half_range = buckets // 2
    exact_range = half_range // 2
    levels = half_range - exact_range
    return [
        math.ceil(exact_range * (max_reach / exact_range) ** (k / levels) - 1e-09)
        for k in range(1, levels)
    ]


def bucket_of(diff, buckets, reach):
    n = jnp.abs(diff)
    out = jnp.minimum(n, buckets // 4) + jnp.where(diff > 0, buckets // 2, 0)
    for t in thresholds(buckets, reach):
        out = out + jnp.where(n >= t, 1, 0)
    return out


def parts_of(blk):
    s, n = BLOCKS[blk]
    return ((s, n, OFFS[blk]), (TEXT, VIS, OFFS[blk] + n))


def nt(a, b):
    return lax.dot_general(a, b, (((1,), (1,)), ((), ())), preferred_element_type=f32)


def nn(a, b):
    return lax.dot_general(a, b, (((1,), (0,)), ((), ())), preferred_element_type=f32)


def unpack(ids):
    return ids & 255, (ids >> 8) & 255, ids >> 16


def take(tab, idx):
    return jnp.take_along_axis(
        jnp.broadcast_to(tab, idx.shape), idx, axis=1, mode="promise_in_bounds"
    )


def ids_kernel(place_ref, len_ref, box_ref, ids_ref, vis_ref, some_ref, c_s, r_s, *, valid):
    page = place_ref[0]
    row = lax.broadcasted_iota(i32, (8, ROWS), 1)
    segment = jnp.zeros((8, ROWS), i32)
    end = 0
    for i in range(len_ref.shape[1]):
        end = end + len_ref[page, i]
        segment = segment + jnp.where(row >= end, 1, 0)
    c_s[...] = jnp.zeros_like(c_s)
    c_s[0:8, :] = segment.astype(f32)
    c_s[8:10, 0:valid] = box_ref[page].astype(f32)
    r_s[...] = c_s[...].T.astype(i32)

    def query(lo, hi):
        return tuple(c_s[i : i + 1, lo:hi].astype(i32) for i in (0, 8, 9))

    def tiles(row, out, rows, q_first, q):
        qseg, qx, qy = (jnp.broadcast_to(v, (CHUNK, LANES)) for v in q)
        lane = lax.broadcasted_iota(i32, (CHUNK, LANES), 1)
        if q_first == TEXT:
            q_pos, high = TEXT + (lane & (VIS - 1)), jnp.where(lane >= VIS, NB2, 0)
        else:
            q_pos, high = q_first + lane, 0

        def tile(c, _):
            at = pl.ds(pl.multiple_of(row + c * CHUNK, CHUNK), CHUNK)
            here = pl.ds(pl.multiple_of(out + c * CHUNK, CHUNK), CHUNK)
            seg, kx, ky = (jnp.broadcast_to(r_s[at, i : i + 1], (CHUNK, LANES)) for i in (0, 8, 9))
            k_pos = lax.broadcasted_iota(i32, (CHUNK, LANES), 0) + (row + c * CHUNK)
            x_id = bucket_of(kx - qx, NB2, MD2)
            y_id = bucket_of(ky - qy, NB2, MD2)
            p_id = bucket_of(k_pos - q_pos, NB1, MD1)
            ok = ((seg == qseg) | (k_pos >= TEXT) | (q_pos >= TEXT)) & (k_pos < valid)
            p_id = jnp.where(ok, p_id, NB1)
            y_id = y_id + (high if q_first == TEXT else NB2)
            ref, at = (vis_ref, at) if q_first == TEXT else (ids_ref, here)
            ref[at, :] = (x_id + high) + y_id * 256 + (p_id + high) * 65536
            if q_first != TEXT:
                some_ref[out // CHUNK + c] = jnp.max(jnp.where(ok, 1, 0))
            return 0

        lax.fori_loop(0, rows // CHUNK, tile, 0)

    for blk in range(4):
        q = query(blk * LANES, (blk + 1) * LANES)
        for s, n, o in parts_of(blk):
            tiles(s, o, n, blk * LANES, q)
    q = tuple(jnp.concatenate((v, v), axis=1) for v in query(TEXT, ROWS))
    tiles(0, 0, ROWS, TEXT, q)


def make_ids(place, lengths, boxes):
    return pl.pallas_call(
        functools.partial(ids_kernel, valid=boxes.shape[2]),
        in_specs=[
            pl.BlockSpec(memory_space=pltpu.SMEM),
            pl.BlockSpec(memory_space=pltpu.SMEM),
            pl.BlockSpec(memory_space=pltpu.VMEM),
        ],
        out_specs=[
            pl.BlockSpec(memory_space=pltpu.VMEM),
            pl.BlockSpec(memory_space=pltpu.VMEM),
            pl.BlockSpec(memory_space=pltpu.SMEM),
        ],
        out_shape=[
            jax.ShapeDtypeStruct((SPAN, LANES), i32),
            jax.ShapeDtypeStruct((ROWS, LANES), i32),
            jax.ShapeDtypeStruct((SPAN // CHUNK,), i32),
        ],
        scratch_shapes=[pltpu.VMEM((LANES, ROWS), f32), pltpu.VMEM((ROWS, LANES), i32)],
        name="ids",
        cost_estimate=pl.CostEstimate(flops=0, bytes_accessed=0, transcendentals=0),
        compiler_params=pltpu.CompilerParams(vmem_limit_bytes=12 << 20),
    )(place, lengths, boxes)


def place(dst_ref, pair, first, side, cols):
    at = slice(side * 192, side * 192 + 64)
    dst_ref[pair, first : first + ROWS, at] = cols


def stacked(both):
    return jnp.concatenate((both[:, :LANES], both[:, LANES:]), 0)


def block(ref, pair, first, blk):
    rows = LANES if blk < 4 else VIS
    return stacked(ref[pair, first + blk * LANES : first + blk * LANES + rows, :])


def load_rows(refs, odd, dst):
    if len(refs) == 1:
        dst[0 : refs[0].shape[0], :] = refs[0][...]
    else:
        half = dst.shape[0] // 2
        for first in range(2):

            @pl.when(odd == first)
            def _(first=first):
                dst[first * half : (first + 1) * half, :] = refs[0][0:half, :]
                dst[(1 - first) * half : (2 - first) * half, :] = refs[1][0:half, :]


def pad_rows(v):
    return jnp.concatenate((v, jnp.zeros((ROWS - v.shape[0], v.shape[1]), v.dtype)), 0)


def fold(both):
    n = both.shape[1] // 2
    t = both.T
    lane = lax.broadcasted_iota(i32, (n, LANES), 1)
    return jnp.where(lane < 64, t[:n], t[n:])


def fwd_kernel(place_ref, tok_ref, *refs, pieces, pairs):
    *refs, n_s, b_s = refs
    for i in range(3):
        far = lax.broadcasted_iota(i32, (LANES, LANES), 0) - lax.broadcasted_iota(i32, (LANES, LANES), 1)
        n_s[i] = bucket_of(far + (i - 1) * LANES, NB1, MD1)
    n = 2 * pieces
    weights = (refs[:pieces], refs[pieces:n])
    small, (ids_ref, vis_ref) = refs[n : n + 2], refs[n + 2 : n + 4]
    wo_refs, refs = (refs[n + 4 : n + 6], refs[n + 6 :]) if pieces == 1 else (None, refs[n + 4 :])
    out_ref, bias_ref, wo_ref, kept_ref = refs[:4]
    w_s = refs[4] if pieces > 1 else None
    vt_s, s_s, i_s, f_s, o_s, l_s = refs[-6:]
    first = small[0].shape[0] - 16
    inner = pairs * HEAD_DIM
    units = 4 * pairs // 6
    bias_ref[...] = jnp.zeros_like(bias_ref)
    for g in range(2):
        bias_ref[g : g + 1, :] = small[g][first + units : first + units + 1, :].astype(f32)
        for i in range(4 * pairs):
            at = slice(i % 6 * LANES, (i % 6 + 1) * LANES)
            row = first + i // 6
            high, rest = (small[g][r : r + 1, at].astype(f32) for r in (row, row + 8))
            l_s[g, i : i + 1, :] = high + rest
    small = [l_s.at[g] for g in range(2)]
    tok = pad_rows(tok_ref[...])
    for pair in range(pairs):
        kept_ref[pair, Q_AT:KV_AT, :] = jnp.zeros((ROWS, 256), bf16)
    for g in range(2):
        if pieces > 1:
            load_rows(weights[g], place_ref[1], w_s.at[g])
            w_ref = w_s.at[g]
            wo_ref[g * inner : (g + 1) * inner, :] = w_ref[3 * inner :, :]
        else:
            w_ref = weights[g][0]
            wo_ref[g * inner : (g + 1) * inner, :] = wo_refs[g][...]
        for part in range(3):
            mixed = nt(tok, w_ref[part * inner : (part + 1) * inner, :])
            for local in range(pairs):
                pair, side = divmod(g * pairs + local, 2)
                at = slice(side * 64, side * 64 + 64)
                cols = mixed[:, local * 64 : local * 64 + 64]
                if part == 0:
                    cols = cols + small[g][2 * pairs + local : 2 * pairs + local + 1, :64]
                    place(kept_ref, pair, Q_AT, side, (cols * (UNIT / 8)).astype(bf16))
                elif part == 1:
                    kept_ref[pair, KV_AT:PV_AT, at] = cols.astype(bf16)
                else:
                    cols = cols + small[g][3 * pairs + local : 3 * pairs + local + 1, :64]
                    low = slice(LANES + side * 64, LANES + side * 64 + 64)
                    kept_ref[pair, KV_AT:PV_AT, low] = cols.astype(bf16)
                    vt_s[pair, at, :] = cols.T.astype(bf16)
    for pair in range(pairs):
        (ga, la), (gb, lb) = divmod(2 * pair, pairs), divmod(2 * pair + 1, pairs)
        for row, start in ((0, 0), (1, pairs)):
            a = small[ga][start + la : start + la + 1, :] * UNIT
            b = small[gb][start + lb : start + lb + 1, :] * UNIT
            i_s[pair, row : row + 1, :] = (
                jnp.round(a).astype(i32) * 65536 + jnp.round(b).astype(i32)
            )
            f_s[pair, 2 * row : 2 * row + 1, :] = jnp.concatenate((a[:, :64], b[:, :64]), 1)
            f_s[pair, 2 * row + 1 : 2 * row + 2, :] = jnp.concatenate((a[:, 64:], b[:, 64:]), 1)

    def softmax(total, wide, p_at):
        m = jnp.full((8, wide), -3e38, f32)
        for c in range(0, total, 8):
            m = jnp.maximum(m, s_s[c : c + 8, :wide])
        m = jnp.max(m, axis=0, keepdims=True)
        l = jnp.zeros((8, wide), f32)
        for c in range(0, total, 8):
            e = jnp.exp2((s_s[c : c + 8, :wide] - m) * (math.log2(math.e) / UNIT))
            s_s[c : c + 8, :wide] = e
            l = l + e
        inv = 1.0 / jnp.sum(l, axis=0, keepdims=True)
        for c in range(0, total, 16):
            p_at(c, (s_s[c : c + 16, :wide] * inv).astype(bf16))

    def one_pair(pair, _):
        t_xy, t_p = (i_s[pair, i : i + 1, :] for i in range(2))
        v_x, v_y, v_p = (f_s[pair, i : i + 1, :] for i in range(3))
        for i in range(3):
            for c in range(0, LANES, 16):
                b_s[i, c : c + 16, :] = take(t_p, n_s[i, c : c + 16, :])
        for blk in range(4):
            q = block(kept_ref, pair, Q_AT, blk)
            first = OFFS[blk]
            for s, n, o in parts_of(blk):
                sc = nt(kept_ref[pair, KV_AT + s : KV_AT + s + n, :LANES], q)
                for c in range(0, n, 16):
                    r = slice(o + c, o + c + 16)
                    x, y, p = unpack(ids_ref[r, :])
                    if s < TEXT:
                        tile, row = divmod(s + c, LANES)
                        b_p = b_s[tile - blk + 1, row : row + 16, :]
                    else:
                        b_p = take(t_p, p)
                    b = take(t_xy, x) + take(t_xy, y) + b_p
                    low = (b << 16) >> 16
                    high = (b - low) >> 16
                    add = jnp.where(p == NB1, MASKED_SCORE, 0.0)
                    to = slice(o - first + c, o - first + c + 16)
                    s_s[to, :LANES] = sc[c : c + 16, :LANES] + (high.astype(f32) + add)
                    s_s[to, LANES:] = sc[c : c + 16, LANES:] + (low.astype(f32) + add)

            def put(c, v, first=first):
                kept_ref[pair, first + c : first + c + 16, :] = v

            softmax(BLOCKS[blk][1] + VIS, 256, put)
            ot = sum(
                nn(vt_s[pair, :, s : s + n], kept_ref[pair, o : o + n, :]) for s, n, o in parts_of(blk)
            )
            o_s[pair, blk * LANES : (blk + 1) * LANES, :] = fold(ot).astype(bf16)
        q = block(kept_ref, pair, Q_AT, 4)
        sc = nt(kept_ref[pair, KV_AT:PV_AT, :LANES], q)
        for c in range(0, ROWS, 16):
            x, y, p = unpack(vis_ref[c : c + 16, :])
            b = take(v_x, x) + take(v_y, y) + take(v_p, p)
            add = jnp.where((p & (NB2 - 1)) == NB1, MASKED_SCORE, 0.0)
            s_s[c : c + 16, :LANES] = sc[c : c + 16] + (b + add)

        def put_v(c, v):
            side, row = divmod(c, ROWS // 2)
            at = slice(side * LANES, (side + 1) * LANES)
            kept_ref[pair, PV_AT + row : PV_AT + row + 16, at] = v

        softmax(ROWS, LANES, put_v)
        o_s[pair, TEXT:ROWS, :] = fold(nn(vt_s[pair], stacked(kept_ref[pair, PV_AT:KEPT, :]))).astype(bf16)
        return 0

    lax.fori_loop(0, pairs, one_pair, 0)
    rows = out_ref.shape[0]
    for pair in range(pairs):
        out_ref[:, pair * LANES : (pair + 1) * LANES] = o_s[pair, 0:rows, :]


def attn_fwd(place, tok, weights, small, ids, pairs, w_out=()):
    pieces, (rows, width) = len(weights[0]), tok.shape
    vmem = pl.BlockSpec(memory_space=pltpu.VMEM)
    outs = [((rows, pairs * LANES), bf16), ((8, width), f32), ((pairs * LANES, width), bf16)]
    outs += [((pairs, KEPT, 256), bf16)]
    if pieces > 1:
        outs += [((2, 4 * pairs * HEAD_DIM, width), bf16)]
    args = (place, tok, *weights[0], *weights[1], *small, *ids, *w_out)
    return pl.pallas_call(
        functools.partial(fwd_kernel, pieces=pieces, pairs=pairs),
        in_specs=[pl.BlockSpec(memory_space=pltpu.SMEM)] + [vmem] * (len(args) - 1),
        out_specs=[vmem] * len(outs),
        out_shape=[jax.ShapeDtypeStruct(shape, dtype) for shape, dtype in outs],
        scratch_shapes=[
            pltpu.VMEM((pairs, LANES, ROWS), bf16),
            pltpu.VMEM((ROWS, 256), f32),
            pltpu.VMEM((pairs, 8, LANES), i32),
            pltpu.VMEM((pairs, 8, LANES), f32),
            pltpu.VMEM((pairs, ROWS, LANES), bf16),
            pltpu.VMEM((2, SMALL, LANES), f32),
            pltpu.VMEM((3, LANES, LANES), i32),
            pltpu.VMEM((3, LANES, LANES), i32),
        ],
        name="attn_fwd",
        cost_estimate=pl.CostEstimate(flops=0, bytes_accessed=0, transcendentals=0),
        compiler_params=pltpu.CompilerParams(vmem_limit_bytes=14 << 20),
    )(*args)


def bwd_kernel(kept_ref, do_ref, out0_ref, out1_ref, sum_ref, ds_ref, dsv_ref, do_s, kt_s, dq_s, dk_s, dv_s, *, pairs):
    rows = out0_ref.shape[0]
    sum_ref[...] = jnp.zeros_like(sum_ref)
    do_s[...] = jnp.zeros_like(do_s)
    for h in range(2 * pairs):
        pair, side = divmod(h, 2)
        place(do_s, pair, 0, side, pad_rows(do_ref[:, h * 64 : h * 64 + 64]))
    for pair in range(pairs):
        kt_s[pair] = kept_ref[pair, KV_AT:PV_AT, :LANES].astype(f32).T.astype(bf16)

    def grad_scores(dps, ps, put):
        d = jnp.zeros((8, dps[0].shape[1]), f32)
        for dp, p in zip(dps, ps):
            for c in range(0, dp.shape[0], 16):
                t = p(c).astype(f32) * dp[c : c + 16]
                d = d + (t[:8] + t[8:])
        d = jnp.sum(d, axis=0, keepdims=True)
        for i, (dp, p) in enumerate(zip(dps, ps)):
            for c in range(0, dp.shape[0], 16):
                put(i, c, (p(c).astype(f32) * (dp[c : c + 16] - d)).astype(bf16))

    def one_pair(pair, _):
        dv_s[...] = jnp.zeros_like(dv_s)
        dk_s[...] = jnp.zeros_like(dk_s)
        for blk in range(4):
            q = block(kept_ref, pair, Q_AT, blk)
            do = block(do_s, pair, 0, blk)
            parts = parts_of(blk)

            def put(i, c, v, parts=parts):
                ds_ref[pair, parts[i][2] + c : parts[i][2] + c + 16, :] = v

            grad_scores(
                [nt(kept_ref[pair, KV_AT + s : KV_AT + s + n, LANES:], do) for s, n, o in parts],
                [lambda c, o=o: kept_ref[pair, o + c : o + c + 16, :] for s, n, o in parts],
                put,
            )
            dq = 0.0
            for s, n, o in parts:
                ds = ds_ref[pair, o : o + n, :]
                dq = dq + nn(kt_s[pair, :, s : s + n], ds)
                dv_s[s : s + n, :] += nn(kept_ref[pair, o : o + n, :], do)
                dk_s[s : s + n, :] += nn(ds, q)
            dq_s[pair, 0, blk * LANES : (blk + 1) * LANES, :] = (fold(dq) * 0.125).astype(bf16)
        q = block(kept_ref, pair, Q_AT, 4)
        do = block(do_s, pair, 0, 4)
        pv = stacked(kept_ref[pair, PV_AT:KEPT, :])

        def put_v(i, c, v):
            dsv_ref[pair, c : c + 16, :] = v

        grad_scores([nt(kept_ref[pair, KV_AT:PV_AT, LANES:], do)], [lambda c: pv[c : c + 16]], put_v)
        ds = dsv_ref[pair]
        dq_s[pair, 0, TEXT:ROWS, :] = (fold(nn(kt_s[pair], ds)) * 0.125).astype(bf16)
        dq_s[pair, 1] = ((dk_s[...] + nn(ds, q)) * (1.0 / UNIT)).astype(bf16)
        dq_s[pair, 2] = (dv_s[...] + nn(pv, do)).astype(bf16)
        return 0

    lax.fori_loop(0, pairs, one_pair, 0)
    for h in range(2 * pairs):
        pair, side = divmod(h, 2)
        g, local = divmod(h, pairs)
        for part in range(3):
            col = part * pairs * HEAD_DIM + local * HEAD_DIM
            here = dq_s[pair, part, 0:rows, side * 64 : side * 64 + 64]
            (out0_ref, out1_ref)[g][:, col : col + 64] = here
            if part != 1:
                total = jnp.sum(here.astype(f32), axis=0, keepdims=True)
                sum_ref[g : g + 1, col : col + 64] = total


def attn_bwd(rows, kept, d_att):
    pairs = kept.shape[0]
    cols = 3 * pairs * HEAD_DIM
    vmem = pl.BlockSpec(memory_space=pltpu.VMEM)
    outs = [((rows, cols), bf16)] * 2 + [((8, cols), f32)]
    outs += [((pairs, SPAN, 256), bf16), ((pairs, ROWS, LANES), bf16)]
    return pl.pallas_call(
        functools.partial(bwd_kernel, pairs=pairs),
        in_specs=[vmem] * 2,
        out_specs=[vmem] * 5,
        out_shape=[jax.ShapeDtypeStruct(shape, dtype) for shape, dtype in outs],
        scratch_shapes=[
            pltpu.VMEM((pairs, ROWS, 256), bf16),
            pltpu.VMEM((pairs, LANES, ROWS), bf16),
            pltpu.VMEM((pairs, 3, ROWS, LANES), bf16),
            pltpu.VMEM((ROWS, LANES), f32),
            pltpu.VMEM((ROWS, LANES), f32),
        ],
        name="attn_bwd",
        cost_estimate=pl.CostEstimate(flops=0, bytes_accessed=0, transcendentals=0),
        compiler_params=pltpu.CompilerParams(vmem_limit_bytes=14 << 20),
    )(kept, d_att)


HSTEP = 64
HBLOCK = 192


def hist_kernel(some_ref, acc_ref, ids_ref, *refs, sets, pairs, first_id):
    ds_refs, hist_ref, l_s = refs[:sets], refs[-2], refs[-1]
    heads = 2 * sets * pairs

    @pl.when(pl.program_id(0) == 0)
    def _():
        hist_ref[...] = acc_ref[...]

    for h in range(heads, 16):
        l_s[pl.ds(h, HSTEP, stride=16), :] = jnp.zeros((HSTEP, LANES), f32)
    steps = HBLOCK // HSTEP

    @pl.loop(0, steps)
    def _(r):
        @pl.when(some_ref[(first_id + pl.program_id(0)) * steps + r] > 0)
        def _():
            first = pl.multiple_of(r * HSTEP, HSTEP)
            for pair in range(sets * pairs):
                ref = ds_refs[pair // pairs]
                for side in range(2):
                    at = slice(side * LANES, (side + 1) * LANES)
                    v = ref[pair % pairs, pl.ds(first, HSTEP), at].astype(f32)
                    l_s[pl.ds(2 * pair + side, HSTEP, stride=16), :] = v
            ids = lambda u: ids_ref[pl.ds(first + u, 1), :]
            hist_ref[...] += hot_sums(l_s, ids, HSTEP, NB2)


def hot_sums(l_s, ids, rows, y_from):
    io = lax.broadcasted_iota(i32, (NB2, LANES), 0)
    lhs, rhs = [], []
    for u in range(rows):
        x, y, p = unpack(ids(u))
        if y_from:
            y = y - y_from
        else:
            x, y, p = (v & (NB2 - 1) for v in (x, y, p))
        hot = [jnp.where(io == x, 1.0, 0.0), jnp.where(io == y, 1.0, 0.0)]
        hot.append(jnp.where(io[:NB1] == p, 1.0, 0.0))
        rhs.append(jnp.concatenate(hot, 0).astype(bf16))
        lhs.append(l_s[u * 16 : u * 16 + 16, :].astype(bf16))
    return nt(jnp.concatenate(lhs, 1), jnp.concatenate(rhs, 1))


VSTEP = 72


def visual_kernel(acc_ref, ids_ref, *refs, sets, pairs):
    ds_refs, hist_ref, l_s, i_s = refs[:sets], refs[-3], refs[-2], refs[-1]
    heads = 2 * sets * pairs
    far = ROWS // 2
    lane = lax.broadcasted_iota(i32, (VSTEP, LANES), 1)
    hist_ref[...] = acc_ref[...]
    for h in range(heads, 16):
        l_s[pl.ds(h, VSTEP, stride=16), :] = jnp.zeros((VSTEP, LANES), f32)

    @pl.loop(0, far // VSTEP)
    def _(r):
        here = pl.ds(pl.multiple_of(r * VSTEP, 8), VSTEP)
        there = pl.ds(pl.multiple_of(far + r * VSTEP, 8), VSTEP)
        i_s[...] = jnp.where(lane < VIS, ids_ref[here, :], ids_ref[there, :])
        for pair in range(sets * pairs):
            ref = ds_refs[pair // pairs]
            a, b = (ref[pair % pairs, at, :].astype(f32) for at in (here, there))
            one = jnp.where(lane < VIS, a, pltpu.roll(b, VIS, axis=1))
            two = jnp.where(lane < VIS, pltpu.roll(a, VIS, axis=1), b)
            l_s[pl.ds(2 * pair, VSTEP, stride=16), :] = one
            l_s[pl.ds(2 * pair + 1, VSTEP, stride=16), :] = two
        hist_ref[...] += hot_sums(l_s, lambda u: i_s[u : u + 1, :], VSTEP, 0)


def add_visual(acc, ids, ds):
    vmem = pl.BlockSpec(memory_space=pltpu.VMEM)
    return pl.pallas_call(
        functools.partial(visual_kernel, sets=len(ds), pairs=ds[0].shape[0]),
        grid=(1,),
        in_specs=[
            pl.BlockSpec((16, 160), lambda i: (0, 0)),
            pl.BlockSpec((ROWS, LANES), lambda i: (0, 0)),
        ]
        + [pl.BlockSpec(t.shape, lambda i: (0, 0, 0)) for t in ds],
        out_specs=pl.BlockSpec((16, 160), lambda i: (0, 0)),
        out_shape=jax.ShapeDtypeStruct((16, 160), f32),
        scratch_shapes=[pltpu.VMEM((VSTEP * 16, LANES), f32), pltpu.VMEM((VSTEP, LANES), i32)],
        name="hist",
        cost_estimate=pl.CostEstimate(flops=0, bytes_accessed=0, transcendentals=0),
        compiler_params=pltpu.CompilerParams(vmem_limit_bytes=12 << 20),
    )(acc, ids, *ds)


def add_hist(acc, ids, some, ds, first_row, rows):
    first = first_row // HBLOCK
    specs = [
        pl.BlockSpec(memory_space=pltpu.SMEM),
        pl.BlockSpec((16, 160), lambda i: (0, 0)),
        pl.BlockSpec((HBLOCK, LANES), lambda i: (first + i, 0)),
    ]
    for t in ds:
        specs.append(pl.BlockSpec((t.shape[0], HBLOCK, t.shape[2]), lambda i: (0, first + i, 0)))
    return pl.pallas_call(
        functools.partial(hist_kernel, sets=len(ds), pairs=ds[0].shape[0], first_id=first),
        grid=(rows // HBLOCK,),
        in_specs=specs,
        out_specs=pl.BlockSpec((16, 160), lambda i: (0, 0)),
        out_shape=jax.ShapeDtypeStruct((16, 160), f32),
        scratch_shapes=[pltpu.VMEM((HSTEP * 16, LANES), f32)],
        name="hist",
        cost_estimate=pl.CostEstimate(flops=0, bytes_accessed=0, transcendentals=0),
        compiler_params=pltpu.CompilerParams(vmem_limit_bytes=12 << 20),
    )(some, acc, ids, *ds)


def call(kernel, name, args, outs, scratch=(), smem=0):
    vmem = pl.BlockSpec(memory_space=pltpu.VMEM)
    return pl.pallas_call(
        kernel,
        in_specs=[pl.BlockSpec(memory_space=pltpu.SMEM)] * smem + [vmem] * (len(args) - smem),
        out_shape=[jax.ShapeDtypeStruct(shape, dtype) for shape, dtype in outs],
        scratch_shapes=[pltpu.VMEM(shape, dtype) for shape, dtype in scratch],
        name=name,
        cost_estimate=pl.CostEstimate(flops=0, bytes_accessed=0, transcendentals=0),
        compiler_params=pltpu.CompilerParams(vmem_limit_bytes=12 << 20),
    )(*args)


def start_kernel(place_ref, qkv_ref, wo_ref, up_ref, box_ref, pos_ref, qv_ref, ub_ref, a_ref, b_ref, small_ref, s_s, o_s, sems):
    half = b_ref.shape[0]
    inner = wo_ref.shape[0]
    odd = place_ref[1]

    def copy(src, dst, i):
        return pltpu.make_async_copy(src, dst, sems.at[i])

    tail = qkv_ref.shape[0] - half
    firsts = [copy(qkv_ref.at[0:half, :], a_ref.at[0:half, :], 0)]
    seconds = [
        copy(qkv_ref.at[half:, :], a_ref.at[0:tail, :], 0),
        copy(wo_ref, a_ref.at[tail:half, :], 1),
    ]

    @pl.when(odd == 0)
    def _():
        for c in firsts:
            c.start()

    @pl.when(odd == 1)
    def _():
        for c in seconds:
            c.start()

    at = pl.ds(pl.multiple_of(odd * half, half), half)
    others = [copy(up_ref.at[at, :], b_ref, 2)]
    for c in others:
        c.start()
    heads = pos_ref.shape[0]
    s_s[...] = jnp.zeros_like(s_s)
    for h in range(heads):
        s_s[h : h + 1, :NB2] = box_ref[h, 0:1, :]
        s_s[h : h + 1, NB2:] = box_ref[h, 1:2, :]
        s_s[heads + h : heads + h + 1, :NB1] = pos_ref[h : h + 1, :]
        for i in range(2):
            row = (2 + i) * heads + h
            s_s[row : row + 1, :64] = qv_ref[i : i + 1, h * 64 : h * 64 + 64]
    units = ub_ref.shape[0] // LANES
    s_s[4 * heads : 4 * heads + units, :] = ub_ref[...].astype(f32).reshape(units, LANES)
    o_s[...] = jnp.zeros_like(o_s)
    for i in range(SMALL):
        at = slice(i % 6 * LANES, (i % 6 + 1) * LANES)
        value = s_s[i : i + 1, :]
        high = value.astype(bf16).astype(f32)
        o_s[i // 6 : i // 6 + 1, at] = high
        o_s[8 + i // 6 : 9 + i // 6, at] = value - high
    small_ref[...] = o_s[...].astype(bf16)
    last = copy(small_ref, a_ref.at[half : half + 16, :], 4)
    last.start()

    @pl.when(odd == 0)
    def _():
        for c in firsts:
            c.wait()

    @pl.when(odd == 1)
    def _():
        for c in seconds:
            c.wait()

    for c in others + [last]:
        c.wait()


def start_parts(place, qkv, w_out, w_up, box, pos, qv, up):
    width = qkv.shape[1]
    vmem, hbm = (pl.BlockSpec(memory_space=m) for m in (pltpu.VMEM, pltpu.HBM))
    shapes = [(width // 2 + 16, width), (width // 2, width), (16, width)]
    return pl.pallas_call(
        start_kernel,
        in_specs=[pl.BlockSpec(memory_space=pltpu.SMEM)] + [hbm] * 3 + [vmem] * 4,
        out_specs=[vmem] * 3,
        out_shape=[jax.ShapeDtypeStruct(shape, bf16) for shape in shapes],
        scratch_shapes=[
            pltpu.VMEM((SMALL, LANES), f32),
            pltpu.VMEM((16, width), f32),
            pltpu.SemaphoreType.DMA((5,)),
        ],
        name="start_parts",
        cost_estimate=pl.CostEstimate(flops=0, bytes_accessed=0, transcendentals=0),
        compiler_params=pltpu.CompilerParams(vmem_limit_bytes=58 << 20),
    )(place, qkv, w_out, w_up, box.transpose(1, 0, 2), pos, qv, up)


def join_kernel(place_ref, mine_ref, theirs_ref, *refs):
    outs, sems = refs[:-1], refs[-1]
    half = mine_ref.shape[0] // len(outs)
    odd = place_ref[1]
    copies = []
    for i, out in enumerate(outs):
        for j, (ref, first) in enumerate(((mine_ref, odd * half), (theirs_ref, (1 - odd) * half))):
            to = out.at[pl.ds(pl.multiple_of(first, half), half), :]
            at = slice(i * half, (i + 1) * half)
            copies.append(pltpu.make_async_copy(ref.at[at, :], to, sems.at[i, j]))
    for c in copies:
        c.start()
    for c in copies:
        c.wait()


def join_rows(place, mine, theirs, number):
    rows, cols = mine.shape
    vmem = pl.BlockSpec(memory_space=pltpu.VMEM)
    return pl.pallas_call(
        join_kernel,
        in_specs=[pl.BlockSpec(memory_space=pltpu.SMEM), vmem, vmem],
        out_specs=[vmem] * number,
        out_shape=[jax.ShapeDtypeStruct((2 * rows // number, cols), bf16)] * number,
        scratch_shapes=[pltpu.SemaphoreType.DMA((number, 2))],
        name="join_rows",
        cost_estimate=pl.CostEstimate(flops=0, bytes_accessed=0, transcendentals=0),
        compiler_params=pltpu.CompilerParams(vmem_limit_bytes=8 << 20),
    )(place, mine, theirs)


def tn(a, b):
    return lax.dot_general(a, b, (((0,), (0,)), ((), ())), preferred_element_type=f32)


def parity_split(cur_ref, keep_ref, send_ref, first, chunk, bit):
    for mine in range(2):

        @pl.when(bit == mine)
        def _(mine=mine):
            for i in range(cur_ref.shape[0] // chunk // 2):
                to = slice(first + i * chunk, first + (i + 1) * chunk)
                at = (2 * i + mine) * chunk
                keep_ref[to, :] = cur_ref[at : at + chunk, :]
                at = (2 * i + 1 - mine) * chunk
                send_ref[to, :] = cur_ref[at : at + chunk, :]


def products_kernel(place_ref, *refs, lefts, plan, chunk):
    left, refs = refs[:lefts], list(refs[lefts:])
    rights = [[refs.pop(0) for _ in terms] for terms, _, _ in plan]
    gots = [[[refs.pop(0) for _ in range(n)] for n in counts] for _, counts, _ in plan]
    cur_s = refs.pop()
    split = 0
    for (terms, _, mode), right, got in zip(plan, rights, gots):
        outs = [cur_s] if mode == "halve" else [refs.pop(0) for _ in range(mode)]
        col = 0
        for (i, lanes), r in zip(terms, right):
            lanes = lanes or (0, r.shape[1])
            at = slice(col, col + lanes[1] - lanes[0])
            total = tn(left[i][...], r[:, lanes[0] : lanes[1]])
            for pieces in got:
                wide = [g[:, at].astype(f32) for g in pieces]
                total = total + (wide[0] if len(wide) == 1 else jnp.concatenate(wide, 0))
            rows = total.shape[0] // len(outs)
            for k, out in enumerate(outs):
                out[:, at] = total[k * rows : (k + 1) * rows].astype(bf16)
            col += lanes[1] - lanes[0]
        if mode == "halve":
            if split == 0:
                keep, send = refs.pop(0), refs.pop(0)
            parity_split(cur_s, keep, send, split, chunk, place_ref[1])
            split += cur_s.shape[0] // 2


def plain_split(place, cur, bit, chunk):
    view = cur.reshape(-1, 2, chunk, cur.shape[1])
    pick = lambda i: lax.dynamic_index_in_dim(view, i, axis=1, keepdims=False)
    mine = place[1 + bit]
    return tuple(pick(i).reshape(-1, cur.shape[1]) for i in (mine, 1 - mine))


def products(place, lefts, specs, chunk):
    width = lefts[0].shape[1]
    halved = sum(mode == "halve" for _, _, mode in specs)
    if chunk % 16 and halved:
        whole = products(place, lefts, [(t, g, 1) for t, g, _ in specs], chunk)
        parts = [plain_split(place, cur, 0, chunk) for cur in whole]
        return [jnp.concatenate(side, axis=0) for side in zip(*parts)]
    plan = [
        ([(t[0], t[2] if len(t) > 2 else None) for t in terms], [len(p) for p in gots], mode)
        for terms, gots, mode in specs
    ]
    args = [place, *lefts]
    args += [t[1] for terms, _, _ in specs for t in terms]
    args += [g for _, gots, _ in specs for pieces in gots for g in pieces]
    cols = sum(t[2][1] - t[2][0] if len(t) > 2 else t[1].shape[1] for t in specs[0][0])
    outs = []
    for _, _, mode in specs:
        if mode != "halve":
            outs += [((width // mode, cols), bf16)] * mode
    if halved:
        outs += [((halved * width // 2, cols), bf16)] * 2
    kernel = functools.partial(products_kernel, lefts=len(lefts), plan=plan, chunk=chunk)
    return call(kernel, "products", args, outs, [((width, cols), bf16)], smem=1)


def add_split_kernel(place_ref, *refs, number, bit, chunk):
    keep_ref, send_ref, cur_s = refs[2 * number :]
    first = 0
    for a, b in zip(refs[:number], refs[number : 2 * number]):
        rows = a.shape[0]
        cur_s[first : first + rows] = (a[...].astype(f32) + b[...].astype(f32)).astype(bf16)
        first += rows
    parity_split(cur_s, keep_ref, send_ref, 0, chunk, place_ref[1 + bit])


def add_split(place, keeps, gots, bit, chunk):
    rows, cols = sum(v.shape[0] for v in keeps), keeps[0].shape[1]
    if chunk % 16:
        parts = [(a.astype(f32) + b.astype(f32)).astype(bf16) for a, b in zip(keeps, gots)]
        return plain_split(place, jnp.concatenate(parts, axis=0), bit, chunk)
    half = ((rows // 2, cols), bf16)
    kernel = functools.partial(add_split_kernel, number=len(keeps), bit=bit, chunk=chunk)
    args = (place, *keeps, *gots)
    return call(kernel, "add_split", args, [half, half], [((rows, cols), bf16)], smem=1)


def tokens_kernel(d0, d1, d2, d3, w0, w1, w_ref, first_ref, out_ref):
    cols = d0.shape[1]
    total = first_ref[...] + nn(d0[...], w0[...]) + nn(d1[...], w1[...])
    total = total + nn(d2[...], w_ref[0, 0:cols, :]) + nn(d3[...], w_ref[1, 0:cols, :])
    out_ref[...] = total.astype(bf16)


def tokens_grad(dmixed, weights, d_first):
    args = (*dmixed, *weights, d_first)
    return call(tokens_kernel, "tokens_grad", args, [(d_first.shape, bf16)])[0]


SHARED = 40
EACH = 16


def pack_kernel(hist_ref, near_ref, far_ref, u0, u1, u2, u3, v0, v1, v2, v3, v4, v5, keep_ref, send_ref, *, heads):
    keep_ref[...] = jnp.zeros_like(keep_ref)
    send_ref[...] = jnp.zeros_like(send_ref)
    for g, up in enumerate((u0, u1, u2, u3)):
        ref, first = (keep_ref, send_ref)[g // 2], (g % 2) * EACH
        for h in range(heads):
            for i, part in ((0, 0), (1, 2)):
                col = (part * heads + h) * HEAD_DIM
                row = (near_ref, far_ref)[g // 2][g % 2 : g % 2 + 1, col : col + 64]
                ref[first + h : first + h + 1, i * 64 : i * 64 + 64] = row
            row = hist_ref[g * heads + h : g * heads + h + 1, :]
            ref[first + heads + h : first + heads + h + 1, :] = row[:, :LANES]
            ref[first + 2 * heads + h : first + 2 * heads + h + 1, :NB1] = row[:, LANES:]
        for i in range(6):
            at = slice(first + 3 * heads + i, first + 3 * heads + i + 1)
            ref[at, :] = up[:, i * LANES : (i + 1) * LANES]
    for j, v in enumerate((v0, v1, v2, v3, v4, v5)):
        for i in range(6):
            at = slice(2 * EACH + 6 * j + i, 2 * EACH + 6 * j + i + 1)
            row = v[:, i * LANES : (i + 1) * LANES]
            keep_ref[at, :] = row
            send_ref[at, :] = row


def pack_sums(hist, near, far, ups, shared):
    args = (hist, near, far, *(v.reshape(1, -1) for v in ups), *(v.reshape(1, -1) for v in shared))
    outs = [((2 * EACH + SHARED, LANES), f32)] * 2
    heads = near.shape[1] // (3 * HEAD_DIM)
    return call(functools.partial(pack_kernel, heads=heads), "pack_sums", args, outs)


def unpack_kernel(keep_ref, got_ref, qv_ref, pos_ref, box_ref, up_ref, *shared, heads):
    total = keep_ref[...] + got_ref[...]
    for h in range(heads):
        for i in range(2):
            qv_ref[i : i + 1, h * 64 : h * 64 + 64] = total[h : h + 1, i * 64 : i * 64 + 64]
            box_ref[h, i : i + 1, :] = total[heads + h : heads + h + 1, i * NB2 : (i + 1) * NB2]
        pos_ref[h : h + 1, :] = total[2 * heads + h : 2 * heads + h + 1, :NB1]
    units = up_ref.shape[0] // LANES
    up_ref[...] = total[3 * heads : 3 * heads + units].reshape(up_ref.shape)
    for j, ref in enumerate(shared):
        rows = ref.shape[0] // LANES
        ref[...] = total[EACH + j * rows : EACH + (j + 1) * rows].reshape(ref.shape)


def unpack_sums(keep, got, heads, units, width):
    outs = [((2, heads * HEAD_DIM), f32), ((heads, NB1), f32), ((heads, 2, NB2), f32), ((units,), f32)]
    outs += [((width,), f32)] * 6
    return call(functools.partial(unpack_kernel, heads=heads), "unpack_sums", (keep, got), outs)


def last_kernel(keep_ref, got_ref, qkv_ref, out_ref):
    inner = qkv_ref.shape[2]
    for part in range(3):
        at = slice(part * inner, (part + 1) * inner)
        qkv_ref[part] = keep_ref[:, at].astype(f32) + got_ref[:, at].astype(f32)
    at = slice(3 * inner, 4 * inner)
    out_ref[...] = (keep_ref[:, at].astype(f32) + got_ref[:, at].astype(f32)).T


def last_sums(place, keep, got, bit, chunk):
    inner = keep.shape[1] // 4
    if chunk % 16 == 0 and lax.axis_size("pages") == 2 << bit:
        outs = [((3, chunk, inner), f32), ((inner, chunk), f32)]
        qkv, out = call(last_kernel, "last_sums", (keep, got), outs)
        return qkv.transpose(1, 0, 2), out
    total = finish(place, keep, got, bit, chunk)
    return total[:, : 3 * inner].reshape(-1, 3, inner), total[:, 3 * inner :].T


def core_swap(v):
    return lax.ppermute(v, "heads", [(i, i ^ 1) for i in range(4)])


def x_swap(v):
    return lax.ppermute(v, "heads", [(i, i ^ 2) for i in range(4)])


def page_swap(v, bit):
    return lax.ppermute(v, "pages", [(i, i ^ bit) for i in range(lax.axis_size("pages"))])


def after(value, *others):
    return lax.optimization_barrier((value, *others))[0]


def finish(place, keep, got, bit, chunk):
    last = lax.axis_size("pages").bit_length() - 1
    while bit + 1 < last:
        bit += 1
        keep, send = add_split(place, [keep], [got], bit, chunk)
        got = page_swap(send, 1 << bit)
    return keep.astype(f32) + got.astype(f32)


def add_all(v, bits):
    for bit in bits:
        v = v + page_swap(v, bit)
    return v


def unit_norm(values):
    centered = values - jnp.mean(values, axis=-1, keepdims=True)
    inv_std = lax.rsqrt(jnp.mean(centered * centered, axis=-1, keepdims=True) + EPSILON)
    return centered * inv_std, inv_std


def norm_grad(unit, inv_std, e):
    return inv_std * (
        e - jnp.mean(e, axis=-1, keepdims=True) - unit * jnp.mean(e * unit, axis=-1, keepdims=True)
    )


def on_device(
    tokens,
    w_qkv,
    qv_bias,
    w_out,
    out_bias,
    norm1_gain,
    norm1_shift,
    w_up,
    up_bias,
    w_down,
    down_bias,
    norm2_gain,
    norm2_shift,
    pos_table,
    box_table,
    receipt_lengths,
    page_boxes,
    out_cotangent,
):
    seq_len = tokens.shape[1]
    width = tokens.shape[2]
    heads_here = pos_table.shape[0]
    inner = heads_here * HEAD_DIM
    units = w_up.shape[1]
    own_page = lax.axis_index("heads")
    page_bits = [1 << b for b in range(lax.axis_size("pages").bit_length() - 1)]
    chunk = width // lax.axis_size("pages")
    me = lax.axis_index("pages")
    place = jnp.stack([own_page] + [(me >> b) & 1 for b in range(len(page_bits))]).astype(i32)
    tok = tokens.reshape(seq_len, width)

    own_qkv = w_qkv.reshape(width, 3 * inner).T
    c_qkv, c_out = core_swap(own_qkv), core_swap(w_out)
    half_a, half_b, small = start_parts(
        place, own_qkv, w_out, w_up, box_table, pos_table, qv_bias, up_bias
    )
    c_small = core_swap(small)
    mine_a = x_swap(half_a)
    mine_b = x_swap(half_b)
    x_down = x_swap(w_down)
    ids, vis_ids, some = make_ids(place, receipt_lengths, page_boxes)
    mine_a = after(mine_a, ids)

    c_up, c_down = core_swap(w_up), core_swap(w_down)
    near_w = ((own_qkv,), (after(c_qkv, mine_a, c_up, c_down),))
    near_att, near_bias, near_out, near_kept = attn_fwd(
        place, tok, near_w, (small, c_small), (ids, vis_ids), heads_here, (w_out, c_out)
    )
    half = width // 2
    theirs_a = page_swap(mine_a, 1)
    xc_mine_a, xc_theirs_a = core_swap(mine_a), core_swap(after(theirs_a, near_att))
    theirs_b = page_swap(after(mine_b, near_att), 1)
    xc_mine_b = core_swap(after(mine_b, near_att))
    far_w = ((mine_a, theirs_a), (after(xc_mine_a, xc_mine_b), xc_theirs_a))
    far_att, far_bias, far_out, far_kept, far_w = attn_fwd(
        place, tok, far_w, (mine_a, xc_mine_a), (ids, vis_ids), heads_here
    )
    far_proj = nn(far_att, far_out)
    mine_b, theirs_b = lax.optimization_barrier((mine_b, theirs_b, far_proj))[:2]
    xc_theirs_b = core_swap(theirs_b)
    first_in = nn(near_att, near_out) + far_proj + out_bias + tok.astype(f32)
    unit1, inv1 = unit_norm(first_in)
    first_out = unit1 * norm1_gain + norm1_shift
    first_low = first_out.astype(bf16)

    def units_of(weights, little):
        up = nn(first_low, weights) + little
        cdf = 0.5 * (1.0 + lax.erf(up * math.sqrt(0.5)))
        slope = cdf + up * jnp.exp(-0.5 * up * up) * (1.0 / math.sqrt(2.0 * math.pi))
        return (up * cdf).astype(bf16), lax.optimization_barrier(slope.astype(bf16))

    littles = (near_bias[0], near_bias[1], far_bias[0], far_bias[1])
    own_units = units_of(w_up, littles[0])
    theirs_b = after(theirs_b, own_units[0])
    (x_up,) = join_rows(place, mine_b, theirs_b, 1)
    c_units = units_of(after(c_up, theirs_b), littles[1])
    (xc_up,) = join_rows(place, xc_mine_b, after(xc_theirs_b, x_up), 1)
    far_units = [units_of(w, t) for w, t in zip((x_up, xc_up), littles[2:])]
    hiddens, slopes = zip(own_units, c_units, *far_units)
    x_down = after(x_down, *hiddens)
    xc_down = core_swap(x_down)
    ups, downs = (w_up, c_up, x_up, xc_up), (w_down, c_down, x_down, xc_down)
    second_in = sum(nn(h, w) for h, w in zip(hiddens, downs)) + down_bias + first_out
    unit2, inv2 = unit_norm(second_in)
    layer_out = (unit2 * norm2_gain + norm2_shift).astype(bf16)

    def norm_back(unit, inv_std, gain, dy):
        return norm_grad(unit, inv_std, dy * gain), jnp.sum(dy * unit, axis=0), jnp.sum(dy, axis=0)

    ct = out_cotangent.reshape(seq_len, width).astype(f32)
    d_second, g_gain2, g_shift2 = norm_back(unit2, inv2, norm2_gain, ct)
    g_down_bias = jnp.sum(d_second, axis=0)
    d_ffn = d_second.astype(bf16)

    def core_swaps(pieces):
        return [core_swap(v) for v in pieces]

    to_c = products(
        place, [d_ffn], [([(0, hiddens[3])], [], 2), ([(0, hiddens[1])], [], 2)], chunk
    )
    got_xc, got_c = core_swaps(to_c[:2]), core_swaps(to_c[2:])
    d_ups = [(nt(d_ffn, w) * s.astype(f32)).astype(bf16) for w, s in zip(downs, slopes)]
    far_gd, own_gd = products(
        place,
        [after(d_ffn, *d_ups)],
        [([(0, hiddens[2])], [got_xc], 1), ([(0, hiddens[0])], [got_c], 1)],
        chunk,
    )
    got_xd = x_swap(far_gd)

    to_c = products(
        place,
        [after(first_low, far_gd)],
        [([(0, d_ups[3])], [], 2), ([(0, d_ups[1])], [], 2)],
        chunk,
    )
    got_xc, got_c = core_swaps(to_c[:2]), core_swaps(to_c[2:])
    d_mid = sum(nt(d, w) for d, w in zip([after(d_ups[0], *to_c), *d_ups[1:]], ups))
    keep_u, send_u = products(
        place,
        [after(first_low, d_mid)],
        [([(0, d_ups[0])], [got_c], "halve"), ([(0, d_ups[2])], [got_xc], "halve")],
        chunk,
    )
    got_yu = page_swap(send_u, 1)
    d_first, g_gain1, g_shift1 = norm_back(unit1, inv1, norm1_gain, after(d_second, send_u) + d_mid)
    g_out_bias = jnp.sum(d_first, axis=0)
    d_proj = d_first.astype(bf16)
    far_datt = nt(d_proj, far_out).astype(bf16)
    x_dmixed, xc_dmixed, far_sums, far_ds, far_dsv = attn_bwd(seq_len, far_kept, far_datt)

    lefts = [tok, d_proj]
    low, high = (0, inner), (inner, 2 * inner)
    to_c = products(place, lefts, [([(0, xc_dmixed), (1, far_att, high)], [], 2)], chunk)
    got_xc = core_swaps(to_c)
    near_datt = nt(after(d_proj, *to_c), near_out).astype(bf16)
    (far_gq,) = products(
        place, [after(tok, near_datt), d_proj], [([(0, x_dmixed), (1, far_att, low)], [got_xc], 1)], chunk
    )
    got_xq = x_swap(far_gq)
    own_dmixed, c_dmixed, near_sums, near_ds, near_dsv = attn_bwd(
        seq_len, near_kept, after(near_datt, far_gq)
    )
    dmixed = (own_dmixed, c_dmixed, x_dmixed, xc_dmixed)

    got_xd, got_yu = lax.optimization_barrier((got_xd, got_yu, near_sums))[:2]
    keep_d, send_d = add_split(place, [own_gd], [got_xd], 0, chunk)
    got_yd = page_swap(send_d, 1)
    keep_u, send_u = add_split(place, [keep_u], [got_yu], 1, chunk)
    got_zu = page_swap(send_u, 2)
    to_c = products(
        place,
        [after(tok, send_u, send_d), d_proj],
        [([(0, c_dmixed), (1, near_att, high)], [], 2)],
        chunk,
    )
    got_cq = core_swaps(to_c)
    text, near_far = (near_ds, far_ds), (near_dsv, far_dsv)
    acc = after(jnp.zeros((16, 160), f32), *to_c)
    acc = add_hist(acc, ids, some, text, 0, SPAN // 2)
    keep_q, send_q = products(
        place,
        [after(tok, acc), d_proj],
        [([(0, own_dmixed), (1, near_att, low)], [got_cq, [got_xq]], "halve")],
        chunk,
    )
    got_yq = page_swap(send_q, 1)
    keep_u, send_u = add_split(place, [keep_u], [after(got_zu, send_q)], 2, chunk)
    got_zu = page_swap(send_u, 4)
    keep_d, send_d = add_split(place, [keep_d], [after(got_yd, send_u)], 1, chunk)
    got_zd = page_swap(send_d, 2)
    acc = add_hist(after(acc, send_q, send_d), ids, some, text, SPAN // 2, SPAN // 2)
    acc = add_visual(acc, vis_ids, near_far)
    g_up_bias = [jnp.sum(d.astype(f32), axis=0) for d in d_ups]
    shared = (g_out_bias, g_gain1, g_shift1, g_down_bias, g_gain2, g_shift2)
    keep, send = pack_sums(acc, near_sums, far_sums, g_up_bias, shared)
    got = x_swap(send)
    keep_q, send_q = add_split(place, [keep_q], [after(got_yq, send)], 1, chunk)
    got_zq = page_swap(send_q, 2)
    keep_d, send_d = add_split(place, [keep_d], [after(got_zd, send_q)], 2, chunk)
    got_zd = page_swap(send_d, 4)
    got_zu = after(got_zu, send_d)
    both_u = finish(place, keep_u, got_zu, 2, chunk)
    got_xu = x_swap(both_u[chunk:].astype(bf16))
    sums = keep + after(got, send_d)
    sums = jnp.concatenate((sums[:EACH], sums[2 * EACH :])) + core_swap(sums[EACH:])
    got = page_swap(sums, 1)
    grad_tokens = tokens_grad(dmixed, (own_qkv, c_qkv, after(far_w, sums)), d_first)
    sums = sums + after(got, grad_tokens)
    got = page_swap(sums, 2)
    keep_q, send_q = add_split(place, [keep_q], [after(got_zq, sums)], 2, chunk)
    got_zq = page_swap(send_q, 4)
    sums = sums + after(got, send_q)
    got = page_swap(sums, 4)
    for bit in page_bits[3:]:
        sums = sums + got
        got = page_swap(sums, bit)
    got_zd, got_xu = lax.optimization_barrier((got_zd, got_xu, sums))[:2]
    g_w_down = finish(place, keep_d, got_zd, 2, chunk).T
    g_w_up = both_u[:chunk] + got_xu.astype(f32)
    got, got_zq, g_w_down, g_w_up = lax.optimization_barrier((got, got_zq, g_w_down, g_w_up))
    g_w_qkv, g_w_out = last_sums(place, keep_q, got_zq, 2, chunk)
    g_qv_bias, g_pos, g_box, g_up_bias, *shared = unpack_sums(sums, got, heads_here, units, width)
    g_box = g_box.transpose(1, 0, 2)
    return (
        layer_out.reshape(tokens.shape),
        grad_tokens.reshape(tokens.shape),
        g_w_qkv,
        g_qv_bias,
        g_w_out,
        shared[0],
        shared[1],
        shared[2],
        g_w_up,
        g_up_bias,
        g_w_down,
        shared[3],
        shared[4],
        shared[5],
        g_pos,
        g_box,
    )


def solution(mesh):
    placed = (
        P(("pages", "heads"), None, None),
        P(None, None, "heads"),
        P(None, "heads"),
        P("heads", None),
        P(),
        P(),
        P(),
        P(None, "heads"),
        P("heads"),
        P("heads", None),
        P(),
        P(),
        P(),
        P("heads", None),
        P(None, "heads", None),
        P("pages", None),
        P("pages", None, None),
        P(("pages", "heads"), None, None),
    )
    return jax.shard_map(
        on_device,
        mesh=mesh,
        in_specs=placed,
        out_specs=(
            P(("pages", "heads"), None, None),
            P(("pages", "heads"), None, None),
            P("pages", None, "heads"),
            P(None, "heads"),
            P("heads", "pages"),
            P(),
            P(),
            P(),
            P("pages", "heads"),
            P("heads"),
            P("heads", "pages"),
            P(),
            P(),
            P(),
            P("heads", None),
            P(None, "heads", None),
        ),
        check_vma=False,
    )
```

```python
import functools
import math

import jax
import jax.numpy as jnp
from jax import lax
from jax.experimental import pallas as pl
from jax.experimental.pallas import tpu as pltpu
from jax.sharding import PartitionSpec as P

f32 = jnp.float32
bf16 = jnp.bfloat16
i32 = jnp.int32
EPSILON = 1e-05
MASKED_SCORE = -1e30


HEAD_DIM = 64
TEXT = 512
NB1 = 32
MD1 = 128
NB2 = 64
MD2 = 256
ROWS = 576
VIS = ROWS - TEXT
QROWS = 640
LANES = 128
CHUNK = 64
UNIT = 2048.0
BLOCKS = ((0, 256), (0, 384), (128, 384), (256, 256))
OFFS = (0, 320, 768, 1216)
SPAN = 1536
Q_AT = SPAN
KV_AT = Q_AT + ROWS
PV_AT = KV_AT + ROWS
KEPT = PV_AT + ROWS // 2
SMALL = 24


def thresholds(buckets, max_reach):
    half_range = buckets // 2
    exact_range = half_range // 2
    levels = half_range - exact_range
    return [
        math.ceil(exact_range * (max_reach / exact_range) ** (k / levels) - 1e-09)
        for k in range(1, levels)
    ]


def bucket_of(diff, buckets, reach):
    n = jnp.abs(diff)
    out = jnp.minimum(n, buckets // 4) + jnp.where(diff > 0, buckets // 2, 0)
    for t in thresholds(buckets, reach):
        out = out + jnp.where(n >= t, 1, 0)
    return out


def parts_of(blk):
    s, n = BLOCKS[blk]
    return ((s, n, OFFS[blk]), (TEXT, VIS, OFFS[blk] + n))


def nt(a, b):
    return lax.dot_general(a, b, (((1,), (1,)), ((), ())), preferred_element_type=f32)


def nn(a, b):
    return lax.dot_general(a, b, (((1,), (0,)), ((), ())), preferred_element_type=f32)


def unpack(ids):
    return ids & 255, (ids >> 8) & 255, ids >> 16


def take(tab, idx):
    return jnp.take_along_axis(
        jnp.broadcast_to(tab, idx.shape), idx, axis=1, mode="promise_in_bounds"
    )


def ids_kernel(place_ref, len_ref, box_ref, ids_ref, vis_ref, some_ref, c_s, r_s, *, valid):
    page = place_ref[0]
    row = lax.broadcasted_iota(i32, (8, ROWS), 1)
    segment = jnp.zeros((8, ROWS), i32)
    end = 0
    for i in range(len_ref.shape[1]):
        end = end + len_ref[page, i]
        segment = segment + jnp.where(row >= end, 1, 0)
    c_s[...] = jnp.zeros_like(c_s)
    c_s[0:8, :] = segment.astype(f32)
    c_s[8:10, 0:valid] = box_ref[page].astype(f32)
    r_s[...] = c_s[...].T.astype(i32)

    def query(lo, hi):
        return tuple(c_s[i : i + 1, lo:hi].astype(i32) for i in (0, 8, 9))

    def tiles(row, out, rows, q_first, q):
        qseg, qx, qy = (jnp.broadcast_to(v, (CHUNK, LANES)) for v in q)
        lane = lax.broadcasted_iota(i32, (CHUNK, LANES), 1)
        if q_first == TEXT:
            q_pos, high = TEXT + (lane & (VIS - 1)), jnp.where(lane >= VIS, NB2, 0)
        else:
            q_pos, high = q_first + lane, 0

        def tile(c, _):
            at = pl.ds(pl.multiple_of(row + c * CHUNK, CHUNK), CHUNK)
            here = pl.ds(pl.multiple_of(out + c * CHUNK, CHUNK), CHUNK)
            seg, kx, ky = (jnp.broadcast_to(r_s[at, i : i + 1], (CHUNK, LANES)) for i in (0, 8, 9))
            k_pos = lax.broadcasted_iota(i32, (CHUNK, LANES), 0) + (row + c * CHUNK)
            x_id = bucket_of(kx - qx, NB2, MD2)
            y_id = bucket_of(ky - qy, NB2, MD2)
            p_id = bucket_of(k_pos - q_pos, NB1, MD1)
            ok = ((seg == qseg) | (k_pos >= TEXT) | (q_pos >= TEXT)) & (k_pos < valid)
            p_id = jnp.where(ok, p_id, NB1)
            y_id = y_id + (high if q_first == TEXT else NB2)
            ref, at = (vis_ref, at) if q_first == TEXT else (ids_ref, here)
            ref[at, :] = (x_id + high) + y_id * 256 + (p_id + high) * 65536
            if q_first != TEXT:
                some_ref[out // CHUNK + c] = jnp.max(jnp.where(ok, 1, 0))
            return 0

        lax.fori_loop(0, rows // CHUNK, tile, 0)

    for blk in range(4):
        q = query(blk * LANES, (blk + 1) * LANES)
        for s, n, o in parts_of(blk):
            tiles(s, o, n, blk * LANES, q)
    q = tuple(jnp.concatenate((v, v), axis=1) for v in query(TEXT, ROWS))
    tiles(0, 0, ROWS, TEXT, q)


def make_ids(place, lengths, boxes):
    return pl.pallas_call(
        functools.partial(ids_kernel, valid=boxes.shape[2]),
        in_specs=[
            pl.BlockSpec(memory_space=pltpu.SMEM),
            pl.BlockSpec(memory_space=pltpu.SMEM),
            pl.BlockSpec(memory_space=pltpu.VMEM),
        ],
        out_specs=[
            pl.BlockSpec(memory_space=pltpu.VMEM),
            pl.BlockSpec(memory_space=pltpu.VMEM),
            pl.BlockSpec(memory_space=pltpu.SMEM),
        ],
        out_shape=[
            jax.ShapeDtypeStruct((SPAN, LANES), i32),
            jax.ShapeDtypeStruct((ROWS, LANES), i32),
            jax.ShapeDtypeStruct((SPAN // CHUNK,), i32),
        ],
        scratch_shapes=[pltpu.VMEM((LANES, ROWS), f32), pltpu.VMEM((ROWS, LANES), i32)],
        name="ids",
        cost_estimate=pl.CostEstimate(flops=0, bytes_accessed=0, transcendentals=0),
        compiler_params=pltpu.CompilerParams(vmem_limit_bytes=12 << 20),
    )(place, lengths, boxes)


def place(dst_ref, pair, first, side, cols):
    at = slice(side * 192, side * 192 + 64)
    dst_ref[pair, first : first + ROWS, at] = cols


def stacked(both):
    return jnp.concatenate((both[:, :LANES], both[:, LANES:]), 0)


def block(ref, pair, first, blk):
    rows = LANES if blk < 4 else VIS
    return stacked(ref[pair, first + blk * LANES : first + blk * LANES + rows, :])


def load_rows(refs, odd, dst):
    if len(refs) == 1:
        dst[0 : refs[0].shape[0], :] = refs[0][...]
    else:
        half = dst.shape[0] // 2
        for first in range(2):

            @pl.when(odd == first)
            def _(first=first):
                dst[first * half : (first + 1) * half, :] = refs[0][0:half, :]
                dst[(1 - first) * half : (2 - first) * half, :] = refs[1][0:half, :]


def pad_rows(v):
    return jnp.concatenate((v, jnp.zeros((ROWS - v.shape[0], v.shape[1]), v.dtype)), 0)


def fold(both):
    n = both.shape[1] // 2
    t = both.T
    lane = lax.broadcasted_iota(i32, (n, LANES), 1)
    return jnp.where(lane < 64, t[:n], t[n:])


def fwd_kernel(place_ref, tok_ref, *refs, pieces, pairs):
    *refs, n_s, b_s = refs
    for i in range(3):
        far = lax.broadcasted_iota(i32, (LANES, LANES), 0) - lax.broadcasted_iota(i32, (LANES, LANES), 1)
        n_s[i] = bucket_of(far + (i - 1) * LANES, NB1, MD1)
    n = 2 * pieces
    weights = (refs[:pieces], refs[pieces:n])
    small, (ids_ref, vis_ref) = refs[n : n + 2], refs[n + 2 : n + 4]
    wo_refs, refs = (refs[n + 4 : n + 6], refs[n + 6 :]) if pieces == 1 else (None, refs[n + 4 :])
    out_ref, bias_ref, wo_ref, kept_ref = refs[:4]
    w_s = refs[4] if pieces > 1 else None
    vt_s, s_s, i_s, f_s, o_s, l_s = refs[-6:]
    first = small[0].shape[0] - 16
    inner = pairs * HEAD_DIM
    units = 4 * pairs // 6
    bias_ref[...] = jnp.zeros_like(bias_ref)
    for g in range(2):
        bias_ref[g : g + 1, :] = small[g][first + units : first + units + 1, :].astype(f32)
        for i in range(4 * pairs):
            at = slice(i % 6 * LANES, (i % 6 + 1) * LANES)
            row = first + i // 6
            high, rest = (small[g][r : r + 1, at].astype(f32) for r in (row, row + 8))
            l_s[g, i : i + 1, :] = high + rest
    small = [l_s.at[g] for g in range(2)]
    tok = pad_rows(tok_ref[...])
    for pair in range(pairs):
        kept_ref[pair, Q_AT:KV_AT, :] = jnp.zeros((ROWS, 256), bf16)
    for g in range(2):
        if pieces > 1:
            load_rows(weights[g], place_ref[1], w_s.at[g])
            w_ref = w_s.at[g]
            wo_ref[g * inner : (g + 1) * inner, :] = w_ref[3 * inner :, :]
        else:
            w_ref = weights[g][0]
            wo_ref[g * inner : (g + 1) * inner, :] = wo_refs[g][...]
        for part in range(3):
            mixed = nt(tok, w_ref[part * inner : (part + 1) * inner, :])
            for local in range(pairs):
                pair, side = divmod(g * pairs + local, 2)
                at = slice(side * 64, side * 64 + 64)
                cols = mixed[:, local * 64 : local * 64 + 64]
                if part == 0:
                    cols = cols + small[g][2 * pairs + local : 2 * pairs + local + 1, :64]
                    place(kept_ref, pair, Q_AT, side, (cols * (UNIT / 8)).astype(bf16))
                elif part == 1:
                    kept_ref[pair, KV_AT:PV_AT, at] = cols.astype(bf16)
                else:
                    cols = cols + small[g][3 * pairs + local : 3 * pairs + local + 1, :64]
                    low = slice(LANES + side * 64, LANES + side * 64 + 64)
                    kept_ref[pair, KV_AT:PV_AT, low] = cols.astype(bf16)
                    vt_s[pair, at, :] = cols.T.astype(bf16)
    for pair in range(pairs):
        (ga, la), (gb, lb) = divmod(2 * pair, pairs), divmod(2 * pair + 1, pairs)
        for row, start in ((0, 0), (1, pairs)):
            a = small[ga][start + la : start + la + 1, :] * UNIT
            b = small[gb][start + lb : start + lb + 1, :] * UNIT
            i_s[pair, row : row + 1, :] = (
                jnp.round(a).astype(i32) * 65536 + jnp.round(b).astype(i32)
            )
            f_s[pair, 2 * row : 2 * row + 1, :] = jnp.concatenate((a[:, :64], b[:, :64]), 1)
            f_s[pair, 2 * row + 1 : 2 * row + 2, :] = jnp.concatenate((a[:, 64:], b[:, 64:]), 1)

    def softmax(total, wide, p_at):
        m = jnp.full((8, wide), -3e38, f32)
        for c in range(0, total, 8):
            m = jnp.maximum(m, s_s[c : c + 8, :wide])
        m = jnp.max(m, axis=0, keepdims=True)
        l = jnp.zeros((8, wide), f32)
        for c in range(0, total, 8):
            e = jnp.exp2((s_s[c : c + 8, :wide] - m) * (math.log2(math.e) / UNIT))
            s_s[c : c + 8, :wide] = e
            l = l + e
        inv = 1.0 / jnp.sum(l, axis=0, keepdims=True)
        for c in range(0, total, 16):
            p_at(c, (s_s[c : c + 16, :wide] * inv).astype(bf16))

    def one_pair(pair, _):
        t_xy, t_p = (i_s[pair, i : i + 1, :] for i in range(2))
        v_x, v_y, v_p = (f_s[pair, i : i + 1, :] for i in range(3))
        for i in range(3):
            for c in range(0, LANES, 16):
                b_s[i, c : c + 16, :] = take(t_p, n_s[i, c : c + 16, :])
        for blk in range(4):
            q = block(kept_ref, pair, Q_AT, blk)
            first = OFFS[blk]
            for s, n, o in parts_of(blk):
                sc = nt(kept_ref[pair, KV_AT + s : KV_AT + s + n, :LANES], q)
                for c in range(0, n, 16):
                    r = slice(o + c, o + c + 16)
                    x, y, p = unpack(ids_ref[r, :])
                    if s < TEXT:
                        tile, row = divmod(s + c, LANES)
                        b_p = b_s[tile - blk + 1, row : row + 16, :]
                    else:
                        b_p = take(t_p, p)
                    b = take(t_xy, x) + take(t_xy, y) + b_p
                    low = (b << 16) >> 16
                    high = (b - low) >> 16
                    add = jnp.where(p == NB1, MASKED_SCORE, 0.0)
                    to = slice(o - first + c, o - first + c + 16)
                    s_s[to, :LANES] = sc[c : c + 16, :LANES] + (high.astype(f32) + add)
                    s_s[to, LANES:] = sc[c : c + 16, LANES:] + (low.astype(f32) + add)

            def put(c, v, first=first):
                kept_ref[pair, first + c : first + c + 16, :] = v

            softmax(BLOCKS[blk][1] + VIS, 256, put)
            ot = sum(
                nn(vt_s[pair, :, s : s + n], kept_ref[pair, o : o + n, :]) for s, n, o in parts_of(blk)
            )
            o_s[pair, blk * LANES : (blk + 1) * LANES, :] = fold(ot).astype(bf16)
        q = block(kept_ref, pair, Q_AT, 4)
        sc = nt(kept_ref[pair, KV_AT:PV_AT, :LANES], q)
        for c in range(0, ROWS, 16):
            x, y, p = unpack(vis_ref[c : c + 16, :])
            b = take(v_x, x) + take(v_y, y) + take(v_p, p)
            add = jnp.where((p & (NB2 - 1)) == NB1, MASKED_SCORE, 0.0)
            s_s[c : c + 16, :LANES] = sc[c : c + 16] + (b + add)

        def put_v(c, v):
            side, row = divmod(c, ROWS // 2)
            at = slice(side * LANES, (side + 1) * LANES)
            kept_ref[pair, PV_AT + row : PV_AT + row + 16, at] = v

        softmax(ROWS, LANES, put_v)
        o_s[pair, TEXT:ROWS, :] = fold(nn(vt_s[pair], stacked(kept_ref[pair, PV_AT:KEPT, :]))).astype(bf16)
        return 0

    lax.fori_loop(0, pairs, one_pair, 0, unroll=True)
    rows = out_ref.shape[0]
    for pair in range(pairs):
        out_ref[:, pair * LANES : (pair + 1) * LANES] = o_s[pair, 0:rows, :]


def attn_fwd(place, tok, weights, small, ids, pairs, w_out=()):
    pieces, (rows, width) = len(weights[0]), tok.shape
    vmem = pl.BlockSpec(memory_space=pltpu.VMEM)
    outs = [((rows, pairs * LANES), bf16), ((8, width), f32), ((pairs * LANES, width), bf16)]
    outs += [((pairs, KEPT, 256), bf16)]
    if pieces > 1:
        outs += [((2, 4 * pairs * HEAD_DIM, width), bf16)]
    args = (place, tok, *weights[0], *weights[1], *small, *ids, *w_out)
    return pl.pallas_call(
        functools.partial(fwd_kernel, pieces=pieces, pairs=pairs),
        in_specs=[pl.BlockSpec(memory_space=pltpu.SMEM)] + [vmem] * (len(args) - 1),
        out_specs=[vmem] * len(outs),
        out_shape=[jax.ShapeDtypeStruct(shape, dtype) for shape, dtype in outs],
        scratch_shapes=[
            pltpu.VMEM((pairs, LANES, ROWS), bf16),
            pltpu.VMEM((ROWS, 256), f32),
            pltpu.VMEM((pairs, 8, LANES), i32),
            pltpu.VMEM((pairs, 8, LANES), f32),
            pltpu.VMEM((pairs, ROWS, LANES), bf16),
            pltpu.VMEM((2, SMALL, LANES), f32),
            pltpu.VMEM((3, LANES, LANES), i32),
            pltpu.VMEM((3, LANES, LANES), i32),
        ],
        name="attn_fwd",
        cost_estimate=pl.CostEstimate(flops=0, bytes_accessed=0, transcendentals=0),
        compiler_params=pltpu.CompilerParams(vmem_limit_bytes=14 << 20),
    )(*args)


def bwd_kernel(kept_ref, do_ref, out0_ref, out1_ref, sum_ref, ds_ref, dsv_ref, do_s, kt_s, dq_s, dk_s, dv_s, *, pairs):
    rows = out0_ref.shape[0]
    sum_ref[...] = jnp.zeros_like(sum_ref)
    do_s[...] = jnp.zeros_like(do_s)
    for h in range(2 * pairs):
        pair, side = divmod(h, 2)
        place(do_s, pair, 0, side, pad_rows(do_ref[:, h * 64 : h * 64 + 64]))
    for pair in range(pairs):
        kt_s[pair] = kept_ref[pair, KV_AT:PV_AT, :LANES].astype(f32).T.astype(bf16)

    def grad_scores(dps, ps, put):
        d = jnp.zeros((8, dps[0].shape[1]), f32)
        for dp, p in zip(dps, ps):
            for c in range(0, dp.shape[0], 16):
                t = p(c).astype(f32) * dp[c : c + 16]
                d = d + (t[:8] + t[8:])
        d = jnp.sum(d, axis=0, keepdims=True)
        for i, (dp, p) in enumerate(zip(dps, ps)):
            for c in range(0, dp.shape[0], 16):
                put(i, c, (p(c).astype(f32) * (dp[c : c + 16] - d)).astype(bf16))

    def one_pair(pair, _):
        dv_s[...] = jnp.zeros_like(dv_s)
        dk_s[...] = jnp.zeros_like(dk_s)
        for blk in range(4):
            q = block(kept_ref, pair, Q_AT, blk)
            do = block(do_s, pair, 0, blk)
            parts = parts_of(blk)

            def put(i, c, v, parts=parts):
                ds_ref[pair, parts[i][2] + c : parts[i][2] + c + 16, :] = v

            grad_scores(
                [nt(kept_ref[pair, KV_AT + s : KV_AT + s + n, LANES:], do) for s, n, o in parts],
                [lambda c, o=o: kept_ref[pair, o + c : o + c + 16, :] for s, n, o in parts],
                put,
            )
            dq = 0.0
            for s, n, o in parts:
                ds = ds_ref[pair, o : o + n, :]
                dq = dq + nn(kt_s[pair, :, s : s + n], ds)
                dv_s[s : s + n, :] += nn(kept_ref[pair, o : o + n, :], do)
                dk_s[s : s + n, :] += nn(ds, q)
            dq_s[pair, 0, blk * LANES : (blk + 1) * LANES, :] = (fold(dq) * 0.125).astype(bf16)
        q = block(kept_ref, pair, Q_AT, 4)
        do = block(do_s, pair, 0, 4)
        pv = stacked(kept_ref[pair, PV_AT:KEPT, :])

        def put_v(i, c, v):
            dsv_ref[pair, c : c + 16, :] = v

        grad_scores([nt(kept_ref[pair, KV_AT:PV_AT, LANES:], do)], [lambda c: pv[c : c + 16]], put_v)
        ds = dsv_ref[pair]
        dq_s[pair, 0, TEXT:ROWS, :] = (fold(nn(kt_s[pair], ds)) * 0.125).astype(bf16)
        dq_s[pair, 1] = ((dk_s[...] + nn(ds, q)) * (1.0 / UNIT)).astype(bf16)
        dq_s[pair, 2] = (dv_s[...] + nn(pv, do)).astype(bf16)
        return 0

    lax.fori_loop(0, pairs, one_pair, 0)
    for h in range(2 * pairs):
        pair, side = divmod(h, 2)
        g, local = divmod(h, pairs)
        for part in range(3):
            col = part * pairs * HEAD_DIM + local * HEAD_DIM
            here = dq_s[pair, part, 0:rows, side * 64 : side * 64 + 64]
            (out0_ref, out1_ref)[g][:, col : col + 64] = here
            if part != 1:
                total = jnp.sum(here.astype(f32), axis=0, keepdims=True)
                sum_ref[g : g + 1, col : col + 64] = total


def attn_bwd(rows, kept, d_att):
    pairs = kept.shape[0]
    cols = 3 * pairs * HEAD_DIM
    vmem = pl.BlockSpec(memory_space=pltpu.VMEM)
    outs = [((rows, cols), bf16)] * 2 + [((8, cols), f32)]
    outs += [((pairs, SPAN, 256), bf16), ((pairs, ROWS, LANES), bf16)]
    return pl.pallas_call(
        functools.partial(bwd_kernel, pairs=pairs),
        in_specs=[vmem] * 2,
        out_specs=[vmem] * 5,
        out_shape=[jax.ShapeDtypeStruct(shape, dtype) for shape, dtype in outs],
        scratch_shapes=[
            pltpu.VMEM((pairs, ROWS, 256), bf16),
            pltpu.VMEM((pairs, LANES, ROWS), bf16),
            pltpu.VMEM((pairs, 3, ROWS, LANES), bf16),
            pltpu.VMEM((ROWS, LANES), f32),
            pltpu.VMEM((ROWS, LANES), f32),
        ],
        name="attn_bwd",
        cost_estimate=pl.CostEstimate(flops=0, bytes_accessed=0, transcendentals=0),
        compiler_params=pltpu.CompilerParams(vmem_limit_bytes=14 << 20),
    )(kept, d_att)


HSTEP = 64
HBLOCK = 192


def hist_kernel(some_ref, acc_ref, ids_ref, *refs, sets, pairs, first_id):
    ds_refs, hist_ref, l_s = refs[:sets], refs[-2], refs[-1]
    heads = 2 * sets * pairs

    @pl.when(pl.program_id(0) == 0)
    def _():
        hist_ref[...] = acc_ref[...]

    for h in range(heads, 16):
        l_s[pl.ds(h, HSTEP, stride=16), :] = jnp.zeros((HSTEP, LANES), f32)
    steps = HBLOCK // HSTEP

    @pl.loop(0, steps)
    def _(r):
        @pl.when(some_ref[(first_id + pl.program_id(0)) * steps + r] > 0)
        def _():
            first = pl.multiple_of(r * HSTEP, HSTEP)
            for pair in range(sets * pairs):
                ref = ds_refs[pair // pairs]
                for side in range(2):
                    at = slice(side * LANES, (side + 1) * LANES)
                    v = ref[pair % pairs, pl.ds(first, HSTEP), at].astype(f32)
                    l_s[pl.ds(2 * pair + side, HSTEP, stride=16), :] = v
            ids = lambda u: ids_ref[pl.ds(first + u, 1), :]
            hist_ref[...] += hot_sums(l_s, ids, HSTEP, NB2)


def hot_sums(l_s, ids, rows, y_from):
    io = lax.broadcasted_iota(i32, (NB2, LANES), 0)
    lhs, rhs = [], []
    for u in range(rows):
        x, y, p = unpack(ids(u))
        if y_from:
            y = y - y_from
        else:
            x, y, p = (v & (NB2 - 1) for v in (x, y, p))
        hot = [jnp.where(io == x, 1.0, 0.0), jnp.where(io == y, 1.0, 0.0)]
        hot.append(jnp.where(io[:NB1] == p, 1.0, 0.0))
        rhs.append(jnp.concatenate(hot, 0).astype(bf16))
        lhs.append(l_s[u * 16 : u * 16 + 16, :].astype(bf16))
    return nt(jnp.concatenate(lhs, 1), jnp.concatenate(rhs, 1))


VSTEP = 72


def visual_kernel(acc_ref, ids_ref, *refs, sets, pairs):
    ds_refs, hist_ref, l_s, i_s = refs[:sets], refs[-3], refs[-2], refs[-1]
    heads = 2 * sets * pairs
    far = ROWS // 2
    lane = lax.broadcasted_iota(i32, (VSTEP, LANES), 1)
    hist_ref[...] = acc_ref[...]
    for h in range(heads, 16):
        l_s[pl.ds(h, VSTEP, stride=16), :] = jnp.zeros((VSTEP, LANES), f32)

    @pl.loop(0, far // VSTEP)
    def _(r):
        here = pl.ds(pl.multiple_of(r * VSTEP, 8), VSTEP)
        there = pl.ds(pl.multiple_of(far + r * VSTEP, 8), VSTEP)
        i_s[...] = jnp.where(lane < VIS, ids_ref[here, :], ids_ref[there, :])
        for pair in range(sets * pairs):
            ref = ds_refs[pair // pairs]
            a, b = (ref[pair % pairs, at, :].astype(f32) for at in (here, there))
            one = jnp.where(lane < VIS, a, pltpu.roll(b, VIS, axis=1))
            two = jnp.where(lane < VIS, pltpu.roll(a, VIS, axis=1), b)
            l_s[pl.ds(2 * pair, VSTEP, stride=16), :] = one
            l_s[pl.ds(2 * pair + 1, VSTEP, stride=16), :] = two
        hist_ref[...] += hot_sums(l_s, lambda u: i_s[u : u + 1, :], VSTEP, 0)


def add_visual(acc, ids, ds):
    vmem = pl.BlockSpec(memory_space=pltpu.VMEM)
    return pl.pallas_call(
        functools.partial(visual_kernel, sets=len(ds), pairs=ds[0].shape[0]),
        grid=(1,),
        in_specs=[
            pl.BlockSpec((16, 160), lambda i: (0, 0)),
            pl.BlockSpec((ROWS, LANES), lambda i: (0, 0)),
        ]
        + [pl.BlockSpec(t.shape, lambda i: (0, 0, 0)) for t in ds],
        out_specs=pl.BlockSpec((16, 160), lambda i: (0, 0)),
        out_shape=jax.ShapeDtypeStruct((16, 160), f32),
        scratch_shapes=[pltpu.VMEM((VSTEP * 16, LANES), f32), pltpu.VMEM((VSTEP, LANES), i32)],
        name="hist",
        cost_estimate=pl.CostEstimate(flops=0, bytes_accessed=0, transcendentals=0),
        compiler_params=pltpu.CompilerParams(vmem_limit_bytes=12 << 20),
    )(acc, ids, *ds)


def add_hist(acc, ids, some, ds, first_row, rows):
    first = first_row // HBLOCK
    specs = [
        pl.BlockSpec(memory_space=pltpu.SMEM),
        pl.BlockSpec((16, 160), lambda i: (0, 0)),
        pl.BlockSpec((HBLOCK, LANES), lambda i: (first + i, 0)),
    ]
    for t in ds:
        specs.append(pl.BlockSpec((t.shape[0], HBLOCK, t.shape[2]), lambda i: (0, first + i, 0)))
    return pl.pallas_call(
        functools.partial(hist_kernel, sets=len(ds), pairs=ds[0].shape[0], first_id=first),
        grid=(rows // HBLOCK,),
        in_specs=specs,
        out_specs=pl.BlockSpec((16, 160), lambda i: (0, 0)),
        out_shape=jax.ShapeDtypeStruct((16, 160), f32),
        scratch_shapes=[pltpu.VMEM((HSTEP * 16, LANES), f32)],
        name="hist",
        cost_estimate=pl.CostEstimate(flops=0, bytes_accessed=0, transcendentals=0),
        compiler_params=pltpu.CompilerParams(vmem_limit_bytes=12 << 20),
    )(some, acc, ids, *ds)


def call(kernel, name, args, outs, scratch=(), smem=0):
    vmem = pl.BlockSpec(memory_space=pltpu.VMEM)
    return pl.pallas_call(
        kernel,
        in_specs=[pl.BlockSpec(memory_space=pltpu.SMEM)] * smem + [vmem] * (len(args) - smem),
        out_shape=[jax.ShapeDtypeStruct(shape, dtype) for shape, dtype in outs],
        scratch_shapes=[pltpu.VMEM(shape, dtype) for shape, dtype in scratch],
        name=name,
        cost_estimate=pl.CostEstimate(flops=0, bytes_accessed=0, transcendentals=0),
        compiler_params=pltpu.CompilerParams(vmem_limit_bytes=12 << 20),
    )(*args)


def start_kernel(place_ref, qkv_ref, wo_ref, up_ref, box_ref, pos_ref, qv_ref, ub_ref, a_ref, b_ref, small_ref, s_s, o_s, sems):
    half = a_ref.shape[0]
    odd = place_ref[1]

    def copy(src, dst, i):
        return pltpu.make_async_copy(src, dst, sems.at[i])

    tail = qkv_ref.shape[0] - half
    firsts = [copy(qkv_ref.at[0:half, :], a_ref.at[0:half, :], 0)]
    seconds = [
        copy(qkv_ref.at[half:, :], a_ref.at[0:tail, :], 0),
        copy(wo_ref, a_ref.at[tail:half, :], 1),
    ]

    @pl.when(odd == 0)
    def _():
        for c in firsts:
            c.start()

    @pl.when(odd == 1)
    def _():
        for c in seconds:
            c.start()

    at = pl.ds(pl.multiple_of(odd * half, half), half)
    others = [copy(up_ref.at[at, :], b_ref.at[0:half, :], 2)]
    for c in others:
        c.start()
    heads = pos_ref.shape[0]
    s_s[...] = jnp.zeros_like(s_s)
    for h in range(heads):
        s_s[h : h + 1, :NB2] = box_ref[h, 0:1, :]
        s_s[h : h + 1, NB2:] = box_ref[h, 1:2, :]
        s_s[heads + h : heads + h + 1, :NB1] = pos_ref[h : h + 1, :]
        for i in range(2):
            row = (2 + i) * heads + h
            s_s[row : row + 1, :64] = qv_ref[i : i + 1, h * 64 : h * 64 + 64]
    units = ub_ref.shape[0] // LANES
    s_s[4 * heads : 4 * heads + units, :] = ub_ref[...].astype(f32).reshape(units, LANES)
    o_s[...] = jnp.zeros_like(o_s)
    for i in range(SMALL):
        at = slice(i % 6 * LANES, (i % 6 + 1) * LANES)
        value = s_s[i : i + 1, :]
        high = value.astype(bf16).astype(f32)
        o_s[i // 6 : i // 6 + 1, at] = high
        o_s[8 + i // 6 : 9 + i // 6, at] = value - high
    small_ref[...] = o_s[...].astype(bf16)
    last = copy(small_ref, b_ref.at[half : half + 16, :], 4)
    last.start()

    @pl.when(odd == 0)
    def _():
        for c in firsts:
            c.wait()

    @pl.when(odd == 1)
    def _():
        for c in seconds:
            c.wait()

    for c in others + [last]:
        c.wait()


def start_parts(place, qkv, w_out, w_up, box, pos, qv, up):
    width = qkv.shape[1]
    vmem, hbm = (pl.BlockSpec(memory_space=m) for m in (pltpu.VMEM, pltpu.HBM))
    shapes = [(width // 2, width), (width // 2 + 16, width), (16, width)]
    return pl.pallas_call(
        start_kernel,
        in_specs=[pl.BlockSpec(memory_space=pltpu.SMEM)] + [hbm] * 3 + [vmem] * 4,
        out_specs=[vmem] * 3,
        out_shape=[jax.ShapeDtypeStruct(shape, bf16) for shape in shapes],
        scratch_shapes=[
            pltpu.VMEM((SMALL, LANES), f32),
            pltpu.VMEM((16, width), f32),
            pltpu.SemaphoreType.DMA((5,)),
        ],
        name="start_parts",
        cost_estimate=pl.CostEstimate(flops=0, bytes_accessed=0, transcendentals=0),
        compiler_params=pltpu.CompilerParams(vmem_limit_bytes=58 << 20),
    )(place, qkv, w_out, w_up, box.transpose(1, 0, 2), pos, qv, up)


def join_kernel(place_ref, mine_ref, theirs_ref, *refs):
    outs, sems = refs[:-1], refs[-1]
    half = outs[0].shape[0] // 2
    odd = place_ref[1]
    copies = []
    for i, out in enumerate(outs):
        for j, (ref, first) in enumerate(((mine_ref, odd * half), (theirs_ref, (1 - odd) * half))):
            to = out.at[pl.ds(pl.multiple_of(first, half), half), :]
            at = slice(i * half, (i + 1) * half)
            copies.append(pltpu.make_async_copy(ref.at[at, :], to, sems.at[i, j]))
    for c in copies:
        c.start()
    for c in copies:
        c.wait()


def join_rows(place, mine, theirs, number, rows):
    cols = mine.shape[1]
    vmem = pl.BlockSpec(memory_space=pltpu.VMEM)
    return pl.pallas_call(
        join_kernel,
        in_specs=[pl.BlockSpec(memory_space=pltpu.SMEM), vmem, vmem],
        out_specs=[vmem] * number,
        out_shape=[jax.ShapeDtypeStruct((rows, cols), bf16)] * number,
        scratch_shapes=[pltpu.SemaphoreType.DMA((number, 2))],
        name="join_rows",
        cost_estimate=pl.CostEstimate(flops=0, bytes_accessed=0, transcendentals=0),
        compiler_params=pltpu.CompilerParams(vmem_limit_bytes=8 << 20),
    )(place, mine, theirs)


def tn(a, b):
    return lax.dot_general(a, b, (((0,), (0,)), ((), ())), preferred_element_type=f32)


def parity_split(cur_ref, keep_ref, send_ref, first, chunk, bit):
    for mine in range(2):

        @pl.when(bit == mine)
        def _(mine=mine):
            for i in range(cur_ref.shape[0] // chunk // 2):
                to = slice(first + i * chunk, first + (i + 1) * chunk)
                at = (2 * i + mine) * chunk
                keep_ref[to, :] = cur_ref[at : at + chunk, :]
                at = (2 * i + 1 - mine) * chunk
                send_ref[to, :] = cur_ref[at : at + chunk, :]


def products_kernel(place_ref, *refs, lefts, plan, chunk):
    left, refs = refs[:lefts], list(refs[lefts:])
    rights = [[refs.pop(0) for _ in terms] for terms, _, _ in plan]
    gots = [[[refs.pop(0) for _ in range(n)] for n in counts] for _, counts, _ in plan]
    cur_s = refs.pop()
    split = 0
    for (terms, _, mode), right, got in zip(plan, rights, gots):
        outs = [cur_s] if mode == "halve" else [refs.pop(0) for _ in range(mode)]
        col = 0
        for (i, lanes), r in zip(terms, right):
            lanes = lanes or (0, r.shape[1])
            at = slice(col, col + lanes[1] - lanes[0])
            total = tn(left[i][...], r[:, lanes[0] : lanes[1]])
            for pieces in got:
                wide = [g[:, at].astype(f32) for g in pieces]
                total = total + (wide[0] if len(wide) == 1 else jnp.concatenate(wide, 0))
            rows = total.shape[0] // len(outs)
            for k, out in enumerate(outs):
                out[:, at] = total[k * rows : (k + 1) * rows].astype(bf16)
            col += lanes[1] - lanes[0]
        if mode == "halve":
            if split == 0:
                keep, send = refs.pop(0), refs.pop(0)
            parity_split(cur_s, keep, send, split, chunk, place_ref[1])
            split += cur_s.shape[0] // 2


def plain_split(place, cur, bit, chunk):
    view = cur.reshape(-1, 2, chunk, cur.shape[1])
    pick = lambda i: lax.dynamic_index_in_dim(view, i, axis=1, keepdims=False)
    mine = place[1 + bit]
    return tuple(pick(i).reshape(-1, cur.shape[1]) for i in (mine, 1 - mine))


def products(place, lefts, specs, chunk):
    width = lefts[0].shape[1]
    halved = sum(mode == "halve" for _, _, mode in specs)
    if chunk % 16 and halved:
        whole = products(place, lefts, [(t, g, 1) for t, g, _ in specs], chunk)
        parts = [plain_split(place, cur, 0, chunk) for cur in whole]
        return [jnp.concatenate(side, axis=0) for side in zip(*parts)]
    plan = [
        ([(t[0], t[2] if len(t) > 2 else None) for t in terms], [len(p) for p in gots], mode)
        for terms, gots, mode in specs
    ]
    args = [place, *lefts]
    args += [t[1] for terms, _, _ in specs for t in terms]
    args += [g for _, gots, _ in specs for pieces in gots for g in pieces]
    cols = sum(t[2][1] - t[2][0] if len(t) > 2 else t[1].shape[1] for t in specs[0][0])
    outs = []
    for _, _, mode in specs:
        if mode != "halve":
            outs += [((width // mode, cols), bf16)] * mode
    if halved:
        outs += [((halved * width // 2, cols), bf16)] * 2
    kernel = functools.partial(products_kernel, lefts=len(lefts), plan=plan, chunk=chunk)
    return call(kernel, "products", args, outs, [((width, cols), bf16)], smem=1)


def add_split_kernel(place_ref, *refs, number, bit, chunk):
    keep_ref, send_ref, cur_s = refs[2 * number :]
    first = 0
    for a, b in zip(refs[:number], refs[number : 2 * number]):
        rows = a.shape[0]
        cur_s[first : first + rows] = (a[...].astype(f32) + b[...].astype(f32)).astype(bf16)
        first += rows
    parity_split(cur_s, keep_ref, send_ref, 0, chunk, place_ref[1 + bit])


def add_split(place, keeps, gots, bit, chunk):
    rows, cols = sum(v.shape[0] for v in keeps), keeps[0].shape[1]
    if chunk % 16:
        parts = [(a.astype(f32) + b.astype(f32)).astype(bf16) for a, b in zip(keeps, gots)]
        return plain_split(place, jnp.concatenate(parts, axis=0), bit, chunk)
    half = ((rows // 2, cols), bf16)
    kernel = functools.partial(add_split_kernel, number=len(keeps), bit=bit, chunk=chunk)
    args = (place, *keeps, *gots)
    return call(kernel, "add_split", args, [half, half], [((rows, cols), bf16)], smem=1)


def tokens_kernel(d0, d1, d2, d3, w0, w1, w_ref, first_ref, out_ref):
    cols = d0.shape[1]
    total = first_ref[...] + nn(d0[...], w0[...]) + nn(d1[...], w1[...])
    total = total + nn(d2[...], w_ref[0, 0:cols, :]) + nn(d3[...], w_ref[1, 0:cols, :])
    out_ref[...] = total.astype(bf16)


def tokens_grad(dmixed, weights, d_first):
    args = (*dmixed, *weights, d_first)
    return call(tokens_kernel, "tokens_grad", args, [(d_first.shape, bf16)])[0]


SHARED = 40
EACH = 16


def pack_kernel(hist_ref, near_ref, far_ref, u0, u1, u2, u3, v0, v1, v2, v3, v4, v5, keep_ref, send_ref, *, heads):
    keep_ref[...] = jnp.zeros_like(keep_ref)
    send_ref[...] = jnp.zeros_like(send_ref)
    for g, up in enumerate((u0, u1, u2, u3)):
        ref, first = (keep_ref, send_ref)[g // 2], (g % 2) * EACH
        for h in range(heads):
            for i, part in ((0, 0), (1, 2)):
                col = (part * heads + h) * HEAD_DIM
                row = (near_ref, far_ref)[g // 2][g % 2 : g % 2 + 1, col : col + 64]
                ref[first + h : first + h + 1, i * 64 : i * 64 + 64] = row
            row = hist_ref[g * heads + h : g * heads + h + 1, :]
            ref[first + heads + h : first + heads + h + 1, :] = row[:, :LANES]
            ref[first + 2 * heads + h : first + 2 * heads + h + 1, :NB1] = row[:, LANES:]
        for i in range(6):
            at = slice(first + 3 * heads + i, first + 3 * heads + i + 1)
            ref[at, :] = up[:, i * LANES : (i + 1) * LANES]
    for j, v in enumerate((v0, v1, v2, v3, v4, v5)):
        for i in range(6):
            at = slice(2 * EACH + 6 * j + i, 2 * EACH + 6 * j + i + 1)
            row = v[:, i * LANES : (i + 1) * LANES]
            keep_ref[at, :] = row
            send_ref[at, :] = row


def pack_sums(hist, near, far, ups, shared):
    args = (hist, near, far, *(v.reshape(1, -1) for v in ups), *(v.reshape(1, -1) for v in shared))
    outs = [((2 * EACH + SHARED, LANES), f32)] * 2
    heads = near.shape[1] // (3 * HEAD_DIM)
    return call(functools.partial(pack_kernel, heads=heads), "pack_sums", args, outs)


def unpack_kernel(keep_ref, got_ref, qv_ref, pos_ref, box_ref, up_ref, *shared, heads):
    total = keep_ref[...] + got_ref[...]
    for h in range(heads):
        for i in range(2):
            qv_ref[i : i + 1, h * 64 : h * 64 + 64] = total[h : h + 1, i * 64 : i * 64 + 64]
            box_ref[h, i : i + 1, :] = total[heads + h : heads + h + 1, i * NB2 : (i + 1) * NB2]
        pos_ref[h : h + 1, :] = total[2 * heads + h : 2 * heads + h + 1, :NB1]
    units = up_ref.shape[0] // LANES
    up_ref[...] = total[3 * heads : 3 * heads + units].reshape(up_ref.shape)
    for j, ref in enumerate(shared):
        rows = ref.shape[0] // LANES
        ref[...] = total[EACH + j * rows : EACH + (j + 1) * rows].reshape(ref.shape)


def unpack_sums(keep, got, heads, units, width):
    outs = [((2, heads * HEAD_DIM), f32), ((heads, NB1), f32), ((heads, 2, NB2), f32), ((units,), f32)]
    outs += [((width,), f32)] * 6
    return call(functools.partial(unpack_kernel, heads=heads), "unpack_sums", (keep, got), outs)


def last_kernel(keep_ref, got_ref, qkv_ref, out_ref):
    inner = qkv_ref.shape[2]
    for part in range(3):
        at = slice(part * inner, (part + 1) * inner)
        qkv_ref[part] = keep_ref[:, at].astype(f32) + got_ref[:, at].astype(f32)
    at = slice(3 * inner, 4 * inner)
    out_ref[...] = (keep_ref[:, at].astype(f32) + got_ref[:, at].astype(f32)).T


def last_sums(place, keep, got, bit, chunk):
    inner = keep.shape[1] // 4
    if chunk % 16 == 0 and lax.axis_size("pages") == 2 << bit:
        outs = [((3, chunk, inner), f32), ((inner, chunk), f32)]
        qkv, out = call(last_kernel, "last_sums", (keep, got), outs)
        return qkv.transpose(1, 0, 2), out
    total = finish(place, keep, got, bit, chunk)
    return total[:, : 3 * inner].reshape(-1, 3, inner), total[:, 3 * inner :].T


def core_swap(v):
    return lax.ppermute(v, "heads", [(i, i ^ 1) for i in range(4)])


def x_swap(v):
    return lax.ppermute(v, "heads", [(i, i ^ 2) for i in range(4)])


def page_swap(v, bit):
    return lax.ppermute(v, "pages", [(i, i ^ bit) for i in range(lax.axis_size("pages"))])


def after(value, *others):
    return lax.optimization_barrier((value, *others))[0]


def finish(place, keep, got, bit, chunk):
    last = lax.axis_size("pages").bit_length() - 1
    while bit + 1 < last:
        bit += 1
        keep, send = add_split(place, [keep], [got], bit, chunk)
        got = page_swap(send, 1 << bit)
    return keep.astype(f32) + got.astype(f32)


def add_all(v, bits):
    for bit in bits:
        v = v + page_swap(v, bit)
    return v


def unit_norm(values):
    centered = values - jnp.mean(values, axis=-1, keepdims=True)
    inv_std = lax.rsqrt(jnp.mean(centered * centered, axis=-1, keepdims=True) + EPSILON)
    return centered * inv_std, inv_std


def norm_grad(unit, inv_std, e):
    return inv_std * (
        e - jnp.mean(e, axis=-1, keepdims=True) - unit * jnp.mean(e * unit, axis=-1, keepdims=True)
    )


def on_device(
    tokens,
    w_qkv,
    qv_bias,
    w_out,
    out_bias,
    norm1_gain,
    norm1_shift,
    w_up,
    up_bias,
    w_down,
    down_bias,
    norm2_gain,
    norm2_shift,
    pos_table,
    box_table,
    receipt_lengths,
    page_boxes,
    out_cotangent,
):
    seq_len = tokens.shape[1]
    width = tokens.shape[2]
    heads_here = pos_table.shape[0]
    inner = heads_here * HEAD_DIM
    units = w_up.shape[1]
    own_page = lax.axis_index("heads")
    page_bits = [1 << b for b in range(lax.axis_size("pages").bit_length() - 1)]
    chunk = width // lax.axis_size("pages")
    me = lax.axis_index("pages")
    place = jnp.stack([own_page] + [(me >> b) & 1 for b in range(len(page_bits))]).astype(i32)
    tok = tokens.reshape(seq_len, width)

    own_qkv = w_qkv.reshape(width, 3 * inner).T
    c_qkv, c_out = core_swap(own_qkv), core_swap(w_out)
    half_a, half_b, small = start_parts(
        place, own_qkv, w_out, w_up, box_table, pos_table, qv_bias, up_bias
    )
    c_small = core_swap(small)
    mine_a = x_swap(half_a)
    mine_b = x_swap(half_b)
    x_down = x_swap(w_down)
    ids, vis_ids, some = make_ids(place, receipt_lengths, page_boxes)
    mine_a = after(mine_a, ids)

    near_w = ((own_qkv,), (after(c_qkv, mine_a),))
    near_att, near_bias, near_out, near_kept = attn_fwd(
        place, tok, near_w, (small, c_small), (ids, vis_ids), heads_here, (w_out, c_out)
    )
    half = width // 2
    theirs_a = page_swap(mine_a, 1)
    xc_mine_a, xc_theirs_a = core_swap(mine_a), core_swap(after(theirs_a, near_att))
    theirs_b = page_swap(after(mine_b, near_att), 1)
    xc_mine_b = core_swap(after(mine_b, near_att))
    far_w = ((mine_a, theirs_a), (after(xc_mine_a, xc_mine_b), xc_theirs_a))
    far_att, far_bias, far_out, far_kept, far_w = attn_fwd(
        place, tok, far_w, (mine_b, xc_mine_b), (ids, vis_ids), heads_here
    )
    far_proj = nn(far_att, far_out)
    c_up, c_down = core_swap(after(w_up, far_proj)), core_swap(after(w_down, far_proj))
    mine_b, theirs_b = lax.optimization_barrier((mine_b, theirs_b, far_proj))[:2]
    xc_theirs_b = core_swap(theirs_b)
    first_in = nn(near_att, near_out) + far_proj + out_bias + tok.astype(f32)
    unit1, inv1 = unit_norm(first_in)
    first_out = unit1 * norm1_gain + norm1_shift
    first_low = first_out.astype(bf16)

    def units_of(weights, little):
        up = nn(first_low, weights) + little
        cdf = 0.5 * (1.0 + lax.erf(up * math.sqrt(0.5)))
        slope = cdf + up * jnp.exp(-0.5 * up * up) * (1.0 / math.sqrt(2.0 * math.pi))
        return (up * cdf).astype(bf16), lax.optimization_barrier(slope.astype(bf16))

    littles = (near_bias[0], near_bias[1], far_bias[0], far_bias[1])
    own_units = units_of(w_up, littles[0])
    theirs_b = after(theirs_b, own_units[0])
    (x_up,) = join_rows(place, mine_b, theirs_b, 1, width)
    c_units = units_of(after(c_up, theirs_b), littles[1])
    (xc_up,) = join_rows(place, xc_mine_b, after(xc_theirs_b, x_up), 1, width)
    far_units = [units_of(w, t) for w, t in zip((x_up, xc_up), littles[2:])]
    hiddens, slopes = zip(own_units, c_units, *far_units)
    x_down = after(x_down, *hiddens)
    xc_down = core_swap(x_down)
    ups, downs = (w_up, c_up, x_up, xc_up), (w_down, c_down, x_down, xc_down)
    second_in = sum(nn(h, w) for h, w in zip(hiddens, downs)) + down_bias + first_out
    unit2, inv2 = unit_norm(second_in)
    layer_out = (unit2 * norm2_gain + norm2_shift).astype(bf16)

    def norm_back(unit, inv_std, gain, dy):
        return norm_grad(unit, inv_std, dy * gain), jnp.sum(dy * unit, axis=0), jnp.sum(dy, axis=0)

    ct = out_cotangent.reshape(seq_len, width).astype(f32)
    d_second, g_gain2, g_shift2 = norm_back(unit2, inv2, norm2_gain, ct)
    g_down_bias = jnp.sum(d_second, axis=0)
    d_ffn = d_second.astype(bf16)

    def core_swaps(pieces):
        return [core_swap(v) for v in pieces]

    to_c = products(
        place, [d_ffn], [([(0, hiddens[3])], [], 2), ([(0, hiddens[1])], [], 2)], chunk
    )
    got_xc, got_c = core_swaps(to_c[:2]), core_swaps(to_c[2:])
    d_ups = [(nt(d_ffn, w) * s.astype(f32)).astype(bf16) for w, s in zip(downs, slopes)]
    far_gd, own_gd = products(
        place,
        [after(d_ffn, *d_ups)],
        [([(0, hiddens[2])], [got_xc], 1), ([(0, hiddens[0])], [got_c], 1)],
        chunk,
    )
    got_xd = x_swap(far_gd)

    to_c = products(
        place,
        [after(first_low, far_gd)],
        [([(0, d_ups[3])], [], 2), ([(0, d_ups[1])], [], 2)],
        chunk,
    )
    got_xc, got_c = core_swaps(to_c[:2]), core_swaps(to_c[2:])
    d_mid = sum(nt(d, w) for d, w in zip([after(d_ups[0], *to_c), *d_ups[1:]], ups))
    keep_u, send_u = products(
        place,
        [after(first_low, d_mid)],
        [([(0, d_ups[0])], [got_c], "halve"), ([(0, d_ups[2])], [got_xc], "halve")],
        chunk,
    )
    got_yu = page_swap(send_u, 1)
    d_first, g_gain1, g_shift1 = norm_back(unit1, inv1, norm1_gain, after(d_second, send_u) + d_mid)
    g_out_bias = jnp.sum(d_first, axis=0)
    d_proj = d_first.astype(bf16)
    far_datt = nt(d_proj, far_out).astype(bf16)
    x_dmixed, xc_dmixed, far_sums, far_ds, far_dsv = attn_bwd(seq_len, far_kept, far_datt)

    lefts = [tok, d_proj]
    low, high = (0, inner), (inner, 2 * inner)
    to_c = products(place, lefts, [([(0, xc_dmixed), (1, far_att, high)], [], 2)], chunk)
    got_xc = core_swaps(to_c)
    near_datt = nt(after(d_proj, *to_c), near_out).astype(bf16)
    (far_gq,) = products(
        place, [after(tok, near_datt), d_proj], [([(0, x_dmixed), (1, far_att, low)], [got_xc], 1)], chunk
    )
    got_xq = x_swap(far_gq)
    own_dmixed, c_dmixed, near_sums, near_ds, near_dsv = attn_bwd(
        seq_len, near_kept, after(near_datt, far_gq)
    )
    dmixed = (own_dmixed, c_dmixed, x_dmixed, xc_dmixed)

    got_xd, got_yu = lax.optimization_barrier((got_xd, got_yu, near_sums))[:2]
    keep_d, send_d = add_split(place, [own_gd], [got_xd], 0, chunk)
    got_yd = page_swap(send_d, 1)
    keep_u, send_u = add_split(place, [keep_u], [got_yu], 1, chunk)
    got_zu = page_swap(send_u, 2)
    to_c = products(
        place,
        [after(tok, send_u, send_d), d_proj],
        [([(0, c_dmixed), (1, near_att, high)], [], 2)],
        chunk,
    )
    got_cq = core_swaps(to_c)
    text, near_far = (near_ds, far_ds), (near_dsv, far_dsv)
    acc = after(jnp.zeros((16, 160), f32), *to_c)
    acc = add_hist(acc, ids, some, text, 0, SPAN // 2)
    keep_q, send_q = products(
        place,
        [after(tok, acc), d_proj],
        [([(0, own_dmixed), (1, near_att, low)], [got_cq, [got_xq]], "halve")],
        chunk,
    )
    got_yq = page_swap(send_q, 1)
    keep_u, send_u = add_split(place, [keep_u], [after(got_zu, send_q)], 2, chunk)
    got_zu = page_swap(send_u, 4)
    keep_d, send_d = add_split(place, [keep_d], [after(got_yd, send_u)], 1, chunk)
    got_zd = page_swap(send_d, 2)
    acc = add_hist(after(acc, send_q, send_d), ids, some, text, SPAN // 2, SPAN // 2)
    acc = add_visual(acc, vis_ids, near_far)
    g_up_bias = [jnp.sum(d.astype(f32), axis=0) for d in d_ups]
    shared = (g_out_bias, g_gain1, g_shift1, g_down_bias, g_gain2, g_shift2)
    keep, send = pack_sums(acc, near_sums, far_sums, g_up_bias, shared)
    got = x_swap(send)
    keep_q, send_q = add_split(place, [keep_q], [after(got_yq, send)], 1, chunk)
    got_zq = page_swap(send_q, 2)
    keep_d, send_d = add_split(place, [keep_d], [after(got_zd, send_q)], 2, chunk)
    got_zd = page_swap(send_d, 4)
    got_zu = after(got_zu, send_d)
    both_u = finish(place, keep_u, got_zu, 2, chunk)
    got_xu = x_swap(both_u[chunk:].astype(bf16))
    sums = keep + after(got, send_d)
    sums = jnp.concatenate((sums[:EACH], sums[2 * EACH :])) + core_swap(sums[EACH:])
    got = page_swap(sums, 1)
    grad_tokens = tokens_grad(dmixed, (own_qkv, c_qkv, after(far_w, sums)), d_first)
    sums = sums + after(got, grad_tokens)
    got = page_swap(sums, 2)
    keep_q, send_q = add_split(place, [keep_q], [after(got_zq, sums)], 2, chunk)
    got_zq = page_swap(send_q, 4)
    sums = sums + after(got, send_q)
    got = page_swap(sums, 4)
    for bit in page_bits[3:]:
        sums = sums + got
        got = page_swap(sums, bit)
    got_zd, got_xu = lax.optimization_barrier((got_zd, got_xu, sums))[:2]
    g_w_down = finish(place, keep_d, got_zd, 2, chunk).T
    g_w_up = both_u[:chunk] + got_xu.astype(f32)
    got, got_zq, g_w_down, g_w_up = lax.optimization_barrier((got, got_zq, g_w_down, g_w_up))
    g_w_qkv, g_w_out = last_sums(place, keep_q, got_zq, 2, chunk)
    g_qv_bias, g_pos, g_box, g_up_bias, *shared = unpack_sums(sums, got, heads_here, units, width)
    g_box = g_box.transpose(1, 0, 2)
    return (
        layer_out.reshape(tokens.shape),
        grad_tokens.reshape(tokens.shape),
        g_w_qkv,
        g_qv_bias,
        g_w_out,
        shared[0],
        shared[1],
        shared[2],
        g_w_up,
        g_up_bias,
        g_w_down,
        shared[3],
        shared[4],
        shared[5],
        g_pos,
        g_box,
    )


def solution(mesh):
    placed = (
        P(("pages", "heads"), None, None),
        P(None, None, "heads"),
        P(None, "heads"),
        P("heads", None),
        P(),
        P(),
        P(),
        P(None, "heads"),
        P("heads"),
        P("heads", None),
        P(),
        P(),
        P(),
        P("heads", None),
        P(None, "heads", None),
        P("pages", None),
        P("pages", None, None),
        P(("pages", "heads"), None, None),
    )
    return jax.shard_map(
        on_device,
        mesh=mesh,
        in_specs=placed,
        out_specs=(
            P(("pages", "heads"), None, None),
            P(("pages", "heads"), None, None),
            P("pages", None, "heads"),
            P(None, "heads"),
            P("heads", "pages"),
            P(),
            P(),
            P(),
            P("pages", "heads"),
            P("heads"),
            P("heads", "pages"),
            P(),
            P(),
            P(),
            P("heads", None),
            P(None, "heads", None),
        ),
        check_vma=False,
    )
```

```python
import functools
import math

import jax
import jax.numpy as jnp
from jax import lax
from jax.experimental import pallas as pl
from jax.experimental.pallas import tpu as pltpu
from jax.sharding import PartitionSpec as P

f32 = jnp.float32
bf16 = jnp.bfloat16
i32 = jnp.int32
EPSILON = 1e-05
MASKED_SCORE = -1e30


HEAD_DIM = 64
TEXT = 512
NB1 = 32
MD1 = 128
NB2 = 64
MD2 = 256
ROWS = 576
VIS = ROWS - TEXT
QROWS = 640
LANES = 128
CHUNK = 64
UNIT = 2048.0
BLOCKS = ((0, 256), (0, 384), (128, 384), (256, 256))
OFFS = (0, 320, 768, 1216)
SPAN = 1536
Q_AT = SPAN
KV_AT = Q_AT + ROWS
PV_AT = KV_AT + ROWS
KEPT = PV_AT + ROWS // 2
SMALL = 24


def thresholds(buckets, max_reach):
    half_range = buckets // 2
    exact_range = half_range // 2
    levels = half_range - exact_range
    return [
        math.ceil(exact_range * (max_reach / exact_range) ** (k / levels) - 1e-09)
        for k in range(1, levels)
    ]


def bucket_of(diff, buckets, reach):
    n = jnp.abs(diff)
    out = jnp.minimum(n, buckets // 4) + jnp.where(diff > 0, buckets // 2, 0)
    for t in thresholds(buckets, reach):
        out = out + jnp.where(n >= t, 1, 0)
    return out


def parts_of(blk):
    s, n = BLOCKS[blk]
    return ((s, n, OFFS[blk]), (TEXT, VIS, OFFS[blk] + n))


def nt(a, b):
    return lax.dot_general(a, b, (((1,), (1,)), ((), ())), preferred_element_type=f32)


def nn(a, b):
    return lax.dot_general(a, b, (((1,), (0,)), ((), ())), preferred_element_type=f32)


def unpack(ids):
    return ids & 255, (ids >> 8) & 255, ids >> 16


def take(tab, idx):
    return jnp.take_along_axis(
        jnp.broadcast_to(tab, idx.shape), idx, axis=1, mode="promise_in_bounds"
    )


def ids_kernel(place_ref, len_ref, box_ref, ids_ref, vis_ref, c_s, r_s, *, valid):
    page = place_ref[0]
    row = lax.broadcasted_iota(i32, (8, ROWS), 1)
    segment = jnp.zeros((8, ROWS), i32)
    end = 0
    for i in range(len_ref.shape[1]):
        end = end + len_ref[page, i]
        segment = segment + jnp.where(row >= end, 1, 0)
    c_s[...] = jnp.zeros_like(c_s)
    c_s[0:8, :] = segment.astype(f32)
    c_s[8:10, 0:valid] = box_ref[page].astype(f32)
    r_s[...] = c_s[...].T.astype(i32)

    def query(lo, hi):
        return tuple(c_s[i : i + 1, lo:hi].astype(i32) for i in (0, 8, 9))

    def tiles(row, out, rows, q_first, q):
        qseg, qx, qy = (jnp.broadcast_to(v, (CHUNK, LANES)) for v in q)
        lane = lax.broadcasted_iota(i32, (CHUNK, LANES), 1)
        if q_first == TEXT:
            q_pos, high = TEXT + (lane & (VIS - 1)), jnp.where(lane >= VIS, NB2, 0)
        else:
            q_pos, high = q_first + lane, 0

        def tile(c, _):
            at = pl.ds(pl.multiple_of(row + c * CHUNK, CHUNK), CHUNK)
            here = pl.ds(pl.multiple_of(out + c * CHUNK, CHUNK), CHUNK)
            seg, kx, ky = (jnp.broadcast_to(r_s[at, i : i + 1], (CHUNK, LANES)) for i in (0, 8, 9))
            k_pos = lax.broadcasted_iota(i32, (CHUNK, LANES), 0) + (row + c * CHUNK)
            x_id = bucket_of(kx - qx, NB2, MD2)
            y_id = bucket_of(ky - qy, NB2, MD2)
            p_id = bucket_of(k_pos - q_pos, NB1, MD1)
            ok = ((seg == qseg) | (k_pos >= TEXT) | (q_pos >= TEXT)) & (k_pos < valid)
            p_id = jnp.where(ok, p_id, NB1)
            y_id = y_id + (high if q_first == TEXT else NB2)
            ref, at = (vis_ref, at) if q_first == TEXT else (ids_ref, here)
            ref[at, :] = (x_id + high) + y_id * 256 + (p_id + high) * 65536
            return 0

        lax.fori_loop(0, rows // CHUNK, tile, 0)

    for blk in range(4):
        q = query(blk * LANES, (blk + 1) * LANES)
        for s, n, o in parts_of(blk):
            tiles(s, o, n, blk * LANES, q)
    q = tuple(jnp.concatenate((v, v), axis=1) for v in query(TEXT, ROWS))
    tiles(0, 0, ROWS, TEXT, q)


def make_ids(place, lengths, boxes):
    return pl.pallas_call(
        functools.partial(ids_kernel, valid=boxes.shape[2]),
        in_specs=[
            pl.BlockSpec(memory_space=pltpu.SMEM),
            pl.BlockSpec(memory_space=pltpu.SMEM),
            pl.BlockSpec(memory_space=pltpu.VMEM),
        ],
        out_shape=[
            jax.ShapeDtypeStruct((SPAN, LANES), i32),
            jax.ShapeDtypeStruct((ROWS, LANES), i32),
        ],
        scratch_shapes=[pltpu.VMEM((LANES, ROWS), f32), pltpu.VMEM((ROWS, LANES), i32)],
        name="ids",
        cost_estimate=pl.CostEstimate(flops=0, bytes_accessed=0, transcendentals=0),
        compiler_params=pltpu.CompilerParams(vmem_limit_bytes=12 << 20),
    )(place, lengths, boxes)


def place(dst_ref, pair, first, side, cols):
    at = slice(side * 192, side * 192 + 64)
    dst_ref[pair, first : first + ROWS, at] = cols


def stacked(both):
    return jnp.concatenate((both[:, :LANES], both[:, LANES:]), 0)


def block(ref, pair, first, blk):
    rows = LANES if blk < 4 else VIS
    return stacked(ref[pair, first + blk * LANES : first + blk * LANES + rows, :])


def load_rows(refs, odd, dst):
    if len(refs) == 1:
        dst[0 : refs[0].shape[0], :] = refs[0][...]
    else:
        half = dst.shape[0] // 2
        for first in range(2):

            @pl.when(odd == first)
            def _(first=first):
                dst[first * half : (first + 1) * half, :] = refs[0][0:half, :]
                dst[(1 - first) * half : (2 - first) * half, :] = refs[1][0:half, :]


def pad_rows(v):
    return jnp.concatenate((v, jnp.zeros((ROWS - v.shape[0], v.shape[1]), v.dtype)), 0)


def fold(both):
    n = both.shape[1] // 2
    t = both.T
    lane = lax.broadcasted_iota(i32, (n, LANES), 1)
    return jnp.where(lane < 64, t[:n], t[n:])


def fwd_kernel(place_ref, tok_ref, *refs, pieces, pairs):
    *refs, n_s, b_s = refs
    for i in range(3):
        far = lax.broadcasted_iota(i32, (LANES, LANES), 0) - lax.broadcasted_iota(i32, (LANES, LANES), 1)
        n_s[i] = bucket_of(far + (i - 1) * LANES, NB1, MD1)
    n = 2 * pieces
    weights = (refs[:pieces], refs[pieces:n])
    small, (ids_ref, vis_ref) = refs[n : n + 2], refs[n + 2 : n + 4]
    wo_refs, refs = (refs[n + 4 : n + 6], refs[n + 6 :]) if pieces == 1 else (None, refs[n + 4 :])
    out_ref, bias_ref, wo_ref, kept_ref = refs[:4]
    w_s = refs[4] if pieces > 1 else None
    vt_s, s_s, i_s, f_s, o_s, l_s = refs[-6:]
    first = small[0].shape[0] - 16
    inner = pairs * HEAD_DIM
    units = 4 * pairs // 6
    bias_ref[...] = jnp.zeros_like(bias_ref)
    for g in range(2):
        bias_ref[g : g + 1, :] = small[g][first + units : first + units + 1, :].astype(f32)
        for i in range(4 * pairs):
            at = slice(i % 6 * LANES, (i % 6 + 1) * LANES)
            row = first + i // 6
            high, rest = (small[g][r : r + 1, at].astype(f32) for r in (row, row + 8))
            l_s[g, i : i + 1, :] = high + rest
    small = [l_s.at[g] for g in range(2)]
    tok = pad_rows(tok_ref[...])
    for pair in range(pairs):
        kept_ref[pair, Q_AT:KV_AT, :] = jnp.zeros((ROWS, 256), bf16)
    for g in range(2):
        if pieces > 1:
            load_rows(weights[g], place_ref[1], w_s.at[g])
            w_ref = w_s.at[g]
            wo_ref[g * inner : (g + 1) * inner, :] = w_ref[3 * inner :, :]
        else:
            w_ref = weights[g][0]
            wo_ref[g * inner : (g + 1) * inner, :] = wo_refs[g][...]
        for part in range(3):
            mixed = nt(tok, w_ref[part * inner : (part + 1) * inner, :])
            for local in range(pairs):
                pair, side = divmod(g * pairs + local, 2)
                at = slice(side * 64, side * 64 + 64)
                cols = mixed[:, local * 64 : local * 64 + 64]
                if part == 0:
                    cols = cols + small[g][2 * pairs + local : 2 * pairs + local + 1, :64]
                    place(kept_ref, pair, Q_AT, side, (cols * (UNIT / 8)).astype(bf16))
                elif part == 1:
                    kept_ref[pair, KV_AT:PV_AT, at] = cols.astype(bf16)
                else:
                    cols = cols + small[g][3 * pairs + local : 3 * pairs + local + 1, :64]
                    low = slice(LANES + side * 64, LANES + side * 64 + 64)
                    kept_ref[pair, KV_AT:PV_AT, low] = cols.astype(bf16)
                    vt_s[pair, at, :] = cols.T.astype(bf16)
    for pair in range(pairs):
        (ga, la), (gb, lb) = divmod(2 * pair, pairs), divmod(2 * pair + 1, pairs)
        for row, start in ((0, 0), (1, pairs)):
            a = small[ga][start + la : start + la + 1, :] * UNIT
            b = small[gb][start + lb : start + lb + 1, :] * UNIT
            i_s[pair, row : row + 1, :] = (
                jnp.round(a).astype(i32) * 65536 + jnp.round(b).astype(i32)
            )
            f_s[pair, 2 * row : 2 * row + 1, :] = jnp.concatenate((a[:, :64], b[:, :64]), 1)
            f_s[pair, 2 * row + 1 : 2 * row + 2, :] = jnp.concatenate((a[:, 64:], b[:, 64:]), 1)

    def softmax(total, wide, p_at):
        m = jnp.full((8, wide), -3e38, f32)
        for c in range(0, total, 8):
            m = jnp.maximum(m, s_s[c : c + 8, :wide])
        m = jnp.max(m, axis=0, keepdims=True)
        l = jnp.zeros((8, wide), f32)
        for c in range(0, total, 8):
            e = jnp.exp2((s_s[c : c + 8, :wide] - m) * (math.log2(math.e) / UNIT))
            s_s[c : c + 8, :wide] = e
            l = l + e
        inv = 1.0 / jnp.sum(l, axis=0, keepdims=True)
        for c in range(0, total, 16):
            p_at(c, (s_s[c : c + 16, :wide] * inv).astype(bf16))

    def one_pair(pair, _):
        t_xy, t_p = (i_s[pair, i : i + 1, :] for i in range(2))
        v_x, v_y, v_p = (f_s[pair, i : i + 1, :] for i in range(3))
        for i in range(3):
            for c in range(0, LANES, 16):
                b_s[i, c : c + 16, :] = take(t_p, n_s[i, c : c + 16, :])
        for blk in range(4):
            q = block(kept_ref, pair, Q_AT, blk)
            first = OFFS[blk]
            for s, n, o in parts_of(blk):
                sc = nt(kept_ref[pair, KV_AT + s : KV_AT + s + n, :LANES], q)
                for c in range(0, n, 16):
                    r = slice(o + c, o + c + 16)
                    x, y, p = unpack(ids_ref[r, :])
                    if s < TEXT:
                        tile, row = divmod(s + c, LANES)
                        b_p = b_s[tile - blk + 1, row : row + 16, :]
                    else:
                        b_p = take(t_p, p)
                    b = take(t_xy, x) + take(t_xy, y) + b_p
                    low = (b << 16) >> 16
                    high = (b - low) >> 16
                    add = jnp.where(p == NB1, MASKED_SCORE, 0.0)
                    to = slice(o - first + c, o - first + c + 16)
                    s_s[to, :LANES] = sc[c : c + 16, :LANES] + (high.astype(f32) + add)
                    s_s[to, LANES:] = sc[c : c + 16, LANES:] + (low.astype(f32) + add)

            def put(c, v, first=first):
                kept_ref[pair, first + c : first + c + 16, :] = v

            softmax(BLOCKS[blk][1] + VIS, 256, put)
            ot = sum(
                nn(vt_s[pair, :, s : s + n], kept_ref[pair, o : o + n, :]) for s, n, o in parts_of(blk)
            )
            o_s[pair, blk * LANES : (blk + 1) * LANES, :] = fold(ot).astype(bf16)
        q = block(kept_ref, pair, Q_AT, 4)
        sc = nt(kept_ref[pair, KV_AT:PV_AT, :LANES], q)
        for c in range(0, ROWS, 16):
            x, y, p = unpack(vis_ref[c : c + 16, :])
            b = take(v_x, x) + take(v_y, y) + take(v_p, p)
            add = jnp.where((p & (NB2 - 1)) == NB1, MASKED_SCORE, 0.0)
            s_s[c : c + 16, :LANES] = sc[c : c + 16] + (b + add)

        def put_v(c, v):
            side, row = divmod(c, ROWS // 2)
            at = slice(side * LANES, (side + 1) * LANES)
            kept_ref[pair, PV_AT + row : PV_AT + row + 16, at] = v

        softmax(ROWS, LANES, put_v)
        o_s[pair, TEXT:ROWS, :] = fold(nn(vt_s[pair], stacked(kept_ref[pair, PV_AT:KEPT, :]))).astype(bf16)
        return 0

    lax.fori_loop(0, pairs, one_pair, 0, unroll=True)
    rows = out_ref.shape[0]
    for pair in range(pairs):
        out_ref[:, pair * LANES : (pair + 1) * LANES] = o_s[pair, 0:rows, :]


def attn_fwd(place, tok, weights, small, ids, pairs, w_out=()):
    pieces, (rows, width) = len(weights[0]), tok.shape
    vmem = pl.BlockSpec(memory_space=pltpu.VMEM)
    outs = [((rows, pairs * LANES), bf16), ((8, width), f32), ((pairs * LANES, width), bf16)]
    outs += [((pairs, KEPT, 256), bf16)]
    if pieces > 1:
        outs += [((2, 4 * pairs * HEAD_DIM, width), bf16)]
    args = (place, tok, *weights[0], *weights[1], *small, *ids, *w_out)
    return pl.pallas_call(
        functools.partial(fwd_kernel, pieces=pieces, pairs=pairs),
        in_specs=[pl.BlockSpec(memory_space=pltpu.SMEM)] + [vmem] * (len(args) - 1),
        out_specs=[vmem] * len(outs),
        out_shape=[jax.ShapeDtypeStruct(shape, dtype) for shape, dtype in outs],
        scratch_shapes=[
            pltpu.VMEM((pairs, LANES, ROWS), bf16),
            pltpu.VMEM((ROWS, 256), f32),
            pltpu.VMEM((pairs, 8, LANES), i32),
            pltpu.VMEM((pairs, 8, LANES), f32),
            pltpu.VMEM((pairs, ROWS, LANES), bf16),
            pltpu.VMEM((2, SMALL, LANES), f32),
            pltpu.VMEM((3, LANES, LANES), i32),
            pltpu.VMEM((3, LANES, LANES), i32),
        ],
        name="attn_fwd",
        cost_estimate=pl.CostEstimate(flops=0, bytes_accessed=0, transcendentals=0),
        compiler_params=pltpu.CompilerParams(vmem_limit_bytes=14 << 20),
    )(*args)


def bwd_kernel(kept_ref, do_ref, out0_ref, out1_ref, sum_ref, ds_ref, dsv_ref, do_s, kt_s, dq_s, dk_s, dv_s, *, pairs):
    rows = out0_ref.shape[0]
    sum_ref[...] = jnp.zeros_like(sum_ref)
    do_s[...] = jnp.zeros_like(do_s)
    for h in range(2 * pairs):
        pair, side = divmod(h, 2)
        place(do_s, pair, 0, side, pad_rows(do_ref[:, h * 64 : h * 64 + 64]))
    for pair in range(pairs):
        kt_s[pair] = kept_ref[pair, KV_AT:PV_AT, :LANES].astype(f32).T.astype(bf16)

    def grad_scores(dps, ps, put):
        d = jnp.zeros((8, dps[0].shape[1]), f32)
        for dp, p in zip(dps, ps):
            for c in range(0, dp.shape[0], 16):
                t = p(c).astype(f32) * dp[c : c + 16]
                d = d + (t[:8] + t[8:])
        d = jnp.sum(d, axis=0, keepdims=True)
        for i, (dp, p) in enumerate(zip(dps, ps)):
            for c in range(0, dp.shape[0], 16):
                put(i, c, (p(c).astype(f32) * (dp[c : c + 16] - d)).astype(bf16))

    def one_pair(pair, _):
        dv_s[...] = jnp.zeros_like(dv_s)
        dk_s[...] = jnp.zeros_like(dk_s)
        for blk in range(4):
            q = block(kept_ref, pair, Q_AT, blk)
            do = block(do_s, pair, 0, blk)
            parts = parts_of(blk)

            def put(i, c, v, parts=parts):
                ds_ref[pair, parts[i][2] + c : parts[i][2] + c + 16, :] = v

            grad_scores(
                [nt(kept_ref[pair, KV_AT + s : KV_AT + s + n, LANES:], do) for s, n, o in parts],
                [lambda c, o=o: kept_ref[pair, o + c : o + c + 16, :] for s, n, o in parts],
                put,
            )
            dq = 0.0
            for s, n, o in parts:
                ds = ds_ref[pair, o : o + n, :]
                dq = dq + nn(kt_s[pair, :, s : s + n], ds)
                dv_s[s : s + n, :] += nn(kept_ref[pair, o : o + n, :], do)
                dk_s[s : s + n, :] += nn(ds, q)
            dq_s[pair, 0, blk * LANES : (blk + 1) * LANES, :] = (fold(dq) * 0.125).astype(bf16)
        q = block(kept_ref, pair, Q_AT, 4)
        do = block(do_s, pair, 0, 4)
        pv = stacked(kept_ref[pair, PV_AT:KEPT, :])

        def put_v(i, c, v):
            dsv_ref[pair, c : c + 16, :] = v

        grad_scores([nt(kept_ref[pair, KV_AT:PV_AT, LANES:], do)], [lambda c: pv[c : c + 16]], put_v)
        ds = dsv_ref[pair]
        dq_s[pair, 0, TEXT:ROWS, :] = (fold(nn(kt_s[pair], ds)) * 0.125).astype(bf16)
        dq_s[pair, 1] = ((dk_s[...] + nn(ds, q)) * (1.0 / UNIT)).astype(bf16)
        dq_s[pair, 2] = (dv_s[...] + nn(pv, do)).astype(bf16)
        return 0

    lax.fori_loop(0, pairs, one_pair, 0)
    for h in range(2 * pairs):
        pair, side = divmod(h, 2)
        g, local = divmod(h, pairs)
        for part in range(3):
            col = part * pairs * HEAD_DIM + local * HEAD_DIM
            here = dq_s[pair, part, 0:rows, side * 64 : side * 64 + 64]
            (out0_ref, out1_ref)[g][:, col : col + 64] = here
            if part != 1:
                total = jnp.sum(here.astype(f32), axis=0, keepdims=True)
                sum_ref[g : g + 1, col : col + 64] = total


def attn_bwd(rows, kept, d_att):
    pairs = kept.shape[0]
    cols = 3 * pairs * HEAD_DIM
    vmem = pl.BlockSpec(memory_space=pltpu.VMEM)
    outs = [((rows, cols), bf16)] * 2 + [((8, cols), f32)]
    outs += [((pairs, SPAN, 256), bf16), ((pairs, ROWS, LANES), bf16)]
    return pl.pallas_call(
        functools.partial(bwd_kernel, pairs=pairs),
        in_specs=[vmem] * 2,
        out_specs=[vmem] * 5,
        out_shape=[jax.ShapeDtypeStruct(shape, dtype) for shape, dtype in outs],
        scratch_shapes=[
            pltpu.VMEM((pairs, ROWS, 256), bf16),
            pltpu.VMEM((pairs, LANES, ROWS), bf16),
            pltpu.VMEM((pairs, 3, ROWS, LANES), bf16),
            pltpu.VMEM((ROWS, LANES), f32),
            pltpu.VMEM((ROWS, LANES), f32),
        ],
        name="attn_bwd",
        cost_estimate=pl.CostEstimate(flops=0, bytes_accessed=0, transcendentals=0),
        compiler_params=pltpu.CompilerParams(vmem_limit_bytes=14 << 20),
    )(kept, d_att)


HSTEP = 64
MOST = 128
ID_SLOT = 12


def hot_sums(values, ids, rows, y_from):
    io = lax.broadcasted_iota(i32, (NB2, LANES), 0)
    lhs, rhs = [], []
    for u in range(rows):
        x, y, p = unpack(ids(u))
        if y_from:
            y = y - y_from
        else:
            x, y, p = (v & (NB2 - 1) for v in (x, y, p))
        hot = [jnp.where(io == x, 1.0, 0.0), jnp.where(io == y, 1.0, 0.0)]
        hot.append(jnp.where(io[:NB1] == p, 1.0, 0.0))
        rhs.append(jnp.concatenate(hot, 0).astype(bf16))
        lhs.append(values(u).astype(bf16))
    return nt(jnp.concatenate(lhs, 1), jnp.concatenate(rhs, 1))


def hist_kernel(place_ref, len_ref, acc_ref, ids_ref, *refs, sets, pairs, blocks, visual):
    ds_refs, (hist_ref, l_s, o_s) = refs[:sets], refs[sets:]
    heads = 2 * sets * pairs
    page = place_ref[0]
    hist_ref[...] = acc_ref[...]
    bounds = [0]
    for i in range(len_ref.shape[1]):
        bounds.append(bounds[-1] + len_ref[page, i])
    lane = lax.broadcasted_iota(i32, (8 * 16, LANES), 1)

    def bring(first, rows):
        @pl.loop(0, rows // HSTEP)
        def _(c):
            at = pl.ds(pl.multiple_of(first + c * HSTEP, HSTEP), HSTEP)
            for h in range(heads):
                pair, side = divmod(h, 2)
                half = slice(side * LANES, (side + 1) * LANES)
                v = ds_refs[pair // pairs][pair % pairs, at, half].astype(f32)
                l_s[pl.ds(c * (HSTEP * 16) + h, HSTEP, stride=16), :] = v
            l_s[pl.ds(c * (HSTEP * 16) + ID_SLOT, HSTEP, stride=16), :] = ids_ref[at, :].astype(f32)

    def add(ref, first, rows):
        row = lambda u: ref[pl.ds(pl.multiple_of((first + u) * 16, 16), 16), :]
        hist_ref[...] += hot_sums(
            row, lambda u: row(u)[ID_SLOT : ID_SLOT + 1].astype(i32), rows, NB2
        )

    for blk in blocks:
        start, rows = BLOCKS[blk]
        bring(OFFS[blk], rows)
        if start + rows == TEXT and rows < l_s.shape[0] // 16:
            l_s[rows * 16 : (rows + MOST) * 16, :] = jnp.zeros((MOST * 16, LANES), f32)
        q = lane + blk * LANES
        longest = 0
        for lo, hi in zip(bounds[:-1], bounds[1:]):
            meets = (lo < (blk + 1) * LANES) & (hi > blk * LANES)
            longest = jnp.maximum(longest, jnp.where(meets, hi - lo, 0))

            @pl.when(meets)
            def _(lo=lo, hi=hi):
                mine = (q >= lo) & (q < hi)

                @pl.loop(0, MOST // 8)
                def _(i):
                    to = pl.ds(pl.multiple_of(i * 128, 128), 128)
                    at = pl.ds(pl.multiple_of((lo - start) * 16 + i * 128, 16), 128)
                    o_s[to, :] = jnp.where(mine, l_s[at, :], o_s[to, :])

        @pl.loop(0, (longest + (HSTEP - 1)) >> 6)
        def _(r):
            add(o_s, r * HSTEP, HSTEP)

        bring(OFFS[blk] + rows, VIS)
        add(l_s, 0, visual)


def add_hist(place, lengths, acc, ids, ds, blocks, visual):
    vmem = pl.BlockSpec(memory_space=pltpu.VMEM)
    rows = max(max(BLOCKS[b][1] for b in blocks), BLOCKS[3][1] + MOST)
    return pl.pallas_call(
        functools.partial(
            hist_kernel, sets=len(ds), pairs=ds[0].shape[0], blocks=blocks, visual=visual
        ),
        in_specs=[pl.BlockSpec(memory_space=pltpu.SMEM)] * 2 + [vmem] * (2 + len(ds)),
        out_specs=vmem,
        out_shape=jax.ShapeDtypeStruct((16, 160), f32),
        scratch_shapes=[
            pltpu.VMEM((rows * 16, LANES), f32),
            pltpu.VMEM((MOST * 16, LANES), f32),
        ],
        name="hist",
        cost_estimate=pl.CostEstimate(flops=0, bytes_accessed=0, transcendentals=0),
        compiler_params=pltpu.CompilerParams(vmem_limit_bytes=12 << 20),
    )(place, lengths, acc, ids, *ds)


VSTEP = 72


def visual_kernel(acc_ref, ids_ref, *refs, sets, pairs):
    ds_refs, hist_ref, l_s, i_s = refs[:sets], refs[-3], refs[-2], refs[-1]
    heads = 2 * sets * pairs
    far = ROWS // 2
    lane = lax.broadcasted_iota(i32, (VSTEP, LANES), 1)
    hist_ref[...] = acc_ref[...]
    for h in range(heads, 16):
        l_s[pl.ds(h, VSTEP, stride=16), :] = jnp.zeros((VSTEP, LANES), f32)

    @pl.loop(0, far // VSTEP)
    def _(r):
        here = pl.ds(pl.multiple_of(r * VSTEP, 8), VSTEP)
        there = pl.ds(pl.multiple_of(far + r * VSTEP, 8), VSTEP)
        i_s[...] = jnp.where(lane < VIS, ids_ref[here, :], ids_ref[there, :])
        for pair in range(sets * pairs):
            ref = ds_refs[pair // pairs]
            a, b = (ref[pair % pairs, at, :].astype(f32) for at in (here, there))
            one = jnp.where(lane < VIS, a, pltpu.roll(b, VIS, axis=1))
            two = jnp.where(lane < VIS, pltpu.roll(a, VIS, axis=1), b)
            l_s[pl.ds(2 * pair, VSTEP, stride=16), :] = one
            l_s[pl.ds(2 * pair + 1, VSTEP, stride=16), :] = two
        hist_ref[...] += hot_sums(
            lambda u: l_s[u * 16 : u * 16 + 16, :], lambda u: i_s[u : u + 1, :], VSTEP, 0
        )


def add_visual(acc, ids, ds):
    vmem = pl.BlockSpec(memory_space=pltpu.VMEM)
    return pl.pallas_call(
        functools.partial(visual_kernel, sets=len(ds), pairs=ds[0].shape[0]),
        grid=(1,),
        in_specs=[
            pl.BlockSpec((16, 160), lambda i: (0, 0)),
            pl.BlockSpec((ROWS, LANES), lambda i: (0, 0)),
        ]
        + [pl.BlockSpec(t.shape, lambda i: (0, 0, 0)) for t in ds],
        out_specs=pl.BlockSpec((16, 160), lambda i: (0, 0)),
        out_shape=jax.ShapeDtypeStruct((16, 160), f32),
        scratch_shapes=[pltpu.VMEM((VSTEP * 16, LANES), f32), pltpu.VMEM((VSTEP, LANES), i32)],
        name="hist",
        cost_estimate=pl.CostEstimate(flops=0, bytes_accessed=0, transcendentals=0),
        compiler_params=pltpu.CompilerParams(vmem_limit_bytes=12 << 20),
    )(acc, ids, *ds)


def call(kernel, name, args, outs, scratch=(), smem=0):
    vmem = pl.BlockSpec(memory_space=pltpu.VMEM)
    return pl.pallas_call(
        kernel,
        in_specs=[pl.BlockSpec(memory_space=pltpu.SMEM)] * smem + [vmem] * (len(args) - smem),
        out_shape=[jax.ShapeDtypeStruct(shape, dtype) for shape, dtype in outs],
        scratch_shapes=[pltpu.VMEM(shape, dtype) for shape, dtype in scratch],
        name=name,
        cost_estimate=pl.CostEstimate(flops=0, bytes_accessed=0, transcendentals=0),
        compiler_params=pltpu.CompilerParams(vmem_limit_bytes=12 << 20),
    )(*args)


def start_kernel(place_ref, qkv_ref, wo_ref, up_ref, box_ref, pos_ref, qv_ref, ub_ref, a_ref, b_ref, small_ref, s_s, o_s, sems):
    half = a_ref.shape[0]
    odd = place_ref[1]

    def copy(src, dst, i):
        return pltpu.make_async_copy(src, dst, sems.at[i])

    tail = qkv_ref.shape[0] - half
    firsts = [copy(qkv_ref.at[0:half, :], a_ref.at[0:half, :], 0)]
    seconds = [
        copy(qkv_ref.at[half:, :], a_ref.at[0:tail, :], 0),
        copy(wo_ref, a_ref.at[tail:half, :], 1),
    ]

    @pl.when(odd == 0)
    def _():
        for c in firsts:
            c.start()

    @pl.when(odd == 1)
    def _():
        for c in seconds:
            c.start()

    at = pl.ds(pl.multiple_of(odd * half, half), half)
    others = [copy(up_ref.at[at, :], b_ref.at[0:half, :], 2)]
    for c in others:
        c.start()
    heads = pos_ref.shape[0]
    s_s[...] = jnp.zeros_like(s_s)
    for h in range(heads):
        s_s[h : h + 1, :NB2] = box_ref[h, 0:1, :]
        s_s[h : h + 1, NB2:] = box_ref[h, 1:2, :]
        s_s[heads + h : heads + h + 1, :NB1] = pos_ref[h : h + 1, :]
        for i in range(2):
            row = (2 + i) * heads + h
            s_s[row : row + 1, :64] = qv_ref[i : i + 1, h * 64 : h * 64 + 64]
    units = ub_ref.shape[0] // LANES
    s_s[4 * heads : 4 * heads + units, :] = ub_ref[...].astype(f32).reshape(units, LANES)
    o_s[...] = jnp.zeros_like(o_s)
    for i in range(SMALL):
        at = slice(i % 6 * LANES, (i % 6 + 1) * LANES)
        value = s_s[i : i + 1, :]
        high = value.astype(bf16).astype(f32)
        o_s[i // 6 : i // 6 + 1, at] = high
        o_s[8 + i // 6 : 9 + i // 6, at] = value - high
    small_ref[...] = o_s[...].astype(bf16)
    last = copy(small_ref, b_ref.at[half : half + 16, :], 4)
    last.start()

    @pl.when(odd == 0)
    def _():
        for c in firsts:
            c.wait()

    @pl.when(odd == 1)
    def _():
        for c in seconds:
            c.wait()

    for c in others + [last]:
        c.wait()


def start_parts(place, qkv, w_out, w_up, box, pos, qv, up):
    width = qkv.shape[1]
    vmem, hbm = (pl.BlockSpec(memory_space=m) for m in (pltpu.VMEM, pltpu.HBM))
    shapes = [(width // 2, width), (width // 2 + 16, width), (16, width)]
    return pl.pallas_call(
        start_kernel,
        in_specs=[pl.BlockSpec(memory_space=pltpu.SMEM)] + [hbm] * 3 + [vmem] * 4,
        out_specs=[vmem] * 3,
        out_shape=[jax.ShapeDtypeStruct(shape, bf16) for shape in shapes],
        scratch_shapes=[
            pltpu.VMEM((SMALL, LANES), f32),
            pltpu.VMEM((16, width), f32),
            pltpu.SemaphoreType.DMA((5,)),
        ],
        name="start_parts",
        cost_estimate=pl.CostEstimate(flops=0, bytes_accessed=0, transcendentals=0),
        compiler_params=pltpu.CompilerParams(vmem_limit_bytes=58 << 20),
    )(place, qkv, w_out, w_up, box.transpose(1, 0, 2), pos, qv, up)


def join_kernel(place_ref, mine_ref, theirs_ref, *refs):
    outs, sems = refs[:-1], refs[-1]
    half = outs[0].shape[0] // 2
    odd = place_ref[1]
    copies = []
    for i, out in enumerate(outs):
        for j, (ref, first) in enumerate(((mine_ref, odd * half), (theirs_ref, (1 - odd) * half))):
            to = out.at[pl.ds(pl.multiple_of(first, half), half), :]
            at = slice(i * half, (i + 1) * half)
            copies.append(pltpu.make_async_copy(ref.at[at, :], to, sems.at[i, j]))
    for c in copies:
        c.start()
    for c in copies:
        c.wait()


def join_rows(place, mine, theirs, number, rows):
    cols = mine.shape[1]
    vmem = pl.BlockSpec(memory_space=pltpu.VMEM)
    return pl.pallas_call(
        join_kernel,
        in_specs=[pl.BlockSpec(memory_space=pltpu.SMEM), vmem, vmem],
        out_specs=[vmem] * number,
        out_shape=[jax.ShapeDtypeStruct((rows, cols), bf16)] * number,
        scratch_shapes=[pltpu.SemaphoreType.DMA((number, 2))],
        name="join_rows",
        cost_estimate=pl.CostEstimate(flops=0, bytes_accessed=0, transcendentals=0),
        compiler_params=pltpu.CompilerParams(vmem_limit_bytes=8 << 20),
    )(place, mine, theirs)


def tn(a, b):
    return lax.dot_general(a, b, (((0,), (0,)), ((), ())), preferred_element_type=f32)


def parity_split(cur_ref, keep_ref, send_ref, first, chunk, bit):
    for mine in range(2):

        @pl.when(bit == mine)
        def _(mine=mine):
            for i in range(cur_ref.shape[0] // chunk // 2):
                to = slice(first + i * chunk, first + (i + 1) * chunk)
                at = (2 * i + mine) * chunk
                keep_ref[to, :] = cur_ref[at : at + chunk, :]
                at = (2 * i + 1 - mine) * chunk
                send_ref[to, :] = cur_ref[at : at + chunk, :]


def products_kernel(place_ref, *refs, lefts, plan, chunk):
    left, refs = refs[:lefts], list(refs[lefts:])
    rights = [[refs.pop(0) for _ in terms] for terms, _, _ in plan]
    gots = [[[refs.pop(0) for _ in range(n)] for n in counts] for _, counts, _ in plan]
    cur_s = refs.pop()
    split = 0
    for (terms, _, mode), right, got in zip(plan, rights, gots):
        outs = [cur_s] if mode == "halve" else [refs.pop(0) for _ in range(mode)]
        col = 0
        for (i, lanes), r in zip(terms, right):
            lanes = lanes or (0, r.shape[1])
            at = slice(col, col + lanes[1] - lanes[0])
            total = tn(left[i][...], r[:, lanes[0] : lanes[1]])
            for pieces in got:
                wide = [g[:, at].astype(f32) for g in pieces]
                total = total + (wide[0] if len(wide) == 1 else jnp.concatenate(wide, 0))
            rows = total.shape[0] // len(outs)
            for k, out in enumerate(outs):
                out[:, at] = total[k * rows : (k + 1) * rows].astype(bf16)
            col += lanes[1] - lanes[0]
        if mode == "halve":
            if split == 0:
                keep, send = refs.pop(0), refs.pop(0)
            parity_split(cur_s, keep, send, split, chunk, place_ref[1])
            split += cur_s.shape[0] // 2


def plain_split(place, cur, bit, chunk):
    view = cur.reshape(-1, 2, chunk, cur.shape[1])
    pick = lambda i: lax.dynamic_index_in_dim(view, i, axis=1, keepdims=False)
    mine = place[1 + bit]
    return tuple(pick(i).reshape(-1, cur.shape[1]) for i in (mine, 1 - mine))


def products(place, lefts, specs, chunk):
    width = lefts[0].shape[1]
    halved = sum(mode == "halve" for _, _, mode in specs)
    if chunk % 16 and halved:
        whole = products(place, lefts, [(t, g, 1) for t, g, _ in specs], chunk)
        parts = [plain_split(place, cur, 0, chunk) for cur in whole]
        return [jnp.concatenate(side, axis=0) for side in zip(*parts)]
    plan = [
        ([(t[0], t[2] if len(t) > 2 else None) for t in terms], [len(p) for p in gots], mode)
        for terms, gots, mode in specs
    ]
    args = [place, *lefts]
    args += [t[1] for terms, _, _ in specs for t in terms]
    args += [g for _, gots, _ in specs for pieces in gots for g in pieces]
    cols = sum(t[2][1] - t[2][0] if len(t) > 2 else t[1].shape[1] for t in specs[0][0])
    outs = []
    for _, _, mode in specs:
        if mode != "halve":
            outs += [((width // mode, cols), bf16)] * mode
    if halved:
        outs += [((halved * width // 2, cols), bf16)] * 2
    kernel = functools.partial(products_kernel, lefts=len(lefts), plan=plan, chunk=chunk)
    return call(kernel, "products", args, outs, [((width, cols), bf16)], smem=1)


def add_split_kernel(place_ref, *refs, number, bit, chunk):
    keep_ref, send_ref, cur_s = refs[2 * number :]
    first = 0
    for a, b in zip(refs[:number], refs[number : 2 * number]):
        rows = a.shape[0]
        cur_s[first : first + rows] = (a[...].astype(f32) + b[...].astype(f32)).astype(bf16)
        first += rows
    parity_split(cur_s, keep_ref, send_ref, 0, chunk, place_ref[1 + bit])


def add_split(place, keeps, gots, bit, chunk):
    rows, cols = sum(v.shape[0] for v in keeps), keeps[0].shape[1]
    if chunk % 16:
        parts = [(a.astype(f32) + b.astype(f32)).astype(bf16) for a, b in zip(keeps, gots)]
        return plain_split(place, jnp.concatenate(parts, axis=0), bit, chunk)
    half = ((rows // 2, cols), bf16)
    kernel = functools.partial(add_split_kernel, number=len(keeps), bit=bit, chunk=chunk)
    args = (place, *keeps, *gots)
    return call(kernel, "add_split", args, [half, half], [((rows, cols), bf16)], smem=1)


def tokens_kernel(d0, d1, d2, d3, w0, w1, w_ref, first_ref, out_ref):
    cols = d0.shape[1]
    total = first_ref[...] + nn(d0[...], w0[...]) + nn(d1[...], w1[...])
    total = total + nn(d2[...], w_ref[0, 0:cols, :]) + nn(d3[...], w_ref[1, 0:cols, :])
    out_ref[...] = total.astype(bf16)


def tokens_grad(dmixed, weights, d_first):
    args = (*dmixed, *weights, d_first)
    return call(tokens_kernel, "tokens_grad", args, [(d_first.shape, bf16)])[0]


SHARED = 40
EACH = 16


def pack_kernel(hist_ref, near_ref, far_ref, u0, u1, u2, u3, v0, v1, v2, v3, v4, v5, keep_ref, send_ref, *, heads):
    keep_ref[...] = jnp.zeros_like(keep_ref)
    send_ref[...] = jnp.zeros_like(send_ref)
    for g, up in enumerate((u0, u1, u2, u3)):
        ref, first = (keep_ref, send_ref)[g // 2], (g % 2) * EACH
        for h in range(heads):
            for i, part in ((0, 0), (1, 2)):
                col = (part * heads + h) * HEAD_DIM
                row = (near_ref, far_ref)[g // 2][g % 2 : g % 2 + 1, col : col + 64]
                ref[first + h : first + h + 1, i * 64 : i * 64 + 64] = row
            row = hist_ref[g * heads + h : g * heads + h + 1, :]
            ref[first + heads + h : first + heads + h + 1, :] = row[:, :LANES]
            ref[first + 2 * heads + h : first + 2 * heads + h + 1, :NB1] = row[:, LANES:]
        for i in range(6):
            at = slice(first + 3 * heads + i, first + 3 * heads + i + 1)
            ref[at, :] = up[:, i * LANES : (i + 1) * LANES]
    for j, v in enumerate((v0, v1, v2, v3, v4, v5)):
        for i in range(6):
            at = slice(2 * EACH + 6 * j + i, 2 * EACH + 6 * j + i + 1)
            row = v[:, i * LANES : (i + 1) * LANES]
            keep_ref[at, :] = row
            send_ref[at, :] = row


def pack_sums(hist, near, far, ups, shared):
    args = (hist, near, far, *(v.reshape(1, -1) for v in ups), *(v.reshape(1, -1) for v in shared))
    outs = [((2 * EACH + SHARED, LANES), f32)] * 2
    heads = near.shape[1] // (3 * HEAD_DIM)
    return call(functools.partial(pack_kernel, heads=heads), "pack_sums", args, outs)


def unpack_kernel(keep_ref, got_ref, qv_ref, pos_ref, box_ref, up_ref, *shared, heads):
    total = keep_ref[...] + got_ref[...]
    for h in range(heads):
        for i in range(2):
            qv_ref[i : i + 1, h * 64 : h * 64 + 64] = total[h : h + 1, i * 64 : i * 64 + 64]
            box_ref[h, i : i + 1, :] = total[heads + h : heads + h + 1, i * NB2 : (i + 1) * NB2]
        pos_ref[h : h + 1, :] = total[2 * heads + h : 2 * heads + h + 1, :NB1]
    units = up_ref.shape[0] // LANES
    up_ref[...] = total[3 * heads : 3 * heads + units].reshape(up_ref.shape)
    for j, ref in enumerate(shared):
        rows = ref.shape[0] // LANES
        ref[...] = total[EACH + j * rows : EACH + (j + 1) * rows].reshape(ref.shape)


def unpack_sums(keep, got, heads, units, width):
    outs = [((2, heads * HEAD_DIM), f32), ((heads, NB1), f32), ((heads, 2, NB2), f32), ((units,), f32)]
    outs += [((width,), f32)] * 6
    return call(functools.partial(unpack_kernel, heads=heads), "unpack_sums", (keep, got), outs)


def last_kernel(keep_ref, got_ref, qkv_ref, out_ref):
    inner = qkv_ref.shape[2]
    for part in range(3):
        at = slice(part * inner, (part + 1) * inner)
        qkv_ref[part] = keep_ref[:, at].astype(f32) + got_ref[:, at].astype(f32)
    at = slice(3 * inner, 4 * inner)
    out_ref[...] = (keep_ref[:, at].astype(f32) + got_ref[:, at].astype(f32)).T


def last_sums(place, keep, got, bit, chunk):
    inner = keep.shape[1] // 4
    if chunk % 16 == 0 and lax.axis_size("pages") == 2 << bit:
        outs = [((3, chunk, inner), f32), ((inner, chunk), f32)]
        qkv, out = call(last_kernel, "last_sums", (keep, got), outs)
        return qkv.transpose(1, 0, 2), out
    total = finish(place, keep, got, bit, chunk)
    return total[:, : 3 * inner].reshape(-1, 3, inner), total[:, 3 * inner :].T


def core_swap(v):
    return lax.ppermute(v, "heads", [(i, i ^ 1) for i in range(4)])


def x_swap(v):
    return lax.ppermute(v, "heads", [(i, i ^ 2) for i in range(4)])


def page_swap(v, bit):
    return lax.ppermute(v, "pages", [(i, i ^ bit) for i in range(lax.axis_size("pages"))])


def after(value, *others):
    return lax.optimization_barrier((value, *others))[0]


def finish(place, keep, got, bit, chunk):
    last = lax.axis_size("pages").bit_length() - 1
    while bit + 1 < last:
        bit += 1
        keep, send = add_split(place, [keep], [got], bit, chunk)
        got = page_swap(send, 1 << bit)
    return keep.astype(f32) + got.astype(f32)


def add_all(v, bits):
    for bit in bits:
        v = v + page_swap(v, bit)
    return v


def unit_norm(values):
    centered = values - jnp.mean(values, axis=-1, keepdims=True)
    inv_std = lax.rsqrt(jnp.mean(centered * centered, axis=-1, keepdims=True) + EPSILON)
    return centered * inv_std, inv_std


def norm_grad(unit, inv_std, e):
    return inv_std * (
        e - jnp.mean(e, axis=-1, keepdims=True) - unit * jnp.mean(e * unit, axis=-1, keepdims=True)
    )


def on_device(
    tokens,
    w_qkv,
    qv_bias,
    w_out,
    out_bias,
    norm1_gain,
    norm1_shift,
    w_up,
    up_bias,
    w_down,
    down_bias,
    norm2_gain,
    norm2_shift,
    pos_table,
    box_table,
    receipt_lengths,
    page_boxes,
    out_cotangent,
):
    seq_len = tokens.shape[1]
    width = tokens.shape[2]
    heads_here = pos_table.shape[0]
    inner = heads_here * HEAD_DIM
    units = w_up.shape[1]
    own_page = lax.axis_index("heads")
    page_bits = [1 << b for b in range(lax.axis_size("pages").bit_length() - 1)]
    chunk = width // lax.axis_size("pages")
    me = lax.axis_index("pages")
    place = jnp.stack([own_page] + [(me >> b) & 1 for b in range(len(page_bits))]).astype(i32)
    tok = tokens.reshape(seq_len, width)

    own_qkv = w_qkv.reshape(width, 3 * inner).T
    c_qkv, c_out = core_swap(own_qkv), core_swap(w_out)
    half_a, half_b, small = start_parts(
        place, own_qkv, w_out, w_up, box_table, pos_table, qv_bias, up_bias
    )
    c_small = core_swap(small)
    mine_a = x_swap(half_a)
    mine_b = x_swap(half_b)
    x_down = x_swap(w_down)
    ids, vis_ids = make_ids(place, receipt_lengths, page_boxes)
    mine_a = after(mine_a, ids)

    near_w = ((own_qkv,), (after(c_qkv, mine_a),))
    near_att, near_bias, near_out, near_kept = attn_fwd(
        place, tok, near_w, (small, c_small), (ids, vis_ids), heads_here, (w_out, c_out)
    )
    half = width // 2
    theirs_a = page_swap(mine_a, 1)
    xc_mine_a, xc_theirs_a = core_swap(mine_a), core_swap(after(theirs_a, near_att))
    theirs_b = page_swap(after(mine_b, near_att), 1)
    xc_mine_b = core_swap(after(mine_b, near_att))
    far_w = ((mine_a, theirs_a), (after(xc_mine_a, xc_mine_b), xc_theirs_a))
    far_att, far_bias, far_out, far_kept, far_w = attn_fwd(
        place, tok, far_w, (mine_b, xc_mine_b), (ids, vis_ids), heads_here
    )
    far_proj = nn(far_att, far_out)
    c_up, c_down = core_swap(after(w_up, far_proj)), core_swap(after(w_down, far_proj))
    mine_b, theirs_b = lax.optimization_barrier((mine_b, theirs_b, far_proj))[:2]
    xc_theirs_b = core_swap(theirs_b)
    first_in = nn(near_att, near_out) + far_proj + out_bias + tok.astype(f32)
    unit1, inv1 = unit_norm(first_in)
    first_out = unit1 * norm1_gain + norm1_shift
    first_low = first_out.astype(bf16)

    def units_of(weights, little):
        up = nn(first_low, weights) + little
        cdf = 0.5 * (1.0 + lax.erf(up * math.sqrt(0.5)))
        slope = cdf + up * jnp.exp(-0.5 * up * up) * (1.0 / math.sqrt(2.0 * math.pi))
        return (up * cdf).astype(bf16), lax.optimization_barrier(slope.astype(bf16))

    littles = (near_bias[0], near_bias[1], far_bias[0], far_bias[1])
    own_units = units_of(w_up, littles[0])
    theirs_b = after(theirs_b, own_units[0])
    (x_up,) = join_rows(place, mine_b, theirs_b, 1, width)
    c_units = units_of(after(c_up, theirs_b), littles[1])
    (xc_up,) = join_rows(place, xc_mine_b, after(xc_theirs_b, x_up), 1, width)
    far_units = [units_of(w, t) for w, t in zip((x_up, xc_up), littles[2:])]
    hiddens, slopes = zip(own_units, c_units, *far_units)
    x_down = after(x_down, *hiddens)
    xc_down = core_swap(x_down)
    ups, downs = (w_up, c_up, x_up, xc_up), (w_down, c_down, x_down, xc_down)
    second_in = sum(nn(h, w) for h, w in zip(hiddens, downs)) + down_bias + first_out
    unit2, inv2 = unit_norm(second_in)
    layer_out = (unit2 * norm2_gain + norm2_shift).astype(bf16)

    def norm_back(unit, inv_std, gain, dy):
        return norm_grad(unit, inv_std, dy * gain), jnp.sum(dy * unit, axis=0), jnp.sum(dy, axis=0)

    ct = out_cotangent.reshape(seq_len, width).astype(f32)
    d_second, g_gain2, g_shift2 = norm_back(unit2, inv2, norm2_gain, ct)
    g_down_bias = jnp.sum(d_second, axis=0)
    d_ffn = d_second.astype(bf16)

    def core_swaps(pieces):
        return [core_swap(v) for v in pieces]

    to_c = products(
        place, [d_ffn], [([(0, hiddens[3])], [], 2), ([(0, hiddens[1])], [], 2)], chunk
    )
    got_xc, got_c = core_swaps(to_c[:2]), core_swaps(to_c[2:])
    d_ups = [(nt(d_ffn, w) * s.astype(f32)).astype(bf16) for w, s in zip(downs, slopes)]
    far_gd, own_gd = products(
        place,
        [after(d_ffn, *d_ups)],
        [([(0, hiddens[2])], [got_xc], 1), ([(0, hiddens[0])], [got_c], 1)],
        chunk,
    )
    got_xd = x_swap(far_gd)

    to_c = products(
        place,
        [after(first_low, far_gd)],
        [([(0, d_ups[3])], [], 2), ([(0, d_ups[1])], [], 2)],
        chunk,
    )
    got_xc, got_c = core_swaps(to_c[:2]), core_swaps(to_c[2:])
    d_mid = nt(d_ups[3], ups[3]) + nt(d_ups[1], ups[1])
    d_mid, d_own = lax.optimization_barrier((d_mid, d_ups[0], *to_c))[:2]
    d_mid = lax.optimization_barrier(d_mid + nt(d_own, ups[0])) + nt(d_ups[2], ups[2])
    keep_u, send_u = products(
        place,
        [after(first_low, d_mid)],
        [([(0, d_ups[0])], [got_c], "halve"), ([(0, d_ups[2])], [got_xc], "halve")],
        chunk,
    )
    got_yu = page_swap(send_u, 1)
    d_first, g_gain1, g_shift1 = norm_back(unit1, inv1, norm1_gain, after(d_second, send_u) + d_mid)
    g_out_bias = jnp.sum(d_first, axis=0)
    d_proj = d_first.astype(bf16)
    far_datt = nt(d_proj, far_out).astype(bf16)
    x_dmixed, xc_dmixed, far_sums, far_ds, far_dsv = attn_bwd(seq_len, far_kept, far_datt)

    lefts = [tok, d_proj]
    low, high = (0, inner), (inner, 2 * inner)
    to_c = products(place, lefts, [([(0, xc_dmixed), (1, far_att, high)], [], 2)], chunk)
    got_xc = core_swaps(to_c)
    near_datt = nt(after(d_proj, *to_c), near_out).astype(bf16)
    (far_gq,) = products(
        place, [after(tok, near_datt), d_proj], [([(0, x_dmixed), (1, far_att, low)], [got_xc], 1)], chunk
    )
    got_xq = x_swap(far_gq)
    own_dmixed, c_dmixed, near_sums, near_ds, near_dsv = attn_bwd(
        seq_len, near_kept, after(near_datt, far_gq)
    )
    dmixed = (own_dmixed, c_dmixed, x_dmixed, xc_dmixed)

    got_xd, got_yu = lax.optimization_barrier((got_xd, got_yu, near_sums))[:2]
    keep_d, send_d = add_split(place, [own_gd], [got_xd], 0, chunk)
    got_yd = page_swap(send_d, 1)
    keep_u, send_u = add_split(place, [keep_u], [got_yu], 1, chunk)
    got_zu = page_swap(send_u, 2)
    to_c = products(
        place,
        [after(tok, send_u, send_d), d_proj],
        [([(0, c_dmixed), (1, near_att, high)], [], 2)],
        chunk,
    )
    got_cq = core_swaps(to_c)
    near_far = (near_dsv, far_dsv)
    hist = lambda acc, blocks: add_hist(
        place, receipt_lengths, acc, ids, (near_ds, far_ds), blocks, seq_len - TEXT
    )
    acc = after(jnp.zeros((16, 160), f32), *to_c)
    acc = hist(acc, (0, 1))
    keep_q, send_q = products(
        place,
        [after(tok, acc), d_proj],
        [([(0, own_dmixed), (1, near_att, low)], [got_cq, [got_xq]], "halve")],
        chunk,
    )
    got_yq = page_swap(send_q, 1)
    keep_u, send_u = add_split(place, [keep_u], [after(got_zu, send_q)], 2, chunk)
    got_zu = page_swap(send_u, 4)
    keep_d, send_d = add_split(place, [keep_d], [after(got_yd, send_u)], 1, chunk)
    got_zd = page_swap(send_d, 2)
    acc = hist(after(acc, send_q, send_d), (2, 3))
    keep_q, send_q = add_split(place, [keep_q], [after(got_yq, acc)], 1, chunk)
    got_zq = page_swap(send_q, 2)
    acc = add_visual(after(acc, send_q), vis_ids, near_far)
    g_up_bias = [jnp.sum(d.astype(f32), axis=0) for d in d_ups]
    shared = (g_out_bias, g_gain1, g_shift1, g_down_bias, g_gain2, g_shift2)
    keep, send = pack_sums(acc, near_sums, far_sums, g_up_bias, shared)
    got = x_swap(send)
    keep_d, send_d = add_split(place, [keep_d], [after(got_zd, send)], 2, chunk)
    got_zd = page_swap(send_d, 4)
    got_zu = after(got_zu, send_d)
    both_u = finish(place, keep_u, got_zu, 2, chunk)
    got_xu = x_swap(both_u[chunk:].astype(bf16))
    sums = keep + after(got, send_d)
    sums = jnp.concatenate((sums[:EACH], sums[2 * EACH :])) + core_swap(sums[EACH:])
    got = page_swap(sums, 1)
    grad_tokens = tokens_grad(dmixed, (own_qkv, c_qkv, after(far_w, sums)), d_first)
    sums = sums + after(got, grad_tokens)
    got = page_swap(sums, 2)
    keep_q, send_q = add_split(place, [keep_q], [after(got_zq, sums)], 2, chunk)
    got_zq = page_swap(send_q, 4)
    sums = sums + after(got, send_q)
    got = page_swap(sums, 4)
    for bit in page_bits[3:]:
        sums = sums + got
        got = page_swap(sums, bit)
    got_zd, got_xu = lax.optimization_barrier((got_zd, got_xu, sums))[:2]
    g_w_down = finish(place, keep_d, got_zd, 2, chunk).T
    g_w_up = both_u[:chunk] + got_xu.astype(f32)
    got, got_zq, g_w_down, g_w_up = lax.optimization_barrier((got, got_zq, g_w_down, g_w_up))
    g_w_qkv, g_w_out = last_sums(place, keep_q, got_zq, 2, chunk)
    g_qv_bias, g_pos, g_box, g_up_bias, *shared = unpack_sums(sums, got, heads_here, units, width)
    g_box = g_box.transpose(1, 0, 2)
    return (
        layer_out.reshape(tokens.shape),
        grad_tokens.reshape(tokens.shape),
        g_w_qkv,
        g_qv_bias,
        g_w_out,
        shared[0],
        shared[1],
        shared[2],
        g_w_up,
        g_up_bias,
        g_w_down,
        shared[3],
        shared[4],
        shared[5],
        g_pos,
        g_box,
    )


def solution(mesh):
    placed = (
        P(("pages", "heads"), None, None),
        P(None, None, "heads"),
        P(None, "heads"),
        P("heads", None),
        P(),
        P(),
        P(),
        P(None, "heads"),
        P("heads"),
        P("heads", None),
        P(),
        P(),
        P(),
        P("heads", None),
        P(None, "heads", None),
        P("pages", None),
        P("pages", None, None),
        P(("pages", "heads"), None, None),
    )
    return jax.shard_map(
        on_device,
        mesh=mesh,
        in_specs=placed,
        out_specs=(
            P(("pages", "heads"), None, None),
            P(("pages", "heads"), None, None),
            P("pages", None, "heads"),
            P(None, "heads"),
            P("heads", "pages"),
            P(),
            P(),
            P(),
            P("pages", "heads"),
            P("heads"),
            P("heads", "pages"),
            P(),
            P(),
            P(),
            P("heads", None),
            P(None, "heads", None),
        ),
        check_vma=False,
    )
```

```python
import functools
import math

import jax
import jax.numpy as jnp
from jax import lax
from jax.experimental import pallas as pl
from jax.experimental.pallas import tpu as pltpu
from jax.sharding import PartitionSpec as P

f32 = jnp.float32
bf16 = jnp.bfloat16
i32 = jnp.int32
EPSILON = 1e-05
MASKED_SCORE = -1e30


HEAD_DIM = 64
TEXT = 512
NB1 = 32
MD1 = 128
NB2 = 64
MD2 = 256
ROWS = 576
VIS = ROWS - TEXT
QROWS = 640
LANES = 128
CHUNK = 64
UNIT = 2048.0
BLOCKS = ((0, 256), (0, 384), (128, 384), (256, 256))
OFFS = (0, 320, 768, 1216)
SPAN = 1536
Q_AT = SPAN
KV_AT = Q_AT + ROWS
PV_AT = KV_AT + ROWS
KEPT = PV_AT + ROWS // 2
SMALL = 24


def thresholds(buckets, max_reach):
    half_range = buckets // 2
    exact_range = half_range // 2
    levels = half_range - exact_range
    return [
        math.ceil(exact_range * (max_reach / exact_range) ** (k / levels) - 1e-09)
        for k in range(1, levels)
    ]


def bucket_of(diff, buckets, reach):
    n = jnp.abs(diff)
    out = jnp.minimum(n, buckets // 4) + jnp.where(diff > 0, buckets // 2, 0)
    for t in thresholds(buckets, reach):
        out = out + jnp.where(n >= t, 1, 0)
    return out


def parts_of(blk):
    s, n = BLOCKS[blk]
    return ((s, n, OFFS[blk]), (TEXT, VIS, OFFS[blk] + n))


def nt(a, b):
    return lax.dot_general(a, b, (((1,), (1,)), ((), ())), preferred_element_type=f32)


def nn(a, b):
    return lax.dot_general(a, b, (((1,), (0,)), ((), ())), preferred_element_type=f32)


def unpack(ids):
    return ids & 255, (ids >> 8) & 255, ids >> 16


def take(tab, idx):
    return jnp.take_along_axis(
        jnp.broadcast_to(tab, idx.shape), idx, axis=1, mode="promise_in_bounds"
    )


def ids_kernel(place_ref, len_ref, box_ref, ids_ref, vis_ref, some_ref, c_s, r_s, *, valid):
    page = place_ref[0]
    row = lax.broadcasted_iota(i32, (8, ROWS), 1)
    segment = jnp.zeros((8, ROWS), i32)
    end = 0
    for i in range(len_ref.shape[1]):
        end = end + len_ref[page, i]
        segment = segment + jnp.where(row >= end, 1, 0)
    c_s[...] = jnp.zeros_like(c_s)
    c_s[0:8, :] = segment.astype(f32)
    c_s[8:10, 0:valid] = box_ref[page].astype(f32)
    r_s[...] = c_s[...].T.astype(i32)

    def query(lo, hi):
        return tuple(c_s[i : i + 1, lo:hi].astype(i32) for i in (0, 8, 9))

    def tiles(row, out, rows, q_first, q):
        qseg, qx, qy = (jnp.broadcast_to(v, (CHUNK, LANES)) for v in q)
        lane = lax.broadcasted_iota(i32, (CHUNK, LANES), 1)
        if q_first == TEXT:
            q_pos, high = TEXT + (lane & (VIS - 1)), jnp.where(lane >= VIS, NB2, 0)
        else:
            q_pos, high = q_first + lane, 0

        def tile(c, _):
            at = pl.ds(pl.multiple_of(row + c * CHUNK, CHUNK), CHUNK)
            here = pl.ds(pl.multiple_of(out + c * CHUNK, CHUNK), CHUNK)
            seg, kx, ky = (jnp.broadcast_to(r_s[at, i : i + 1], (CHUNK, LANES)) for i in (0, 8, 9))
            k_pos = lax.broadcasted_iota(i32, (CHUNK, LANES), 0) + (row + c * CHUNK)
            x_id = bucket_of(kx - qx, NB2, MD2)
            y_id = bucket_of(ky - qy, NB2, MD2)
            p_id = bucket_of(k_pos - q_pos, NB1, MD1)
            ok = ((seg == qseg) | (k_pos >= TEXT) | (q_pos >= TEXT)) & (k_pos < valid)
            p_id = jnp.where(ok, p_id, NB1)
            y_id = y_id + (high if q_first == TEXT else NB2)
            ref, at = (vis_ref, at) if q_first == TEXT else (ids_ref, here)
            ref[at, :] = (x_id + high) + y_id * 256 + (p_id + high) * 65536
            if q_first != TEXT:
                some_ref[out // CHUNK + c] = jnp.max(jnp.where(ok, 1, 0))
            return 0

        lax.fori_loop(0, rows // CHUNK, tile, 0)

    for blk in range(4):
        q = query(blk * LANES, (blk + 1) * LANES)
        for s, n, o in parts_of(blk):
            tiles(s, o, n, blk * LANES, q)
    q = tuple(jnp.concatenate((v, v), axis=1) for v in query(TEXT, ROWS))
    tiles(0, 0, ROWS, TEXT, q)


def make_ids(place, lengths, boxes):
    return pl.pallas_call(
        functools.partial(ids_kernel, valid=boxes.shape[2]),
        in_specs=[
            pl.BlockSpec(memory_space=pltpu.SMEM),
            pl.BlockSpec(memory_space=pltpu.SMEM),
            pl.BlockSpec(memory_space=pltpu.VMEM),
        ],
        out_specs=[
            pl.BlockSpec(memory_space=pltpu.VMEM),
            pl.BlockSpec(memory_space=pltpu.VMEM),
            pl.BlockSpec(memory_space=pltpu.SMEM),
        ],
        out_shape=[
            jax.ShapeDtypeStruct((SPAN, LANES), i32),
            jax.ShapeDtypeStruct((ROWS, LANES), i32),
            jax.ShapeDtypeStruct((SPAN // CHUNK,), i32),
        ],
        scratch_shapes=[pltpu.VMEM((LANES, ROWS), f32), pltpu.VMEM((ROWS, LANES), i32)],
        name="ids",
        cost_estimate=pl.CostEstimate(flops=0, bytes_accessed=0, transcendentals=0),
        compiler_params=pltpu.CompilerParams(vmem_limit_bytes=12 << 20),
    )(place, lengths, boxes)


def place(dst_ref, pair, first, side, cols):
    at = slice(side * 192, side * 192 + 64)
    dst_ref[pair, first : first + ROWS, at] = cols


def stacked(both):
    return jnp.concatenate((both[:, :LANES], both[:, LANES:]), 0)


def block(ref, pair, first, blk):
    rows = LANES if blk < 4 else VIS
    return stacked(ref[pair, first + blk * LANES : first + blk * LANES + rows, :])


def load_rows(refs, odd, dst):
    if len(refs) == 1:
        dst[0 : refs[0].shape[0], :] = refs[0][...]
    else:
        half = dst.shape[0] // 2
        for first in range(2):

            @pl.when(odd == first)
            def _(first=first):
                dst[first * half : (first + 1) * half, :] = refs[0][0:half, :]
                dst[(1 - first) * half : (2 - first) * half, :] = refs[1][0:half, :]


def pad_rows(v):
    return jnp.concatenate((v, jnp.zeros((ROWS - v.shape[0], v.shape[1]), v.dtype)), 0)


def fold(both):
    n = both.shape[1] // 2
    t = both.T
    lane = lax.broadcasted_iota(i32, (n, LANES), 1)
    return jnp.where(lane < 64, t[:n], t[n:])


def fwd_kernel(place_ref, tok_ref, *refs, pieces, pairs):
    *refs, n_s, b_s = refs
    for i in range(3):
        far = lax.broadcasted_iota(i32, (LANES, LANES), 0) - lax.broadcasted_iota(i32, (LANES, LANES), 1)
        n_s[i] = bucket_of(far + (i - 1) * LANES, NB1, MD1)
    n = 2 * pieces
    weights = (refs[:pieces], refs[pieces:n])
    small, (ids_ref, vis_ref) = refs[n : n + 2], refs[n + 2 : n + 4]
    wo_refs, refs = (refs[n + 4 : n + 6], refs[n + 6 :]) if pieces == 1 else (None, refs[n + 4 :])
    out_ref, bias_ref, wo_ref, kept_ref = refs[:4]
    w_s = refs[4] if pieces > 1 else None
    vt_s, s_s, i_s, f_s, o_s, l_s = refs[-6:]
    first = small[0].shape[0] - 16
    inner = pairs * HEAD_DIM
    units = 4 * pairs // 6
    bias_ref[...] = jnp.zeros_like(bias_ref)
    for g in range(2):
        bias_ref[g : g + 1, :] = small[g][first + units : first + units + 1, :].astype(f32)
        for i in range(4 * pairs):
            at = slice(i % 6 * LANES, (i % 6 + 1) * LANES)
            row = first + i // 6
            high, rest = (small[g][r : r + 1, at].astype(f32) for r in (row, row + 8))
            l_s[g, i : i + 1, :] = high + rest
    small = [l_s.at[g] for g in range(2)]
    tok = pad_rows(tok_ref[...])
    for pair in range(pairs):
        kept_ref[pair, Q_AT:KV_AT, :] = jnp.zeros((ROWS, 256), bf16)
    for g in range(2):
        if pieces > 1:
            load_rows(weights[g], place_ref[1], w_s.at[g])
            w_ref = w_s.at[g]
            wo_ref[g * inner : (g + 1) * inner, :] = w_ref[3 * inner :, :]
        else:
            w_ref = weights[g][0]
            wo_ref[g * inner : (g + 1) * inner, :] = wo_refs[g][...]
        for part in range(3):
            mixed = nt(tok, w_ref[part * inner : (part + 1) * inner, :])
            for local in range(pairs):
                pair, side = divmod(g * pairs + local, 2)
                at = slice(side * 64, side * 64 + 64)
                cols = mixed[:, local * 64 : local * 64 + 64]
                if part == 0:
                    cols = cols + small[g][2 * pairs + local : 2 * pairs + local + 1, :64]
                    place(kept_ref, pair, Q_AT, side, (cols * (UNIT / 8)).astype(bf16))
                elif part == 1:
                    kept_ref[pair, KV_AT:PV_AT, at] = cols.astype(bf16)
                else:
                    cols = cols + small[g][3 * pairs + local : 3 * pairs + local + 1, :64]
                    low = slice(LANES + side * 64, LANES + side * 64 + 64)
                    kept_ref[pair, KV_AT:PV_AT, low] = cols.astype(bf16)
                    vt_s[pair, at, :] = cols.T.astype(bf16)
    for pair in range(pairs):
        (ga, la), (gb, lb) = divmod(2 * pair, pairs), divmod(2 * pair + 1, pairs)
        for row, start in ((0, 0), (1, pairs)):
            a = small[ga][start + la : start + la + 1, :] * UNIT
            b = small[gb][start + lb : start + lb + 1, :] * UNIT
            i_s[pair, row : row + 1, :] = (
                jnp.round(a).astype(i32) * 65536 + jnp.round(b).astype(i32)
            )
            f_s[pair, 2 * row : 2 * row + 1, :] = jnp.concatenate((a[:, :64], b[:, :64]), 1)
            f_s[pair, 2 * row + 1 : 2 * row + 2, :] = jnp.concatenate((a[:, 64:], b[:, 64:]), 1)

    def softmax(total, wide, p_at):
        m = jnp.full((8, wide), -3e38, f32)
        for c in range(0, total, 8):
            m = jnp.maximum(m, s_s[c : c + 8, :wide])
        m = jnp.max(m, axis=0, keepdims=True)
        l = jnp.zeros((8, wide), f32)
        for c in range(0, total, 8):
            e = jnp.exp2((s_s[c : c + 8, :wide] - m) * (math.log2(math.e) / UNIT))
            s_s[c : c + 8, :wide] = e
            l = l + e
        inv = 1.0 / jnp.sum(l, axis=0, keepdims=True)
        for c in range(0, total, 16):
            p_at(c, (s_s[c : c + 16, :wide] * inv).astype(bf16))

    def one_pair(pair, _):
        t_xy, t_p = (i_s[pair, i : i + 1, :] for i in range(2))
        v_x, v_y, v_p = (f_s[pair, i : i + 1, :] for i in range(3))
        for i in range(3):
            for c in range(0, LANES, 16):
                b_s[i, c : c + 16, :] = take(t_p, n_s[i, c : c + 16, :])
        for blk in range(4):
            q = block(kept_ref, pair, Q_AT, blk)
            first = OFFS[blk]
            for s, n, o in parts_of(blk):
                sc = nt(kept_ref[pair, KV_AT + s : KV_AT + s + n, :LANES], q)
                for c in range(0, n, 16):
                    r = slice(o + c, o + c + 16)
                    x, y, p = unpack(ids_ref[r, :])
                    if s < TEXT:
                        tile, row = divmod(s + c, LANES)
                        b_p = b_s[tile - blk + 1, row : row + 16, :]
                    else:
                        b_p = take(t_p, p)
                    b = take(t_xy, x) + take(t_xy, y) + b_p
                    low = (b << 16) >> 16
                    high = (b - low) >> 16
                    add = jnp.where(p == NB1, MASKED_SCORE, 0.0)
                    to = slice(o - first + c, o - first + c + 16)
                    s_s[to, :LANES] = sc[c : c + 16, :LANES] + (high.astype(f32) + add)
                    s_s[to, LANES:] = sc[c : c + 16, LANES:] + (low.astype(f32) + add)

            def put(c, v, first=first):
                kept_ref[pair, first + c : first + c + 16, :] = v

            softmax(BLOCKS[blk][1] + VIS, 256, put)
            ot = sum(
                nn(vt_s[pair, :, s : s + n], kept_ref[pair, o : o + n, :]) for s, n, o in parts_of(blk)
            )
            o_s[pair, blk * LANES : (blk + 1) * LANES, :] = fold(ot).astype(bf16)
        q = block(kept_ref, pair, Q_AT, 4)
        sc = nt(kept_ref[pair, KV_AT:PV_AT, :LANES], q)
        for c in range(0, ROWS, 16):
            x, y, p = unpack(vis_ref[c : c + 16, :])
            b = take(v_x, x) + take(v_y, y) + take(v_p, p)
            add = jnp.where((p & (NB2 - 1)) == NB1, MASKED_SCORE, 0.0)
            s_s[c : c + 16, :LANES] = sc[c : c + 16] + (b + add)

        def put_v(c, v):
            side, row = divmod(c, ROWS // 2)
            at = slice(side * LANES, (side + 1) * LANES)
            kept_ref[pair, PV_AT + row : PV_AT + row + 16, at] = v

        softmax(ROWS, LANES, put_v)
        o_s[pair, TEXT:ROWS, :] = fold(nn(vt_s[pair], stacked(kept_ref[pair, PV_AT:KEPT, :]))).astype(bf16)
        return 0

    lax.fori_loop(0, pairs, one_pair, 0, unroll=True)
    rows = out_ref.shape[0]
    for pair in range(pairs):
        out_ref[:, pair * LANES : (pair + 1) * LANES] = o_s[pair, 0:rows, :]


def attn_fwd(place, tok, weights, small, ids, pairs, w_out=()):
    pieces, (rows, width) = len(weights[0]), tok.shape
    vmem = pl.BlockSpec(memory_space=pltpu.VMEM)
    outs = [((rows, pairs * LANES), bf16), ((8, width), f32), ((pairs * LANES, width), bf16)]
    outs += [((pairs, KEPT, 256), bf16)]
    if pieces > 1:
        outs += [((2, 4 * pairs * HEAD_DIM, width), bf16)]
    args = (place, tok, *weights[0], *weights[1], *small, *ids, *w_out)
    return pl.pallas_call(
        functools.partial(fwd_kernel, pieces=pieces, pairs=pairs),
        in_specs=[pl.BlockSpec(memory_space=pltpu.SMEM)] + [vmem] * (len(args) - 1),
        out_specs=[vmem] * len(outs),
        out_shape=[jax.ShapeDtypeStruct(shape, dtype) for shape, dtype in outs],
        scratch_shapes=[
            pltpu.VMEM((pairs, LANES, ROWS), bf16),
            pltpu.VMEM((ROWS, 256), f32),
            pltpu.VMEM((pairs, 8, LANES), i32),
            pltpu.VMEM((pairs, 8, LANES), f32),
            pltpu.VMEM((pairs, ROWS, LANES), bf16),
            pltpu.VMEM((2, SMALL, LANES), f32),
            pltpu.VMEM((3, LANES, LANES), i32),
            pltpu.VMEM((3, LANES, LANES), i32),
        ],
        name="attn_fwd",
        cost_estimate=pl.CostEstimate(flops=0, bytes_accessed=0, transcendentals=0),
        compiler_params=pltpu.CompilerParams(vmem_limit_bytes=14 << 20),
    )(*args)


def bwd_kernel(kept_ref, do_ref, out0_ref, out1_ref, sum_ref, ds_ref, dsv_ref, do_s, kt_s, dq_s, dk_s, dv_s, *, pairs):
    rows = out0_ref.shape[0]
    sum_ref[...] = jnp.zeros_like(sum_ref)
    do_s[...] = jnp.zeros_like(do_s)
    for h in range(2 * pairs):
        pair, side = divmod(h, 2)
        place(do_s, pair, 0, side, pad_rows(do_ref[:, h * 64 : h * 64 + 64]))
    for pair in range(pairs):
        kt_s[pair] = kept_ref[pair, KV_AT:PV_AT, :LANES].astype(f32).T.astype(bf16)

    def grad_scores(dps, ps, put):
        d = jnp.zeros((8, dps[0].shape[1]), f32)
        for dp, p in zip(dps, ps):
            for c in range(0, dp.shape[0], 16):
                t = p(c).astype(f32) * dp[c : c + 16]
                d = d + (t[:8] + t[8:])
        d = jnp.sum(d, axis=0, keepdims=True)
        for i, (dp, p) in enumerate(zip(dps, ps)):
            for c in range(0, dp.shape[0], 16):
                put(i, c, (p(c).astype(f32) * (dp[c : c + 16] - d)).astype(bf16))

    def one_pair(pair, _):
        dv_s[...] = jnp.zeros_like(dv_s)
        dk_s[...] = jnp.zeros_like(dk_s)
        for blk in range(4):
            q = block(kept_ref, pair, Q_AT, blk)
            do = block(do_s, pair, 0, blk)
            parts = parts_of(blk)

            def put(i, c, v, parts=parts):
                ds_ref[pair, parts[i][2] + c : parts[i][2] + c + 16, :] = v

            grad_scores(
                [nt(kept_ref[pair, KV_AT + s : KV_AT + s + n, LANES:], do) for s, n, o in parts],
                [lambda c, o=o: kept_ref[pair, o + c : o + c + 16, :] for s, n, o in parts],
                put,
            )
            dq = 0.0
            for s, n, o in parts:
                ds = ds_ref[pair, o : o + n, :]
                dq = dq + nn(kt_s[pair, :, s : s + n], ds)
                dv_s[s : s + n, :] += nn(kept_ref[pair, o : o + n, :], do)
                dk_s[s : s + n, :] += nn(ds, q)
            dq_s[pair, 0, blk * LANES : (blk + 1) * LANES, :] = (fold(dq) * 0.125).astype(bf16)
        q = block(kept_ref, pair, Q_AT, 4)
        do = block(do_s, pair, 0, 4)
        pv = stacked(kept_ref[pair, PV_AT:KEPT, :])

        def put_v(i, c, v):
            dsv_ref[pair, c : c + 16, :] = v

        grad_scores([nt(kept_ref[pair, KV_AT:PV_AT, LANES:], do)], [lambda c: pv[c : c + 16]], put_v)
        ds = dsv_ref[pair]
        dq_s[pair, 0, TEXT:ROWS, :] = (fold(nn(kt_s[pair], ds)) * 0.125).astype(bf16)
        dq_s[pair, 1] = ((dk_s[...] + nn(ds, q)) * (1.0 / UNIT)).astype(bf16)
        dq_s[pair, 2] = (dv_s[...] + nn(pv, do)).astype(bf16)
        return 0

    lax.fori_loop(0, pairs, one_pair, 0)
    for h in range(2 * pairs):
        pair, side = divmod(h, 2)
        g, local = divmod(h, pairs)
        for part in range(3):
            col = part * pairs * HEAD_DIM + local * HEAD_DIM
            here = dq_s[pair, part, 0:rows, side * 64 : side * 64 + 64]
            (out0_ref, out1_ref)[g][:, col : col + 64] = here
            if part != 1:
                total = jnp.sum(here.astype(f32), axis=0, keepdims=True)
                sum_ref[g : g + 1, col : col + 64] = total


def attn_bwd(rows, kept, d_att):
    pairs = kept.shape[0]
    cols = 3 * pairs * HEAD_DIM
    vmem = pl.BlockSpec(memory_space=pltpu.VMEM)
    outs = [((rows, cols), bf16)] * 2 + [((8, cols), f32)]
    outs += [((pairs, SPAN, 256), bf16), ((pairs, ROWS, LANES), bf16)]
    return pl.pallas_call(
        functools.partial(bwd_kernel, pairs=pairs),
        in_specs=[vmem] * 2,
        out_specs=[vmem] * 5,
        out_shape=[jax.ShapeDtypeStruct(shape, dtype) for shape, dtype in outs],
        scratch_shapes=[
            pltpu.VMEM((pairs, ROWS, 256), bf16),
            pltpu.VMEM((pairs, LANES, ROWS), bf16),
            pltpu.VMEM((pairs, 3, ROWS, LANES), bf16),
            pltpu.VMEM((ROWS, LANES), f32),
            pltpu.VMEM((ROWS, LANES), f32),
        ],
        name="attn_bwd",
        cost_estimate=pl.CostEstimate(flops=0, bytes_accessed=0, transcendentals=0),
        compiler_params=pltpu.CompilerParams(vmem_limit_bytes=14 << 20),
    )(kept, d_att)


HSTEP = 64
HBLOCK = 192


def hist_kernel(some_ref, acc_ref, ids_ref, *refs, sets, pairs, first_id):
    ds_refs, hist_ref, l_s = refs[:sets], refs[-2], refs[-1]
    heads = 2 * sets * pairs

    @pl.when(pl.program_id(0) == 0)
    def _():
        hist_ref[...] = acc_ref[...]

    for h in range(heads, 16):
        l_s[pl.ds(h, HSTEP, stride=16), :] = jnp.zeros((HSTEP, LANES), f32)
    steps = HBLOCK // HSTEP

    @pl.loop(0, steps)
    def _(r):
        @pl.when(some_ref[(first_id + pl.program_id(0)) * steps + r] > 0)
        def _():
            first = pl.multiple_of(r * HSTEP, HSTEP)
            for pair in range(sets * pairs):
                ref = ds_refs[pair // pairs]
                for side in range(2):
                    at = slice(side * LANES, (side + 1) * LANES)
                    v = ref[pair % pairs, pl.ds(first, HSTEP), at].astype(f32)
                    l_s[pl.ds(2 * pair + side, HSTEP, stride=16), :] = v
            ids = lambda u: ids_ref[pl.ds(first + u, 1), :]
            hist_ref[...] += hot_sums(l_s, ids, HSTEP, NB2)


def hot_sums(l_s, ids, rows, y_from):
    io = lax.broadcasted_iota(i32, (NB2, LANES), 0)
    lhs, rhs = [], []
    for u in range(rows):
        x, y, p = unpack(ids(u))
        if y_from:
            y = y - y_from
        else:
            x, y, p = (v & (NB2 - 1) for v in (x, y, p))
        hot = [jnp.where(io == x, 1.0, 0.0), jnp.where(io == y, 1.0, 0.0)]
        hot.append(jnp.where(io[:NB1] == p, 1.0, 0.0))
        rhs.append(jnp.concatenate(hot, 0).astype(bf16))
        lhs.append(l_s[u * 16 : u * 16 + 16, :].astype(bf16))
    return nt(jnp.concatenate(lhs, 1), jnp.concatenate(rhs, 1))


VSTEP = 72


def visual_kernel(acc_ref, ids_ref, *refs, sets, pairs):
    ds_refs, hist_ref, l_s, i_s = refs[:sets], refs[-3], refs[-2], refs[-1]
    heads = 2 * sets * pairs
    far = ROWS // 2
    lane = lax.broadcasted_iota(i32, (VSTEP, LANES), 1)
    hist_ref[...] = acc_ref[...]
    for h in range(heads, 16):
        l_s[pl.ds(h, VSTEP, stride=16), :] = jnp.zeros((VSTEP, LANES), f32)

    @pl.loop(0, far // VSTEP)
    def _(r):
        here = pl.ds(pl.multiple_of(r * VSTEP, 8), VSTEP)
        there = pl.ds(pl.multiple_of(far + r * VSTEP, 8), VSTEP)
        i_s[...] = jnp.where(lane < VIS, ids_ref[here, :], ids_ref[there, :])
        for pair in range(sets * pairs):
            ref = ds_refs[pair // pairs]
            a, b = (ref[pair % pairs, at, :].astype(f32) for at in (here, there))
            one = jnp.where(lane < VIS, a, pltpu.roll(b, VIS, axis=1))
            two = jnp.where(lane < VIS, pltpu.roll(a, VIS, axis=1), b)
            l_s[pl.ds(2 * pair, VSTEP, stride=16), :] = one
            l_s[pl.ds(2 * pair + 1, VSTEP, stride=16), :] = two
        hist_ref[...] += hot_sums(l_s, lambda u: i_s[u : u + 1, :], VSTEP, 0)


def add_visual(acc, ids, ds):
    vmem = pl.BlockSpec(memory_space=pltpu.VMEM)
    return pl.pallas_call(
        functools.partial(visual_kernel, sets=len(ds), pairs=ds[0].shape[0]),
        grid=(1,),
        in_specs=[
            pl.BlockSpec((16, 160), lambda i: (0, 0)),
            pl.BlockSpec((ROWS, LANES), lambda i: (0, 0)),
        ]
        + [pl.BlockSpec(t.shape, lambda i: (0, 0, 0)) for t in ds],
        out_specs=pl.BlockSpec((16, 160), lambda i: (0, 0)),
        out_shape=jax.ShapeDtypeStruct((16, 160), f32),
        scratch_shapes=[pltpu.VMEM((VSTEP * 16, LANES), f32), pltpu.VMEM((VSTEP, LANES), i32)],
        name="hist",
        cost_estimate=pl.CostEstimate(flops=0, bytes_accessed=0, transcendentals=0),
        compiler_params=pltpu.CompilerParams(vmem_limit_bytes=12 << 20),
    )(acc, ids, *ds)


def add_hist(acc, ids, some, ds, first_row, rows):
    first = first_row // HBLOCK
    specs = [
        pl.BlockSpec(memory_space=pltpu.SMEM),
        pl.BlockSpec((16, 160), lambda i: (0, 0)),
        pl.BlockSpec((HBLOCK, LANES), lambda i: (first + i, 0)),
    ]
    for t in ds:
        specs.append(pl.BlockSpec((t.shape[0], HBLOCK, t.shape[2]), lambda i: (0, first + i, 0)))
    return pl.pallas_call(
        functools.partial(hist_kernel, sets=len(ds), pairs=ds[0].shape[0], first_id=first),
        grid=(rows // HBLOCK,),
        in_specs=specs,
        out_specs=pl.BlockSpec((16, 160), lambda i: (0, 0)),
        out_shape=jax.ShapeDtypeStruct((16, 160), f32),
        scratch_shapes=[pltpu.VMEM((HSTEP * 16, LANES), f32)],
        name="hist",
        cost_estimate=pl.CostEstimate(flops=0, bytes_accessed=0, transcendentals=0),
        compiler_params=pltpu.CompilerParams(vmem_limit_bytes=12 << 20),
    )(some, acc, ids, *ds)


def call(kernel, name, args, outs, scratch=(), smem=0):
    vmem = pl.BlockSpec(memory_space=pltpu.VMEM)
    return pl.pallas_call(
        kernel,
        in_specs=[pl.BlockSpec(memory_space=pltpu.SMEM)] * smem + [vmem] * (len(args) - smem),
        out_shape=[jax.ShapeDtypeStruct(shape, dtype) for shape, dtype in outs],
        scratch_shapes=[pltpu.VMEM(shape, dtype) for shape, dtype in scratch],
        name=name,
        cost_estimate=pl.CostEstimate(flops=0, bytes_accessed=0, transcendentals=0),
        compiler_params=pltpu.CompilerParams(vmem_limit_bytes=12 << 20),
    )(*args)


def start_kernel(place_ref, qkv_ref, wo_ref, up_ref, box_ref, pos_ref, qv_ref, ub_ref, a_ref, b_ref, small_ref, s_s, o_s, sems):
    half = a_ref.shape[0]
    odd = place_ref[1]

    def copy(src, dst, i):
        return pltpu.make_async_copy(src, dst, sems.at[i])

    tail = qkv_ref.shape[0] - half
    firsts = [copy(qkv_ref.at[0:half, :], a_ref.at[0:half, :], 0)]
    seconds = [
        copy(qkv_ref.at[half:, :], a_ref.at[0:tail, :], 0),
        copy(wo_ref, a_ref.at[tail:half, :], 1),
    ]

    @pl.when(odd == 0)
    def _():
        for c in firsts:
            c.start()

    @pl.when(odd == 1)
    def _():
        for c in seconds:
            c.start()

    at = pl.ds(pl.multiple_of(odd * half, half), half)
    others = [copy(up_ref.at[at, :], b_ref.at[0:half, :], 2)]
    for c in others:
        c.start()
    heads = pos_ref.shape[0]
    s_s[...] = jnp.zeros_like(s_s)
    for h in range(heads):
        s_s[h : h + 1, :NB2] = box_ref[h, 0:1, :]
        s_s[h : h + 1, NB2:] = box_ref[h, 1:2, :]
        s_s[heads + h : heads + h + 1, :NB1] = pos_ref[h : h + 1, :]
        for i in range(2):
            row = (2 + i) * heads + h
            s_s[row : row + 1, :64] = qv_ref[i : i + 1, h * 64 : h * 64 + 64]
    units = ub_ref.shape[0] // LANES
    s_s[4 * heads : 4 * heads + units, :] = ub_ref[...].astype(f32).reshape(units, LANES)
    o_s[...] = jnp.zeros_like(o_s)
    for i in range(SMALL):
        at = slice(i % 6 * LANES, (i % 6 + 1) * LANES)
        value = s_s[i : i + 1, :]
        high = value.astype(bf16).astype(f32)
        o_s[i // 6 : i // 6 + 1, at] = high
        o_s[8 + i // 6 : 9 + i // 6, at] = value - high
    small_ref[...] = o_s[...].astype(bf16)
    last = copy(small_ref, b_ref.at[half : half + 16, :], 4)
    last.start()

    @pl.when(odd == 0)
    def _():
        for c in firsts:
            c.wait()

    @pl.when(odd == 1)
    def _():
        for c in seconds:
            c.wait()

    for c in others + [last]:
        c.wait()


def start_parts(place, qkv, w_out, w_up, box, pos, qv, up):
    width = qkv.shape[1]
    vmem, hbm = (pl.BlockSpec(memory_space=m) for m in (pltpu.VMEM, pltpu.HBM))
    shapes = [(width // 2, width), (width // 2 + 16, width), (16, width)]
    return pl.pallas_call(
        start_kernel,
        in_specs=[pl.BlockSpec(memory_space=pltpu.SMEM)] + [hbm] * 3 + [vmem] * 4,
        out_specs=[vmem] * 3,
        out_shape=[jax.ShapeDtypeStruct(shape, bf16) for shape in shapes],
        scratch_shapes=[
            pltpu.VMEM((SMALL, LANES), f32),
            pltpu.VMEM((16, width), f32),
            pltpu.SemaphoreType.DMA((5,)),
        ],
        name="start_parts",
        cost_estimate=pl.CostEstimate(flops=0, bytes_accessed=0, transcendentals=0),
        compiler_params=pltpu.CompilerParams(vmem_limit_bytes=58 << 20),
    )(place, qkv, w_out, w_up, box.transpose(1, 0, 2), pos, qv, up)


def join_kernel(place_ref, mine_ref, theirs_ref, *refs):
    outs, sems = refs[:-1], refs[-1]
    half = outs[0].shape[0] // 2
    odd = place_ref[1]
    copies = []
    for i, out in enumerate(outs):
        for j, (ref, first) in enumerate(((mine_ref, odd * half), (theirs_ref, (1 - odd) * half))):
            to = out.at[pl.ds(pl.multiple_of(first, half), half), :]
            at = slice(i * half, (i + 1) * half)
            copies.append(pltpu.make_async_copy(ref.at[at, :], to, sems.at[i, j]))
    for c in copies:
        c.start()
    for c in copies:
        c.wait()


def join_rows(place, mine, theirs, number, rows):
    cols = mine.shape[1]
    vmem = pl.BlockSpec(memory_space=pltpu.VMEM)
    return pl.pallas_call(
        join_kernel,
        in_specs=[pl.BlockSpec(memory_space=pltpu.SMEM), vmem, vmem],
        out_specs=[vmem] * number,
        out_shape=[jax.ShapeDtypeStruct((rows, cols), bf16)] * number,
        scratch_shapes=[pltpu.SemaphoreType.DMA((number, 2))],
        name="join_rows",
        cost_estimate=pl.CostEstimate(flops=0, bytes_accessed=0, transcendentals=0),
        compiler_params=pltpu.CompilerParams(vmem_limit_bytes=8 << 20),
    )(place, mine, theirs)


def tn(a, b):
    return lax.dot_general(a, b, (((0,), (0,)), ((), ())), preferred_element_type=f32)


def parity_split(cur_ref, keep_ref, send_ref, first, chunk, bit):
    for mine in range(2):

        @pl.when(bit == mine)
        def _(mine=mine):
            for i in range(cur_ref.shape[0] // chunk // 2):
                to = slice(first + i * chunk, first + (i + 1) * chunk)
                at = (2 * i + mine) * chunk
                keep_ref[to, :] = cur_ref[at : at + chunk, :]
                at = (2 * i + 1 - mine) * chunk
                send_ref[to, :] = cur_ref[at : at + chunk, :]


def products_kernel(place_ref, *refs, lefts, plan, chunk):
    left, refs = refs[:lefts], list(refs[lefts:])
    rights = [[refs.pop(0) for _ in terms] for terms, _, _ in plan]
    gots = [[[refs.pop(0) for _ in range(n)] for n in counts] for _, counts, _ in plan]
    cur_s = refs.pop()
    split = 0
    for (terms, _, mode), right, got in zip(plan, rights, gots):
        outs = [cur_s] if mode == "halve" else [refs.pop(0) for _ in range(mode)]
        col = 0
        for (i, lanes), r in zip(terms, right):
            lanes = lanes or (0, r.shape[1])
            at = slice(col, col + lanes[1] - lanes[0])
            total = tn(left[i][...], r[:, lanes[0] : lanes[1]])
            for pieces in got:
                wide = [g[:, at].astype(f32) for g in pieces]
                total = total + (wide[0] if len(wide) == 1 else jnp.concatenate(wide, 0))
            rows = total.shape[0] // len(outs)
            for k, out in enumerate(outs):
                out[:, at] = total[k * rows : (k + 1) * rows].astype(bf16)
            col += lanes[1] - lanes[0]
        if mode == "halve":
            if split == 0:
                keep, send = refs.pop(0), refs.pop(0)
            parity_split(cur_s, keep, send, split, chunk, place_ref[1])
            split += cur_s.shape[0] // 2


def plain_split(place, cur, bit, chunk):
    view = cur.reshape(-1, 2, chunk, cur.shape[1])
    pick = lambda i: lax.dynamic_index_in_dim(view, i, axis=1, keepdims=False)
    mine = place[1 + bit]
    return tuple(pick(i).reshape(-1, cur.shape[1]) for i in (mine, 1 - mine))


def products(place, lefts, specs, chunk):
    width = lefts[0].shape[1]
    halved = sum(mode == "halve" for _, _, mode in specs)
    if chunk % 16 and halved:
        whole = products(place, lefts, [(t, g, 1) for t, g, _ in specs], chunk)
        parts = [plain_split(place, cur, 0, chunk) for cur in whole]
        return [jnp.concatenate(side, axis=0) for side in zip(*parts)]
    plan = [
        ([(t[0], t[2] if len(t) > 2 else None) for t in terms], [len(p) for p in gots], mode)
        for terms, gots, mode in specs
    ]
    args = [place, *lefts]
    args += [t[1] for terms, _, _ in specs for t in terms]
    args += [g for _, gots, _ in specs for pieces in gots for g in pieces]
    cols = sum(t[2][1] - t[2][0] if len(t) > 2 else t[1].shape[1] for t in specs[0][0])
    outs = []
    for _, _, mode in specs:
        if mode != "halve":
            outs += [((width // mode, cols), bf16)] * mode
    if halved:
        outs += [((halved * width // 2, cols), bf16)] * 2
    kernel = functools.partial(products_kernel, lefts=len(lefts), plan=plan, chunk=chunk)
    return call(kernel, "products", args, outs, [((width, cols), bf16)], smem=1)


def add_split_kernel(place_ref, *refs, number, bit, chunk):
    keep_ref, send_ref, cur_s = refs[2 * number :]
    first = 0
    for a, b in zip(refs[:number], refs[number : 2 * number]):
        rows = a.shape[0]
        cur_s[first : first + rows] = (a[...].astype(f32) + b[...].astype(f32)).astype(bf16)
        first += rows
    parity_split(cur_s, keep_ref, send_ref, 0, chunk, place_ref[1 + bit])


def add_split(place, keeps, gots, bit, chunk):
    rows, cols = sum(v.shape[0] for v in keeps), keeps[0].shape[1]
    if chunk % 16:
        parts = [(a.astype(f32) + b.astype(f32)).astype(bf16) for a, b in zip(keeps, gots)]
        return plain_split(place, jnp.concatenate(parts, axis=0), bit, chunk)
    half = ((rows // 2, cols), bf16)
    kernel = functools.partial(add_split_kernel, number=len(keeps), bit=bit, chunk=chunk)
    args = (place, *keeps, *gots)
    return call(kernel, "add_split", args, [half, half], [((rows, cols), bf16)], smem=1)


def tokens_kernel(d0, d1, d2, d3, w0, w1, w_ref, first_ref, out_ref):
    cols = d0.shape[1]
    total = first_ref[...] + nn(d0[...], w0[...]) + nn(d1[...], w1[...])
    total = total + nn(d2[...], w_ref[0, 0:cols, :]) + nn(d3[...], w_ref[1, 0:cols, :])
    out_ref[...] = total.astype(bf16)


def tokens_grad(dmixed, weights, d_first):
    args = (*dmixed, *weights, d_first)
    return call(tokens_kernel, "tokens_grad", args, [(d_first.shape, bf16)])[0]


SHARED = 40
EACH = 16


def pack_kernel(hist_ref, near_ref, far_ref, u0, u1, u2, u3, v0, v1, v2, v3, v4, v5, keep_ref, send_ref, *, heads):
    keep_ref[...] = jnp.zeros_like(keep_ref)
    send_ref[...] = jnp.zeros_like(send_ref)
    for g, up in enumerate((u0, u1, u2, u3)):
        ref, first = (keep_ref, send_ref)[g // 2], (g % 2) * EACH
        for h in range(heads):
            for i, part in ((0, 0), (1, 2)):
                col = (part * heads + h) * HEAD_DIM
                row = (near_ref, far_ref)[g // 2][g % 2 : g % 2 + 1, col : col + 64]
                ref[first + h : first + h + 1, i * 64 : i * 64 + 64] = row
            row = hist_ref[g * heads + h : g * heads + h + 1, :]
            ref[first + heads + h : first + heads + h + 1, :] = row[:, :LANES]
            ref[first + 2 * heads + h : first + 2 * heads + h + 1, :NB1] = row[:, LANES:]
        for i in range(6):
            at = slice(first + 3 * heads + i, first + 3 * heads + i + 1)
            ref[at, :] = up[:, i * LANES : (i + 1) * LANES]
    for j, v in enumerate((v0, v1, v2, v3, v4, v5)):
        for i in range(6):
            at = slice(2 * EACH + 6 * j + i, 2 * EACH + 6 * j + i + 1)
            row = v[:, i * LANES : (i + 1) * LANES]
            keep_ref[at, :] = row
            send_ref[at, :] = row


def pack_sums(hist, near, far, ups, shared):
    args = (hist, near, far, *(v.reshape(1, -1) for v in ups), *(v.reshape(1, -1) for v in shared))
    outs = [((2 * EACH + SHARED, LANES), f32)] * 2
    heads = near.shape[1] // (3 * HEAD_DIM)
    return call(functools.partial(pack_kernel, heads=heads), "pack_sums", args, outs)


def unpack_kernel(keep_ref, got_ref, qv_ref, pos_ref, box_ref, up_ref, *shared, heads):
    total = keep_ref[...] + got_ref[...]
    for h in range(heads):
        for i in range(2):
            qv_ref[i : i + 1, h * 64 : h * 64 + 64] = total[h : h + 1, i * 64 : i * 64 + 64]
            box_ref[h, i : i + 1, :] = total[heads + h : heads + h + 1, i * NB2 : (i + 1) * NB2]
        pos_ref[h : h + 1, :] = total[2 * heads + h : 2 * heads + h + 1, :NB1]
    units = up_ref.shape[0] // LANES
    up_ref[...] = total[3 * heads : 3 * heads + units].reshape(up_ref.shape)
    for j, ref in enumerate(shared):
        rows = ref.shape[0] // LANES
        ref[...] = total[EACH + j * rows : EACH + (j + 1) * rows].reshape(ref.shape)


def unpack_sums(keep, got, heads, units, width):
    outs = [((2, heads * HEAD_DIM), f32), ((heads, NB1), f32), ((heads, 2, NB2), f32), ((units,), f32)]
    outs += [((width,), f32)] * 6
    return call(functools.partial(unpack_kernel, heads=heads), "unpack_sums", (keep, got), outs)


def last_kernel(keep_ref, got_ref, qkv_ref, out_ref):
    inner = qkv_ref.shape[2]
    for part in range(3):
        at = slice(part * inner, (part + 1) * inner)
        qkv_ref[part] = keep_ref[:, at].astype(f32) + got_ref[:, at].astype(f32)
    at = slice(3 * inner, 4 * inner)
    out_ref[...] = (keep_ref[:, at].astype(f32) + got_ref[:, at].astype(f32)).T


def last_sums(place, keep, got, bit, chunk):
    inner = keep.shape[1] // 4
    if chunk % 16 == 0 and lax.axis_size("pages") == 2 << bit:
        outs = [((3, chunk, inner), f32), ((inner, chunk), f32)]
        qkv, out = call(last_kernel, "last_sums", (keep, got), outs)
        return qkv.transpose(1, 0, 2), out
    total = finish(place, keep, got, bit, chunk)
    return total[:, : 3 * inner].reshape(-1, 3, inner), total[:, 3 * inner :].T


def core_swap(v):
    return lax.ppermute(v, "heads", [(i, i ^ 1) for i in range(4)])


def x_swap(v):
    return lax.ppermute(v, "heads", [(i, i ^ 2) for i in range(4)])


def page_swap(v, bit):
    return lax.ppermute(v, "pages", [(i, i ^ bit) for i in range(lax.axis_size("pages"))])


def after(value, *others):
    return lax.optimization_barrier((value, *others))[0]


def finish(place, keep, got, bit, chunk):
    last = lax.axis_size("pages").bit_length() - 1
    while bit + 1 < last:
        bit += 1
        keep, send = add_split(place, [keep], [got], bit, chunk)
        got = page_swap(send, 1 << bit)
    return keep.astype(f32) + got.astype(f32)


def add_all(v, bits):
    for bit in bits:
        v = v + page_swap(v, bit)
    return v


def unit_norm(values):
    centered = values - jnp.mean(values, axis=-1, keepdims=True)
    inv_std = lax.rsqrt(jnp.mean(centered * centered, axis=-1, keepdims=True) + EPSILON)
    return centered * inv_std, inv_std


def norm_grad(unit, inv_std, e):
    return inv_std * (
        e - jnp.mean(e, axis=-1, keepdims=True) - unit * jnp.mean(e * unit, axis=-1, keepdims=True)
    )


def on_device(
    tokens,
    w_qkv,
    qv_bias,
    w_out,
    out_bias,
    norm1_gain,
    norm1_shift,
    w_up,
    up_bias,
    w_down,
    down_bias,
    norm2_gain,
    norm2_shift,
    pos_table,
    box_table,
    receipt_lengths,
    page_boxes,
    out_cotangent,
):
    seq_len = tokens.shape[1]
    width = tokens.shape[2]
    heads_here = pos_table.shape[0]
    inner = heads_here * HEAD_DIM
    units = w_up.shape[1]
    own_page = lax.axis_index("heads")
    page_bits = [1 << b for b in range(lax.axis_size("pages").bit_length() - 1)]
    chunk = width // lax.axis_size("pages")
    me = lax.axis_index("pages")
    place = jnp.stack([own_page] + [(me >> b) & 1 for b in range(len(page_bits))]).astype(i32)
    tok = tokens.reshape(seq_len, width)

    own_qkv = w_qkv.reshape(width, 3 * inner).T
    c_qkv, c_out = core_swap(own_qkv), core_swap(w_out)
    half_a, half_b, small = start_parts(
        place, own_qkv, w_out, w_up, box_table, pos_table, qv_bias, up_bias
    )
    c_small = core_swap(small)
    mine_a = x_swap(half_a)
    mine_b = x_swap(half_b)
    x_down = x_swap(w_down)
    ids, vis_ids, some = make_ids(place, receipt_lengths, page_boxes)
    mine_a = after(mine_a, ids)

    near_w = ((own_qkv,), (after(c_qkv, mine_a),))
    near_att, near_bias, near_out, near_kept = attn_fwd(
        place, tok, near_w, (small, c_small), (ids, vis_ids), heads_here, (w_out, c_out)
    )
    half = width // 2
    theirs_a = page_swap(mine_a, 1)
    xc_mine_a, xc_theirs_a = core_swap(mine_a), core_swap(after(theirs_a, near_att))
    theirs_b = page_swap(after(mine_b, near_att), 1)
    xc_mine_b = core_swap(after(mine_b, near_att))
    far_w = ((mine_a, theirs_a), (after(xc_mine_a, xc_mine_b), xc_theirs_a))
    far_att, far_bias, far_out, far_kept, far_w = attn_fwd(
        place, tok, far_w, (mine_b, xc_mine_b), (ids, vis_ids), heads_here
    )
    far_proj = nn(far_att, far_out)
    c_up, c_down = core_swap(after(w_up, far_proj)), core_swap(after(w_down, far_proj))
    mine_b, theirs_b = lax.optimization_barrier((mine_b, theirs_b, far_proj))[:2]
    xc_theirs_b = core_swap(theirs_b)
    first_in = nn(near_att, near_out) + far_proj + out_bias + tok.astype(f32)
    unit1, inv1 = unit_norm(first_in)
    first_out = unit1 * norm1_gain + norm1_shift
    first_low = first_out.astype(bf16)

    def units_of(weights, little):
        up = nn(first_low, weights) + little
        cdf = 0.5 * (1.0 + lax.erf(up * math.sqrt(0.5)))
        slope = cdf + up * jnp.exp(-0.5 * up * up) * (1.0 / math.sqrt(2.0 * math.pi))
        return (up * cdf).astype(bf16), lax.optimization_barrier(slope.astype(bf16))

    littles = (near_bias[0], near_bias[1], far_bias[0], far_bias[1])
    own_units = units_of(w_up, littles[0])
    theirs_b = after(theirs_b, own_units[0])
    (x_up,) = join_rows(place, mine_b, theirs_b, 1, width)
    c_units = units_of(after(c_up, theirs_b), littles[1])
    (xc_up,) = join_rows(place, xc_mine_b, after(xc_theirs_b, x_up), 1, width)
    far_units = [units_of(w, t) for w, t in zip((x_up, xc_up), littles[2:])]
    hiddens, slopes = zip(own_units, c_units, *far_units)
    x_down = after(x_down, *hiddens)
    xc_down = core_swap(x_down)
    ups, downs = (w_up, c_up, x_up, xc_up), (w_down, c_down, x_down, xc_down)
    second_in = sum(nn(h, w) for h, w in zip(hiddens, downs)) + down_bias + first_out
    unit2, inv2 = unit_norm(second_in)
    layer_out = (unit2 * norm2_gain + norm2_shift).astype(bf16)

    def norm_back(unit, inv_std, gain, dy):
        return norm_grad(unit, inv_std, dy * gain), jnp.sum(dy * unit, axis=0), jnp.sum(dy, axis=0)

    ct = out_cotangent.reshape(seq_len, width).astype(f32)
    d_second, g_gain2, g_shift2 = norm_back(unit2, inv2, norm2_gain, ct)
    g_down_bias = jnp.sum(d_second, axis=0)
    d_ffn = d_second.astype(bf16)

    def core_swaps(pieces):
        return [core_swap(v) for v in pieces]

    to_c = products(
        place, [d_ffn], [([(0, hiddens[3])], [], 2), ([(0, hiddens[1])], [], 2)], chunk
    )
    got_xc, got_c = core_swaps(to_c[:2]), core_swaps(to_c[2:])
    d_ups = [(nt(d_ffn, w) * s.astype(f32)).astype(bf16) for w, s in zip(downs, slopes)]
    far_gd, own_gd = products(
        place,
        [after(d_ffn, *d_ups)],
        [([(0, hiddens[2])], [got_xc], 1), ([(0, hiddens[0])], [got_c], 1)],
        chunk,
    )
    got_xd = x_swap(far_gd)

    to_c = products(
        place,
        [after(first_low, far_gd)],
        [([(0, d_ups[3])], [], 2), ([(0, d_ups[1])], [], 2)],
        chunk,
    )
    got_xc, got_c = core_swaps(to_c[:2]), core_swaps(to_c[2:])
    d_mid = nt(d_ups[3], ups[3]) + nt(d_ups[1], ups[1])
    d_mid, d_own = lax.optimization_barrier((d_mid, d_ups[0], *to_c))[:2]
    d_mid = lax.optimization_barrier(d_mid + nt(d_own, ups[0])) + nt(d_ups[2], ups[2])
    keep_u, send_u = products(
        place,
        [after(first_low, d_mid)],
        [([(0, d_ups[0])], [got_c], "halve"), ([(0, d_ups[2])], [got_xc], "halve")],
        chunk,
    )
    got_yu = page_swap(send_u, 1)
    d_first, g_gain1, g_shift1 = norm_back(unit1, inv1, norm1_gain, after(d_second, send_u) + d_mid)
    g_out_bias = jnp.sum(d_first, axis=0)
    d_proj = d_first.astype(bf16)
    far_datt = nt(d_proj, far_out).astype(bf16)
    x_dmixed, xc_dmixed, far_sums, far_ds, far_dsv = attn_bwd(seq_len, far_kept, far_datt)

    lefts = [tok, d_proj]
    low, high = (0, inner), (inner, 2 * inner)
    to_c = products(place, lefts, [([(0, xc_dmixed), (1, far_att, high)], [], 2)], chunk)
    got_xc = core_swaps(to_c)
    near_datt = nt(after(d_proj, *to_c), near_out).astype(bf16)
    (far_gq,) = products(
        place, [after(tok, near_datt), d_proj], [([(0, x_dmixed), (1, far_att, low)], [got_xc], 1)], chunk
    )
    got_xq = x_swap(far_gq)
    own_dmixed, c_dmixed, near_sums, near_ds, near_dsv = attn_bwd(
        seq_len, near_kept, after(near_datt, far_gq)
    )
    dmixed = (own_dmixed, c_dmixed, x_dmixed, xc_dmixed)

    got_xd, got_yu = lax.optimization_barrier((got_xd, got_yu, near_sums))[:2]
    keep_d, send_d = add_split(place, [own_gd], [got_xd], 0, chunk)
    got_yd = page_swap(send_d, 1)
    keep_u, send_u = add_split(place, [keep_u], [got_yu], 1, chunk)
    got_zu = page_swap(send_u, 2)
    to_c = products(
        place,
        [after(tok, send_u, send_d), d_proj],
        [([(0, c_dmixed), (1, near_att, high)], [], 2)],
        chunk,
    )
    got_cq = core_swaps(to_c)
    text, near_far = (near_ds, far_ds), (near_dsv, far_dsv)
    acc = after(jnp.zeros((16, 160), f32), *to_c)
    acc = add_hist(acc, ids, some, text, 0, SPAN // 2)
    keep_q, send_q = products(
        place,
        [after(tok, acc), d_proj],
        [([(0, own_dmixed), (1, near_att, low)], [got_cq, [got_xq]], "halve")],
        chunk,
    )
    got_yq = page_swap(send_q, 1)
    keep_u, send_u = add_split(place, [keep_u], [after(got_zu, send_q)], 2, chunk)
    got_zu = page_swap(send_u, 4)
    keep_d, send_d = add_split(place, [keep_d], [after(got_yd, send_u)], 1, chunk)
    got_zd = page_swap(send_d, 2)
    acc = add_hist(after(acc, send_q, send_d), ids, some, text, SPAN // 2, SPAN // 2)
    acc = add_visual(acc, vis_ids, near_far)
    g_up_bias = [jnp.sum(d.astype(f32), axis=0) for d in d_ups]
    shared = (g_out_bias, g_gain1, g_shift1, g_down_bias, g_gain2, g_shift2)
    keep, send = pack_sums(acc, near_sums, far_sums, g_up_bias, shared)
    got = x_swap(send)
    keep_q, send_q = add_split(place, [keep_q], [after(got_yq, send)], 1, chunk)
    got_zq = page_swap(send_q, 2)
    keep_d, send_d = add_split(place, [keep_d], [after(got_zd, send_q)], 2, chunk)
    got_zd = page_swap(send_d, 4)
    got_zu = after(got_zu, send_d)
    both_u = finish(place, keep_u, got_zu, 2, chunk)
    got_xu = x_swap(both_u[chunk:].astype(bf16))
    sums = keep + after(got, send_d)
    sums = jnp.concatenate((sums[:EACH], sums[2 * EACH :])) + core_swap(sums[EACH:])
    got = page_swap(sums, 1)
    grad_tokens = tokens_grad(dmixed, (own_qkv, c_qkv, after(far_w, sums)), d_first)
    sums = sums + after(got, grad_tokens)
    got = page_swap(sums, 2)
    keep_q, send_q = add_split(place, [keep_q], [after(got_zq, sums)], 2, chunk)
    got_zq = page_swap(send_q, 4)
    sums = sums + after(got, send_q)
    got = page_swap(sums, 4)
    for bit in page_bits[3:]:
        sums = sums + got
        got = page_swap(sums, bit)
    got_zd, got_xu = lax.optimization_barrier((got_zd, got_xu, sums))[:2]
    g_w_down = finish(place, keep_d, got_zd, 2, chunk).T
    g_w_up = both_u[:chunk] + got_xu.astype(f32)
    got, got_zq, g_w_down, g_w_up = lax.optimization_barrier((got, got_zq, g_w_down, g_w_up))
    g_w_qkv, g_w_out = last_sums(place, keep_q, got_zq, 2, chunk)
    g_qv_bias, g_pos, g_box, g_up_bias, *shared = unpack_sums(sums, got, heads_here, units, width)
    g_box = g_box.transpose(1, 0, 2)
    return (
        layer_out.reshape(tokens.shape),
        grad_tokens.reshape(tokens.shape),
        g_w_qkv,
        g_qv_bias,
        g_w_out,
        shared[0],
        shared[1],
        shared[2],
        g_w_up,
        g_up_bias,
        g_w_down,
        shared[3],
        shared[4],
        shared[5],
        g_pos,
        g_box,
    )


def solution(mesh):
    placed = (
        P(("pages", "heads"), None, None),
        P(None, None, "heads"),
        P(None, "heads"),
        P("heads", None),
        P(),
        P(),
        P(),
        P(None, "heads"),
        P("heads"),
        P("heads", None),
        P(),
        P(),
        P(),
        P("heads", None),
        P(None, "heads", None),
        P("pages", None),
        P("pages", None, None),
        P(("pages", "heads"), None, None),
    )
    return jax.shard_map(
        on_device,
        mesh=mesh,
        in_specs=placed,
        out_specs=(
            P(("pages", "heads"), None, None),
            P(("pages", "heads"), None, None),
            P("pages", None, "heads"),
            P(None, "heads"),
            P("heads", "pages"),
            P(),
            P(),
            P(),
            P("pages", "heads"),
            P("heads"),
            P("heads", "pages"),
            P(),
            P(),
            P(),
            P("heads", None),
            P(None, "heads", None),
        ),
        check_vma=False,
    )
```
